32 devices in a mesh: ctx: 8 (over z, x), head: 4 (over y, core).
Axes of the slice: x: 2, y: 2, z: 4, core: 2. Of those that a mesh axis runs over, the one named last changes fastest.
Arguments:
- queries: bfloat16 [1024, 4096], P('ctx', 'head'), may hold values from -40 to 40
- keys: bfloat16 [1024, 4096], P('ctx', 'head'), may hold values from -40 to 40
- values: bfloat16 [1024, 4096], P('ctx', 'head'), may hold values from -50 to 50
- pattern: int32 [8, 8], replicated, may hold values from -1 to 7, as said below
- upstream: bfloat16 [1024, 4096], P('ctx', 'head'), may hold values from -6 to 6
Outputs:
- normed: bfloat16 [1024, 4096], P('ctx', 'head')
- grad_queries: bfloat16 [1024, 4096], P('ctx', 'head')
- grad_keys: bfloat16 [1024, 4096], P('ctx', 'head')
- grad_values: bfloat16 [1024, 4096], P('ctx', 'head')
The draws below stay inside these ranges and needn't reach their ends.
Inputs may be any that keep to these rules, and one draw needn't show every extreme that they name: `pattern`: entry [i, k] for k < 7 is either i - 2^k or -1, and always -1 where i < 2^k; entry [i, 7] is i.
All inputs are finite; a program needn't handle non-finite values.
Results may differ from the reference program's by a relative error of at most 0.04.
Values may be sent and summed in bfloat16 or wider, within the bound.
No kernel may reach another device: no remote copies, remote signals or barrier semaphores. Data moves between devices by JAX's collectives and lax.ppermute only.
A program may use at most 64 MiB of HBM per device.

```python
import jax
import jax.numpy as jnp
from jax import lax

HEADS = 32
HD = 128
BLOCK = 128
LEVELS = 7
TOKENS = 1024
WIDTH = 4096


def base_field(key):
    return jnp.clip(jax.random.normal(key, (TOKENS, HEADS * HD), jnp.float32), -4.0, 4.0)


def draw_queries(key, part):
    field = base_field(jax.random.fold_in(key, 1))
    return field.astype(jnp.bfloat16)


def draw_keys(key, part):
    field = base_field(jax.random.fold_in(key, 2))
    return field.astype(jnp.bfloat16)


def draw_values(key, part):
    field = base_field(jax.random.fold_in(key, 3))
    head_ids = (jnp.arange(HEADS * HD)[None, :] // HD).astype(jnp.float32)
    rising = head_ids / (HEADS - 1)
    head_scale = 3.0 ** rising
    row_scale = jnp.exp(jax.random.uniform(jax.random.fold_in(key, 4), (TOKENS, 1), jnp.float32, 0.0, 1.0986))
    return (field * head_scale * row_scale).astype(jnp.bfloat16)


def draw_pattern(key, part):
    blocks_all = TOKENS // BLOCK
    block_rows = jnp.arange(blocks_all, dtype=jnp.int32)[:, None]
    distances = (2 ** jnp.arange(LEVELS, dtype=jnp.int32))[None, :]
    kept_bits = jax.random.randint(key, (blocks_all, LEVELS), 0, 4) > 0
    target = block_rows - distances
    entries = jnp.where(kept_bits & (target >= 0), target, -1)
    return jnp.concatenate([entries, block_rows], axis=1).astype(jnp.int32)


def steps_of(own_key, dims, split, least, largest):
    loudness, own = 1.0, jax.random.fold_in(own_key, 6)
    for axis_at, blocks in split:
        steps = jnp.exp(jax.random.uniform(jax.random.fold_in(own, axis_at), (blocks,), jnp.float32, least / len(split), largest / len(split)))
        loudness = loudness * jnp.repeat(steps, dims[axis_at] // blocks).reshape([-1 if axis == axis_at else 1 for axis in range(len(dims))])
    return loudness


def normal_values(stream_key, dims, width, limit, split=(), held_as=jnp.bfloat16):
    array = width * jax.random.normal(stream_key, dims, jnp.float32)
    if split:
        array = array * steps_of(stream_key, dims, split, -0.22, 0.18)
    return jnp.clip(array, -limit, limit).astype(held_as)


def setup_inputs(seed: int = 0) -> dict:
    arg_keys = jax.random.split(jax.random.key(seed), 6)
    return {
        "queries": draw_queries(jax.random.fold_in(arg_keys[5], 71), 0),
        "keys": draw_keys(jax.random.fold_in(arg_keys[5], 71), 0),
        "values": draw_values(jax.random.fold_in(arg_keys[5], 71), 0),
        "pattern": draw_pattern(jax.random.fold_in(arg_keys[5], 71), 0),
        "upstream": normal_values(arg_keys[4], (TOKENS, WIDTH), 1.0, 6.0, ((0, 8), (1, 4))),
    }


NEG_BIG = -1e+30
EPSILON = 1e-06

def reference(queries, keys, values, pattern, upstream):
    block_count = TOKENS // BLOCK
    slot_count = LEVELS + 1
    score_scale = HD ** (-0.5)
    shape_blocks = (block_count, BLOCK, HEADS, HD)
    query_blocks = queries.reshape(shape_blocks)
    key_blocks = keys.reshape(shape_blocks)
    value_blocks = values.reshape(shape_blocks)
    positions = jnp.arange(BLOCK)
    causal = positions[None, :] <= positions[:, None]
    self_slot = jnp.arange(slot_count) == LEVELS

    def tiles_of(block_index):
        entries = pattern[block_index]
        live_slots = entries >= 0
        safe_index = jnp.maximum(entries, 0)
        keep_mask = live_slots[:, None, None] & (jnp.logical_not(self_slot)[:, None, None] | causal[None])
        return (safe_index, keep_mask)

    def scores_of(block_index, safe_index, keep_mask):
        key_tiles = key_blocks[safe_index].astype(jnp.float32)
        scores = jnp.einsum('qhd,skhd->hqsk', query_blocks[block_index].astype(jnp.float32), key_tiles) * score_scale
        return jnp.where(jnp.transpose(keep_mask, (1, 0, 2))[None], scores, NEG_BIG)

    def forward_block(block_index):
        safe_index, keep_mask = tiles_of(block_index)
        scores = scores_of(block_index, safe_index, keep_mask)
        highest = lax.optimization_barrier(jnp.max(scores, axis=(2, 3)))
        log_total = highest + jnp.log(lax.optimization_barrier(jnp.sum(jnp.exp(scores - highest[:, :, None, None]), axis=(2, 3))))
        prob_tiles = jnp.exp(scores - log_total[:, :, None, None]).astype(jnp.bfloat16)
        attention = jnp.einsum('hqsk,skhd->qhd', prob_tiles.astype(jnp.float32), value_blocks[safe_index].astype(jnp.float32))
        return (attention.astype(jnp.bfloat16), log_total)
    attention, log_total = lax.map(forward_block, jnp.arange(block_count))
    attn_wide = attention.reshape(TOKENS, WIDTH).astype(jnp.float32)
    square_sum = lax.optimization_barrier(jnp.sum(attn_wide * attn_wide, axis=1))
    inverse = lax.rsqrt(square_sum / WIDTH + EPSILON)
    normed = (attn_wide * inverse[:, None]).astype(jnp.bfloat16)
    upstream_wide = upstream.astype(jnp.float32)
    cross_term = lax.optimization_barrier(jnp.sum(upstream_wide * attn_wide, axis=1))
    grad_attn = (inverse[:, None] * upstream_wide - attn_wide * (inverse ** 3 * cross_term / WIDTH)[:, None]).astype(jnp.bfloat16)
    row_delta = lax.optimization_barrier(jnp.sum((grad_attn.astype(jnp.float32) * attn_wide).reshape(TOKENS, HEADS, HD), axis=2))
    row_delta = jnp.transpose(row_delta.reshape(block_count, BLOCK, HEADS), (0, 2, 1))
    grad_blocks = grad_attn.reshape(shape_blocks)

    def backward_block(accumulated, block_index):
        key_sum, value_sum = accumulated
        safe_index, keep_mask = tiles_of(block_index)
        scores = scores_of(block_index, safe_index, keep_mask)
        weights = jnp.exp(scores - log_total[block_index][:, :, None, None])
        prob_tiles = weights.astype(jnp.bfloat16)
        grad_here = grad_blocks[block_index].astype(jnp.float32)
        grad_probs = jnp.einsum('qhd,skhd->hqsk', grad_here, value_blocks[safe_index].astype(jnp.float32))
        dscore = (weights * (grad_probs - row_delta[block_index][:, :, None, None]) * score_scale).astype(jnp.bfloat16)
        dscore_wide = dscore.astype(jnp.float32)
        grad_query = jnp.einsum('hqsk,skhd->qhd', dscore_wide, key_blocks[safe_index].astype(jnp.float32))
        key_part = jnp.einsum('hqsk,qhd->skhd', dscore_wide, query_blocks[block_index].astype(jnp.float32))
        value_part = jnp.einsum('hqsk,qhd->skhd', prob_tiles.astype(jnp.float32), grad_here)
        key_sum = key_sum.at[safe_index].add(key_part)
        value_sum = value_sum.at[safe_index].add(value_part)
        return ((key_sum, value_sum), grad_query.astype(jnp.bfloat16))
    zeros_init = jnp.zeros(shape_blocks, jnp.float32)
    (key_sum, value_sum), grad_query = lax.scan(backward_block, (zeros_init, zeros_init), jnp.arange(block_count))
    grad_queries = grad_query.reshape(TOKENS, WIDTH)
    grad_keys = key_sum.astype(jnp.bfloat16).reshape(TOKENS, WIDTH)
    grad_values = value_sum.astype(jnp.bfloat16).reshape(TOKENS, WIDTH)
    return (normed, grad_queries, grad_keys, grad_values)
```

```python
import functools

import jax
import jax.numpy as jnp
from jax import lax
from jax.experimental import pallas as pl
from jax.experimental.pallas import tpu as pltpu
from jax.sharding import PartitionSpec as P

HD = 128
BLOCK = 128
LEVELS = 7
WIDTH = 4096


NEG_BIG = -1e30
EPSILON = 1e-06


def shifted(block, axis, distance):
    devices = range(lax.axis_size(axis))
    route = [(i - distance, i) for i in devices if i - distance in devices]
    return lax.ppermute(block, axis, route)


def for_sending(x):
    return jax.tree.map(lambda a: a.astype(jnp.bfloat16) if a.dtype == jnp.float32 else a, x)


def route_table(blocks, levels):
    routing = []
    for query_block in range(blocks):
        for level_index in range(levels + 1):
            if level_index == levels:
                routing.append((0, query_block))
            else:
                distance = 2**level_index
                routing.append(
                    (-((query_block - distance) // blocks), (query_block - distance) % blocks)
                )
    return routing


def pair_grads(
    query_tiles, grad_tiles, lse_tiles, delta_tiles, key_tiles, value_tiles, keep_mask, score_scale
):
    scores = (
        jnp.einsum("pqhd,pkhd->phqk", query_tiles, key_tiles, preferred_element_type=jnp.float32)
        * score_scale
    )
    scores = jnp.where(keep_mask[:, None], scores, NEG_BIG)
    weights = jnp.exp(scores - lse_tiles[..., None])
    prob_tiles = weights.astype(jnp.bfloat16)
    grad_probs = jnp.einsum(
        "pqhd,pkhd->phqk", grad_tiles, value_tiles, preferred_element_type=jnp.float32
    )
    dscore = (weights * (grad_probs - delta_tiles[..., None]) * score_scale).astype(jnp.bfloat16)
    return (dscore, prob_tiles)


def key_grads(dscore, prob_tiles, query_tiles, grad_tiles):
    key_part = jnp.einsum(
        "phqk,pqhd->pkhd", dscore, query_tiles, preferred_element_type=jnp.float32
    )
    value_part = jnp.einsum(
        "phqk,pqhd->pkhd", prob_tiles, grad_tiles, preferred_element_type=jnp.float32
    )
    return jnp.stack((key_part, value_part))


def collect(partials, targets, blocks):
    pieces = []
    for key_index in range(blocks):
        summed = jnp.zeros((2,) + partials.shape[2:], jnp.float32)
        for row_index, target in enumerate(targets):
            if target == key_index:
                summed = summed + partials[:, row_index]
        pieces.append(summed)
    return jnp.stack(pieces, axis=1)


def generic_shards(queries, keys, values, pattern, upstream):
    tokens_here = queries.shape[0]
    heads_here = queries.shape[1] // HD
    blocks = tokens_here // BLOCK
    slot_count = LEVELS + 1
    pair_count = blocks * slot_count
    score_scale = HD ** (-0.5)
    ctx_count = lax.axis_size("ctx")
    device_index = lax.axis_index("ctx")
    routing = route_table(blocks, LEVELS)
    offsets = sorted(
        set((route_entry[0] for route_entry in routing if 0 < route_entry[0] < ctx_count))
    )
    tile_shape = (blocks, BLOCK, heads_here, HD)
    query_blocks = queries.reshape(tile_shape)
    own_pairs = jnp.stack((keys, values)).reshape((2,) + tile_shape)
    sources = {0: own_pairs}
    for offset in offsets:
        fetched = shifted(jnp.stack((keys, values)), "ctx", offset)
        sources[offset] = fetched.reshape((2,) + tile_shape)
    empty_tile = jnp.zeros((2, BLOCK, heads_here, HD), jnp.bfloat16)
    gathered = []
    for source, key_index in routing:
        if source in sources:
            gathered.append(sources[source][:, key_index])
        else:
            gathered.append(empty_tile)
    pair_kv = jnp.stack(gathered, axis=1)
    key_tiles = pair_kv[0]
    value_tiles = pair_kv[1]
    key_stack = key_tiles.reshape((blocks, slot_count) + tile_shape[1:])
    value_stack = value_tiles.reshape((blocks, slot_count) + tile_shape[1:])
    own_rows = lax.dynamic_slice_in_dim(pattern, device_index * blocks, blocks, 0)
    positions = jnp.arange(BLOCK)
    causal = positions[None, :] <= positions[:, None]
    self_slot = jnp.arange(slot_count) == LEVELS
    tile_keep = (own_rows >= 0)[:, :, None, None] & (
        jnp.logical_not(self_slot)[None, :, None, None] | causal[None, None]
    )
    scores = (
        jnp.einsum("bqhd,bskhd->bhqsk", query_blocks, key_stack, preferred_element_type=jnp.float32)
        * score_scale
    )
    scores = jnp.where(jnp.transpose(tile_keep, (0, 2, 1, 3))[:, None], scores, NEG_BIG)
    highest = jnp.max(scores, axis=(3, 4))
    log_total = highest + jnp.log(jnp.sum(jnp.exp(scores - highest[..., None, None]), axis=(3, 4)))
    prob_stack = jnp.exp(scores - log_total[..., None, None]).astype(jnp.bfloat16)
    attention = jnp.einsum(
        "bhqsk,bskhd->bqhd", prob_stack, value_stack, preferred_element_type=jnp.float32
    ).astype(jnp.bfloat16)
    attn_wide = attention.reshape(tokens_here, heads_here * HD).astype(jnp.float32)
    square_sum = lax.psum(jnp.sum(attn_wide * attn_wide, axis=1), "head")
    inverse = lax.rsqrt(square_sum / WIDTH + EPSILON)
    normed = (attn_wide * inverse[:, None]).astype(jnp.bfloat16)
    upstream_wide = upstream.astype(jnp.float32)
    cross_term = lax.psum(jnp.sum(upstream_wide * attn_wide, axis=1), "head")
    grad_attn = (
        inverse[:, None] * upstream_wide - attn_wide * (inverse**3 * cross_term / WIDTH)[:, None]
    ).astype(jnp.bfloat16)
    row_delta = jnp.sum(
        (grad_attn.astype(jnp.float32) * attn_wide).reshape(tokens_here, heads_here, HD), axis=2
    )
    row_delta = jnp.transpose(row_delta.reshape(blocks, BLOCK, heads_here), (0, 2, 1))

    def spread(array):
        return jnp.broadcast_to(array[:, None], (blocks, slot_count) + array.shape[1:]).reshape(
            (pair_count,) + array.shape[1:]
        )

    grad_blocks = grad_attn.reshape(tile_shape)
    query_pairs = spread(query_blocks)
    grad_pairs = spread(grad_blocks)
    keep_pairs = tile_keep.reshape(pair_count, BLOCK, BLOCK)
    dscore, prob_pairs = pair_grads(
        query_pairs,
        grad_pairs,
        spread(log_total),
        spread(row_delta),
        key_tiles,
        value_tiles,
        keep_pairs,
        score_scale,
    )
    grad_query = jnp.einsum(
        "phqk,pkhd->pqhd", dscore, key_tiles, preferred_element_type=jnp.float32
    )
    grad_query = jnp.sum(grad_query.reshape((blocks, slot_count) + tile_shape[1:]), axis=1)
    grad_queries = grad_query.astype(jnp.bfloat16).reshape(tokens_here, heads_here * HD)
    local_rows = [row_index for row_index in range(pair_count) if routing[row_index][0] == 0]
    chosen = jnp.array(local_rows, jnp.int32)
    local_terms = key_grads(
        dscore[chosen], prob_pairs[chosen], query_pairs[chosen], grad_pairs[chosen]
    )
    key_sum = collect(local_terms, [routing[row_index][1] for row_index in local_rows], blocks)
    for offset in offsets:
        remote_rows = [
            row_index for row_index in range(pair_count) if routing[row_index][0] == offset
        ]
        chosen = jnp.array(remote_rows, jnp.int32)
        remote_terms = key_grads(
            dscore[chosen], prob_pairs[chosen], query_pairs[chosen], grad_pairs[chosen]
        )
        outgoing = collect(
            remote_terms, [routing[row_index][1] for row_index in remote_rows], blocks
        )
        key_sum = key_sum + shifted(for_sending(outgoing), "ctx", -offset).astype(outgoing.dtype)
    grad_keys = key_sum[0].astype(jnp.bfloat16).reshape(tokens_here, heads_here * HD)
    grad_values = key_sum[1].astype(jnp.bfloat16).reshape(tokens_here, heads_here * HD)
    return (normed, grad_queries, grad_keys, grad_values)


NT = (((1,), (1,)), ((), ()))
NN = (((1,), (0,)), ((), ()))
TN = (((0,), (0,)), ((), ()))
SCALE = HD ** (-0.5)
PACK = 128


def mm(a, b, dims):
    return lax.dot_general(a, b, dims, preferred_element_type=jnp.float32)


def lane_ids(shape):
    return lax.broadcasted_iota(jnp.int32, shape, len(shape) - 1)


def causal_mask():
    rows = lax.broadcasted_iota(jnp.int32, (BLOCK, BLOCK), 0)
    return lane_ids((BLOCK, BLOCK)) <= rows


def pack_columns(columns):
    count = len(columns)
    lanes = lane_ids((BLOCK, PACK))
    wide = jnp.zeros((BLOCK, PACK), jnp.float32)
    for index, column in enumerate(columns):
        wide = jnp.where(lanes % count == index, column, wide)
    first = wide.astype(jnp.bfloat16)
    left = wide - first.astype(jnp.float32)
    second = left.astype(jnp.bfloat16)
    third = (left - second.astype(jnp.float32)).astype(jnp.bfloat16)
    return jnp.where(lanes < count, first, jnp.where(lanes < 2 * count, second, third))


def unpack_column(tile, count, index):
    wide = tile.astype(jnp.float32)
    return (
        wide[:, index : index + 1]
        + wide[:, count + index : count + index + 1]
        + wide[:, 2 * count + index : 2 * count + index + 1]
    )


def pair_flags(me_ref, pattern_ref):
    me = me_ref[0]
    blocks = pattern_ref.shape[0]
    odd = lax.rem(me, 2)
    ahead = jnp.minimum(me + 2, blocks - 1)
    partner = me + 1 - 2 * odd
    near = pattern_ref[me, 1] >= 0
    far = jnp.logical_and(me + 2 < blocks, pattern_ref[ahead, 2] >= 0)
    side = jnp.logical_and(jnp.logical_or(odd == 0, me >= 2), pattern_ref[partner, 0] >= 0)
    return odd, near, far, side


def softmax_part(score_list, value_list):
    highest = score_list[0].max(axis=1, keepdims=True)
    for scores in score_list[1:]:
        highest = jnp.maximum(highest, scores.max(axis=1, keepdims=True))
    total, out = 0.0, 0.0
    for scores, value in zip(score_list, value_list):
        weights = jnp.exp(scores - highest)
        total = total + weights.sum(axis=1, keepdims=True)
        out = out + mm(weights.astype(jnp.bfloat16), value, NN)
    return out / total, highest + jnp.log(total)


def forward_kernel(
    heads, me_ref, pattern_ref, q_ref, qz_ref, qx_ref, k_ref, v_ref, k2_ref, v2_ref, own_ref, lse_ref, oz_ref, ox_ref
):
    odd, near, _, _ = pair_flags(me_ref, pattern_ref)
    causal = causal_mask()
    own_lse, z_lse, x_lse = [], [], []
    for h in range(heads):
        at = slice(h * HD, (h + 1) * HD)
        k, v, k2, v2 = k_ref[:, at], v_ref[:, at], k2_ref[:, at], v2_ref[:, at]
        q = q_ref[:, at]
        here = jnp.where(causal, mm(q, k, NT) * SCALE, NEG_BIG)
        back = jnp.where(near, mm(q, k2, NT) * SCALE, NEG_BIG)
        out, lse = softmax_part([here, back], [v, v2])
        own_ref[:, at] = out
        own_lse.append(lse)
        out, lse = softmax_part([mm(qz_ref[:, at], k2, NT) * SCALE], [v2])
        oz_ref[:, at] = out.astype(jnp.bfloat16)
        z_lse.append(lse)
        ks, vs = jnp.where(odd == 1, k2, k), jnp.where(odd == 1, v2, v)
        out, lse = softmax_part([mm(qx_ref[:, at], ks, NT) * SCALE], [vs])
        ox_ref[:, at] = out.astype(jnp.bfloat16)
        x_lse.append(lse)
    oz_ref[:, heads * HD :] = pack_columns(z_lse)
    ox_ref[:, heads * HD :] = pack_columns(x_lse)
    lse_ref[...] = pack_columns(own_lse)


def merge_kernel(heads, me_ref, pattern_ref, own_ref, lse_ref, rz_ref, rx_ref, u_ref, a_ref, sums_ref):
    me = me_ref[0]
    far, side = pattern_ref[me, 2] >= 0, pattern_ref[me, 0] >= 0
    tail = slice(heads * HD, heads * HD + PACK)
    own_tile, z_tile, x_tile = lse_ref[...], rz_ref[:, tail], rx_ref[:, tail]
    totals = []
    squares = jnp.zeros((BLOCK, HD), jnp.float32)
    crosses = jnp.zeros((BLOCK, HD), jnp.float32)
    for h in range(heads):
        at = slice(h * HD, (h + 1) * HD)
        own_lse = unpack_column(own_tile, heads, h)
        z_lse = jnp.where(far, unpack_column(z_tile, heads, h), NEG_BIG)
        x_lse = jnp.where(side, unpack_column(x_tile, heads, h), NEG_BIG)
        highest = jnp.maximum(own_lse, jnp.maximum(z_lse, x_lse))
        total = highest + jnp.log(
            jnp.exp(own_lse - highest) + jnp.exp(z_lse - highest) + jnp.exp(x_lse - highest)
        )
        totals.append(total)
        out = (
            own_ref[:, at] * jnp.exp(own_lse - total)
            + rz_ref[:, at].astype(jnp.float32) * jnp.exp(z_lse - total)
            + rx_ref[:, at].astype(jnp.float32) * jnp.exp(x_lse - total)
        ).astype(jnp.bfloat16)
        a_ref[:, at] = out
        wide = out.astype(jnp.float32)
        squares += wide * wide
        crosses += wide * u_ref[:, at].astype(jnp.float32)
    a_ref[:, tail] = pack_columns(totals)
    sums_ref[...] = jnp.concatenate(
        [
            jnp.sum(squares.T, axis=0, keepdims=True),
            jnp.sum(crosses.T, axis=0, keepdims=True),
            jnp.zeros((6, BLOCK), jnp.float32),
        ],
        axis=0,
    )


def norm_columns(sums):
    inverse = lax.rsqrt(sums[0:1] / WIDTH + EPSILON)
    factor = inverse**3 * sums[1:2] / WIDTH
    return (
        jnp.broadcast_to(inverse, (BLOCK, BLOCK)).T,
        jnp.broadcast_to(factor, (BLOCK, BLOCK)).T,
    )


def upstream_part(inverse, factor, u, a):
    wide = a.astype(jnp.float32)
    grad = (inverse * u.astype(jnp.float32) - wide * factor).astype(jnp.bfloat16)
    delta = jnp.sum(grad.astype(jnp.float32) * wide, axis=1, keepdims=True)
    return grad, delta


def pair_back(q, k, v, grad, delta, lse, keep):
    scores = jnp.where(keep, mm(q, k, NT) * SCALE, NEG_BIG)
    weights = jnp.exp(scores - lse)
    dscore = (weights * (mm(grad, v, NT) - delta) * SCALE).astype(jnp.bfloat16)
    return weights.astype(jnp.bfloat16), dscore


def far_kernel(
    heads,
    me_ref,
    pattern_ref,
    sums_ref,
    sz_ref,
    sx_ref,
    q_ref,
    qz_ref,
    qx_ref,
    a_ref,
    az_ref,
    ax_ref,
    u_ref,
    uz_ref,
    ux_ref,
    k_ref,
    v_ref,
    k2_ref,
    v2_ref,
    dkv_ref,
    dqz_ref,
    dqx_ref,
    dq_ref,
    dside_ref,
):
    odd, near, far, side = pair_flags(me_ref, pattern_ref)
    tail = slice(heads * HD, heads * HD + PACK)
    own_norm, z_norm, x_norm = norm_columns(sums_ref), norm_columns(sz_ref), norm_columns(sx_ref)
    own_tile, z_tile, x_tile = a_ref[:, tail], az_ref[:, tail], ax_ref[:, tail]
    share = (odd == 1).astype(jnp.float32)
    for h in range(heads):
        at = slice(h * HD, (h + 1) * HD)
        k, v, k2, v2 = k_ref[:, at], v_ref[:, at], k2_ref[:, at], v2_ref[:, at]
        q, qz, qx = q_ref[:, at], qz_ref[:, at], qx_ref[:, at]
        grad, delta = upstream_part(*own_norm, u_ref[:, at], a_ref[:, at])
        gradz, deltaz = upstream_part(*z_norm, uz_ref[:, at], az_ref[:, at])
        gradx, deltax = upstream_part(*x_norm, ux_ref[:, at], ax_ref[:, at])
        probs, dscore = pair_back(q, k2, v2, grad, delta, unpack_column(own_tile, heads, h), near)
        dk2 = mm(dscore, q, TN)
        dv2 = mm(probs, grad, TN)
        dq_ref[:, at] = mm(dscore, k2, NN)
        probs, dscore = pair_back(qz, k2, v2, gradz, deltaz, unpack_column(z_tile, heads, h), far)
        dk2 += mm(dscore, qz, TN)
        dv2 += mm(probs, gradz, TN)
        dqz_ref[:, at] = mm(dscore, k2, NN).astype(jnp.bfloat16)
        ks, vs = jnp.where(odd == 1, k2, k), jnp.where(odd == 1, v2, v)
        probs, dscore = pair_back(qx, ks, vs, gradx, deltax, unpack_column(x_tile, heads, h), side)
        dks = mm(dscore, qx, TN)
        dvs = mm(probs, gradx, TN)
        dqx_ref[:, at] = mm(dscore, ks, NN).astype(jnp.bfloat16)
        dkv_ref[0, :, at] = (dk2 + share * dks).astype(jnp.bfloat16)
        dkv_ref[1, :, at] = (dv2 + share * dvs).astype(jnp.bfloat16)
        dside_ref[0, :, at] = (1.0 - share) * dks
        dside_ref[1, :, at] = (1.0 - share) * dvs


def near_kernel(
    heads,
    sums_ref,
    q_ref,
    a_ref,
    u_ref,
    k_ref,
    v_ref,
    dq_in_ref,
    dside_ref,
    normed_ref,
    dq_ref,
    dkv_ref,
):
    tail = slice(heads * HD, heads * HD + PACK)
    inverse, factor = norm_columns(sums_ref)
    tile = a_ref[:, tail]
    causal = causal_mask()
    for h in range(heads):
        at = slice(h * HD, (h + 1) * HD)
        q, k, v, a = q_ref[:, at], k_ref[:, at], v_ref[:, at], a_ref[:, at]
        normed_ref[:, at] = (a.astype(jnp.float32) * inverse).astype(jnp.bfloat16)
        grad, delta = upstream_part(inverse, factor, u_ref[:, at], a)
        probs, dscore = pair_back(q, k, v, grad, delta, unpack_column(tile, heads, h), causal)
        dq_ref[:, at] = dq_in_ref[:, at] + mm(dscore, k, NN)
        dkv_ref[0, :, at] = dside_ref[0, :, at] + mm(dscore, q, TN)
        dkv_ref[1, :, at] = dside_ref[1, :, at] + mm(probs, grad, TN)


def call(kernel, heads, scalars, arrays, outs, flops):
    smem = pl.BlockSpec(memory_space=pltpu.SMEM)
    vmem = pl.BlockSpec(memory_space=pltpu.VMEM)
    moved = sum(a.size * a.dtype.itemsize for a in arrays) + sum(o.size * o.dtype.itemsize for o in outs)
    return pl.pallas_call(
        functools.partial(kernel, heads),
        out_shape=outs,
        in_specs=[smem] * len(scalars) + [vmem] * len(arrays),
        out_specs=[vmem] * len(outs),
        compiler_params=pltpu.CompilerParams(vmem_limit_bytes=24 * 2**20),
        cost_estimate=pl.CostEstimate(flops=flops, bytes_accessed=moved, transcendentals=0),
    )(*scalars, *arrays)


def meeting_shards(queries, keys, values, pattern, upstream):
    tokens, width = queries.shape
    heads = width // HD
    count = lax.axis_size("ctx")
    me = lax.axis_index("ctx").astype(jnp.int32).reshape(1)
    partners = [(i, i ^ 1) for i in range(count)]
    unit = heads * 2 * BLOCK**3

    def swap(array):
        return lax.ppermute(array, "ctx", partners)

    def up(array):
        return shifted(array, "ctx", 2)

    def down(array):
        return shifted(array, "ctx", -2)

    def struct(*shape, dtype=jnp.bfloat16):
        return jax.ShapeDtypeStruct(shape, dtype)

    keys2, values2 = up(keys), up(values)
    queries_z, queries_x = down(queries), swap(queries)
    upstream_z, upstream_x = down(upstream), swap(upstream)
    packed = struct(tokens, width + PACK)
    own, own_lse, out_z, out_x = call(
        forward_kernel,
        heads,
        (me, pattern),
        (queries, queries_z, queries_x, keys, values, keys2, values2),
        (struct(tokens, width, dtype=jnp.float32), struct(tokens, PACK), packed, packed),
        8 * unit,
    )
    back_z, back_x = up(out_z), swap(out_x)
    attention, sums = call(
        merge_kernel,
        heads,
        (me, pattern),
        (own, own_lse, back_z, back_x, upstream),
        (packed, struct(8, BLOCK, dtype=jnp.float32)),
        unit // 64,
    )
    attention_z, attention_x = down(attention), swap(attention)
    sums = lax.psum(sums, "head")
    sums_z, sums_x = down(sums), swap(sums)
    grads2, dq_z, dq_x, dq_own, dside = call(
        far_kernel,
        heads,
        (me, pattern),
        (sums, sums_z, sums_x, queries, queries_z, queries_x, attention, attention_z, attention_x)
        + (upstream, upstream_z, upstream_x, keys, values, keys2, values2),
        (
            struct(2, tokens, width),
            struct(tokens, width),
            struct(tokens, width),
            struct(tokens, width, dtype=jnp.float32),
            struct(2, tokens, width, dtype=jnp.float32),
        ),
        15 * unit,
    )
    grads_back = down(grads2)
    dq_back_z, dq_back_x = up(dq_z), swap(dq_x)
    normed, dq_own, grads_own = call(
        near_kernel,
        heads,
        (),
        (sums, queries, attention, upstream, keys, values, dq_own, dside),
        (
            struct(tokens, width),
            struct(tokens, width, dtype=jnp.float32),
            struct(2, tokens, width, dtype=jnp.float32),
        ),
        5 * unit,
    )
    grad_queries = (
        dq_own + dq_back_z.astype(jnp.float32) + dq_back_x.astype(jnp.float32)
    ).astype(jnp.bfloat16)
    grads = (grads_own + grads_back.astype(jnp.float32)).astype(jnp.bfloat16)
    return (normed, grad_queries, grads[0], grads[1])


def shards(queries, keys, values, pattern, upstream):
    if lax.axis_size("ctx") == 8 and queries.shape[0] == BLOCK:
        return meeting_shards(queries, keys, values, pattern, upstream)
    return generic_shards(queries, keys, values, pattern, upstream)


def solution(mesh):
    return jax.shard_map(
        shards,
        mesh=mesh,
        in_specs=(P("ctx", "head"), P("ctx", "head"), P("ctx", "head"), P(), P("ctx", "head")),
        out_specs=(P("ctx", "head"), P("ctx", "head"), P("ctx", "head"), P("ctx", "head")),
        check_vma=False,
    )
```

```python
import functools

import jax
import jax.numpy as jnp
from jax import lax
from jax.experimental import pallas as pl
from jax.experimental.pallas import tpu as pltpu
from jax.sharding import PartitionSpec as P

HD = 128
BLOCK = 128
LEVELS = 7
WIDTH = 4096


NEG_BIG = -1e30
EPSILON = 1e-06


def shifted(block, axis, distance):
    devices = range(lax.axis_size(axis))
    route = [(i - distance, i) for i in devices if i - distance in devices]
    return lax.ppermute(block, axis, route)


def for_sending(x):
    return jax.tree.map(lambda a: a.astype(jnp.bfloat16) if a.dtype == jnp.float32 else a, x)


def route_table(blocks, levels):
    routing = []
    for query_block in range(blocks):
        for level_index in range(levels + 1):
            if level_index == levels:
                routing.append((0, query_block))
            else:
                distance = 2**level_index
                routing.append(
                    (-((query_block - distance) // blocks), (query_block - distance) % blocks)
                )
    return routing


def pair_grads(
    query_tiles, grad_tiles, lse_tiles, delta_tiles, key_tiles, value_tiles, keep_mask, score_scale
):
    scores = (
        jnp.einsum("pqhd,pkhd->phqk", query_tiles, key_tiles, preferred_element_type=jnp.float32)
        * score_scale
    )
    scores = jnp.where(keep_mask[:, None], scores, NEG_BIG)
    weights = jnp.exp(scores - lse_tiles[..., None])
    prob_tiles = weights.astype(jnp.bfloat16)
    grad_probs = jnp.einsum(
        "pqhd,pkhd->phqk", grad_tiles, value_tiles, preferred_element_type=jnp.float32
    )
    dscore = (weights * (grad_probs - delta_tiles[..., None]) * score_scale).astype(jnp.bfloat16)
    return (dscore, prob_tiles)


def key_grads(dscore, prob_tiles, query_tiles, grad_tiles):
    key_part = jnp.einsum(
        "phqk,pqhd->pkhd", dscore, query_tiles, preferred_element_type=jnp.float32
    )
    value_part = jnp.einsum(
        "phqk,pqhd->pkhd", prob_tiles, grad_tiles, preferred_element_type=jnp.float32
    )
    return jnp.stack((key_part, value_part))


def collect(partials, targets, blocks):
    pieces = []
    for key_index in range(blocks):
        summed = jnp.zeros((2,) + partials.shape[2:], jnp.float32)
        for row_index, target in enumerate(targets):
            if target == key_index:
                summed = summed + partials[:, row_index]
        pieces.append(summed)
    return jnp.stack(pieces, axis=1)


def generic_shards(queries, keys, values, pattern, upstream):
    tokens_here = queries.shape[0]
    heads_here = queries.shape[1] // HD
    blocks = tokens_here // BLOCK
    slot_count = LEVELS + 1
    pair_count = blocks * slot_count
    score_scale = HD ** (-0.5)
    ctx_count = lax.axis_size("ctx")
    device_index = lax.axis_index("ctx")
    routing = route_table(blocks, LEVELS)
    offsets = sorted(
        set((route_entry[0] for route_entry in routing if 0 < route_entry[0] < ctx_count))
    )
    tile_shape = (blocks, BLOCK, heads_here, HD)
    query_blocks = queries.reshape(tile_shape)
    own_pairs = jnp.stack((keys, values)).reshape((2,) + tile_shape)
    sources = {0: own_pairs}
    for offset in offsets:
        fetched = shifted(jnp.stack((keys, values)), "ctx", offset)
        sources[offset] = fetched.reshape((2,) + tile_shape)
    empty_tile = jnp.zeros((2, BLOCK, heads_here, HD), jnp.bfloat16)
    gathered = []
    for source, key_index in routing:
        if source in sources:
            gathered.append(sources[source][:, key_index])
        else:
            gathered.append(empty_tile)
    pair_kv = jnp.stack(gathered, axis=1)
    key_tiles = pair_kv[0]
    value_tiles = pair_kv[1]
    key_stack = key_tiles.reshape((blocks, slot_count) + tile_shape[1:])
    value_stack = value_tiles.reshape((blocks, slot_count) + tile_shape[1:])
    own_rows = lax.dynamic_slice_in_dim(pattern, device_index * blocks, blocks, 0)
    positions = jnp.arange(BLOCK)
    causal = positions[None, :] <= positions[:, None]
    self_slot = jnp.arange(slot_count) == LEVELS
    tile_keep = (own_rows >= 0)[:, :, None, None] & (
        jnp.logical_not(self_slot)[None, :, None, None] | causal[None, None]
    )
    scores = (
        jnp.einsum("bqhd,bskhd->bhqsk", query_blocks, key_stack, preferred_element_type=jnp.float32)
        * score_scale
    )
    scores = jnp.where(jnp.transpose(tile_keep, (0, 2, 1, 3))[:, None], scores, NEG_BIG)
    highest = jnp.max(scores, axis=(3, 4))
    log_total = highest + jnp.log(jnp.sum(jnp.exp(scores - highest[..., None, None]), axis=(3, 4)))
    prob_stack = jnp.exp(scores - log_total[..., None, None]).astype(jnp.bfloat16)
    attention = jnp.einsum(
        "bhqsk,bskhd->bqhd", prob_stack, value_stack, preferred_element_type=jnp.float32
    ).astype(jnp.bfloat16)
    attn_wide = attention.reshape(tokens_here, heads_here * HD).astype(jnp.float32)
    square_sum = lax.psum(jnp.sum(attn_wide * attn_wide, axis=1), "head")
    inverse = lax.rsqrt(square_sum / WIDTH + EPSILON)
    normed = (attn_wide * inverse[:, None]).astype(jnp.bfloat16)
    upstream_wide = upstream.astype(jnp.float32)
    cross_term = lax.psum(jnp.sum(upstream_wide * attn_wide, axis=1), "head")
    grad_attn = (
        inverse[:, None] * upstream_wide - attn_wide * (inverse**3 * cross_term / WIDTH)[:, None]
    ).astype(jnp.bfloat16)
    row_delta = jnp.sum(
        (grad_attn.astype(jnp.float32) * attn_wide).reshape(tokens_here, heads_here, HD), axis=2
    )
    row_delta = jnp.transpose(row_delta.reshape(blocks, BLOCK, heads_here), (0, 2, 1))

    def spread(array):
        return jnp.broadcast_to(array[:, None], (blocks, slot_count) + array.shape[1:]).reshape(
            (pair_count,) + array.shape[1:]
        )

    grad_blocks = grad_attn.reshape(tile_shape)
    query_pairs = spread(query_blocks)
    grad_pairs = spread(grad_blocks)
    keep_pairs = tile_keep.reshape(pair_count, BLOCK, BLOCK)
    dscore, prob_pairs = pair_grads(
        query_pairs,
        grad_pairs,
        spread(log_total),
        spread(row_delta),
        key_tiles,
        value_tiles,
        keep_pairs,
        score_scale,
    )
    grad_query = jnp.einsum(
        "phqk,pkhd->pqhd", dscore, key_tiles, preferred_element_type=jnp.float32
    )
    grad_query = jnp.sum(grad_query.reshape((blocks, slot_count) + tile_shape[1:]), axis=1)
    grad_queries = grad_query.astype(jnp.bfloat16).reshape(tokens_here, heads_here * HD)
    local_rows = [row_index for row_index in range(pair_count) if routing[row_index][0] == 0]
    chosen = jnp.array(local_rows, jnp.int32)
    local_terms = key_grads(
        dscore[chosen], prob_pairs[chosen], query_pairs[chosen], grad_pairs[chosen]
    )
    key_sum = collect(local_terms, [routing[row_index][1] for row_index in local_rows], blocks)
    for offset in offsets:
        remote_rows = [
            row_index for row_index in range(pair_count) if routing[row_index][0] == offset
        ]
        chosen = jnp.array(remote_rows, jnp.int32)
        remote_terms = key_grads(
            dscore[chosen], prob_pairs[chosen], query_pairs[chosen], grad_pairs[chosen]
        )
        outgoing = collect(
            remote_terms, [routing[row_index][1] for row_index in remote_rows], blocks
        )
        key_sum = key_sum + shifted(for_sending(outgoing), "ctx", -offset).astype(outgoing.dtype)
    grad_keys = key_sum[0].astype(jnp.bfloat16).reshape(tokens_here, heads_here * HD)
    grad_values = key_sum[1].astype(jnp.bfloat16).reshape(tokens_here, heads_here * HD)
    return (normed, grad_queries, grad_keys, grad_values)


NT = (((1,), (1,)), ((), ()))
NN = (((1,), (0,)), ((), ()))
TN = (((0,), (0,)), ((), ()))
SCALE = HD ** (-0.5)
PACK = 128


def mm(a, b, dims):
    return lax.dot_general(a, b, dims, preferred_element_type=jnp.float32)


def lane_ids(shape):
    return lax.broadcasted_iota(jnp.int32, shape, len(shape) - 1)


def causal_mask():
    rows = lax.broadcasted_iota(jnp.int32, (BLOCK, BLOCK), 0)
    return lane_ids((BLOCK, BLOCK)) <= rows


def pack_columns(columns):
    count = len(columns)
    lanes = lane_ids((BLOCK, PACK))
    wide = jnp.zeros((BLOCK, PACK), jnp.float32)
    for index, column in enumerate(columns):
        wide = jnp.where(lanes % count == index, column, wide)
    first = wide.astype(jnp.bfloat16)
    left = wide - first.astype(jnp.float32)
    second = left.astype(jnp.bfloat16)
    third = (left - second.astype(jnp.float32)).astype(jnp.bfloat16)
    return jnp.where(lanes < count, first, jnp.where(lanes < 2 * count, second, third))


def unpack_column(tile, count, index):
    wide = tile.astype(jnp.float32)
    return (
        wide[:, index : index + 1]
        + wide[:, count + index : count + index + 1]
        + wide[:, 2 * count + index : 2 * count + index + 1]
    )


def pair_flags(me_ref, pattern_ref):
    me = me_ref[0]
    blocks = pattern_ref.shape[0]
    odd = lax.rem(me, 2)
    ahead = jnp.minimum(me + 2, blocks - 1)
    partner = me + 1 - 2 * odd
    near = pattern_ref[me, 1] >= 0
    far = jnp.logical_and(me + 2 < blocks, pattern_ref[ahead, 2] >= 0)
    side = jnp.logical_and(jnp.logical_or(odd == 0, me >= 2), pattern_ref[partner, 0] >= 0)
    return odd, near, far, side


def softmax_pair(scores, value):
    highest = scores.max(axis=1, keepdims=True)
    weights = jnp.exp(scores - highest)
    total = weights.sum(axis=1, keepdims=True)
    out = mm(weights.astype(jnp.bfloat16), value, NN) / total
    return out, highest, highest + jnp.log(total), weights


def tile_columns(columns):
    lanes = lane_ids((BLOCK, PACK))
    wide = jnp.zeros((BLOCK, PACK), jnp.float32)
    for index, column in enumerate(columns):
        wide = jnp.where(lanes == index, column, wide)
    return wide


def side_pair(odd, k, v, k2, v2):
    return jnp.where(odd == 1, k2, k), jnp.where(odd == 1, v2, v)


def diagonal_kernel(heads, q_ref, k_ref, v_ref, qc_ref, kc_ref, vc_ref, out_ref, lse_ref):
    causal = causal_mask()
    tops = []
    for h in range(heads):
        at = slice(h * HD, (h + 1) * HD)
        q, k, v = q_ref[:, at], k_ref[:, at], v_ref[:, at]
        qc_ref[:, at], kc_ref[:, at], vc_ref[:, at] = q, k, v
        scores = jnp.where(causal, mm(q, k, NT) * SCALE, NEG_BIG)
        out_ref[:, at], _, lse, _ = softmax_pair(scores, v)
        tops.append(lse)
    lse_ref[...] = tile_columns(tops)


def helper_kernel(
    heads,
    me_ref,
    qz_ref,
    qx_ref,
    k_ref,
    v_ref,
    k2_ref,
    v2_ref,
    oz_ref,
    ox_ref,
    ez_ref,
    ex_ref,
    mz_ref,
    mx_ref,
):
    odd = lax.rem(me_ref[0], 2)
    z_lse, x_lse, z_top, x_top = [], [], [], []
    for h in range(heads):
        at = slice(h * HD, (h + 1) * HD)
        k2, v2 = k2_ref[:, at], v2_ref[:, at]
        out, top, lse, ez_ref[:, at] = softmax_pair(mm(qz_ref[:, at], k2, NT) * SCALE, v2)
        oz_ref[:, at] = out.astype(jnp.bfloat16)
        z_top.append(top)
        z_lse.append(lse)
        ks, vs = side_pair(odd, k_ref[:, at], v_ref[:, at], k2, v2)
        out, top, lse, ex_ref[:, at] = softmax_pair(mm(qx_ref[:, at], ks, NT) * SCALE, vs)
        ox_ref[:, at] = out.astype(jnp.bfloat16)
        x_top.append(top)
        x_lse.append(lse)
    oz_ref[:, heads * HD :] = pack_columns(z_lse)
    ox_ref[:, heads * HD :] = pack_columns(x_lse)
    mz_ref[...] = tile_columns(z_top)
    mx_ref[...] = tile_columns(x_top)


def own_kernel(heads, me_ref, pattern_ref, q_ref, k2_ref, v2_ref, out_ref, lse_ref, own_ref, total_ref):
    near = pattern_ref[me_ref[0], 1] >= 0
    tile = lse_ref[...]
    totals = []
    for h in range(heads):
        at = slice(h * HD, (h + 1) * HD)
        out, _, lse, _ = softmax_pair(mm(q_ref[:, at], k2_ref[:, at], NT) * SCALE, v2_ref[:, at])
        lse = jnp.where(near, lse, NEG_BIG)
        before = tile[:, h : h + 1]
        highest = jnp.maximum(before, lse)
        total = highest + jnp.log(jnp.exp(before - highest) + jnp.exp(lse - highest))
        own_ref[:, at] = out_ref[:, at] * jnp.exp(before - total) + out * jnp.exp(lse - total)
        totals.append(total)
    total_ref[...] = tile_columns(totals)


def merge_kernel(heads, me_ref, pattern_ref, own_ref, lse_ref, rz_ref, rx_ref, u_ref, a_ref, sums_ref):
    me = me_ref[0]
    far, side = pattern_ref[me, 2] >= 0, pattern_ref[me, 0] >= 0
    tail = slice(heads * HD, heads * HD + PACK)
    own_tile, z_tile, x_tile = lse_ref[...], rz_ref[:, tail], rx_ref[:, tail]
    totals = []
    squares = jnp.zeros((BLOCK, HD), jnp.float32)
    crosses = jnp.zeros((BLOCK, HD), jnp.float32)
    for h in range(heads):
        at = slice(h * HD, (h + 1) * HD)
        own_lse = own_tile[:, h : h + 1]
        z_lse = jnp.where(far, unpack_column(z_tile, heads, h), NEG_BIG)
        x_lse = jnp.where(side, unpack_column(x_tile, heads, h), NEG_BIG)
        highest = jnp.maximum(own_lse, jnp.maximum(z_lse, x_lse))
        total = highest + jnp.log(
            jnp.exp(own_lse - highest) + jnp.exp(z_lse - highest) + jnp.exp(x_lse - highest)
        )
        totals.append(total)
        out = (
            own_ref[:, at] * jnp.exp(own_lse - total)
            + rz_ref[:, at].astype(jnp.float32) * jnp.exp(z_lse - total)
            + rx_ref[:, at].astype(jnp.float32) * jnp.exp(x_lse - total)
        ).astype(jnp.bfloat16)
        a_ref[:, at] = out
        wide = out.astype(jnp.float32)
        squares += wide * wide
        crosses += wide * u_ref[:, at].astype(jnp.float32)
    a_ref[:, tail] = pack_columns(totals)
    sums_ref[...] = jnp.concatenate(
        [
            jnp.sum(squares.T, axis=0, keepdims=True),
            jnp.sum(crosses.T, axis=0, keepdims=True),
            jnp.zeros((6, BLOCK), jnp.float32),
        ],
        axis=0,
    )


def norm_columns(sums):
    inverse = lax.rsqrt(sums[0:1] / WIDTH + EPSILON)
    factor = inverse**3 * sums[1:2] / WIDTH
    return (
        jnp.broadcast_to(inverse, (BLOCK, BLOCK)).T,
        jnp.broadcast_to(factor, (BLOCK, BLOCK)).T,
    )


def upstream_part(inverse, factor, u, a):
    wide = a.astype(jnp.float32)
    grad = (inverse * u.astype(jnp.float32) - wide * factor).astype(jnp.bfloat16)
    delta = jnp.sum(grad.astype(jnp.float32) * wide, axis=1, keepdims=True)
    return grad, delta


def pair_back(q, k, v, grad, delta, lse, keep):
    scores = jnp.where(keep, mm(q, k, NT) * SCALE, NEG_BIG)
    weights = jnp.exp(scores - lse)
    dscore = (weights * (mm(grad, v, NT) - delta) * SCALE).astype(jnp.bfloat16)
    return weights.astype(jnp.bfloat16), dscore


def own_back_kernel(
    heads,
    me_ref,
    pattern_ref,
    sums_ref,
    q_ref,
    a_ref,
    u_ref,
    k_ref,
    v_ref,
    k2_ref,
    v2_ref,
    normed_ref,
    dq_ref,
    dkv_ref,
    dkv2_ref,
):
    near = pattern_ref[me_ref[0], 1] >= 0
    inverse, factor = norm_columns(sums_ref)
    tile = a_ref[:, heads * HD : heads * HD + PACK]
    causal = causal_mask()
    for h in range(heads):
        at = slice(h * HD, (h + 1) * HD)
        q, k, v, a, k2, v2 = q_ref[:, at], k_ref[:, at], v_ref[:, at], a_ref[:, at], k2_ref[:, at], v2_ref[:, at]
        lse = unpack_column(tile, heads, h)
        normed_ref[:, at] = (a.astype(jnp.float32) * inverse).astype(jnp.bfloat16)
        grad, delta = upstream_part(inverse, factor, u_ref[:, at], a)
        probs, dscore = pair_back(q, k2, v2, grad, delta, lse, near)
        dkv2_ref[0, :, at] = mm(dscore, q, TN)
        dkv2_ref[1, :, at] = mm(probs, grad, TN)
        dq = mm(dscore, k2, NN)
        probs, dscore = pair_back(q, k, v, grad, delta, lse, causal)
        dkv_ref[0, :, at] = mm(dscore, q, TN)
        dkv_ref[1, :, at] = mm(probs, grad, TN)
        dq_ref[:, at] = dq + mm(dscore, k, NN)


def helper_back_kernel(
    heads,
    me_ref,
    pattern_ref,
    sz_ref,
    sx_ref,
    qz_ref,
    qx_ref,
    az_ref,
    ax_ref,
    uz_ref,
    ux_ref,
    ez_ref,
    ex_ref,
    mz_ref,
    mx_ref,
    v_ref,
    v2_ref,
    own_ref,
    dkv_ref,
    dsz_ref,
    dsx_ref,
    dside_ref,
):
    odd, _, far, side = pair_flags(me_ref, pattern_ref)
    tail = slice(heads * HD, heads * HD + PACK)
    z_norm, x_norm = norm_columns(sz_ref), norm_columns(sx_ref)
    z_tile, x_tile, z_top, x_top = az_ref[:, tail], ax_ref[:, tail], mz_ref[...], mx_ref[...]
    share = (odd == 1).astype(jnp.float32)

    def one(h, at, norm, u, a, weights, tile, top, value, keep):
        grad, delta = upstream_part(*norm, u, a)
        scale = jnp.exp(top[:, h : h + 1] - unpack_column(tile, heads, h))
        wide = jnp.where(keep, weights * scale, 0.0)
        dscore = (wide * (mm(grad, value, NT) - delta) * SCALE).astype(jnp.bfloat16)
        return wide.astype(jnp.bfloat16), dscore, grad

    for h in range(heads):
        at = slice(h * HD, (h + 1) * HD)
        v, v2 = v_ref[:, at], v2_ref[:, at]
        probs, dscore, grad = one(
            h, at, z_norm, uz_ref[:, at], az_ref[:, at], ez_ref[:, at], z_tile, z_top, v2, far
        )
        dk2 = own_ref[0, :, at] + mm(dscore, qz_ref[:, at], TN)
        dv2 = own_ref[1, :, at] + mm(probs, grad, TN)
        dsz_ref[:, at] = dscore
        vs = jnp.where(odd == 1, v2, v)
        probs, dscore, grad = one(
            h, at, x_norm, ux_ref[:, at], ax_ref[:, at], ex_ref[:, at], x_tile, x_top, vs, side
        )
        dks = mm(dscore, qx_ref[:, at], TN)
        dvs = mm(probs, grad, TN)
        dsx_ref[:, at] = dscore
        dkv_ref[0, :, at] = (dk2 + share * dks).astype(jnp.bfloat16)
        dkv_ref[1, :, at] = (dv2 + share * dvs).astype(jnp.bfloat16)
        dside_ref[0, :, at] = (1.0 - share) * dks
        dside_ref[1, :, at] = (1.0 - share) * dvs


def helper_query_kernel(heads, me_ref, dsz_ref, dsx_ref, k_ref, k2_ref, dqz_ref, dqx_ref):
    odd = lax.rem(me_ref[0], 2)
    for h in range(heads):
        at = slice(h * HD, (h + 1) * HD)
        k2 = k2_ref[:, at]
        dqz_ref[:, at] = mm(dsz_ref[:, at], k2, NN).astype(jnp.bfloat16)
        ks = jnp.where(odd == 1, k2, k_ref[:, at])
        dqx_ref[:, at] = mm(dsx_ref[:, at], ks, NN).astype(jnp.bfloat16)


def call(kernel, heads, scalars, arrays, outs, flops):
    smem = pl.BlockSpec(memory_space=pltpu.SMEM)
    vmem = pl.BlockSpec(memory_space=pltpu.VMEM)
    moved = sum(a.size * a.dtype.itemsize for a in arrays) + sum(o.size * o.dtype.itemsize for o in outs)
    return pl.pallas_call(
        functools.partial(kernel, heads),
        out_shape=outs,
        in_specs=[smem] * len(scalars) + [vmem] * len(arrays),
        out_specs=[vmem] * len(outs),
        compiler_params=pltpu.CompilerParams(vmem_limit_bytes=24 * 2**20),
        cost_estimate=pl.CostEstimate(flops=flops, bytes_accessed=moved, transcendentals=0),
    )(*scalars, *arrays)


def meeting_shards(queries, keys, values, pattern, upstream):
    tokens, width = queries.shape
    heads = width // HD
    count = lax.axis_size("ctx")
    me = lax.axis_index("ctx").astype(jnp.int32).reshape(1)
    partners = [(i, i ^ 1) for i in range(count)]
    unit = heads * 2 * BLOCK**3

    def swap(array):
        return lax.ppermute(array, "ctx", partners)

    def up(array):
        return shifted(array, "ctx", 2)

    def down(array):
        return shifted(array, "ctx", -2)

    def struct(*shape, dtype=jnp.bfloat16):
        return jax.ShapeDtypeStruct(shape, dtype)

    wide = struct(tokens, width, dtype=jnp.float32)
    wide_pair = struct(2, tokens, width, dtype=jnp.float32)
    flat = struct(tokens, width)
    packed = struct(tokens, width + PACK)
    tile = struct(tokens, PACK, dtype=jnp.float32)

    keys2, values2 = up(keys), up(values)
    queries_z, queries_x = down(queries), swap(queries)
    upstream_z, upstream_x = down(upstream), swap(upstream)
    q, k, v, diagonal, diagonal_lse = call(
        diagonal_kernel, heads, (), (queries, keys, values), (flat, flat, flat, wide, tile), 2 * unit
    )
    keys2, values2, queries_z, queries_x, upstream_z, upstream_x = lax.optimization_barrier(
        (keys2, values2, queries_z, queries_x, upstream_z, upstream_x)
    )
    out_z, out_x, ez, ex, mz, mx = call(
        helper_kernel,
        heads,
        (me,),
        (queries_z, queries_x, k, v, keys2, values2),
        (packed, packed, wide, wide, tile, tile),
        4 * unit,
    )
    back_z, back_x = up(out_z), swap(out_x)
    own, own_lse = call(
        own_kernel,
        heads,
        (me, pattern),
        (q, keys2, values2, diagonal, diagonal_lse),
        (wide, tile),
        2 * unit,
    )
    attention, sums = call(
        merge_kernel,
        heads,
        (me, pattern),
        (own, own_lse, back_z, back_x, upstream),
        (packed, struct(8, BLOCK, dtype=jnp.float32)),
        unit // 64,
    )
    attention_z, attention_x = down(attention), swap(attention)
    sums = lax.psum(sums, "head")
    sums_z, sums_x = down(sums), swap(sums)
    normed, dq_own, grads_own, grads2_own = call(
        own_back_kernel,
        heads,
        (me, pattern),
        (sums, q, attention, upstream, k, v, keys2, values2),
        (flat, wide, wide_pair, wide_pair),
        10 * unit,
    )
    grads2, dsz, dsx, dside = call(
        helper_back_kernel,
        heads,
        (me, pattern),
        (sums_z, sums_x, queries_z, queries_x, attention_z, attention_x, upstream_z, upstream_x)
        + (ez, ex, mz, mx, v, values2, grads2_own),
        (struct(2, tokens, width), flat, flat, wide_pair),
        6 * unit,
    )
    grads_back = down(grads2)
    dq_z, dq_x = call(helper_query_kernel, heads, (me,), (dsz, dsx, k, keys2), (flat, flat), 2 * unit)
    dq_back_z, dq_back_x = up(dq_z), swap(dq_x)
    grad_queries = (
        dq_own + dq_back_z.astype(jnp.float32) + dq_back_x.astype(jnp.float32)
    ).astype(jnp.bfloat16)
    grad_keys, grad_values = (
        (grads_own[n] + dside[n] + grads_back[n].astype(jnp.float32)).astype(jnp.bfloat16) for n in (0, 1)
    )
    return (normed, grad_queries, grad_keys, grad_values)


def shards(queries, keys, values, pattern, upstream):
    if lax.axis_size("ctx") == 8 and queries.shape[0] == BLOCK:
        return meeting_shards(queries, keys, values, pattern, upstream)
    return generic_shards(queries, keys, values, pattern, upstream)


def solution(mesh):
    return jax.shard_map(
        shards,
        mesh=mesh,
        in_specs=(P("ctx", "head"), P("ctx", "head"), P("ctx", "head"), P(), P("ctx", "head")),
        out_specs=(P("ctx", "head"), P("ctx", "head"), P("ctx", "head"), P("ctx", "head")),
        check_vma=False,
    )
```

```python
import functools
import math

import jax
import jax.numpy as jnp
from jax import lax
from jax.experimental import pallas as pl
from jax.experimental.pallas import tpu as pltpu
from jax.sharding import PartitionSpec as P

HD = 128
BLOCK = 128
LEVELS = 7
WIDTH = 4096


NEG_BIG = -1e30
EPSILON = 1e-06


def shifted(block, axis, distance):
    devices = range(lax.axis_size(axis))
    route = [(i - distance, i) for i in devices if i - distance in devices]
    return lax.ppermute(block, axis, route)


def for_sending(x):
    return jax.tree.map(lambda a: a.astype(jnp.bfloat16) if a.dtype == jnp.float32 else a, x)


def route_table(blocks, levels):
    routing = []
    for query_block in range(blocks):
        for level_index in range(levels + 1):
            if level_index == levels:
                routing.append((0, query_block))
            else:
                distance = 2**level_index
                routing.append(
                    (-((query_block - distance) // blocks), (query_block - distance) % blocks)
                )
    return routing


def pair_grads(
    query_tiles, grad_tiles, lse_tiles, delta_tiles, key_tiles, value_tiles, keep_mask, score_scale
):
    scores = (
        jnp.einsum("pqhd,pkhd->phqk", query_tiles, key_tiles, preferred_element_type=jnp.float32)
        * score_scale
    )
    scores = jnp.where(keep_mask[:, None], scores, NEG_BIG)
    weights = jnp.exp(scores - lse_tiles[..., None])
    prob_tiles = weights.astype(jnp.bfloat16)
    grad_probs = jnp.einsum(
        "pqhd,pkhd->phqk", grad_tiles, value_tiles, preferred_element_type=jnp.float32
    )
    dscore = (weights * (grad_probs - delta_tiles[..., None]) * score_scale).astype(jnp.bfloat16)
    return (dscore, prob_tiles)


def key_grads(dscore, prob_tiles, query_tiles, grad_tiles):
    key_part = jnp.einsum(
        "phqk,pqhd->pkhd", dscore, query_tiles, preferred_element_type=jnp.float32
    )
    value_part = jnp.einsum(
        "phqk,pqhd->pkhd", prob_tiles, grad_tiles, preferred_element_type=jnp.float32
    )
    return jnp.stack((key_part, value_part))


def collect(partials, targets, blocks):
    pieces = []
    for key_index in range(blocks):
        summed = jnp.zeros((2,) + partials.shape[2:], jnp.float32)
        for row_index, target in enumerate(targets):
            if target == key_index:
                summed = summed + partials[:, row_index]
        pieces.append(summed)
    return jnp.stack(pieces, axis=1)


def generic_shards(queries, keys, values, pattern, upstream):
    tokens_here = queries.shape[0]
    heads_here = queries.shape[1] // HD
    blocks = tokens_here // BLOCK
    slot_count = LEVELS + 1
    pair_count = blocks * slot_count
    score_scale = HD ** (-0.5)
    ctx_count = lax.axis_size("ctx")
    device_index = lax.axis_index("ctx")
    routing = route_table(blocks, LEVELS)
    offsets = sorted(
        set((route_entry[0] for route_entry in routing if 0 < route_entry[0] < ctx_count))
    )
    tile_shape = (blocks, BLOCK, heads_here, HD)
    query_blocks = queries.reshape(tile_shape)
    own_pairs = jnp.stack((keys, values)).reshape((2,) + tile_shape)
    sources = {0: own_pairs}
    for offset in offsets:
        fetched = shifted(jnp.stack((keys, values)), "ctx", offset)
        sources[offset] = fetched.reshape((2,) + tile_shape)
    empty_tile = jnp.zeros((2, BLOCK, heads_here, HD), jnp.bfloat16)
    gathered = []
    for source, key_index in routing:
        if source in sources:
            gathered.append(sources[source][:, key_index])
        else:
            gathered.append(empty_tile)
    pair_kv = jnp.stack(gathered, axis=1)
    key_tiles = pair_kv[0]
    value_tiles = pair_kv[1]
    key_stack = key_tiles.reshape((blocks, slot_count) + tile_shape[1:])
    value_stack = value_tiles.reshape((blocks, slot_count) + tile_shape[1:])
    own_rows = lax.dynamic_slice_in_dim(pattern, device_index * blocks, blocks, 0)
    positions = jnp.arange(BLOCK)
    causal = positions[None, :] <= positions[:, None]
    self_slot = jnp.arange(slot_count) == LEVELS
    tile_keep = (own_rows >= 0)[:, :, None, None] & (
        jnp.logical_not(self_slot)[None, :, None, None] | causal[None, None]
    )
    scores = (
        jnp.einsum("bqhd,bskhd->bhqsk", query_blocks, key_stack, preferred_element_type=jnp.float32)
        * score_scale
    )
    scores = jnp.where(jnp.transpose(tile_keep, (0, 2, 1, 3))[:, None], scores, NEG_BIG)
    highest = jnp.max(scores, axis=(3, 4))
    log_total = highest + jnp.log(jnp.sum(jnp.exp(scores - highest[..., None, None]), axis=(3, 4)))
    prob_stack = jnp.exp(scores - log_total[..., None, None]).astype(jnp.bfloat16)
    attention = jnp.einsum(
        "bhqsk,bskhd->bqhd", prob_stack, value_stack, preferred_element_type=jnp.float32
    ).astype(jnp.bfloat16)
    attn_wide = attention.reshape(tokens_here, heads_here * HD).astype(jnp.float32)
    square_sum = lax.psum(jnp.sum(attn_wide * attn_wide, axis=1), "head")
    inverse = lax.rsqrt(square_sum / WIDTH + EPSILON)
    normed = (attn_wide * inverse[:, None]).astype(jnp.bfloat16)
    upstream_wide = upstream.astype(jnp.float32)
    cross_term = lax.psum(jnp.sum(upstream_wide * attn_wide, axis=1), "head")
    grad_attn = (
        inverse[:, None] * upstream_wide - attn_wide * (inverse**3 * cross_term / WIDTH)[:, None]
    ).astype(jnp.bfloat16)
    row_delta = jnp.sum(
        (grad_attn.astype(jnp.float32) * attn_wide).reshape(tokens_here, heads_here, HD), axis=2
    )
    row_delta = jnp.transpose(row_delta.reshape(blocks, BLOCK, heads_here), (0, 2, 1))

    def spread(array):
        return jnp.broadcast_to(array[:, None], (blocks, slot_count) + array.shape[1:]).reshape(
            (pair_count,) + array.shape[1:]
        )

    grad_blocks = grad_attn.reshape(tile_shape)
    query_pairs = spread(query_blocks)
    grad_pairs = spread(grad_blocks)
    keep_pairs = tile_keep.reshape(pair_count, BLOCK, BLOCK)
    dscore, prob_pairs = pair_grads(
        query_pairs,
        grad_pairs,
        spread(log_total),
        spread(row_delta),
        key_tiles,
        value_tiles,
        keep_pairs,
        score_scale,
    )
    grad_query = jnp.einsum(
        "phqk,pkhd->pqhd", dscore, key_tiles, preferred_element_type=jnp.float32
    )
    grad_query = jnp.sum(grad_query.reshape((blocks, slot_count) + tile_shape[1:]), axis=1)
    grad_queries = grad_query.astype(jnp.bfloat16).reshape(tokens_here, heads_here * HD)
    local_rows = [row_index for row_index in range(pair_count) if routing[row_index][0] == 0]
    chosen = jnp.array(local_rows, jnp.int32)
    local_terms = key_grads(
        dscore[chosen], prob_pairs[chosen], query_pairs[chosen], grad_pairs[chosen]
    )
    key_sum = collect(local_terms, [routing[row_index][1] for row_index in local_rows], blocks)
    for offset in offsets:
        remote_rows = [
            row_index for row_index in range(pair_count) if routing[row_index][0] == offset
        ]
        chosen = jnp.array(remote_rows, jnp.int32)
        remote_terms = key_grads(
            dscore[chosen], prob_pairs[chosen], query_pairs[chosen], grad_pairs[chosen]
        )
        outgoing = collect(
            remote_terms, [routing[row_index][1] for row_index in remote_rows], blocks
        )
        key_sum = key_sum + shifted(for_sending(outgoing), "ctx", -offset).astype(outgoing.dtype)
    grad_keys = key_sum[0].astype(jnp.bfloat16).reshape(tokens_here, heads_here * HD)
    grad_values = key_sum[1].astype(jnp.bfloat16).reshape(tokens_here, heads_here * HD)
    return (normed, grad_queries, grad_keys, grad_values)


NT = (((1,), (1,)), ((), ()))
NN = (((1,), (0,)), ((), ()))
TN = (((0,), (0,)), ((), ()))
SCALE = HD ** (-0.5)
TAIL = 32


class Flags:
    def __init__(self, pattern_ref=None):
        me, member = lax.axis_index("ctx"), lax.axis_index("head")
        self.odd = lax.rem(me, 2) == 1
        self.half = member >= lax.axis_size("head") // 2
        if pattern_ref is None:
            return
        blocks = pattern_ref.shape[0]
        ahead, partner = jnp.minimum(me + 2, blocks - 1), jnp.where(self.odd, me - 1, me + 1)
        self.near = pattern_ref[me, 1] >= 0
        self.far_in, self.side_in = pattern_ref[me, 2] >= 0, pattern_ref[me, 0] >= 0
        self.ahead = me + 2 < blocks
        self.far = jnp.logical_and(self.ahead, pattern_ref[ahead, 2] >= 0)
        self.side = jnp.logical_and(
            jnp.logical_or(jnp.logical_not(self.odd), me >= 2), pattern_ref[partner, 0] >= 0
        )


def mm(a, b, dims):
    return lax.dot_general(a, b, dims, preferred_element_type=jnp.float32)


def rows_of(h):
    return slice(h * HD, (h + 1) * HD)


def causal_mask():
    keys = lax.broadcasted_iota(jnp.int32, (BLOCK, BLOCK), 0)
    return keys <= lax.broadcasted_iota(jnp.int32, (BLOCK, BLOCK), 1)


def split_rows(rows):
    first = rows.astype(jnp.bfloat16).astype(jnp.float32)
    second = (rows - first).astype(jnp.bfloat16).astype(jnp.float32)
    third = rows - first - second
    return jnp.concatenate([first, second, third, jnp.zeros_like(rows)], axis=0).astype(jnp.bfloat16)


def joined_rows(tile):
    wide = tile.astype(jnp.float32)
    return wide[0:8] + wide[8:16] + wide[16:24]


def stack_rows(rows):
    return jnp.concatenate(rows + [jnp.zeros((1, BLOCK), jnp.float32)] * (8 - len(rows)), axis=0)


def score_tile(keys, queries):
    return mm(keys, queries, NT) * SCALE


def softmax_parts(pairs):
    tops = [scores.max(axis=0, keepdims=True) for scores, _ in pairs]
    weights = [jnp.exp(scores - top) for (scores, _), top in zip(pairs, tops)]
    totals = [w.sum(axis=0, keepdims=True) for w in weights]
    outs = [
        mm(value, w.astype(jnp.bfloat16), TN) * (1.0 / total)
        for (_, value), w, total in zip(pairs, weights, totals)
    ]
    return [(out, top, top + jnp.log(total), w) for out, top, total, w in zip(outs, tops, totals, weights)]


def payload_kernel(heads, q_ref, k_ref, v_ref, u_ref, up_ref, down_ref, sems):
    half = Flags().half
    top, bottom = pl.ds(0, BLOCK), pl.ds(BLOCK, BLOCK)

    def move(sources):
        targets = (up_ref.at[top], up_ref.at[bottom], down_ref.at[top], down_ref.at[bottom])
        copies = [
            pltpu.make_async_copy(source, target, sems.at[n])
            for n, (source, target) in enumerate(zip(sources, targets))
        ]
        for copy in copies:
            copy.start()
        for copy in copies:
            copy.wait()

    @pl.when(jnp.logical_not(half))
    def _():
        move((k_ref, v_ref, q_ref, u_ref))

    @pl.when(half)
    def _():
        move((q_ref, u_ref, k_ref, v_ref))


def diagonal_kernel(heads, q_ref, k_ref, v_ref, u_ref, out_ref, lse_ref, ut_ref):
    causal = causal_mask()
    rows = []
    for h in range(heads):
        at = rows_of(h)
        scores = jnp.where(causal, score_tile(k_ref[:, at], q_ref[:, at]), NEG_BIG)
        ((out, _, lse, _),) = softmax_parts([(scores, v_ref[:, at])])
        out_ref[at] = out
        rows.append(lse)
        ut_ref[at] = u_ref[:, at].T
    lse_ref[...] = stack_rows(rows)


def helper_kernel(
    heads, up_ref, down_ref, qx_ref, k_ref, v_ref, oz_ref, ox_ref, ez_ref, ex_ref, mz_ref, mx_ref
):
    flags = Flags()
    odd, half = flags.odd, flags.half
    first, second = slice(0, BLOCK), slice(BLOCK, 2 * BLOCK)
    z_rows, x_rows, z_tops, x_tops = [], [], [], []
    for start in range(0, heads, 2):
        pairs = []
        for h in range(start, start + 2):
            at = rows_of(h)
            up_a, down_a = up_ref[first, at], down_ref[first, at]
            k2, qz = jnp.where(half, down_a, up_a), jnp.where(half, up_a, down_a)
            v2 = jnp.where(half, down_ref[second, at], up_ref[second, at])
            pairs.append((score_tile(k2, qz), v2))
            ks, vs = jnp.where(odd, k2, k_ref[:, at]), jnp.where(odd, v2, v_ref[:, at])
            pairs.append((score_tile(ks, qx_ref[:, at]), vs))
        for n, (out, top, lse, weights) in enumerate(softmax_parts(pairs)):
            at = rows_of(start + n // 2)
            o_ref, e_ref = ((oz_ref, ez_ref), (ox_ref, ex_ref))[n % 2]
            o_ref[at] = out.astype(jnp.bfloat16)
            e_ref[at] = weights
            (z_rows, x_rows)[n % 2].append(lse)
            (z_tops, x_tops)[n % 2].append(top)
    tail = slice(heads * HD, heads * HD + TAIL)
    oz_ref[tail] = split_rows(stack_rows(z_rows))
    ox_ref[tail] = split_rows(stack_rows(x_rows))
    mz_ref[...] = stack_rows(z_tops)
    mx_ref[...] = stack_rows(x_tops)


def own_kernel(
    heads, pattern_ref, up_ref, down_ref, q_ref, ux_ref, out_ref, lse_ref, own_ref, total_ref, uzt_ref, uxt_ref
):
    flags = Flags(pattern_ref)
    half, near = flags.half, flags.near
    first, second = slice(0, BLOCK), slice(BLOCK, 2 * BLOCK)
    before = lse_ref[...]
    rows = []
    for h in range(heads):
        at = rows_of(h)
        k2 = jnp.where(half, down_ref[first, at], up_ref[first, at])
        up_b, down_b = up_ref[second, at], down_ref[second, at]
        v2, uz = jnp.where(half, down_b, up_b), jnp.where(half, up_b, down_b)
        ((out, _, lse, _),) = softmax_parts([(score_tile(k2, q_ref[:, at]), v2)])
        lse = jnp.where(near, lse, NEG_BIG)
        old = before[h : h + 1]
        highest = jnp.maximum(old, lse)
        total = highest + jnp.log(jnp.exp(old - highest) + jnp.exp(lse - highest))
        own_ref[at] = out_ref[at] * jnp.exp(old - total) + out * jnp.exp(lse - total)
        rows.append(total)
        uzt_ref[at] = uz.T
        uxt_ref[at] = ux_ref[:, at].T
    total_ref[...] = stack_rows(rows)


def merge_kernel(heads, pattern_ref, own_ref, lse_ref, rz_ref, rx_ref, ut_ref, a_ref, sums_ref):
    flags = Flags(pattern_ref)
    tail = slice(heads * HD, heads * HD + TAIL)
    own = lse_ref[...]
    z = jnp.where(flags.far_in, joined_rows(rz_ref[tail]), NEG_BIG)
    x = jnp.where(flags.side_in, joined_rows(rx_ref[tail]), NEG_BIG)
    highest = jnp.maximum(own, jnp.maximum(z, x))
    total = highest + jnp.log(jnp.exp(own - highest) + jnp.exp(z - highest) + jnp.exp(x - highest))
    own, z, x = jnp.exp(own - total), jnp.exp(z - total), jnp.exp(x - total)
    squares = jnp.zeros((8, BLOCK), jnp.float32)
    crosses = jnp.zeros((8, BLOCK), jnp.float32)
    for h in range(heads):
        at, row = rows_of(h), slice(h, h + 1)
        out = (
            own_ref[at] * own[row]
            + rz_ref[at].astype(jnp.float32) * z[row]
            + rx_ref[at].astype(jnp.float32) * x[row]
        ).astype(jnp.bfloat16)
        a_ref[at] = out
        wide = out.astype(jnp.float32)
        squares += (wide * wide).reshape(HD // 8, 8, BLOCK).sum(axis=0)
        crosses += (wide * ut_ref[at].astype(jnp.float32)).reshape(HD // 8, 8, BLOCK).sum(axis=0)
    a_ref[tail] = split_rows(total)
    sums_ref[...] = stack_rows([squares.sum(axis=0, keepdims=True), crosses.sum(axis=0, keepdims=True)])


def norm_rows(sums_ref):
    inverse = lax.rsqrt(sums_ref[0:1] / WIDTH + EPSILON)
    return inverse, inverse**3 * sums_ref[1:2] / WIDTH


def upstream_part(norm, u, a):
    inverse, factor = norm
    wide = a.astype(jnp.float32)
    grad = (inverse * u.astype(jnp.float32) - wide * factor).astype(jnp.bfloat16)
    return grad, jnp.sum(grad.astype(jnp.float32) * wide, axis=0, keepdims=True)


def pair_back(q, k, v, grad, delta, lse, keep):
    weights = jnp.exp(jnp.where(keep, score_tile(k, q), NEG_BIG) - lse)
    dscore = (weights * (mm(v, grad, NN) - delta) * SCALE).astype(jnp.bfloat16)
    return mm(dscore, q, NN), mm(weights.astype(jnp.bfloat16), grad, NT), mm(dscore, k, TN)


def near_back_kernel(
    heads, pattern_ref, sums_ref, q_ref, up_ref, down_ref, a_ref, ut_ref, dq_ref, dkv2_ref, grad_ref, delta_ref
):
    flags = Flags(pattern_ref)
    half, near = flags.half, flags.near
    first, second = slice(0, BLOCK), slice(BLOCK, 2 * BLOCK)
    norm = norm_rows(sums_ref)
    lse = joined_rows(a_ref[heads * HD : heads * HD + TAIL])
    deltas = []
    for h in range(heads):
        at = rows_of(h)
        grad, delta = upstream_part(norm, ut_ref[at], a_ref[at])
        k2 = jnp.where(half, down_ref[first, at], up_ref[first, at])
        v2 = jnp.where(half, down_ref[second, at], up_ref[second, at])
        dkv2_ref[0, :, at], dkv2_ref[1, :, at], dq_ref[:, at] = pair_back(
            q_ref[:, at], k2, v2, grad, delta, lse[h : h + 1], near
        )
        grad_ref[at] = grad
        deltas.append(delta)
    delta_ref[...] = stack_rows(deltas)


def diagonal_back_kernel(
    heads,
    sums_ref,
    q_ref,
    k_ref,
    v_ref,
    a_ref,
    grad_ref,
    delta_ref,
    dq_in_ref,
    dside_ref,
    normed_ref,
    dq_ref,
    dkv_ref,
):
    inverse, _ = norm_rows(sums_ref)
    lse = joined_rows(a_ref[heads * HD : heads * HD + TAIL])
    causal = causal_mask()
    for h in range(heads):
        at, row = rows_of(h), slice(h, h + 1)
        normed_ref[:, at] = (a_ref[at].astype(jnp.float32) * inverse).astype(jnp.bfloat16).T
        dk, dv, dq = pair_back(
            q_ref[:, at], k_ref[:, at], v_ref[:, at], grad_ref[at], delta_ref[row], lse[row], causal
        )
        dkv_ref[0, :, at] = dside_ref[0, :, at] + dk
        dkv_ref[1, :, at] = dside_ref[1, :, at] + dv
        dq_ref[:, at] = dq_in_ref[:, at] + dq


def helper_back_kernel(
    heads,
    pattern_ref,
    sz_ref,
    sx_ref,
    up_ref,
    down_ref,
    qx_ref,
    k_ref,
    v_ref,
    az_ref,
    ax_ref,
    uzt_ref,
    uxt_ref,
    ez_ref,
    ex_ref,
    mz_ref,
    mx_ref,
    own_ref,
    up_out_ref,
    down_out_ref,
    dqx_ref,
    dside_ref,
):
    flags = Flags(pattern_ref)
    odd, half = flags.odd, flags.half
    first, second = slice(0, BLOCK), slice(BLOCK, 2 * BLOCK)
    tail = slice(heads * HD, heads * HD + TAIL)
    z_norm, x_norm = norm_rows(sz_ref), norm_rows(sx_ref)
    z_scale = jnp.where(flags.far, jnp.exp(mz_ref[...] - joined_rows(az_ref[tail])), 0.0)
    x_scale = jnp.where(flags.side, jnp.exp(mx_ref[...] - joined_rows(ax_ref[tail])), 0.0)
    share = odd.astype(jnp.float32)

    def one(norm, u, a, weights, value):
        grad, delta = upstream_part(norm, u, a)
        dscore = (weights * (mm(value, grad, NN) - delta) * SCALE).astype(jnp.bfloat16)
        return grad, weights.astype(jnp.bfloat16), dscore

    for h in range(heads):
        at, row = rows_of(h), slice(h, h + 1)
        up_a, down_a = up_ref[first, at], down_ref[first, at]
        k2, qz = jnp.where(half, down_a, up_a), jnp.where(half, up_a, down_a)
        v2 = jnp.where(half, down_ref[second, at], up_ref[second, at])
        ks, vs, qx = jnp.where(odd, k2, k_ref[:, at]), jnp.where(odd, v2, v_ref[:, at]), qx_ref[:, at]
        gz, pz, dz = one(z_norm, uzt_ref[at], az_ref[at], ez_ref[at] * z_scale[row], v2)
        gx, px, dx = one(x_norm, uxt_ref[at], ax_ref[at], ex_ref[at] * x_scale[row], vs)
        dks, dvs = mm(dx, qx, NN), mm(px, gx, NT)
        dk2 = (own_ref[0, :, at] + mm(dz, qz, NN) + share * dks).astype(jnp.bfloat16)
        dv2 = (own_ref[1, :, at] + mm(pz, gz, NT) + share * dvs).astype(jnp.bfloat16)
        dqz = mm(dz, k2, TN).astype(jnp.bfloat16)
        dqx_ref[:, at] = mm(dx, ks, TN).astype(jnp.bfloat16)
        up_out_ref[first, at] = jnp.where(half, dk2, dqz)
        up_out_ref[second, at] = dv2
        down_out_ref[first, at] = jnp.where(half, dqz, dk2)
        down_out_ref[second, at] = dv2
        dside_ref[0, :, at] = (1.0 - share) * dks
        dside_ref[1, :, at] = (1.0 - share) * dvs


def final_kernel(heads, pattern_ref, up_ref, down_ref, dqx_ref, dq_own_ref, dkv_own_ref, dq_ref, dk_ref, dv_ref):
    flags = Flags(pattern_ref)
    half = flags.half
    first, second = slice(0, BLOCK), slice(BLOCK, 2 * BLOCK)
    ahead = flags.ahead.astype(jnp.float32)
    far = flags.far_in.astype(jnp.float32)
    for h in range(heads):
        at = rows_of(h)
        up_a, down_a = up_ref[first, at], down_ref[first, at]
        dqz = jnp.where(half, down_a, up_a).astype(jnp.float32) * far
        dk = jnp.where(half, up_a, down_a).astype(jnp.float32) * ahead
        dv = jnp.where(half, up_ref[second, at], down_ref[second, at]).astype(jnp.float32) * ahead
        dq_ref[:, at] = (dq_own_ref[:, at] + dqx_ref[:, at].astype(jnp.float32) + dqz).astype(jnp.bfloat16)
        dk_ref[:, at] = (dkv_own_ref[0, :, at] + dk).astype(jnp.bfloat16)
        dv_ref[:, at] = (dkv_own_ref[1, :, at] + dv).astype(jnp.bfloat16)


def call(kernel, heads, flags, arrays, outs, flops, space=pltpu.VMEM, scratch=(), limit=24):
    moved = sum(math.prod(a.shape) * a.dtype.itemsize for a in (*arrays, *outs))
    return pl.pallas_call(
        functools.partial(kernel, heads),
        out_shape=outs,
        in_specs=[pl.BlockSpec(memory_space=pltpu.SMEM)] * len(flags)
        + [pl.BlockSpec(memory_space=space)] * len(arrays),
        out_specs=[pl.BlockSpec(memory_space=pltpu.VMEM)] * len(outs),
        scratch_shapes=scratch,
        compiler_params=pltpu.CompilerParams(vmem_limit_bytes=limit * 2**20),
        cost_estimate=pl.CostEstimate(flops=flops, bytes_accessed=moved, transcendentals=0),
    )(*flags, *arrays)


def cycles(blocks, members):
    route = []
    for block in range(blocks):
        for member in range(members):
            rising = member < members // 2
            other = member + members // 2 if rising else member - members // 2
            target = block + 2 if rising else block - 2
            inside = 0 <= target < blocks
            route.append(
                (block * members + member, target * members + member if inside else block * members + other)
            )
    return route


def meeting_shards(queries, keys, values, pattern, upstream):
    tokens, width = queries.shape
    heads = width // HD
    blocks, members = lax.axis_size("ctx"), lax.axis_size("head")
    flags = (pattern,)
    unit = heads * 2 * BLOCK**3
    rising = cycles(blocks, members)
    falling = [(target, source) for source, target in rising]

    def cycle(up_array, down_array):
        return lax.ppermute(up_array, ("ctx", "head"), rising), lax.ppermute(
            down_array, ("ctx", "head"), falling
        )

    def swap(array):
        return lax.ppermute(array, "ctx", [(i, i ^ 1) for i in range(blocks)])

    def ring(array, distance):
        return lax.ppermute(array, "ctx", [(i, (i + distance) % blocks) for i in range(blocks)])

    def struct(*shape, dtype=jnp.bfloat16):
        return jax.ShapeDtypeStruct(shape, dtype)

    wide = struct(tokens, width, dtype=jnp.float32)
    wide_t = struct(width, tokens, dtype=jnp.float32)
    wide_pair = struct(2, tokens, width, dtype=jnp.float32)
    flat, flat_t = struct(tokens, width), struct(width, tokens)
    double = struct(2 * tokens, width)
    message = struct(width + TAIL, tokens)
    rows = struct(8, tokens, dtype=jnp.float32)

    up_out, down_out = call(
        payload_kernel,
        heads,
        (),
        [pltpu.with_memory_space_constraint(a, pltpu.HBM) for a in (queries, keys, values, upstream)],
        [pltpu.VMEM((2 * tokens, width), jnp.bfloat16)] * 2,
        0,
        space=pltpu.HBM,
        scratch=(pltpu.SemaphoreType.DMA((4,)),),
    )
    up_in, down_in = cycle(up_out, down_out)
    queries_x, upstream_x = swap(queries), swap(upstream)
    diagonal, diagonal_lse, upstream_t = call(
        diagonal_kernel, heads, (), (queries, keys, values, upstream), (wide_t, rows, flat_t), 3 * unit
    )
    up_in, down_in, queries_x, upstream_x = lax.optimization_barrier((up_in, down_in, queries_x, upstream_x))
    out_z, out_x, ez, ex, mz, mx = call(
        helper_kernel,
        heads,
        (),
        (up_in, down_in, queries_x, keys, values),
        (message, message, wide_t, wide_t, rows, rows),
        4 * unit,
    )
    back_z, back_x = ring(out_z, 2), swap(out_x)
    own, own_lse, upstream_zt, upstream_xt = call(
        own_kernel,
        heads,
        flags,
        (up_in, down_in, queries, upstream_x, diagonal, diagonal_lse),
        (wide_t, rows, flat_t, flat_t),
        3 * unit,
    )
    attention, sums = call(
        merge_kernel, heads, flags, (own, own_lse, back_z, back_x, upstream_t), (message, rows), unit // 64
    )
    others = [
        lax.ppermute(sums, "head", [(i, i ^ step) for i in range(members)]) for step in range(1, members)
    ]
    attention_z, attention_x = ring(attention, -2), swap(attention)
    sums = functools.reduce(jnp.add, others, sums)
    sums_z, sums_x = ring(sums, -2), swap(sums)
    dq_own, grads2_own, grad_t, delta = call(
        near_back_kernel,
        heads,
        flags,
        (sums, queries, up_in, down_in, attention, upstream_t),
        (wide, wide_pair, flat_t, rows),
        5 * unit,
    )
    up_out, down_out, dq_x, dside = call(
        helper_back_kernel,
        heads,
        flags,
        (sums_z, sums_x, up_in, down_in, queries_x, keys, values, attention_z, attention_x)
        + (upstream_zt, upstream_xt, ez, ex, mz, mx, grads2_own),
        (double, double, flat, wide_pair),
        8 * unit,
    )
    up_in, down_in = cycle(up_out, down_out)
    dq_x = swap(dq_x)
    normed, dq_own, grads_own = call(
        diagonal_back_kernel,
        heads,
        (),
        (sums, queries, keys, values, attention, grad_t, delta, dq_own, dside),
        (flat, wide, wide_pair),
        6 * unit,
    )
    grad_queries, grad_keys, grad_values = call(
        final_kernel, heads, flags, (up_in, down_in, dq_x, dq_own, grads_own), (flat, flat, flat), 0
    )
    return (normed, grad_queries, grad_keys, grad_values)


def shards(queries, keys, values, pattern, upstream):
    fits = lax.axis_size("ctx") == 8 and lax.axis_size("head") == 4 and queries.shape == (BLOCK, 8 * HD)
    if fits:
        return meeting_shards(queries, keys, values, pattern, upstream)
    return generic_shards(queries, keys, values, pattern, upstream)


def solution(mesh):
    return jax.shard_map(
        shards,
        mesh=mesh,
        in_specs=(P("ctx", "head"), P("ctx", "head"), P("ctx", "head"), P(), P("ctx", "head")),
        out_specs=(P("ctx", "head"), P("ctx", "head"), P("ctx", "head"), P("ctx", "head")),
        check_vma=False,
    )
```

```python
import functools
import math

import jax
import jax.numpy as jnp
from jax import lax
from jax.experimental import pallas as pl
from jax.experimental.pallas import tpu as pltpu
from jax.sharding import PartitionSpec as P

HD = 128
BLOCK = 128
LEVELS = 7
WIDTH = 4096


NEG_BIG = -1e30
EPSILON = 1e-06


def shifted(block, axis, distance):
    devices = range(lax.axis_size(axis))
    route = [(i - distance, i) for i in devices if i - distance in devices]
    return lax.ppermute(block, axis, route)


def for_sending(x):
    return jax.tree.map(lambda a: a.astype(jnp.bfloat16) if a.dtype == jnp.float32 else a, x)


def route_table(blocks, levels):
    routing = []
    for query_block in range(blocks):
        for level_index in range(levels + 1):
            if level_index == levels:
                routing.append((0, query_block))
            else:
                distance = 2**level_index
                routing.append(
                    (-((query_block - distance) // blocks), (query_block - distance) % blocks)
                )
    return routing


def pair_grads(
    query_tiles, grad_tiles, lse_tiles, delta_tiles, key_tiles, value_tiles, keep_mask, score_scale
):
    scores = (
        jnp.einsum("pqhd,pkhd->phqk", query_tiles, key_tiles, preferred_element_type=jnp.float32)
        * score_scale
    )
    scores = jnp.where(keep_mask[:, None], scores, NEG_BIG)
    weights = jnp.exp(scores - lse_tiles[..., None])
    prob_tiles = weights.astype(jnp.bfloat16)
    grad_probs = jnp.einsum(
        "pqhd,pkhd->phqk", grad_tiles, value_tiles, preferred_element_type=jnp.float32
    )
    dscore = (weights * (grad_probs - delta_tiles[..., None]) * score_scale).astype(jnp.bfloat16)
    return (dscore, prob_tiles)


def key_grads(dscore, prob_tiles, query_tiles, grad_tiles):
    key_part = jnp.einsum(
        "phqk,pqhd->pkhd", dscore, query_tiles, preferred_element_type=jnp.float32
    )
    value_part = jnp.einsum(
        "phqk,pqhd->pkhd", prob_tiles, grad_tiles, preferred_element_type=jnp.float32
    )
    return jnp.stack((key_part, value_part))


def collect(partials, targets, blocks):
    pieces = []
    for key_index in range(blocks):
        summed = jnp.zeros((2,) + partials.shape[2:], jnp.float32)
        for row_index, target in enumerate(targets):
            if target == key_index:
                summed = summed + partials[:, row_index]
        pieces.append(summed)
    return jnp.stack(pieces, axis=1)


def generic_shards(queries, keys, values, pattern, upstream):
    tokens_here = queries.shape[0]
    heads_here = queries.shape[1] // HD
    blocks = tokens_here // BLOCK
    slot_count = LEVELS + 1
    pair_count = blocks * slot_count
    score_scale = HD ** (-0.5)
    ctx_count = lax.axis_size("ctx")
    device_index = lax.axis_index("ctx")
    routing = route_table(blocks, LEVELS)
    offsets = sorted(
        set((route_entry[0] for route_entry in routing if 0 < route_entry[0] < ctx_count))
    )
    tile_shape = (blocks, BLOCK, heads_here, HD)
    query_blocks = queries.reshape(tile_shape)
    own_pairs = jnp.stack((keys, values)).reshape((2,) + tile_shape)
    sources = {0: own_pairs}
    for offset in offsets:
        fetched = shifted(jnp.stack((keys, values)), "ctx", offset)
        sources[offset] = fetched.reshape((2,) + tile_shape)
    empty_tile = jnp.zeros((2, BLOCK, heads_here, HD), jnp.bfloat16)
    gathered = []
    for source, key_index in routing:
        if source in sources:
            gathered.append(sources[source][:, key_index])
        else:
            gathered.append(empty_tile)
    pair_kv = jnp.stack(gathered, axis=1)
    key_tiles = pair_kv[0]
    value_tiles = pair_kv[1]
    key_stack = key_tiles.reshape((blocks, slot_count) + tile_shape[1:])
    value_stack = value_tiles.reshape((blocks, slot_count) + tile_shape[1:])
    own_rows = lax.dynamic_slice_in_dim(pattern, device_index * blocks, blocks, 0)
    positions = jnp.arange(BLOCK)
    causal = positions[None, :] <= positions[:, None]
    self_slot = jnp.arange(slot_count) == LEVELS
    tile_keep = (own_rows >= 0)[:, :, None, None] & (
        jnp.logical_not(self_slot)[None, :, None, None] | causal[None, None]
    )
    scores = (
        jnp.einsum("bqhd,bskhd->bhqsk", query_blocks, key_stack, preferred_element_type=jnp.float32)
        * score_scale
    )
    scores = jnp.where(jnp.transpose(tile_keep, (0, 2, 1, 3))[:, None], scores, NEG_BIG)
    highest = jnp.max(scores, axis=(3, 4))
    log_total = highest + jnp.log(jnp.sum(jnp.exp(scores - highest[..., None, None]), axis=(3, 4)))
    prob_stack = jnp.exp(scores - log_total[..., None, None]).astype(jnp.bfloat16)
    attention = jnp.einsum(
        "bhqsk,bskhd->bqhd", prob_stack, value_stack, preferred_element_type=jnp.float32
    ).astype(jnp.bfloat16)
    attn_wide = attention.reshape(tokens_here, heads_here * HD).astype(jnp.float32)
    square_sum = lax.psum(jnp.sum(attn_wide * attn_wide, axis=1), "head")
    inverse = lax.rsqrt(square_sum / WIDTH + EPSILON)
    normed = (attn_wide * inverse[:, None]).astype(jnp.bfloat16)
    upstream_wide = upstream.astype(jnp.float32)
    cross_term = lax.psum(jnp.sum(upstream_wide * attn_wide, axis=1), "head")
    grad_attn = (
        inverse[:, None] * upstream_wide - attn_wide * (inverse**3 * cross_term / WIDTH)[:, None]
    ).astype(jnp.bfloat16)
    row_delta = jnp.sum(
        (grad_attn.astype(jnp.float32) * attn_wide).reshape(tokens_here, heads_here, HD), axis=2
    )
    row_delta = jnp.transpose(row_delta.reshape(blocks, BLOCK, heads_here), (0, 2, 1))

    def spread(array):
        return jnp.broadcast_to(array[:, None], (blocks, slot_count) + array.shape[1:]).reshape(
            (pair_count,) + array.shape[1:]
        )

    grad_blocks = grad_attn.reshape(tile_shape)
    query_pairs = spread(query_blocks)
    grad_pairs = spread(grad_blocks)
    keep_pairs = tile_keep.reshape(pair_count, BLOCK, BLOCK)
    dscore, prob_pairs = pair_grads(
        query_pairs,
        grad_pairs,
        spread(log_total),
        spread(row_delta),
        key_tiles,
        value_tiles,
        keep_pairs,
        score_scale,
    )
    grad_query = jnp.einsum(
        "phqk,pkhd->pqhd", dscore, key_tiles, preferred_element_type=jnp.float32
    )
    grad_query = jnp.sum(grad_query.reshape((blocks, slot_count) + tile_shape[1:]), axis=1)
    grad_queries = grad_query.astype(jnp.bfloat16).reshape(tokens_here, heads_here * HD)
    local_rows = [row_index for row_index in range(pair_count) if routing[row_index][0] == 0]
    chosen = jnp.array(local_rows, jnp.int32)
    local_terms = key_grads(
        dscore[chosen], prob_pairs[chosen], query_pairs[chosen], grad_pairs[chosen]
    )
    key_sum = collect(local_terms, [routing[row_index][1] for row_index in local_rows], blocks)
    for offset in offsets:
        remote_rows = [
            row_index for row_index in range(pair_count) if routing[row_index][0] == offset
        ]
        chosen = jnp.array(remote_rows, jnp.int32)
        remote_terms = key_grads(
            dscore[chosen], prob_pairs[chosen], query_pairs[chosen], grad_pairs[chosen]
        )
        outgoing = collect(
            remote_terms, [routing[row_index][1] for row_index in remote_rows], blocks
        )
        key_sum = key_sum + shifted(for_sending(outgoing), "ctx", -offset).astype(outgoing.dtype)
    grad_keys = key_sum[0].astype(jnp.bfloat16).reshape(tokens_here, heads_here * HD)
    grad_values = key_sum[1].astype(jnp.bfloat16).reshape(tokens_here, heads_here * HD)
    return (normed, grad_queries, grad_keys, grad_values)


NT = (((1,), (1,)), ((), ()))
NN = (((1,), (0,)), ((), ()))
TN = (((0,), (0,)), ((), ()))
SCALE = HD ** (-0.5)
TAIL = 32


class Flags:
    def __init__(self, pattern_ref=None):
        me, member = lax.axis_index("ctx"), lax.axis_index("head")
        self.odd = lax.rem(me, 2) == 1
        self.half = member >= lax.axis_size("head") // 2
        if pattern_ref is None:
            return
        blocks = pattern_ref.shape[0]
        even = jnp.logical_not(self.odd)
        ahead = jnp.minimum(me + 2, blocks - 1)
        self.ahead = me + 2 < blocks
        self.near = pattern_ref[me, 1] >= 0
        self.far = jnp.logical_and(self.ahead, pattern_ref[ahead, 2] >= 0)
        ahead_side = jnp.logical_and(self.ahead, pattern_ref[ahead, 0] >= 0)
        own_side = pattern_ref[me, 0] >= 0
        self.side = jnp.logical_or(
            jnp.logical_and(self.odd, own_side), jnp.logical_and(even, ahead_side)
        )
        self.helped = jnp.logical_or(pattern_ref[me, 2] >= 0, jnp.logical_and(even, own_side))


def mm(a, b, dims):
    return lax.dot_general(a, b, dims, preferred_element_type=jnp.float32)


def rows_of(h):
    return slice(h * HD, (h + 1) * HD)


def causal_mask():
    keys = lax.broadcasted_iota(jnp.int32, (BLOCK, BLOCK), 0)
    return keys <= lax.broadcasted_iota(jnp.int32, (BLOCK, BLOCK), 1)


def split_rows(rows):
    first = rows.astype(jnp.bfloat16).astype(jnp.float32)
    second = (rows - first).astype(jnp.bfloat16).astype(jnp.float32)
    third = rows - first - second
    return jnp.concatenate([first, second, third, jnp.zeros_like(rows)], axis=0).astype(jnp.bfloat16)


def joined_rows(tile):
    wide = tile.astype(jnp.float32)
    return wide[0:8] + wide[8:16] + wide[16:24]


def stack_rows(rows):
    return jnp.concatenate(rows + [jnp.zeros((1, BLOCK), jnp.float32)] * (8 - len(rows)), axis=0)


def score_tile(keys, queries):
    return mm(keys, queries, NT) * SCALE


def softmax_parts(pairs):
    tops = [scores.max(axis=0, keepdims=True) for scores, _ in pairs]
    weights = [jnp.exp(scores - top) for (scores, _), top in zip(pairs, tops)]
    totals = [w.sum(axis=0, keepdims=True) for w in weights]
    outs = [
        mm(value, w.astype(jnp.bfloat16), TN) * (1.0 / total)
        for (_, value), w, total in zip(pairs, weights, totals)
    ]
    return [(out, top, top + jnp.log(total), w) for out, top, total, w in zip(outs, tops, totals, weights)]


FIRST, SECOND = slice(0, BLOCK), slice(BLOCK, 2 * BLOCK)


def payload_kernel(heads, q_ref, k_ref, v_ref, u_ref, up_ref, down_ref, sems):
    half = Flags().half
    top, bottom = pl.ds(0, BLOCK), pl.ds(BLOCK, BLOCK)

    def move(sources):
        targets = (up_ref.at[top], up_ref.at[bottom], down_ref.at[top], down_ref.at[bottom])
        copies = [
            pltpu.make_async_copy(source, target, sems.at[n])
            for n, (source, target) in enumerate(zip(sources, targets))
        ]
        for copy in copies:
            copy.start()
        for copy in copies:
            copy.wait()

    @pl.when(jnp.logical_not(half))
    def _():
        move((k_ref, v_ref, q_ref, u_ref))

    @pl.when(half)
    def _():
        move((q_ref, u_ref, k_ref, v_ref))


def diagonal_kernel(heads, q_ref, k_ref, v_ref, u_ref, out_ref, lse_ref, ut_ref):
    causal = causal_mask()
    rows = []
    for h in range(heads):
        at = rows_of(h)
        scores = jnp.where(causal, score_tile(k_ref[:, at], q_ref[:, at]), NEG_BIG)
        ((out, _, lse, _),) = softmax_parts([(scores, v_ref[:, at])])
        out_ref[at] = out
        rows.append(lse)
        ut_ref[at] = u_ref[:, at].T
    lse_ref[...] = stack_rows(rows)


def merged(parts):
    highest = functools.reduce(jnp.maximum, [lse for _, lse in parts])
    total = highest + jnp.log(functools.reduce(jnp.add, [jnp.exp(lse - highest) for _, lse in parts]))
    return functools.reduce(jnp.add, [out * jnp.exp(lse - total) for out, lse in parts]), total


def helper_kernel(
    heads,
    pattern_ref,
    up_ref,
    down_ref,
    q_ref,
    kx_ref,
    vx_ref,
    oz_ref,
    ez_ref,
    ex_ref,
    outx_ref,
    mz_ref,
    mx_ref,
    lsex_ref,
):
    flags = Flags(pattern_ref)
    odd, half = flags.odd, flags.half
    joins = jnp.logical_and(flags.side, jnp.logical_not(odd))
    z_rows, x_rows, z_tops, x_tops = [], [], [], []
    for start in range(0, heads, 2):
        pairs = []
        for h in range(start, start + 2):
            at = rows_of(h)
            up_a, down_a = up_ref[FIRST, at], down_ref[FIRST, at]
            k2, qz = jnp.where(half, down_a, up_a), jnp.where(half, up_a, down_a)
            v2 = jnp.where(half, down_ref[SECOND, at], up_ref[SECOND, at])
            pairs.append((score_tile(k2, qz), v2))
            pairs.append((score_tile(kx_ref[:, at], jnp.where(odd, q_ref[:, at], qz)), vx_ref[:, at]))
        parts = softmax_parts(pairs)
        for n, h in enumerate(range(start, start + 2)):
            at = rows_of(h)
            (z_out, z_top, z_lse, ez_ref[at]), (x_out, x_top, x_lse, ex_ref[at]) = parts[2 * n : 2 * n + 2]
            out, lse = merged(
                [(z_out, jnp.where(flags.far, z_lse, NEG_BIG)), (x_out, jnp.where(joins, x_lse, NEG_BIG))]
            )
            oz_ref[at] = out.astype(jnp.bfloat16)
            outx_ref[at] = x_out
            z_rows.append(lse)
            x_rows.append(x_lse)
            z_tops.append(z_top)
            x_tops.append(x_top)
    oz_ref[heads * HD :] = split_rows(stack_rows(z_rows))
    lsex_ref[...] = stack_rows(x_rows)
    mz_ref[...] = stack_rows(z_tops)
    mx_ref[...] = stack_rows(x_tops)


def own_kernel(
    heads,
    pattern_ref,
    up_ref,
    down_ref,
    q_ref,
    out_ref,
    lse_ref,
    outx_ref,
    lsex_ref,
    own_ref,
    total_ref,
    uzt_ref,
    e_ref,
    m_ref,
):
    flags = Flags(pattern_ref)
    half = flags.half
    local = jnp.logical_and(flags.odd, flags.side)
    before, side = lse_ref[...], jnp.where(local, lsex_ref[...], NEG_BIG)
    rows, tops = [], []
    for start in range(0, heads, 2):
        group = range(start, start + 2)
        pairs = []
        for h in group:
            at = rows_of(h)
            k2 = jnp.where(half, down_ref[FIRST, at], up_ref[FIRST, at])
            up_b, down_b = up_ref[SECOND, at], down_ref[SECOND, at]
            uzt_ref[at] = jnp.where(half, up_b, down_b).T
            pairs.append((score_tile(k2, q_ref[:, at]), jnp.where(half, down_b, up_b)))
        for h, (out, top, lse, e_ref[rows_of(h)]) in zip(group, softmax_parts(pairs)):
            at, row = rows_of(h), slice(h, h + 1)
            own_ref[at], total = merged(
                [
                    (out_ref[at], before[row]),
                    (out, jnp.where(flags.near, lse, NEG_BIG)),
                    (outx_ref[at], side[row]),
                ]
            )
            rows.append(total)
            tops.append(top)
    total_ref[...] = stack_rows(rows)
    m_ref[...] = stack_rows(tops)


def merge_kernel(heads, pattern_ref, own_ref, lse_ref, rz_ref, ut_ref, a_ref, sums_ref):
    flags = Flags(pattern_ref)
    tail = slice(heads * HD, heads * HD + TAIL)
    squares = jnp.zeros((8, BLOCK), jnp.float32)
    crosses = jnp.zeros((8, BLOCK), jnp.float32)
    own = lse_ref[...]
    z = jnp.where(flags.helped, joined_rows(rz_ref[tail]), NEG_BIG)
    highest = jnp.maximum(own, z)
    total = highest + jnp.log(jnp.exp(own - highest) + jnp.exp(z - highest))
    own, z = jnp.exp(own - total), jnp.exp(z - total)
    for h in range(heads):
        at, row = rows_of(h), slice(h, h + 1)
        out = (own_ref[at] * own[row] + rz_ref[at].astype(jnp.float32) * z[row]).astype(jnp.bfloat16)
        a_ref[at] = out
        wide = out.astype(jnp.float32)
        squares += (wide * wide).reshape(HD // 8, 8, BLOCK).sum(axis=0)
        crosses += (wide * ut_ref[at].astype(jnp.float32)).reshape(HD // 8, 8, BLOCK).sum(axis=0)
    a_ref[tail] = split_rows(total)
    sums_ref[...] = stack_rows([squares.sum(axis=0, keepdims=True), crosses.sum(axis=0, keepdims=True)])


def norm_rows(sums_ref):
    inverse = lax.rsqrt(sums_ref[0:1] / WIDTH + EPSILON)
    return inverse, inverse**3 * sums_ref[1:2] / WIDTH


def total_rows(a_ref):
    return joined_rows(a_ref[a_ref.shape[0] - TAIL :])


def upstream_part(norm, u, a):
    inverse, factor = norm
    wide = a.astype(jnp.float32)
    grad = (inverse * u.astype(jnp.float32) - wide * factor).astype(jnp.bfloat16)
    return grad, jnp.sum(grad.astype(jnp.float32) * wide, axis=0, keepdims=True)


def near_back_kernel(
    heads,
    pattern_ref,
    sums_ref,
    q_ref,
    a_ref,
    ut_ref,
    up_ref,
    down_ref,
    e_ref,
    m_ref,
    grad_ref,
    delta_ref,
    ds_ref,
    dkv2_ref,
):
    flags = Flags(pattern_ref)
    half = flags.half
    norm = norm_rows(sums_ref)
    scale = jnp.where(flags.near, jnp.exp(m_ref[...] - total_rows(a_ref)), 0.0)
    deltas = []
    for start in range(0, heads, 4):
        group = range(start, start + 4)
        parts = [upstream_part(norm, ut_ref[rows_of(h)], a_ref[rows_of(h)]) for h in group]
        for h, (grad, delta) in zip(group, parts):
            grad_ref[rows_of(h)] = grad
            deltas.append(delta)
        products = []
        for h, (grad, _) in zip(group, parts):
            v2 = jnp.where(half, down_ref[SECOND, rows_of(h)], up_ref[SECOND, rows_of(h)])
            products.append(mm(v2, grad, NN))
        scores = []
        for h, product, (_, delta) in zip(group, products, parts):
            weights = e_ref[rows_of(h)] * scale[h : h + 1]
            dscore = (weights * (product - delta) * SCALE).astype(jnp.bfloat16)
            scores.append((dscore, weights.astype(jnp.bfloat16)))
        for h, (dscore, probs), (grad, _) in zip(group, scores, parts):
            at = rows_of(h)
            ds_ref[at] = dscore
            dkv2_ref[0, :, at] = mm(dscore, q_ref[:, at], NN)
            dkv2_ref[1, :, at] = mm(probs, grad, NT)
    delta_ref[...] = stack_rows(deltas)


def helper_back_kernel(
    heads,
    pattern_ref,
    sz_ref,
    az_ref,
    uzt_ref,
    a_ref,
    grad_ref,
    delta_ref,
    up_ref,
    down_ref,
    q_ref,
    kx_ref,
    vx_ref,
    ez_ref,
    ex_ref,
    mz_ref,
    mx_ref,
    near_ref,
    up_out_ref,
    down_out_ref,
    side_out_ref,
    dsx_ref,
):
    flags = Flags(pattern_ref)
    odd, half = flags.odd, flags.half
    norm = norm_rows(sz_ref)
    z_lse = total_rows(az_ref)
    scales = (
        jnp.where(flags.far, jnp.exp(mz_ref[...] - z_lse), 0.0),
        jnp.where(flags.side, jnp.exp(mx_ref[...] - jnp.where(odd, total_rows(a_ref), z_lse)), 0.0),
    )
    own_deltas = delta_ref[...]
    for start in range(0, heads, 2):
        group = range(start, start + 2)
        parts, products, scores = [], [], []
        for h in group:
            grad, delta = upstream_part(norm, uzt_ref[rows_of(h)], az_ref[rows_of(h)])
            parts.append((grad, delta))
            parts.append(
                (jnp.where(odd, grad_ref[rows_of(h)], grad), jnp.where(odd, own_deltas[h : h + 1], delta))
            )
        for n, h in enumerate(group):
            at = rows_of(h)
            v2 = jnp.where(half, down_ref[SECOND, at], up_ref[SECOND, at])
            products.append(mm(v2, parts[2 * n][0], NN))
            products.append(mm(vx_ref[:, at], parts[2 * n + 1][0], NN))
        for n, ((_, delta), product) in enumerate(zip(parts, products)):
            h = group[n // 2]
            weights = (ez_ref, ex_ref)[n % 2][rows_of(h)] * scales[n % 2][h : h + 1]
            dscore = (weights * (product - delta) * SCALE).astype(jnp.bfloat16)
            scores.append((dscore, weights.astype(jnp.bfloat16)))
        for n, h in enumerate(group):
            at = rows_of(h)
            (gz, _), (gx, _) = parts[2 * n : 2 * n + 2]
            (dz, pz), (dx, px) = scores[2 * n : 2 * n + 2]
            up_a, down_a = up_ref[FIRST, at], down_ref[FIRST, at]
            k2, qz = jnp.where(half, down_a, up_a), jnp.where(half, up_a, down_a)
            dsx_ref[at] = dx
            dk2 = (near_ref[0, :, at] + mm(dz, qz, NN)).astype(jnp.bfloat16)
            dv2 = (near_ref[1, :, at] + mm(pz, gz, NT)).astype(jnp.bfloat16)
            side_out_ref[FIRST, at] = mm(dx, jnp.where(odd, q_ref[:, at], qz), NN).astype(jnp.bfloat16)
            side_out_ref[SECOND, at] = mm(px, gx, NT).astype(jnp.bfloat16)
            joined = jnp.concatenate([dz, jnp.where(odd, jnp.zeros_like(dx), dx)], axis=0)
            dqz = mm(joined, jnp.concatenate([k2, kx_ref[:, at]], axis=0), TN).astype(jnp.bfloat16)
            up_out_ref[FIRST, at] = jnp.where(half, dk2, dqz)
            up_out_ref[SECOND, at] = dv2
            down_out_ref[FIRST, at] = jnp.where(half, dqz, dk2)
            down_out_ref[SECOND, at] = dv2


def diagonal_back_kernel(
    heads,
    sums_ref,
    q_ref,
    k_ref,
    v_ref,
    a_ref,
    grad_ref,
    delta_ref,
    ds_ref,
    dsx_ref,
    kx_ref,
    up_ref,
    down_ref,
    normed_ref,
    dq_ref,
    dkv_ref,
):
    flags = Flags()
    half, odd = flags.half, flags.odd
    inverse, _ = norm_rows(sums_ref)
    lse = total_rows(a_ref)
    causal = causal_mask()
    for h in range(heads):
        at, row = rows_of(h), slice(h, h + 1)
        normed_ref[:, at] = (a_ref[at].astype(jnp.float32) * inverse).astype(jnp.bfloat16).T
        q, k, v, grad = q_ref[:, at], k_ref[:, at], v_ref[:, at], grad_ref[at]
        weights = jnp.exp(jnp.where(causal, score_tile(k, q), NEG_BIG) - lse[row])
        dscore = (weights * (mm(v, grad, NN) - delta_ref[row]) * SCALE).astype(jnp.bfloat16)
        dkv_ref[0, :, at] = mm(dscore, q, NN)
        dkv_ref[1, :, at] = mm(weights.astype(jnp.bfloat16), grad, NT)
        k2 = jnp.where(half, down_ref[FIRST, at], up_ref[FIRST, at])
        dsx = jnp.where(odd, dsx_ref[at], jnp.zeros_like(dsx_ref[at]))
        dq_ref[:, at] = mm(dscore, k, TN) + mm(
            jnp.concatenate([ds_ref[at], dsx], axis=0), jnp.concatenate([k2, kx_ref[:, at]], axis=0), TN
        )


def final_kernel(
    heads, pattern_ref, dq_own_ref, dkv_own_ref, side_ref, up_ref, down_ref, dq_ref, dk_ref, dv_ref
):
    flags = Flags(pattern_ref)
    half = flags.half
    ahead = flags.ahead.astype(jnp.float32)
    helped = flags.helped.astype(jnp.float32)
    for h in range(heads):
        at = rows_of(h)
        up_a, down_a = up_ref[FIRST, at], down_ref[FIRST, at]
        dqz = jnp.where(half, down_a, up_a).astype(jnp.float32) * helped
        dk = jnp.where(half, up_a, down_a).astype(jnp.float32) * ahead
        dv = jnp.where(half, up_ref[SECOND, at], down_ref[SECOND, at]).astype(jnp.float32) * ahead
        dq_ref[:, at] = (dq_own_ref[:, at] + dqz).astype(jnp.bfloat16)
        dk_ref[:, at] = (dkv_own_ref[0, :, at] + side_ref[FIRST, at].astype(jnp.float32) + dk).astype(jnp.bfloat16)
        dv_ref[:, at] = (dkv_own_ref[1, :, at] + side_ref[SECOND, at].astype(jnp.float32) + dv).astype(jnp.bfloat16)


def call(kernel, heads, flags, arrays, outs, flops, space=pltpu.VMEM, scratch=(), after=()):
    moved = sum(math.prod(a.shape) * a.dtype.itemsize for a in (*arrays, *outs))
    return pl.pallas_call(
        lambda *refs: kernel(heads, *refs[len(after) :]),
        out_shape=outs,
        in_specs=[pl.BlockSpec(memory_space=pl.ANY)] * len(after)
        + [pl.BlockSpec(memory_space=pltpu.SMEM)] * len(flags)
        + [pl.BlockSpec(memory_space=space)] * len(arrays),
        out_specs=[pl.BlockSpec(memory_space=pltpu.VMEM)] * len(outs),
        scratch_shapes=scratch,
        compiler_params=pltpu.CompilerParams(vmem_limit_bytes=24 * 2**20),
        cost_estimate=pl.CostEstimate(flops=flops, bytes_accessed=moved, transcendentals=0),
    )(*after, *flags, *arrays)


def cycles(blocks, members):
    route = []
    for block in range(blocks):
        for member in range(members):
            rising = member < members // 2
            other = member + members // 2 if rising else member - members // 2
            target = block + 2 if rising else block - 2
            inside = 0 <= target < blocks
            route.append(
                (block * members + member, target * members + member if inside else block * members + other)
            )
    return route


def meeting_shards(queries, keys, values, pattern, upstream):
    tokens, width = queries.shape
    heads = width // HD
    blocks, members = lax.axis_size("ctx"), lax.axis_size("head")
    flags = (pattern,)
    unit = heads * 2 * BLOCK**3
    rising = cycles(blocks, members)
    falling = [(target, source) for source, target in rising]

    def cycle(up_array, down_array):
        return lax.ppermute(up_array, ("ctx", "head"), rising), lax.ppermute(
            down_array, ("ctx", "head"), falling
        )

    def swap(array):
        return lax.ppermute(array, "ctx", [(i, i ^ 1) for i in range(blocks)])

    def ring(array, distance):
        return lax.ppermute(array, "ctx", [(i, (i + distance) % blocks) for i in range(blocks)])

    def struct(*shape, dtype=jnp.bfloat16):
        return jax.ShapeDtypeStruct(shape, dtype)

    wide = struct(tokens, width, dtype=jnp.float32)
    wide_t = struct(width, tokens, dtype=jnp.float32)
    wide_pair = struct(2, tokens, width, dtype=jnp.float32)
    flat, flat_t = struct(tokens, width), struct(width, tokens)
    double = struct(2 * tokens, width)
    message = struct(width + TAIL, tokens)
    rows = struct(8, tokens, dtype=jnp.float32)

    payload = call(
        payload_kernel,
        heads,
        (),
        [pltpu.with_memory_space_constraint(a, pltpu.HBM) for a in (queries, keys, values, upstream)],
        [pltpu.VMEM((2 * tokens, width), jnp.bfloat16)] * 2,
        0,
        space=pltpu.HBM,
        scratch=(pltpu.SemaphoreType.DMA((4,)),),
    )
    received = cycle(*payload)
    keys_x, values_x = swap(keys), swap(values)
    diagonal, diagonal_lse, upstream_t = call(
        diagonal_kernel,
        heads,
        (),
        (queries, keys, values, upstream),
        (wide_t, rows, flat_t),
        3 * unit,
        after=(payload[0],),
    )
    out_z, ez, ex, out_x, mz, mx, lse_x = call(
        helper_kernel,
        heads,
        flags,
        (*received, queries, keys_x, values_x),
        (message, wide_t, wide_t, wide_t, rows, rows, rows),
        4 * unit,
        after=(diagonal_lse,),
    )
    back_z = ring(out_z, 2)
    own, own_lse, upstream_zt, e2, m2 = call(
        own_kernel,
        heads,
        flags,
        (*received, queries, diagonal, diagonal_lse, out_x, lse_x),
        (wide_t, rows, flat_t, wide_t, rows),
        3 * unit,
    )
    attention, sums = call(
        merge_kernel, heads, flags, (own, own_lse, back_z, upstream_t), (message, rows), unit // 64
    )
    others = [
        lax.ppermute(sums, "head", [(i, i ^ step) for i in range(members)]) for step in range(1, members)
    ]
    attention_z = ring(attention, -2)
    sums = functools.reduce(jnp.add, others, sums)
    sums_z = ring(sums, -2)
    grad_t, delta, near_ds, near_grads = call(
        near_back_kernel,
        heads,
        flags,
        (sums, queries, attention, upstream_t, *received, e2, m2),
        (flat_t, rows, flat_t, wide_pair),
        3 * unit,
    )
    up_out, down_out, side_out, side_ds = call(
        helper_back_kernel,
        heads,
        flags,
        (sums_z, attention_z, upstream_zt, attention, grad_t, delta, *received, queries, keys_x, values_x)
        + (ez, ex, mz, mx, near_grads),
        (double, double, double, flat_t),
        8 * unit,
    )
    returned = cycle(up_out, down_out)
    side_grads = swap(side_out)
    normed, dq_own, grads_own = call(
        diagonal_back_kernel,
        heads,
        (),
        (sums, queries, keys, values, attention, grad_t, delta, near_ds, side_ds, keys_x, *received),
        (flat, wide, wide_pair),
        7 * unit,
    )
    grad_queries, grad_keys, grad_values = call(
        final_kernel, heads, flags, (dq_own, grads_own, side_grads, *returned), (flat, flat, flat), 0
    )
    return (normed, grad_queries, grad_keys, grad_values)


def shards(queries, keys, values, pattern, upstream):
    fits = lax.axis_size("ctx") == 8 and lax.axis_size("head") == 4 and queries.shape == (BLOCK, 8 * HD)
    if fits:
        return meeting_shards(queries, keys, values, pattern, upstream)
    return generic_shards(queries, keys, values, pattern, upstream)


def solution(mesh):
    return jax.shard_map(
        shards,
        mesh=mesh,
        in_specs=(P("ctx", "head"), P("ctx", "head"), P("ctx", "head"), P(), P("ctx", "head")),
        out_specs=(P("ctx", "head"), P("ctx", "head"), P("ctx", "head"), P("ctx", "head")),
        check_vma=False,
    )
```

```python
import functools
import math

import jax
import jax.numpy as jnp
from jax import lax
from jax.experimental import pallas as pl
from jax.experimental.pallas import tpu as pltpu
from jax.sharding import PartitionSpec as P

HD = 128
BLOCK = 128
LEVELS = 7
WIDTH = 4096


NEG_BIG = -1e30
EPSILON = 1e-06


def shifted(block, axis, distance):
    devices = range(lax.axis_size(axis))
    route = [(i - distance, i) for i in devices if i - distance in devices]
    return lax.ppermute(block, axis, route)


def for_sending(x):
    return jax.tree.map(lambda a: a.astype(jnp.bfloat16) if a.dtype == jnp.float32 else a, x)


def route_table(blocks, levels):
    routing = []
    for query_block in range(blocks):
        for level_index in range(levels + 1):
            if level_index == levels:
                routing.append((0, query_block))
            else:
                distance = 2**level_index
                routing.append(
                    (-((query_block - distance) // blocks), (query_block - distance) % blocks)
                )
    return routing


def pair_grads(
    query_tiles, grad_tiles, lse_tiles, delta_tiles, key_tiles, value_tiles, keep_mask, score_scale
):
    scores = (
        jnp.einsum("pqhd,pkhd->phqk", query_tiles, key_tiles, preferred_element_type=jnp.float32)
        * score_scale
    )
    scores = jnp.where(keep_mask[:, None], scores, NEG_BIG)
    weights = jnp.exp(scores - lse_tiles[..., None])
    prob_tiles = weights.astype(jnp.bfloat16)
    grad_probs = jnp.einsum(
        "pqhd,pkhd->phqk", grad_tiles, value_tiles, preferred_element_type=jnp.float32
    )
    dscore = (weights * (grad_probs - delta_tiles[..., None]) * score_scale).astype(jnp.bfloat16)
    return (dscore, prob_tiles)


def key_grads(dscore, prob_tiles, query_tiles, grad_tiles):
    key_part = jnp.einsum(
        "phqk,pqhd->pkhd", dscore, query_tiles, preferred_element_type=jnp.float32
    )
    value_part = jnp.einsum(
        "phqk,pqhd->pkhd", prob_tiles, grad_tiles, preferred_element_type=jnp.float32
    )
    return jnp.stack((key_part, value_part))


def collect(partials, targets, blocks):
    pieces = []
    for key_index in range(blocks):
        summed = jnp.zeros((2,) + partials.shape[2:], jnp.float32)
        for row_index, target in enumerate(targets):
            if target == key_index:
                summed = summed + partials[:, row_index]
        pieces.append(summed)
    return jnp.stack(pieces, axis=1)


def generic_shards(queries, keys, values, pattern, upstream):
    tokens_here = queries.shape[0]
    heads_here = queries.shape[1] // HD
    blocks = tokens_here // BLOCK
    slot_count = LEVELS + 1
    pair_count = blocks * slot_count
    score_scale = HD ** (-0.5)
    ctx_count = lax.axis_size("ctx")
    device_index = lax.axis_index("ctx")
    routing = route_table(blocks, LEVELS)
    offsets = sorted(
        set((route_entry[0] for route_entry in routing if 0 < route_entry[0] < ctx_count))
    )
    tile_shape = (blocks, BLOCK, heads_here, HD)
    query_blocks = queries.reshape(tile_shape)
    own_pairs = jnp.stack((keys, values)).reshape((2,) + tile_shape)
    sources = {0: own_pairs}
    for offset in offsets:
        fetched = shifted(jnp.stack((keys, values)), "ctx", offset)
        sources[offset] = fetched.reshape((2,) + tile_shape)
    empty_tile = jnp.zeros((2, BLOCK, heads_here, HD), jnp.bfloat16)
    gathered = []
    for source, key_index in routing:
        if source in sources:
            gathered.append(sources[source][:, key_index])
        else:
            gathered.append(empty_tile)
    pair_kv = jnp.stack(gathered, axis=1)
    key_tiles = pair_kv[0]
    value_tiles = pair_kv[1]
    key_stack = key_tiles.reshape((blocks, slot_count) + tile_shape[1:])
    value_stack = value_tiles.reshape((blocks, slot_count) + tile_shape[1:])
    own_rows = lax.dynamic_slice_in_dim(pattern, device_index * blocks, blocks, 0)
    positions = jnp.arange(BLOCK)
    causal = positions[None, :] <= positions[:, None]
    self_slot = jnp.arange(slot_count) == LEVELS
    tile_keep = (own_rows >= 0)[:, :, None, None] & (
        jnp.logical_not(self_slot)[None, :, None, None] | causal[None, None]
    )
    scores = (
        jnp.einsum("bqhd,bskhd->bhqsk", query_blocks, key_stack, preferred_element_type=jnp.float32)
        * score_scale
    )
    scores = jnp.where(jnp.transpose(tile_keep, (0, 2, 1, 3))[:, None], scores, NEG_BIG)
    highest = jnp.max(scores, axis=(3, 4))
    log_total = highest + jnp.log(jnp.sum(jnp.exp(scores - highest[..., None, None]), axis=(3, 4)))
    prob_stack = jnp.exp(scores - log_total[..., None, None]).astype(jnp.bfloat16)
    attention = jnp.einsum(
        "bhqsk,bskhd->bqhd", prob_stack, value_stack, preferred_element_type=jnp.float32
    ).astype(jnp.bfloat16)
    attn_wide = attention.reshape(tokens_here, heads_here * HD).astype(jnp.float32)
    square_sum = lax.psum(jnp.sum(attn_wide * attn_wide, axis=1), "head")
    inverse = lax.rsqrt(square_sum / WIDTH + EPSILON)
    normed = (attn_wide * inverse[:, None]).astype(jnp.bfloat16)
    upstream_wide = upstream.astype(jnp.float32)
    cross_term = lax.psum(jnp.sum(upstream_wide * attn_wide, axis=1), "head")
    grad_attn = (
        inverse[:, None] * upstream_wide - attn_wide * (inverse**3 * cross_term / WIDTH)[:, None]
    ).astype(jnp.bfloat16)
    row_delta = jnp.sum(
        (grad_attn.astype(jnp.float32) * attn_wide).reshape(tokens_here, heads_here, HD), axis=2
    )
    row_delta = jnp.transpose(row_delta.reshape(blocks, BLOCK, heads_here), (0, 2, 1))

    def spread(array):
        return jnp.broadcast_to(array[:, None], (blocks, slot_count) + array.shape[1:]).reshape(
            (pair_count,) + array.shape[1:]
        )

    grad_blocks = grad_attn.reshape(tile_shape)
    query_pairs = spread(query_blocks)
    grad_pairs = spread(grad_blocks)
    keep_pairs = tile_keep.reshape(pair_count, BLOCK, BLOCK)
    dscore, prob_pairs = pair_grads(
        query_pairs,
        grad_pairs,
        spread(log_total),
        spread(row_delta),
        key_tiles,
        value_tiles,
        keep_pairs,
        score_scale,
    )
    grad_query = jnp.einsum(
        "phqk,pkhd->pqhd", dscore, key_tiles, preferred_element_type=jnp.float32
    )
    grad_query = jnp.sum(grad_query.reshape((blocks, slot_count) + tile_shape[1:]), axis=1)
    grad_queries = grad_query.astype(jnp.bfloat16).reshape(tokens_here, heads_here * HD)
    local_rows = [row_index for row_index in range(pair_count) if routing[row_index][0] == 0]
    chosen = jnp.array(local_rows, jnp.int32)
    local_terms = key_grads(
        dscore[chosen], prob_pairs[chosen], query_pairs[chosen], grad_pairs[chosen]
    )
    key_sum = collect(local_terms, [routing[row_index][1] for row_index in local_rows], blocks)
    for offset in offsets:
        remote_rows = [
            row_index for row_index in range(pair_count) if routing[row_index][0] == offset
        ]
        chosen = jnp.array(remote_rows, jnp.int32)
        remote_terms = key_grads(
            dscore[chosen], prob_pairs[chosen], query_pairs[chosen], grad_pairs[chosen]
        )
        outgoing = collect(
            remote_terms, [routing[row_index][1] for row_index in remote_rows], blocks
        )
        key_sum = key_sum + shifted(for_sending(outgoing), "ctx", -offset).astype(outgoing.dtype)
    grad_keys = key_sum[0].astype(jnp.bfloat16).reshape(tokens_here, heads_here * HD)
    grad_values = key_sum[1].astype(jnp.bfloat16).reshape(tokens_here, heads_here * HD)
    return (normed, grad_queries, grad_keys, grad_values)


NT = (((1,), (1,)), ((), ()))
NN = (((1,), (0,)), ((), ()))
TN = (((0,), (0,)), ((), ()))
SCALE = HD ** (-0.5)
TAIL = 32


NEAR, FAR, SIDE, HELPED, LOCAL = range(5)


class Place:
    def __init__(self):
        self.me = lax.axis_index("ctx")
        self.odd = lax.rem(self.me, 2) == 1
        self.half = lax.axis_index("head") >= lax.axis_size("head") // 2


def bias_rows(pattern_ref):
    place = Place()
    me, odd, even = place.me, place.odd, jnp.logical_not(place.odd)
    blocks = pattern_ref.shape[0]
    ahead = jnp.minimum(me + 2, blocks - 1)
    has_ahead = me + 2 < blocks
    ahead_side = jnp.logical_and(has_ahead, pattern_ref[ahead, 0] >= 0)
    own_side = pattern_ref[me, 0] >= 0
    local = jnp.logical_and(odd, own_side)
    held = {
        NEAR: pattern_ref[me, 1] >= 0,
        FAR: jnp.logical_and(has_ahead, pattern_ref[ahead, 2] >= 0),
        SIDE: jnp.logical_or(local, jnp.logical_and(even, ahead_side)),
        HELPED: jnp.logical_or(pattern_ref[me, 2] >= 0, jnp.logical_and(even, own_side)),
        LOCAL: local,
    }
    row = lax.broadcasted_iota(jnp.int32, (8, BLOCK), 0)
    rows = jnp.zeros((8, BLOCK), jnp.float32)
    for index, flag in held.items():
        rows = jnp.where(row == index, jnp.where(flag, 0.0, NEG_BIG), rows)
    return rows


def mm(a, b, dims):
    return lax.dot_general(a, b, dims, preferred_element_type=jnp.float32)


def rows_of(h):
    return slice(h * HD, (h + 1) * HD)


def causal_mask():
    keys = lax.broadcasted_iota(jnp.int32, (BLOCK, BLOCK), 0)
    return keys <= lax.broadcasted_iota(jnp.int32, (BLOCK, BLOCK), 1)


def split_rows(rows):
    first = rows.astype(jnp.bfloat16).astype(jnp.float32)
    second = (rows - first).astype(jnp.bfloat16).astype(jnp.float32)
    third = rows - first - second
    return jnp.concatenate([first, second, third, jnp.zeros_like(rows)], axis=0).astype(jnp.bfloat16)


def joined_rows(tile):
    wide = tile.astype(jnp.float32)
    return wide[0:8] + wide[8:16] + wide[16:24]


def stack_rows(rows):
    return jnp.concatenate(rows + [jnp.zeros((1, BLOCK), jnp.float32)] * (8 - len(rows)), axis=0)


def score_tile(keys, queries):
    return mm(keys, queries, NT) * SCALE


def softmax_parts(pairs):
    tops = [scores.max(axis=0, keepdims=True) for scores, _ in pairs]
    weights = [jnp.exp(scores - top) for (scores, _), top in zip(pairs, tops)]
    totals = [w.sum(axis=0, keepdims=True) for w in weights]
    outs = [
        mm(value, w.astype(jnp.bfloat16), TN) * (1.0 / total)
        for (_, value), w, total in zip(pairs, weights, totals)
    ]
    return [(out, top, top + jnp.log(total), w) for out, top, total, w in zip(outs, tops, totals, weights)]


FIRST, SECOND = slice(0, BLOCK), slice(BLOCK, 2 * BLOCK)


def payload_kernel(heads, q_ref, k_ref, v_ref, u_ref, up_ref, down_ref, sems):
    half = Place().half
    top, bottom = pl.ds(0, BLOCK), pl.ds(BLOCK, BLOCK)

    def move(sources):
        targets = (up_ref.at[top], up_ref.at[bottom], down_ref.at[top], down_ref.at[bottom])
        copies = [
            pltpu.make_async_copy(source, target, sems.at[n])
            for n, (source, target) in enumerate(zip(sources, targets))
        ]
        for copy in copies:
            copy.start()
        for copy in copies:
            copy.wait()

    @pl.when(jnp.logical_not(half))
    def _():
        move((k_ref, v_ref, q_ref, u_ref))

    @pl.when(half)
    def _():
        move((q_ref, u_ref, k_ref, v_ref))


def diagonal_kernel(heads, pattern_ref, q_ref, k_ref, v_ref, u_ref, out_ref, lse_ref, ut_ref, bias_ref):
    bias_ref[...] = bias_rows(pattern_ref)
    causal = causal_mask()
    rows = []
    for h in range(heads):
        at = rows_of(h)
        scores = jnp.where(causal, score_tile(k_ref[:, at], q_ref[:, at]), NEG_BIG)
        ((out, _, lse, _),) = softmax_parts([(scores, v_ref[:, at])])
        out_ref[at] = out
        rows.append(lse)
        ut_ref[at] = u_ref[:, at].T
    lse_ref[...] = stack_rows(rows)


def merged(parts):
    highest = functools.reduce(jnp.maximum, [lse for _, lse in parts])
    total = highest + jnp.log(functools.reduce(jnp.add, [jnp.exp(lse - highest) for _, lse in parts]))
    return functools.reduce(jnp.add, [out * jnp.exp(lse - total) for out, lse in parts]), total


def helper_kernel(
    heads, bias_ref, up_ref, down_ref, q_ref, kx_ref, vx_ref, oz_ref, ez_ref, ex_ref, mz_ref, mx_ref
):
    place = Place()
    odd, half = place.odd, place.half
    far, side = bias_ref[FAR : FAR + 1], bias_ref[SIDE : SIDE + 1]
    step = 4
    z_rows, z_tops, x_tops = [], [], []
    for start in range(0, heads, step):
        group = range(start, start + step)
        scores, weights, totals = [], [], []
        for h in group:
            at = rows_of(h)
            up_a, down_a = up_ref[FIRST, at], down_ref[FIRST, at]
            k2, qz = jnp.where(half, down_a, up_a), jnp.where(half, up_a, down_a)
            qx = jnp.where(odd, q_ref[:, at], qz)
            scores.append((score_tile(k2, qz) + far, score_tile(kx_ref[:, at], qx) + side))
        for h, (z, x) in zip(group, scores):
            z_top, x_top = z.max(axis=0, keepdims=True), x.max(axis=0, keepdims=True)
            both = jnp.maximum(z_top, x_top)
            z_top, x_top = jnp.where(odd, z_top, both), jnp.where(odd, x_top, both)
            z, x = jnp.exp(z - z_top), jnp.exp(x - x_top)
            ez_ref[rows_of(h)], ex_ref[rows_of(h)] = z, x
            x = jnp.where(odd, 0.0, x)
            total = z.sum(axis=0, keepdims=True) + x.sum(axis=0, keepdims=True)
            weights.append(jnp.concatenate([z, x], axis=0).astype(jnp.bfloat16))
            totals.append(total)
            z_rows.append(z_top + jnp.log(total))
            z_tops.append(z_top)
            x_tops.append(x_top)
        for h, w, total in zip(group, weights, totals):
            at = rows_of(h)
            v2 = jnp.where(half, down_ref[SECOND, at], up_ref[SECOND, at])
            out = mm(jnp.concatenate([v2, vx_ref[:, at]], axis=0), w, TN) * (1.0 / total)
            oz_ref[at] = out.astype(jnp.bfloat16)
    oz_ref[heads * HD :] = split_rows(stack_rows(z_rows))
    mz_ref[...] = stack_rows(z_tops)
    mx_ref[...] = stack_rows(x_tops)


def own_kernel(
    heads,
    bias_ref,
    up_ref,
    down_ref,
    q_ref,
    out_ref,
    lse_ref,
    vx_ref,
    ex_ref,
    mx_ref,
    own_ref,
    total_ref,
    uzt_ref,
    e_ref,
    m_ref,
):
    half = Place().half
    near, local = bias_ref[NEAR : NEAR + 1], bias_ref[LOCAL : LOCAL + 1]
    before = lse_ref[...]
    rows, tops = [], []
    for start in range(0, heads, 2):
        group = range(start, start + 2)
        pairs = []
        for h in group:
            at = rows_of(h)
            k2 = jnp.where(half, down_ref[FIRST, at], up_ref[FIRST, at])
            up_b, down_b = up_ref[SECOND, at], down_ref[SECOND, at]
            uzt_ref[at] = jnp.where(half, up_b, down_b).T
            pairs.append((score_tile(k2, q_ref[:, at]), jnp.where(half, down_b, up_b)))
        for h, (out, top, lse, e_ref[rows_of(h)]) in zip(group, softmax_parts(pairs)):
            at, row = rows_of(h), slice(h, h + 1)
            weights = ex_ref[at]
            side = jnp.maximum(weights.sum(axis=0, keepdims=True), 1.0)
            side_out = mm(vx_ref[:, at], weights.astype(jnp.bfloat16), TN) * (1.0 / side)
            own_ref[at], total = merged(
                [
                    (out_ref[at], before[row]),
                    (out, lse + near),
                    (side_out, mx_ref[row] + jnp.log(side) + local),
                ]
            )
            rows.append(total)
            tops.append(top)
    total_ref[...] = stack_rows(rows)
    m_ref[...] = stack_rows(tops)


def merge_kernel(heads, bias_ref, own_ref, lse_ref, rz_ref, ut_ref, a_ref, sums_ref):
    tail = slice(heads * HD, heads * HD + TAIL)
    squares = jnp.zeros((8, BLOCK), jnp.float32)
    crosses = jnp.zeros((8, BLOCK), jnp.float32)
    own = lse_ref[...]
    z = joined_rows(rz_ref[tail]) + bias_ref[HELPED : HELPED + 1]
    highest = jnp.maximum(own, z)
    total = highest + jnp.log(jnp.exp(own - highest) + jnp.exp(z - highest))
    own, z = jnp.exp(own - total), jnp.exp(z - total)
    for h in range(heads):
        at, row = rows_of(h), slice(h, h + 1)
        out = (own_ref[at] * own[row] + rz_ref[at].astype(jnp.float32) * z[row]).astype(jnp.bfloat16)
        a_ref[at] = out
        wide = out.astype(jnp.float32)
        squares += (wide * wide).reshape(HD // 8, 8, BLOCK).sum(axis=0)
        crosses += (wide * ut_ref[at].astype(jnp.float32)).reshape(HD // 8, 8, BLOCK).sum(axis=0)
    a_ref[tail] = split_rows(total)
    sums_ref[...] = stack_rows([squares.sum(axis=0, keepdims=True), crosses.sum(axis=0, keepdims=True)])


def norm_rows(sums_ref):
    inverse = lax.rsqrt(sums_ref[0:1] / WIDTH + EPSILON)
    return inverse, inverse**3 * sums_ref[1:2] / WIDTH


def total_rows(a_ref):
    return joined_rows(a_ref[a_ref.shape[0] - TAIL :])


def upstream_part(norm, u, a):
    inverse, factor = norm
    wide = a.astype(jnp.float32)
    grad = (inverse * u.astype(jnp.float32) - wide * factor).astype(jnp.bfloat16)
    return grad, jnp.sum(grad.astype(jnp.float32) * wide, axis=0, keepdims=True)


def near_back_kernel(
    heads,
    bias_ref,
    sums_ref,
    q_ref,
    a_ref,
    ut_ref,
    up_ref,
    down_ref,
    e_ref,
    m_ref,
    grad_ref,
    delta_ref,
    ds_ref,
    dk2_ref,
    dv2_ref,
):
    half = Place().half
    norm = norm_rows(sums_ref)
    scale = jnp.exp(m_ref[...] - total_rows(a_ref) + bias_ref[NEAR : NEAR + 1])
    deltas = []
    for start in range(0, heads, 4):
        group = range(start, start + 4)
        parts = [upstream_part(norm, ut_ref[rows_of(h)], a_ref[rows_of(h)]) for h in group]
        for h, (grad, delta) in zip(group, parts):
            grad_ref[rows_of(h)] = grad
            deltas.append(delta)
        products = []
        for h, (grad, _) in zip(group, parts):
            v2 = jnp.where(half, down_ref[SECOND, rows_of(h)], up_ref[SECOND, rows_of(h)])
            products.append(mm(v2, grad, NN))
        scores = []
        for h, product, (_, delta) in zip(group, products, parts):
            weights = e_ref[rows_of(h)] * scale[h : h + 1]
            dscore = (weights * (product - delta) * SCALE).astype(jnp.bfloat16)
            scores.append((dscore, weights.astype(jnp.bfloat16)))
        for h, (dscore, probs), (grad, _) in zip(group, scores, parts):
            at = rows_of(h)
            ds_ref[at] = dscore
            dk2_ref[:, at] = mm(dscore, q_ref[:, at], NN)
            dv2_ref[:, at] = mm(probs, grad, NT)
    delta_ref[...] = stack_rows(deltas)


def helper_back_kernel(
    heads,
    bias_ref,
    sz_ref,
    az_ref,
    uzt_ref,
    a_ref,
    grad_ref,
    delta_ref,
    up_ref,
    down_ref,
    kx_ref,
    vx_ref,
    ez_ref,
    ex_ref,
    mz_ref,
    mx_ref,
    near_ref,
    up_out_ref,
    down_out_ref,
    dvx_ref,
    dsz_ref,
    dsx_ref,
):
    place = Place()
    odd, half = place.odd, place.half
    norm = norm_rows(sz_ref)
    z_lse = total_rows(az_ref)
    scales = (
        jnp.exp(mz_ref[...] - z_lse + bias_ref[FAR : FAR + 1]),
        jnp.exp(mx_ref[...] - jnp.where(odd, total_rows(a_ref), z_lse) + bias_ref[SIDE : SIDE + 1]),
    )
    own_deltas = delta_ref[...]
    step = 2
    for start in range(0, heads, step):
        group = range(start, start + step)
        parts, products, scores = [], [], []
        for h in group:
            grad, delta = upstream_part(norm, uzt_ref[rows_of(h)], az_ref[rows_of(h)])
            parts.append((grad, delta))
            parts.append(
                (jnp.where(odd, grad_ref[rows_of(h)], grad), jnp.where(odd, own_deltas[h : h + 1], delta))
            )
        for n, h in enumerate(group):
            at = rows_of(h)
            v2 = jnp.where(half, down_ref[SECOND, at], up_ref[SECOND, at])
            products.append(mm(v2, parts[2 * n][0], NN))
            products.append(mm(vx_ref[:, at], parts[2 * n + 1][0], NN))
        for n, ((_, delta), product) in enumerate(zip(parts, products)):
            h = group[n // 2]
            weights = (ez_ref, ex_ref)[n % 2][rows_of(h)] * scales[n % 2][h : h + 1]
            dscore = (weights * (product - delta) * SCALE).astype(jnp.bfloat16)
            scores.append((dscore, weights.astype(jnp.bfloat16)))
        for n, h in enumerate(group):
            at = rows_of(h)
            (gz, _), (gx, _) = parts[2 * n : 2 * n + 2]
            (dz, pz), (dx, px) = scores[2 * n : 2 * n + 2]
            k2 = jnp.where(half, down_ref[FIRST, at], up_ref[FIRST, at])
            dsz_ref[at], dsx_ref[at] = dz, dx
            dv2 = (near_ref[:, at] + mm(pz, gz, NT)).astype(jnp.bfloat16)
            dvx_ref[:, at] = mm(px, gx, NT).astype(jnp.bfloat16)
            joined = jnp.concatenate([dz, jnp.where(odd, jnp.zeros_like(dx), dx)], axis=0)
            dqz = mm(joined, jnp.concatenate([k2, kx_ref[:, at]], axis=0), TN).astype(jnp.bfloat16)
            up_out_ref[:, at] = jnp.where(half, dv2, dqz)
            down_out_ref[:, at] = jnp.where(half, dqz, dv2)


def helper_keys_kernel(heads, q_ref, up_ref, down_ref, dsz_ref, dsx_ref, near_ref, dk_ref, dkx_ref):
    place = Place()
    for h in range(heads):
        at = rows_of(h)
        qz = jnp.where(place.half, up_ref[FIRST, at], down_ref[FIRST, at])
        qx = jnp.where(place.odd, q_ref[:, at], qz)
        dk_ref[:, at] = (near_ref[:, at] + mm(dsz_ref[at], qz, NN)).astype(jnp.bfloat16)
        dkx_ref[:, at] = mm(dsx_ref[at], qx, NN).astype(jnp.bfloat16)


def diagonal_back_kernel(
    heads,
    sums_ref,
    q_ref,
    k_ref,
    v_ref,
    a_ref,
    grad_ref,
    delta_ref,
    ds_ref,
    dsx_ref,
    kx_ref,
    up_ref,
    down_ref,
    normed_ref,
    dq_ref,
    dk_ref,
    dv_ref,
):
    place = Place()
    half, odd = place.half, place.odd
    inverse, _ = norm_rows(sums_ref)
    lse = total_rows(a_ref)
    causal = causal_mask()
    for h in range(heads):
        at, row = rows_of(h), slice(h, h + 1)
        normed_ref[:, at] = (a_ref[at].astype(jnp.float32) * inverse).astype(jnp.bfloat16).T
        q, k, v, grad = q_ref[:, at], k_ref[:, at], v_ref[:, at], grad_ref[at]
        weights = jnp.exp(jnp.where(causal, score_tile(k, q), NEG_BIG) - lse[row])
        dscore = (weights * (mm(v, grad, NN) - delta_ref[row]) * SCALE).astype(jnp.bfloat16)
        dk_ref[:, at] = mm(dscore, q, NN)
        dv_ref[:, at] = mm(weights.astype(jnp.bfloat16), grad, NT)
        k2 = jnp.where(half, down_ref[FIRST, at], up_ref[FIRST, at])
        dsx = jnp.where(odd, dsx_ref[at], jnp.zeros_like(dsx_ref[at]))
        dq_ref[:, at] = mm(dscore, k, TN) + mm(
            jnp.concatenate([ds_ref[at], dsx], axis=0), jnp.concatenate([k2, kx_ref[:, at]], axis=0), TN
        )


def final_first_kernel(heads, dq_own_ref, dv_own_ref, side_ref, up_ref, down_ref, dq_ref, dv_ref, token_ref):
    place = Place()
    half = place.half
    ahead = (place.me + 2 < lax.axis_size("ctx")).astype(jnp.float32)
    behind = (place.me >= 2).astype(jnp.float32)
    for h in range(heads):
        at = rows_of(h)
        up, down = up_ref[:, at], down_ref[:, at]
        dqz = jnp.where(half, down, up).astype(jnp.float32) * behind
        dv = jnp.where(half, up, down).astype(jnp.float32) * ahead
        dq_ref[:, at] = (dq_own_ref[:, at] + dqz).astype(jnp.bfloat16)
        dv_ref[:, at] = (dv_own_ref[:, at] + side_ref[:, at].astype(jnp.float32) + dv).astype(jnp.bfloat16)
    token_ref[...] = jnp.zeros_like(token_ref)


def final_keys_kernel(heads, dk_own_ref, side_ref, back_ref, dk_ref):
    ahead = (Place().me + 2 < lax.axis_size("ctx")).astype(jnp.float32)
    for h in range(heads):
        at = rows_of(h)
        dk = back_ref[:, at].astype(jnp.float32) * ahead
        dk_ref[:, at] = (dk_own_ref[:, at] + side_ref[:, at].astype(jnp.float32) + dk).astype(jnp.bfloat16)


def call(kernel, heads, flags, arrays, outs, flops, space=pltpu.VMEM, scratch=(), after=()):
    moved = sum(math.prod(a.shape) * a.dtype.itemsize for a in (*arrays, *outs))
    return pl.pallas_call(
        lambda *refs: kernel(heads, *refs[len(after) :]),
        out_shape=outs,
        in_specs=[pl.BlockSpec(memory_space=pl.ANY)] * len(after)
        + [pl.BlockSpec(memory_space=pltpu.SMEM)] * len(flags)
        + [pl.BlockSpec(memory_space=space)] * len(arrays),
        out_specs=[pl.BlockSpec(memory_space=pltpu.VMEM)] * len(outs),
        scratch_shapes=scratch,
        compiler_params=pltpu.CompilerParams(vmem_limit_bytes=24 * 2**20),
        cost_estimate=pl.CostEstimate(flops=flops, bytes_accessed=moved, transcendentals=0),
    )(*after, *flags, *arrays)


def cycles(blocks, members):
    route = []
    for block in range(blocks):
        for member in range(members):
            rising = member < members // 2
            other = member + members // 2 if rising else member - members // 2
            target = block + 2 if rising else block - 2
            inside = 0 <= target < blocks
            route.append(
                (block * members + member, target * members + member if inside else block * members + other)
            )
    return route


def meeting_shards(queries, keys, values, pattern, upstream):
    tokens, width = queries.shape
    heads = width // HD
    blocks, members = lax.axis_size("ctx"), lax.axis_size("head")
    unit = heads * 2 * BLOCK**3
    rising = cycles(blocks, members)
    falling = [(target, source) for source, target in rising]

    def cycle(up_array, down_array):
        return lax.ppermute(up_array, ("ctx", "head"), rising), lax.ppermute(
            down_array, ("ctx", "head"), falling
        )

    def swap(array):
        return lax.ppermute(array, "ctx", [(i, i ^ 1) for i in range(blocks)])

    def ring(array, distance):
        return lax.ppermute(array, "ctx", [(i, (i + distance) % blocks) for i in range(blocks)])

    def struct(*shape, dtype=jnp.bfloat16):
        return jax.ShapeDtypeStruct(shape, dtype)

    wide = struct(tokens, width, dtype=jnp.float32)
    wide_t = struct(width, tokens, dtype=jnp.float32)
    flat, flat_t = struct(tokens, width), struct(width, tokens)
    message = struct(width + TAIL, tokens)
    rows = struct(8, tokens, dtype=jnp.float32)

    payload = call(
        payload_kernel,
        heads,
        (),
        [pltpu.with_memory_space_constraint(a, pltpu.HBM) for a in (queries, keys, values, upstream)],
        [pltpu.VMEM((2 * tokens, width), jnp.bfloat16)] * 2,
        0,
        space=pltpu.HBM,
        scratch=(pltpu.SemaphoreType.DMA((4,)),),
    )
    received = cycle(*payload)
    keys_x, values_x = swap(keys), swap(values)
    diagonal, diagonal_lse, upstream_t, bias = call(
        diagonal_kernel,
        heads,
        (pattern,),
        (queries, keys, values, upstream),
        (wide_t, rows, flat_t, rows),
        3 * unit,
        after=(payload[0],),
    )
    out_z, ez, ex, mz, mx = call(
        helper_kernel,
        heads,
        (),
        (bias, *received, queries, keys_x, values_x),
        (message, wide_t, wide_t, rows, rows),
        4 * unit,
    )
    back_z = ring(out_z, 2)
    own, own_lse, upstream_zt, e2, m2 = call(
        own_kernel,
        heads,
        (),
        (bias, *received, queries, diagonal, diagonal_lse, values_x, ex, mx),
        (wide_t, rows, flat_t, wide_t, rows),
        3 * unit,
    )
    attention, sums = call(
        merge_kernel, heads, (), (bias, own, own_lse, back_z, upstream_t), (message, rows), unit // 64
    )
    others = [
        lax.ppermute(sums, "head", [(i, i ^ step) for i in range(members)]) for step in range(1, members)
    ]
    attention_z = ring(attention, -2)
    sums = functools.reduce(jnp.add, others, sums)
    sums_z = ring(sums, -2)
    grad_t, delta, near_ds, near_dk, near_dv = call(
        near_back_kernel,
        heads,
        (),
        (bias, sums, queries, attention, upstream_t, *received, e2, m2),
        (flat_t, rows, flat_t, wide, wide),
        3 * unit,
    )
    up_out, down_out, side_dv, far_ds, side_ds = call(
        helper_back_kernel,
        heads,
        (),
        (bias, sums_z, attention_z, upstream_zt, attention, grad_t, delta, *received, keys_x, values_x)
        + (ez, ex, mz, mx, near_dv),
        (flat, flat, flat, flat_t, flat_t),
        6 * unit,
    )
    returned = cycle(up_out, down_out)
    out_dk, side_dk = call(
        helper_keys_kernel,
        heads,
        (),
        (queries, *received, far_ds, side_ds, near_dk),
        (flat, flat),
        2 * unit,
    )
    back_dk = ring(out_dk, -2)
    side_dv, side_dk = swap(side_dv), swap(side_dk)
    normed, dq_own, dk_own, dv_own = call(
        diagonal_back_kernel,
        heads,
        (),
        (sums, queries, keys, values, attention, grad_t, delta, near_ds, side_ds, keys_x, *received),
        (flat, wide, wide, wide),
        7 * unit,
    )
    grad_queries, grad_values, token = call(
        final_first_kernel, heads, (), (dq_own, dv_own, side_dv, *returned), (flat, flat, rows), 0
    )
    (grad_keys,) = call(final_keys_kernel, heads, (), (dk_own, side_dk, back_dk), (flat,), 0, after=(token,))
    return (normed, grad_queries, grad_keys, grad_values)


def shards(queries, keys, values, pattern, upstream):
    fits = lax.axis_size("ctx") == 8 and lax.axis_size("head") == 4 and queries.shape == (BLOCK, 8 * HD)
    if fits:
        return meeting_shards(queries, keys, values, pattern, upstream)
    return generic_shards(queries, keys, values, pattern, upstream)


def solution(mesh):
    return jax.shard_map(
        shards,
        mesh=mesh,
        in_specs=(P("ctx", "head"), P("ctx", "head"), P("ctx", "head"), P(), P("ctx", "head")),
        out_specs=(P("ctx", "head"), P("ctx", "head"), P("ctx", "head"), P("ctx", "head")),
        check_vma=False,
    )
```

```python
import functools
import math

import jax
import jax.numpy as jnp
from jax import lax
from jax.experimental import pallas as pl
from jax.experimental.pallas import tpu as pltpu
from jax.sharding import PartitionSpec as P

HD = 128
BLOCK = 128
LEVELS = 7
WIDTH = 4096


NEG_BIG = -1e30
EPSILON = 1e-06


def shifted(block, axis, distance):
    devices = range(lax.axis_size(axis))
    route = [(i - distance, i) for i in devices if i - distance in devices]
    return lax.ppermute(block, axis, route)


def for_sending(x):
    return jax.tree.map(lambda a: a.astype(jnp.bfloat16) if a.dtype == jnp.float32 else a, x)


def route_table(blocks, levels):
    routing = []
    for query_block in range(blocks):
        for level_index in range(levels + 1):
            if level_index == levels:
                routing.append((0, query_block))
            else:
                distance = 2**level_index
                routing.append(
                    (-((query_block - distance) // blocks), (query_block - distance) % blocks)
                )
    return routing


def pair_grads(
    query_tiles, grad_tiles, lse_tiles, delta_tiles, key_tiles, value_tiles, keep_mask, score_scale
):
    scores = (
        jnp.einsum("pqhd,pkhd->phqk", query_tiles, key_tiles, preferred_element_type=jnp.float32)
        * score_scale
    )
    scores = jnp.where(keep_mask[:, None], scores, NEG_BIG)
    weights = jnp.exp(scores - lse_tiles[..., None])
    prob_tiles = weights.astype(jnp.bfloat16)
    grad_probs = jnp.einsum(
        "pqhd,pkhd->phqk", grad_tiles, value_tiles, preferred_element_type=jnp.float32
    )
    dscore = (weights * (grad_probs - delta_tiles[..., None]) * score_scale).astype(jnp.bfloat16)
    return (dscore, prob_tiles)


def key_grads(dscore, prob_tiles, query_tiles, grad_tiles):
    key_part = jnp.einsum(
        "phqk,pqhd->pkhd", dscore, query_tiles, preferred_element_type=jnp.float32
    )
    value_part = jnp.einsum(
        "phqk,pqhd->pkhd", prob_tiles, grad_tiles, preferred_element_type=jnp.float32
    )
    return jnp.stack((key_part, value_part))


def collect(partials, targets, blocks):
    pieces = []
    for key_index in range(blocks):
        summed = jnp.zeros((2,) + partials.shape[2:], jnp.float32)
        for row_index, target in enumerate(targets):
            if target == key_index:
                summed = summed + partials[:, row_index]
        pieces.append(summed)
    return jnp.stack(pieces, axis=1)


def generic_shards(queries, keys, values, pattern, upstream):
    tokens_here = queries.shape[0]
    heads_here = queries.shape[1] // HD
    blocks = tokens_here // BLOCK
    slot_count = LEVELS + 1
    pair_count = blocks * slot_count
    score_scale = HD ** (-0.5)
    ctx_count = lax.axis_size("ctx")
    device_index = lax.axis_index("ctx")
    routing = route_table(blocks, LEVELS)
    offsets = sorted(
        set((route_entry[0] for route_entry in routing if 0 < route_entry[0] < ctx_count))
    )
    tile_shape = (blocks, BLOCK, heads_here, HD)
    query_blocks = queries.reshape(tile_shape)
    own_pairs = jnp.stack((keys, values)).reshape((2,) + tile_shape)
    sources = {0: own_pairs}
    for offset in offsets:
        fetched = shifted(jnp.stack((keys, values)), "ctx", offset)
        sources[offset] = fetched.reshape((2,) + tile_shape)
    empty_tile = jnp.zeros((2, BLOCK, heads_here, HD), jnp.bfloat16)
    gathered = []
    for source, key_index in routing:
        if source in sources:
            gathered.append(sources[source][:, key_index])
        else:
            gathered.append(empty_tile)
    pair_kv = jnp.stack(gathered, axis=1)
    key_tiles = pair_kv[0]
    value_tiles = pair_kv[1]
    key_stack = key_tiles.reshape((blocks, slot_count) + tile_shape[1:])
    value_stack = value_tiles.reshape((blocks, slot_count) + tile_shape[1:])
    own_rows = lax.dynamic_slice_in_dim(pattern, device_index * blocks, blocks, 0)
    positions = jnp.arange(BLOCK)
    causal = positions[None, :] <= positions[:, None]
    self_slot = jnp.arange(slot_count) == LEVELS
    tile_keep = (own_rows >= 0)[:, :, None, None] & (
        jnp.logical_not(self_slot)[None, :, None, None] | causal[None, None]
    )
    scores = (
        jnp.einsum("bqhd,bskhd->bhqsk", query_blocks, key_stack, preferred_element_type=jnp.float32)
        * score_scale
    )
    scores = jnp.where(jnp.transpose(tile_keep, (0, 2, 1, 3))[:, None], scores, NEG_BIG)
    highest = jnp.max(scores, axis=(3, 4))
    log_total = highest + jnp.log(jnp.sum(jnp.exp(scores - highest[..., None, None]), axis=(3, 4)))
    prob_stack = jnp.exp(scores - log_total[..., None, None]).astype(jnp.bfloat16)
    attention = jnp.einsum(
        "bhqsk,bskhd->bqhd", prob_stack, value_stack, preferred_element_type=jnp.float32
    ).astype(jnp.bfloat16)
    attn_wide = attention.reshape(tokens_here, heads_here * HD).astype(jnp.float32)
    square_sum = lax.psum(jnp.sum(attn_wide * attn_wide, axis=1), "head")
    inverse = lax.rsqrt(square_sum / WIDTH + EPSILON)
    normed = (attn_wide * inverse[:, None]).astype(jnp.bfloat16)
    upstream_wide = upstream.astype(jnp.float32)
    cross_term = lax.psum(jnp.sum(upstream_wide * attn_wide, axis=1), "head")
    grad_attn = (
        inverse[:, None] * upstream_wide - attn_wide * (inverse**3 * cross_term / WIDTH)[:, None]
    ).astype(jnp.bfloat16)
    row_delta = jnp.sum(
        (grad_attn.astype(jnp.float32) * attn_wide).reshape(tokens_here, heads_here, HD), axis=2
    )
    row_delta = jnp.transpose(row_delta.reshape(blocks, BLOCK, heads_here), (0, 2, 1))

    def spread(array):
        return jnp.broadcast_to(array[:, None], (blocks, slot_count) + array.shape[1:]).reshape(
            (pair_count,) + array.shape[1:]
        )

    grad_blocks = grad_attn.reshape(tile_shape)
    query_pairs = spread(query_blocks)
    grad_pairs = spread(grad_blocks)
    keep_pairs = tile_keep.reshape(pair_count, BLOCK, BLOCK)
    dscore, prob_pairs = pair_grads(
        query_pairs,
        grad_pairs,
        spread(log_total),
        spread(row_delta),
        key_tiles,
        value_tiles,
        keep_pairs,
        score_scale,
    )
    grad_query = jnp.einsum(
        "phqk,pkhd->pqhd", dscore, key_tiles, preferred_element_type=jnp.float32
    )
    grad_query = jnp.sum(grad_query.reshape((blocks, slot_count) + tile_shape[1:]), axis=1)
    grad_queries = grad_query.astype(jnp.bfloat16).reshape(tokens_here, heads_here * HD)
    local_rows = [row_index for row_index in range(pair_count) if routing[row_index][0] == 0]
    chosen = jnp.array(local_rows, jnp.int32)
    local_terms = key_grads(
        dscore[chosen], prob_pairs[chosen], query_pairs[chosen], grad_pairs[chosen]
    )
    key_sum = collect(local_terms, [routing[row_index][1] for row_index in local_rows], blocks)
    for offset in offsets:
        remote_rows = [
            row_index for row_index in range(pair_count) if routing[row_index][0] == offset
        ]
        chosen = jnp.array(remote_rows, jnp.int32)
        remote_terms = key_grads(
            dscore[chosen], prob_pairs[chosen], query_pairs[chosen], grad_pairs[chosen]
        )
        outgoing = collect(
            remote_terms, [routing[row_index][1] for row_index in remote_rows], blocks
        )
        key_sum = key_sum + shifted(for_sending(outgoing), "ctx", -offset).astype(outgoing.dtype)
    grad_keys = key_sum[0].astype(jnp.bfloat16).reshape(tokens_here, heads_here * HD)
    grad_values = key_sum[1].astype(jnp.bfloat16).reshape(tokens_here, heads_here * HD)
    return (normed, grad_queries, grad_keys, grad_values)


NT = (((1,), (1,)), ((), ()))
NN = (((1,), (0,)), ((), ()))
TN = (((0,), (0,)), ((), ()))
SCALE = HD ** (-0.5)
TAIL = 32


NEAR, FAR, SIDE, HELPED, LOCAL = range(5)


class Place:
    def __init__(self):
        self.me = lax.axis_index("ctx")
        self.odd = lax.rem(self.me, 2) == 1
        self.half = lax.axis_index("head") >= lax.axis_size("head") // 2


def bias_rows(pattern_ref):
    place = Place()
    me, odd, even = place.me, place.odd, jnp.logical_not(place.odd)
    blocks = pattern_ref.shape[0]
    ahead = jnp.minimum(me + 2, blocks - 1)
    has_ahead = me + 2 < blocks
    ahead_side = jnp.logical_and(has_ahead, pattern_ref[ahead, 0] >= 0)
    own_side = pattern_ref[me, 0] >= 0
    local = jnp.logical_and(odd, own_side)
    held = {
        NEAR: pattern_ref[me, 1] >= 0,
        FAR: jnp.logical_and(has_ahead, pattern_ref[ahead, 2] >= 0),
        SIDE: jnp.logical_or(local, jnp.logical_and(even, ahead_side)),
        HELPED: jnp.logical_or(pattern_ref[me, 2] >= 0, jnp.logical_and(even, own_side)),
        LOCAL: local,
    }
    row = lax.broadcasted_iota(jnp.int32, (8, BLOCK), 0)
    rows = jnp.zeros((8, BLOCK), jnp.float32)
    for index, flag in held.items():
        rows = jnp.where(row == index, jnp.where(flag, 0.0, NEG_BIG), rows)
    return rows


def mm(a, b, dims):
    return lax.dot_general(a, b, dims, preferred_element_type=jnp.float32)


def rows_of(h):
    return slice(h * HD, (h + 1) * HD)


def causal_mask():
    keys = lax.broadcasted_iota(jnp.int32, (BLOCK, BLOCK), 0)
    return keys <= lax.broadcasted_iota(jnp.int32, (BLOCK, BLOCK), 1)


def split_rows(rows):
    first = rows.astype(jnp.bfloat16).astype(jnp.float32)
    second = (rows - first).astype(jnp.bfloat16).astype(jnp.float32)
    third = rows - first - second
    return jnp.concatenate([first, second, third, jnp.zeros_like(rows)], axis=0).astype(jnp.bfloat16)


def joined_rows(tile):
    wide = tile.astype(jnp.float32)
    return wide[0:8] + wide[8:16] + wide[16:24]


def stack_rows(rows):
    return jnp.concatenate(rows + [jnp.zeros((1, BLOCK), jnp.float32)] * (8 - len(rows)), axis=0)


def score_tile(keys, queries):
    return mm(keys, queries, NT) * SCALE


def softmax_parts(pairs):
    tops = [scores.max(axis=0, keepdims=True) for scores, _ in pairs]
    weights = [jnp.exp(scores - top) for (scores, _), top in zip(pairs, tops)]
    totals = [w.sum(axis=0, keepdims=True) for w in weights]
    outs = [
        mm(value, w.astype(jnp.bfloat16), TN) * (1.0 / total)
        for (_, value), w, total in zip(pairs, weights, totals)
    ]
    return [(out, top, top + jnp.log(total), w) for out, top, total, w in zip(outs, tops, totals, weights)]


FIRST, SECOND = slice(0, BLOCK), slice(BLOCK, 2 * BLOCK)


def payload_kernel(heads, q_ref, k_ref, v_ref, u_ref, up_ref, down_ref, sems):
    half = Place().half
    top, bottom = pl.ds(0, BLOCK), pl.ds(BLOCK, BLOCK)

    def move(sources):
        targets = (up_ref.at[top], up_ref.at[bottom], down_ref.at[top], down_ref.at[bottom])
        copies = [
            pltpu.make_async_copy(source, target, sems.at[n])
            for n, (source, target) in enumerate(zip(sources, targets))
        ]
        for copy in copies:
            copy.start()
        for copy in copies:
            copy.wait()

    @pl.when(jnp.logical_not(half))
    def _():
        move((k_ref, v_ref, q_ref, u_ref))

    @pl.when(half)
    def _():
        move((q_ref, u_ref, k_ref, v_ref))


def diagonal_kernel(heads, pattern_ref, q_ref, k_ref, v_ref, u_ref, out_ref, lse_ref, ut_ref, bias_ref):
    bias_ref[...] = bias_rows(pattern_ref)
    causal = causal_mask()
    rows = []
    for h in range(heads):
        at = rows_of(h)
        scores = jnp.where(causal, score_tile(k_ref[:, at], q_ref[:, at]), NEG_BIG)
        ((out, _, lse, _),) = softmax_parts([(scores, v_ref[:, at])])
        out_ref[at] = out
        rows.append(lse)
        ut_ref[at] = u_ref[:, at].T
    lse_ref[...] = stack_rows(rows)


def merged(parts):
    highest = functools.reduce(jnp.maximum, [lse for _, lse in parts])
    total = highest + jnp.log(functools.reduce(jnp.add, [jnp.exp(lse - highest) for _, lse in parts]))
    return functools.reduce(jnp.add, [out * jnp.exp(lse - total) for out, lse in parts]), total


def forward_kernel(
    heads,
    bias_ref,
    up_ref,
    down_ref,
    q_ref,
    kx_ref,
    vx_ref,
    out_ref,
    lse_ref,
    up_out_ref,
    down_out_ref,
    ez_ref,
    ex_ref,
    en_ref,
    mz_ref,
    mx_ref,
    mn_ref,
):
    place = Place()
    odd, half = place.odd, place.half
    near, far, side, local = (bias_ref[n : n + 1] for n in (NEAR, FAR, SIDE, LOCAL))
    before = lse_ref[...]
    step = 2
    z_rows, own_rows, z_tops, x_tops, n_tops = [], [], [], [], []
    for start in range(0, heads, step):
        group = range(start, start + step)
        scores, weights = [], []
        for h in group:
            at = rows_of(h)
            up_a, down_a = up_ref[FIRST, at], down_ref[FIRST, at]
            k2, qz = jnp.where(half, down_a, up_a), jnp.where(half, up_a, down_a)
            q = q_ref[:, at]
            scores.append(
                (
                    score_tile(k2, qz) + far,
                    score_tile(kx_ref[:, at], jnp.where(odd, q, qz)) + side,
                    score_tile(k2, q) + near,
                )
            )
        for h, (z, x, n) in zip(group, scores):
            z_top, x_top, n_top = (tile.max(axis=0, keepdims=True) for tile in (z, x, n))
            both = jnp.maximum(z_top, x_top)
            z_top, x_top = jnp.where(odd, z_top, both), jnp.where(odd, x_top, both)
            z, x, n = jnp.exp(z - z_top), jnp.exp(x - x_top), jnp.exp(n - n_top)
            at = rows_of(h)
            ez_ref[at], ex_ref[at], en_ref[at] = z, x, n
            z_sum, x_sum, n_sum = (tile.sum(axis=0, keepdims=True) for tile in (z, x, n))
            z_sum = z_sum + jnp.where(odd, 0.0, x_sum)
            x_sum = jnp.maximum(x_sum, 1.0)
            for kept, top in ((z_tops, z_top), (x_tops, x_top), (n_tops, n_top)):
                kept.append(top)
            z_rows.append(z_top + jnp.log(z_sum))
            parts = (before[h : h + 1], n_top + jnp.log(n_sum) + near, x_top + jnp.log(x_sum) + local)
            highest = functools.reduce(jnp.maximum, parts)
            total = highest + jnp.log(functools.reduce(jnp.add, [jnp.exp(part - highest) for part in parts]))
            own_rows.append(total)
            d_share, n_share, x_share = (jnp.exp(part - total) for part in parts)
            xb = x.astype(jnp.bfloat16)
            joined = jnp.concatenate([z.astype(jnp.bfloat16), jnp.where(odd, jnp.zeros_like(xb), xb)], axis=0)
            weights.append(
                (joined, xb, n.astype(jnp.bfloat16), 1.0 / z_sum, d_share, n_share / n_sum, x_share / x_sum)
            )
        for h, (joined, xb, nb, z_scale, d_share, n_share, x_share) in zip(group, weights):
            at = rows_of(h)
            v2, vx = jnp.where(half, down_ref[SECOND, at], up_ref[SECOND, at]), vx_ref[:, at]
            out_z = mm(jnp.concatenate([v2, vx], axis=0), joined, TN) * z_scale
            own = out_ref[at] * d_share + mm(v2, nb, TN) * n_share + mm(vx, xb, TN) * x_share
            out_z, own = out_z.astype(jnp.bfloat16), own.astype(jnp.bfloat16)
            up_out_ref[at] = jnp.where(half, own, out_z)
            down_out_ref[at] = jnp.where(half, out_z, own)
    tail = slice(heads * HD, heads * HD + TAIL)
    z_tail, own_tail = split_rows(stack_rows(z_rows)), split_rows(stack_rows(own_rows))
    up_out_ref[tail] = jnp.where(half, own_tail, z_tail)
    down_out_ref[tail] = jnp.where(half, z_tail, own_tail)
    mz_ref[...] = stack_rows(z_tops)
    mx_ref[...] = stack_rows(x_tops)
    mn_ref[...] = stack_rows(n_tops)


def transpose_kernel(heads, up_ref, down_ref, out_ref):
    half = Place().half
    for h in range(heads):
        at = rows_of(h)
        out_ref[at] = jnp.where(half, up_ref[SECOND, at], down_ref[SECOND, at]).T


def merge_kernel(
    heads,
    bias_ref,
    up_ref,
    down_ref,
    up_in_ref,
    down_in_ref,
    ut_ref,
    uzt_ref,
    a_ref,
    az_ref,
    lse_ref,
    lsez_ref,
    sums_ref,
):
    half = Place().half
    tail = slice(heads * HD, heads * HD + TAIL)

    def select(rising, falling, at):
        first, second = rising[at], falling[at]
        return jnp.where(half, second, first), jnp.where(half, first, second)

    z_part, own_part = select(up_ref, down_ref, tail)
    help_part, ahead_part = select(up_in_ref, down_in_ref, tail)
    rows, shares = [], []
    for first, second in (
        (joined_rows(own_part), joined_rows(help_part) + bias_ref[HELPED : HELPED + 1]),
        (joined_rows(ahead_part), joined_rows(z_part)),
    ):
        highest = jnp.maximum(first, second)
        total = highest + jnp.log(jnp.exp(first - highest) + jnp.exp(second - highest))
        rows.append(total)
        shares.append((jnp.exp(first - total), jnp.exp(second - total)))
    lse_ref[...], lsez_ref[...] = rows
    sums = [jnp.zeros((8, BLOCK), jnp.float32)] * 4
    for h in range(heads):
        at, row = rows_of(h), slice(h, h + 1)
        z_out, own_out = select(up_ref, down_ref, at)
        help_out, ahead_out = select(up_in_ref, down_in_ref, at)
        for n, (first, second, u_ref, target) in enumerate(
            ((own_out, help_out, ut_ref, a_ref), (ahead_out, z_out, uzt_ref, az_ref))
        ):
            out = (
                first.astype(jnp.float32) * shares[n][0][row] + second.astype(jnp.float32) * shares[n][1][row]
            ).astype(jnp.bfloat16)
            target[at] = out
            wide = out.astype(jnp.float32)
            sums[2 * n] += (wide * wide).reshape(HD // 8, 8, BLOCK).sum(axis=0)
            sums[2 * n + 1] += (wide * u_ref[at].astype(jnp.float32)).reshape(HD // 8, 8, BLOCK).sum(axis=0)
    sums_ref[...] = stack_rows([part.sum(axis=0, keepdims=True) for part in sums])


def norm_rows(sums, first):
    inverse = lax.rsqrt(sums[first : first + 1] / WIDTH + EPSILON)
    return inverse, inverse**3 * sums[first + 1 : first + 2] / WIDTH


def upstream_part(norm, u, a):
    inverse, factor = norm
    wide = a.astype(jnp.float32)
    grad = (inverse * u.astype(jnp.float32) - wide * factor).astype(jnp.bfloat16)
    return grad, jnp.sum(grad.astype(jnp.float32) * wide, axis=0, keepdims=True)


def back_kernel(
    heads,
    bias_ref,
    sums_ref,
    a_ref,
    az_ref,
    lse_ref,
    lsez_ref,
    ut_ref,
    uzt_ref,
    up_ref,
    down_ref,
    kx_ref,
    vx_ref,
    ez_ref,
    ex_ref,
    en_ref,
    mz_ref,
    mx_ref,
    mn_ref,
    up_out_ref,
    down_out_ref,
    dvx_ref,
    dsz_ref,
    dsx_ref,
    dsn_ref,
    grad_ref,
    delta_ref,
):
    place = Place()
    odd, half = place.odd, place.half
    sums = sums_ref[...]
    own_norm, z_norm = norm_rows(sums, 0), norm_rows(sums, 2)
    lse, z_lse = lse_ref[...], lsez_ref[...]
    scales = (
        jnp.exp(mn_ref[...] - lse + bias_ref[NEAR : NEAR + 1]),
        jnp.exp(mz_ref[...] - z_lse + bias_ref[FAR : FAR + 1]),
        jnp.exp(mx_ref[...] - jnp.where(odd, lse, z_lse) + bias_ref[SIDE : SIDE + 1]),
    )
    deltas = []
    step = 2
    for start in range(0, heads, step):
        group = range(start, start + step)
        parts, products, scores = [], [], []
        for h in group:
            at = rows_of(h)
            grad, delta = upstream_part(own_norm, ut_ref[at], a_ref[at])
            gz, deltaz = upstream_part(z_norm, uzt_ref[at], az_ref[at])
            grad_ref[at] = grad
            deltas.append(delta)
            gx, deltax = jnp.where(odd, grad, gz), jnp.where(odd, delta, deltaz)
            parts.append(((grad, gz, gx), (delta, deltaz, deltax)))
        for h, ((grad, gz, gx), _) in zip(group, parts):
            at = rows_of(h)
            v2 = jnp.where(half, down_ref[SECOND, at], up_ref[SECOND, at])
            both = mm(v2, jnp.concatenate([grad, gz], axis=1), NN)
            products.append((both[:, :BLOCK], both[:, BLOCK:], mm(vx_ref[:, at], gx, NN)))
        for h, (_, delta), product in zip(group, parts, products):
            at = rows_of(h)
            tiles = []
            for n, (e_ref, ds_ref) in enumerate(((en_ref, dsn_ref), (ez_ref, dsz_ref), (ex_ref, dsx_ref))):
                weights = e_ref[at] * scales[n][h : h + 1]
                dscore = (weights * (product[n] - delta[n]) * SCALE).astype(jnp.bfloat16)
                ds_ref[at] = dscore
                tiles.append((weights.astype(jnp.bfloat16), dscore))
            scores.append(tiles)
        for h, ((grad, gz, gx), _), ((pn, _), (pz, dz), (px, dx)) in zip(group, parts, scores):
            at = rows_of(h)
            k2 = jnp.where(half, down_ref[FIRST, at], up_ref[FIRST, at])
            dv2 = mm(jnp.concatenate([pn, pz], axis=1), jnp.concatenate([grad, gz], axis=1), NT)
            dvx_ref[:, at] = mm(px, gx, NT).astype(jnp.bfloat16)
            joined = jnp.concatenate([dz, jnp.where(odd, jnp.zeros_like(dx), dx)], axis=0)
            dqz = mm(joined, jnp.concatenate([k2, kx_ref[:, at]], axis=0), TN).astype(jnp.bfloat16)
            dv2 = dv2.astype(jnp.bfloat16)
            up_out_ref[:, at] = jnp.where(half, dv2, dqz)
            down_out_ref[:, at] = jnp.where(half, dqz, dv2)
    delta_ref[...] = stack_rows(deltas)


def helper_keys_kernel(heads, q_ref, up_ref, down_ref, dsz_ref, dsx_ref, dsn_ref, dk_ref, dkx_ref):
    place = Place()
    for h in range(heads):
        at = rows_of(h)
        q, qz = q_ref[:, at], jnp.where(place.half, up_ref[FIRST, at], down_ref[FIRST, at])
        dk2 = mm(
            jnp.concatenate([dsn_ref[at], dsz_ref[at]], axis=1), jnp.concatenate([q, qz], axis=0), NN
        )
        dk_ref[:, at] = dk2.astype(jnp.bfloat16)
        dkx_ref[:, at] = mm(dsx_ref[at], jnp.where(place.odd, q, qz), NN).astype(jnp.bfloat16)


def diagonal_back_kernel(
    heads,
    sums_ref,
    q_ref,
    k_ref,
    v_ref,
    a_ref,
    lse_ref,
    grad_ref,
    delta_ref,
    ds_ref,
    dsx_ref,
    kx_ref,
    up_ref,
    down_ref,
    normed_ref,
    dq_ref,
    dk_ref,
    dv_ref,
):
    place = Place()
    half, odd = place.half, place.odd
    inverse, _ = norm_rows(sums_ref[...], 0)
    lse = lse_ref[...]
    causal = causal_mask()
    for h in range(heads):
        at, row = rows_of(h), slice(h, h + 1)
        normed_ref[:, at] = (a_ref[at].astype(jnp.float32) * inverse).astype(jnp.bfloat16).T
        q, k, v, grad = q_ref[:, at], k_ref[:, at], v_ref[:, at], grad_ref[at]
        weights = jnp.exp(jnp.where(causal, score_tile(k, q), NEG_BIG) - lse[row])
        dscore = (weights * (mm(v, grad, NN) - delta_ref[row]) * SCALE).astype(jnp.bfloat16)
        dk_ref[:, at] = mm(dscore, q, NN)
        dv_ref[:, at] = mm(weights.astype(jnp.bfloat16), grad, NT)
        k2 = jnp.where(half, down_ref[FIRST, at], up_ref[FIRST, at])
        dsx = jnp.where(odd, dsx_ref[at], jnp.zeros_like(dsx_ref[at]))
        dq_ref[:, at] = mm(dscore, k, TN) + mm(
            jnp.concatenate([ds_ref[at], dsx], axis=0), jnp.concatenate([k2, kx_ref[:, at]], axis=0), TN
        )


def final_first_kernel(heads, dq_own_ref, dv_own_ref, side_ref, up_ref, down_ref, dq_ref, dv_ref, token_ref):
    place = Place()
    half = place.half
    ahead = (place.me + 2 < lax.axis_size("ctx")).astype(jnp.float32)
    behind = (place.me >= 2).astype(jnp.float32)
    for h in range(heads):
        at = rows_of(h)
        up, down = up_ref[:, at], down_ref[:, at]
        dqz = jnp.where(half, down, up).astype(jnp.float32) * behind
        dv = jnp.where(half, up, down).astype(jnp.float32) * ahead
        dq_ref[:, at] = (dq_own_ref[:, at] + dqz).astype(jnp.bfloat16)
        dv_ref[:, at] = (dv_own_ref[:, at] + side_ref[:, at].astype(jnp.float32) + dv).astype(jnp.bfloat16)
    token_ref[...] = jnp.zeros_like(token_ref)


def final_keys_kernel(heads, dk_own_ref, side_ref, back_ref, dk_ref):
    ahead = (Place().me + 2 < lax.axis_size("ctx")).astype(jnp.float32)
    for h in range(heads):
        at = rows_of(h)
        dk = back_ref[:, at].astype(jnp.float32) * ahead
        dk_ref[:, at] = (dk_own_ref[:, at] + side_ref[:, at].astype(jnp.float32) + dk).astype(jnp.bfloat16)


def call(kernel, heads, flags, arrays, outs, flops, space=pltpu.VMEM, scratch=(), after=()):
    moved = sum(math.prod(a.shape) * a.dtype.itemsize for a in (*arrays, *outs))
    return pl.pallas_call(
        lambda *refs: kernel(heads, *refs[len(after) :]),
        out_shape=outs,
        in_specs=[pl.BlockSpec(memory_space=pl.ANY)] * len(after)
        + [pl.BlockSpec(memory_space=pltpu.SMEM)] * len(flags)
        + [pl.BlockSpec(memory_space=space)] * len(arrays),
        out_specs=[pl.BlockSpec(memory_space=pltpu.VMEM)] * len(outs),
        scratch_shapes=scratch,
        compiler_params=pltpu.CompilerParams(vmem_limit_bytes=24 * 2**20),
        cost_estimate=pl.CostEstimate(flops=flops, bytes_accessed=moved, transcendentals=0),
    )(*after, *flags, *arrays)


def cycles(blocks, members):
    route = []
    for block in range(blocks):
        for member in range(members):
            rising = member < members // 2
            other = member + members // 2 if rising else member - members // 2
            target = block + 2 if rising else block - 2
            inside = 0 <= target < blocks
            route.append(
                (block * members + member, target * members + member if inside else block * members + other)
            )
    return route


def meeting_shards(queries, keys, values, pattern, upstream):
    tokens, width = queries.shape
    heads = width // HD
    blocks, members = lax.axis_size("ctx"), lax.axis_size("head")
    unit = heads * 2 * BLOCK**3
    rising = cycles(blocks, members)
    falling = [(target, source) for source, target in rising]

    def cycle(up_array, down_array):
        return lax.ppermute(up_array, ("ctx", "head"), rising), lax.ppermute(
            down_array, ("ctx", "head"), falling
        )

    def swap(array):
        return lax.ppermute(array, "ctx", [(i, i ^ 1) for i in range(blocks)])

    def ring(array, distance):
        return lax.ppermute(array, "ctx", [(i, (i + distance) % blocks) for i in range(blocks)])

    def struct(*shape, dtype=jnp.bfloat16):
        return jax.ShapeDtypeStruct(shape, dtype)

    wide = struct(tokens, width, dtype=jnp.float32)
    wide_t = struct(width, tokens, dtype=jnp.float32)
    flat, flat_t = struct(tokens, width), struct(width, tokens)
    message = struct(width + TAIL, tokens)
    rows = struct(8, tokens, dtype=jnp.float32)

    payload = call(
        payload_kernel,
        heads,
        (),
        [pltpu.with_memory_space_constraint(a, pltpu.HBM) for a in (queries, keys, values, upstream)],
        [pltpu.VMEM((2 * tokens, width), jnp.bfloat16)] * 2,
        0,
        space=pltpu.HBM,
        scratch=(pltpu.SemaphoreType.DMA((4,)),),
    )
    received = cycle(*payload)
    keys_x, values_x = swap(keys), swap(values)
    diagonal, diagonal_lse, upstream_t, bias = call(
        diagonal_kernel,
        heads,
        (pattern,),
        (queries, keys, values, upstream),
        (wide_t, rows, flat_t, rows),
        3 * unit,
        after=(payload[0],),
    )
    up_out, down_out, *kept = call(
        forward_kernel,
        heads,
        (),
        (bias, *received, queries, keys_x, values_x, diagonal, diagonal_lse),
        (message, message, wide_t, wide_t, wide_t, rows, rows, rows),
        6 * unit,
    )
    up_in, down_in = cycle(up_out, down_out)
    (upstream_zt,) = call(transpose_kernel, heads, (), received, (flat_t,), 0, after=(kept[-1],))
    attention, attention_z, lse, lse_z, sums = call(
        merge_kernel,
        heads,
        (),
        (bias, up_out, down_out, up_in, down_in, upstream_t, upstream_zt),
        (flat_t, flat_t, rows, rows, rows),
        unit // 64,
    )
    others = [
        lax.ppermute(sums, "head", [(i, i ^ step) for i in range(members)]) for step in range(1, members)
    ]
    sums = functools.reduce(jnp.add, others, sums)
    up_out, down_out, side_dv, far_ds, side_ds, near_ds, grad_t, delta = call(
        back_kernel,
        heads,
        (),
        (bias, sums, attention, attention_z, lse, lse_z, upstream_t, upstream_zt, *received, keys_x, values_x)
        + tuple(kept),
        (flat, flat, flat, flat_t, flat_t, flat_t, flat_t, rows),
        8 * unit,
    )
    returned = cycle(up_out, down_out)
    out_dk, side_dk = call(
        helper_keys_kernel,
        heads,
        (),
        (queries, *received, far_ds, side_ds, near_ds),
        (flat, flat),
        3 * unit,
    )
    back_dk = ring(out_dk, -2)
    side_dv, side_dk = swap(side_dv), swap(side_dk)
    normed, dq_own, dk_own, dv_own = call(
        diagonal_back_kernel,
        heads,
        (),
        (sums, queries, keys, values, attention, lse, grad_t, delta, near_ds, side_ds, keys_x, *received),
        (flat, wide, wide, wide),
        7 * unit,
    )
    grad_queries, grad_values, token = call(
        final_first_kernel, heads, (), (dq_own, dv_own, side_dv, *returned), (flat, flat, rows), 0
    )
    (grad_keys,) = call(final_keys_kernel, heads, (), (dk_own, side_dk, back_dk), (flat,), 0, after=(token,))
    return (normed, grad_queries, grad_keys, grad_values)


def shards(queries, keys, values, pattern, upstream):
    fits = lax.axis_size("ctx") == 8 and lax.axis_size("head") == 4 and queries.shape == (BLOCK, 8 * HD)
    if fits:
        return meeting_shards(queries, keys, values, pattern, upstream)
    return generic_shards(queries, keys, values, pattern, upstream)


def solution(mesh):
    return jax.shard_map(
        shards,
        mesh=mesh,
        in_specs=(P("ctx", "head"), P("ctx", "head"), P("ctx", "head"), P(), P("ctx", "head")),
        out_specs=(P("ctx", "head"), P("ctx", "head"), P("ctx", "head"), P("ctx", "head")),
        check_vma=False,
    )
```

```python
import functools
import math

import jax
import jax.numpy as jnp
from jax import lax
from jax.experimental import pallas as pl
from jax.experimental.pallas import tpu as pltpu
from jax.sharding import PartitionSpec as P

HD = 128
BLOCK = 128
LEVELS = 7
WIDTH = 4096


NEG_BIG = -1e30
EPSILON = 1e-06


def shifted(block, axis, distance):
    devices = range(lax.axis_size(axis))
    route = [(i - distance, i) for i in devices if i - distance in devices]
    return lax.ppermute(block, axis, route)


def for_sending(x):
    return jax.tree.map(lambda a: a.astype(jnp.bfloat16) if a.dtype == jnp.float32 else a, x)


def route_table(blocks, levels):
    routing = []
    for query_block in range(blocks):
        for level_index in range(levels + 1):
            if level_index == levels:
                routing.append((0, query_block))
            else:
                distance = 2**level_index
                routing.append(
                    (-((query_block - distance) // blocks), (query_block - distance) % blocks)
                )
    return routing


def pair_grads(
    query_tiles, grad_tiles, lse_tiles, delta_tiles, key_tiles, value_tiles, keep_mask, score_scale
):
    scores = (
        jnp.einsum("pqhd,pkhd->phqk", query_tiles, key_tiles, preferred_element_type=jnp.float32)
        * score_scale
    )
    scores = jnp.where(keep_mask[:, None], scores, NEG_BIG)
    weights = jnp.exp(scores - lse_tiles[..., None])
    prob_tiles = weights.astype(jnp.bfloat16)
    grad_probs = jnp.einsum(
        "pqhd,pkhd->phqk", grad_tiles, value_tiles, preferred_element_type=jnp.float32
    )
    dscore = (weights * (grad_probs - delta_tiles[..., None]) * score_scale).astype(jnp.bfloat16)
    return (dscore, prob_tiles)


def key_grads(dscore, prob_tiles, query_tiles, grad_tiles):
    key_part = jnp.einsum(
        "phqk,pqhd->pkhd", dscore, query_tiles, preferred_element_type=jnp.float32
    )
    value_part = jnp.einsum(
        "phqk,pqhd->pkhd", prob_tiles, grad_tiles, preferred_element_type=jnp.float32
    )
    return jnp.stack((key_part, value_part))


def collect(partials, targets, blocks):
    pieces = []
    for key_index in range(blocks):
        summed = jnp.zeros((2,) + partials.shape[2:], jnp.float32)
        for row_index, target in enumerate(targets):
            if target == key_index:
                summed = summed + partials[:, row_index]
        pieces.append(summed)
    return jnp.stack(pieces, axis=1)


def generic_shards(queries, keys, values, pattern, upstream):
    tokens_here = queries.shape[0]
    heads_here = queries.shape[1] // HD
    blocks = tokens_here // BLOCK
    slot_count = LEVELS + 1
    pair_count = blocks * slot_count
    score_scale = HD ** (-0.5)
    ctx_count = lax.axis_size("ctx")
    device_index = lax.axis_index("ctx")
    routing = route_table(blocks, LEVELS)
    offsets = sorted(
        set((route_entry[0] for route_entry in routing if 0 < route_entry[0] < ctx_count))
    )
    tile_shape = (blocks, BLOCK, heads_here, HD)
    query_blocks = queries.reshape(tile_shape)
    own_pairs = jnp.stack((keys, values)).reshape((2,) + tile_shape)
    sources = {0: own_pairs}
    for offset in offsets:
        fetched = shifted(jnp.stack((keys, values)), "ctx", offset)
        sources[offset] = fetched.reshape((2,) + tile_shape)
    empty_tile = jnp.zeros((2, BLOCK, heads_here, HD), jnp.bfloat16)
    gathered = []
    for source, key_index in routing:
        if source in sources:
            gathered.append(sources[source][:, key_index])
        else:
            gathered.append(empty_tile)
    pair_kv = jnp.stack(gathered, axis=1)
    key_tiles = pair_kv[0]
    value_tiles = pair_kv[1]
    key_stack = key_tiles.reshape((blocks, slot_count) + tile_shape[1:])
    value_stack = value_tiles.reshape((blocks, slot_count) + tile_shape[1:])
    own_rows = lax.dynamic_slice_in_dim(pattern, device_index * blocks, blocks, 0)
    positions = jnp.arange(BLOCK)
    causal = positions[None, :] <= positions[:, None]
    self_slot = jnp.arange(slot_count) == LEVELS
    tile_keep = (own_rows >= 0)[:, :, None, None] & (
        jnp.logical_not(self_slot)[None, :, None, None] | causal[None, None]
    )
    scores = (
        jnp.einsum("bqhd,bskhd->bhqsk", query_blocks, key_stack, preferred_element_type=jnp.float32)
        * score_scale
    )
    scores = jnp.where(jnp.transpose(tile_keep, (0, 2, 1, 3))[:, None], scores, NEG_BIG)
    highest = jnp.max(scores, axis=(3, 4))
    log_total = highest + jnp.log(jnp.sum(jnp.exp(scores - highest[..., None, None]), axis=(3, 4)))
    prob_stack = jnp.exp(scores - log_total[..., None, None]).astype(jnp.bfloat16)
    attention = jnp.einsum(
        "bhqsk,bskhd->bqhd", prob_stack, value_stack, preferred_element_type=jnp.float32
    ).astype(jnp.bfloat16)
    attn_wide = attention.reshape(tokens_here, heads_here * HD).astype(jnp.float32)
    square_sum = lax.psum(jnp.sum(attn_wide * attn_wide, axis=1), "head")
    inverse = lax.rsqrt(square_sum / WIDTH + EPSILON)
    normed = (attn_wide * inverse[:, None]).astype(jnp.bfloat16)
    upstream_wide = upstream.astype(jnp.float32)
    cross_term = lax.psum(jnp.sum(upstream_wide * attn_wide, axis=1), "head")
    grad_attn = (
        inverse[:, None] * upstream_wide - attn_wide * (inverse**3 * cross_term / WIDTH)[:, None]
    ).astype(jnp.bfloat16)
    row_delta = jnp.sum(
        (grad_attn.astype(jnp.float32) * attn_wide).reshape(tokens_here, heads_here, HD), axis=2
    )
    row_delta = jnp.transpose(row_delta.reshape(blocks, BLOCK, heads_here), (0, 2, 1))

    def spread(array):
        return jnp.broadcast_to(array[:, None], (blocks, slot_count) + array.shape[1:]).reshape(
            (pair_count,) + array.shape[1:]
        )

    grad_blocks = grad_attn.reshape(tile_shape)
    query_pairs = spread(query_blocks)
    grad_pairs = spread(grad_blocks)
    keep_pairs = tile_keep.reshape(pair_count, BLOCK, BLOCK)
    dscore, prob_pairs = pair_grads(
        query_pairs,
        grad_pairs,
        spread(log_total),
        spread(row_delta),
        key_tiles,
        value_tiles,
        keep_pairs,
        score_scale,
    )
    grad_query = jnp.einsum(
        "phqk,pkhd->pqhd", dscore, key_tiles, preferred_element_type=jnp.float32
    )
    grad_query = jnp.sum(grad_query.reshape((blocks, slot_count) + tile_shape[1:]), axis=1)
    grad_queries = grad_query.astype(jnp.bfloat16).reshape(tokens_here, heads_here * HD)
    local_rows = [row_index for row_index in range(pair_count) if routing[row_index][0] == 0]
    chosen = jnp.array(local_rows, jnp.int32)
    local_terms = key_grads(
        dscore[chosen], prob_pairs[chosen], query_pairs[chosen], grad_pairs[chosen]
    )
    key_sum = collect(local_terms, [routing[row_index][1] for row_index in local_rows], blocks)
    for offset in offsets:
        remote_rows = [
            row_index for row_index in range(pair_count) if routing[row_index][0] == offset
        ]
        chosen = jnp.array(remote_rows, jnp.int32)
        remote_terms = key_grads(
            dscore[chosen], prob_pairs[chosen], query_pairs[chosen], grad_pairs[chosen]
        )
        outgoing = collect(
            remote_terms, [routing[row_index][1] for row_index in remote_rows], blocks
        )
        key_sum = key_sum + shifted(for_sending(outgoing), "ctx", -offset).astype(outgoing.dtype)
    grad_keys = key_sum[0].astype(jnp.bfloat16).reshape(tokens_here, heads_here * HD)
    grad_values = key_sum[1].astype(jnp.bfloat16).reshape(tokens_here, heads_here * HD)
    return (normed, grad_queries, grad_keys, grad_values)


NT = (((1,), (1,)), ((), ()))
NN = (((1,), (0,)), ((), ()))
TN = (((0,), (0,)), ((), ()))
SCALE = HD ** (-0.5)
TAIL = 32


NEAR, FAR, SIDE, HELPED, LOCAL = range(5)


class Place:
    def __init__(self):
        self.me = lax.axis_index("ctx")
        self.odd = lax.rem(self.me, 2) == 1
        self.half = lax.axis_index("head") >= lax.axis_size("head") // 2


def bias_rows(pattern_ref):
    place = Place()
    me, odd, even = place.me, place.odd, jnp.logical_not(place.odd)
    blocks = pattern_ref.shape[0]
    ahead = jnp.minimum(me + 2, blocks - 1)
    has_ahead = me + 2 < blocks
    ahead_side = jnp.logical_and(has_ahead, pattern_ref[ahead, 0] >= 0)
    own_side = pattern_ref[me, 0] >= 0
    local = jnp.logical_and(odd, own_side)
    held = {
        NEAR: pattern_ref[me, 1] >= 0,
        FAR: jnp.logical_and(has_ahead, pattern_ref[ahead, 2] >= 0),
        SIDE: jnp.logical_or(local, jnp.logical_and(even, ahead_side)),
        HELPED: jnp.logical_or(pattern_ref[me, 2] >= 0, jnp.logical_and(even, own_side)),
        LOCAL: local,
    }
    row = lax.broadcasted_iota(jnp.int32, (8, BLOCK), 0)
    rows = jnp.zeros((8, BLOCK), jnp.float32)
    for index, flag in held.items():
        rows = jnp.where(row == index, jnp.where(flag, 0.0, NEG_BIG), rows)
    return rows


def mm(a, b, dims):
    return lax.dot_general(a, b, dims, preferred_element_type=jnp.float32)


def rows_of(h):
    return slice(h * HD, (h + 1) * HD)


def causal_mask():
    keys = lax.broadcasted_iota(jnp.int32, (BLOCK, BLOCK), 0)
    return keys <= lax.broadcasted_iota(jnp.int32, (BLOCK, BLOCK), 1)


def split_rows(rows):
    first = rows.astype(jnp.bfloat16).astype(jnp.float32)
    second = (rows - first).astype(jnp.bfloat16).astype(jnp.float32)
    third = rows - first - second
    return jnp.concatenate([first, second, third, jnp.zeros_like(rows)], axis=0).astype(jnp.bfloat16)


def joined_rows(tile):
    wide = tile.astype(jnp.float32)
    return wide[0:8] + wide[8:16] + wide[16:24]


def stack_rows(rows):
    return jnp.concatenate(rows + [jnp.zeros((1, BLOCK), jnp.float32)] * (8 - len(rows)), axis=0)


def score_tile(keys, queries):
    return mm(keys, queries, NT) * SCALE


def softmax_parts(pairs):
    tops = [scores.max(axis=0, keepdims=True) for scores, _ in pairs]
    weights = [jnp.exp(scores - top) for (scores, _), top in zip(pairs, tops)]
    totals = [w.sum(axis=0, keepdims=True) for w in weights]
    outs = [
        mm(value, w.astype(jnp.bfloat16), TN) * (1.0 / total)
        for (_, value), w, total in zip(pairs, weights, totals)
    ]
    return [(out, top, top + jnp.log(total), w) for out, top, total, w in zip(outs, tops, totals, weights)]


FIRST, SECOND = slice(0, BLOCK), slice(BLOCK, 2 * BLOCK)


def payload_kernel(heads, q_ref, k_ref, v_ref, u_ref, up_ref, down_ref, sems):
    half = Place().half
    top, bottom = pl.ds(0, BLOCK), pl.ds(BLOCK, BLOCK)

    def move(sources):
        targets = (up_ref.at[top], up_ref.at[bottom], down_ref.at[top], down_ref.at[bottom])
        copies = [
            pltpu.make_async_copy(source, target, sems.at[n])
            for n, (source, target) in enumerate(zip(sources, targets))
        ]
        for copy in copies:
            copy.start()
        for copy in copies:
            copy.wait()

    @pl.when(jnp.logical_not(half))
    def _():
        move((k_ref, v_ref, q_ref, u_ref))

    @pl.when(half)
    def _():
        move((q_ref, u_ref, k_ref, v_ref))


def diagonal_kernel(heads, pattern_ref, q_ref, k_ref, v_ref, u_ref, out_ref, lse_ref, ut_ref, bias_ref):
    bias_ref[...] = bias_rows(pattern_ref)
    causal = causal_mask()
    rows = []
    for h in range(heads):
        at = rows_of(h)
        scores = jnp.where(causal, score_tile(k_ref[:, at], q_ref[:, at]), NEG_BIG)
        ((out, _, lse, _),) = softmax_parts([(scores, v_ref[:, at])])
        out_ref[at] = out
        rows.append(lse)
        ut_ref[at] = u_ref[:, at].T
    lse_ref[...] = stack_rows(rows)


def merged(parts):
    highest = functools.reduce(jnp.maximum, [lse for _, lse in parts])
    total = highest + jnp.log(functools.reduce(jnp.add, [jnp.exp(lse - highest) for _, lse in parts]))
    return functools.reduce(jnp.add, [out * jnp.exp(lse - total) for out, lse in parts]), total


def forward_kernel(
    heads,
    bias_ref,
    up_ref,
    down_ref,
    q_ref,
    kx_ref,
    vx_ref,
    out_ref,
    lse_ref,
    up_out_ref,
    down_out_ref,
    ez_ref,
    ex_ref,
    en_ref,
    mz_ref,
    mx_ref,
    mn_ref,
):
    place = Place()
    odd, half = place.odd, place.half
    near, far, side, local = (bias_ref[n : n + 1] for n in (NEAR, FAR, SIDE, LOCAL))
    before = lse_ref[...]
    step = 2
    z_rows, own_rows, z_tops, x_tops, n_tops = [], [], [], [], []
    for start in range(0, heads, step):
        group = range(start, start + step)
        scores, weights = [], []
        for h in group:
            at = rows_of(h)
            up_a, down_a = up_ref[FIRST, at], down_ref[FIRST, at]
            k2, qz = jnp.where(half, down_a, up_a), jnp.where(half, up_a, down_a)
            q = q_ref[:, at]
            scores.append(
                (
                    score_tile(k2, qz) + far,
                    score_tile(kx_ref[:, at], jnp.where(odd, q, qz)) + side,
                    score_tile(k2, q) + near,
                )
            )
        for h, (z, x, n) in zip(group, scores):
            z_top, x_top, n_top = (tile.max(axis=0, keepdims=True) for tile in (z, x, n))
            both = jnp.maximum(z_top, x_top)
            z_top, x_top = jnp.where(odd, z_top, both), jnp.where(odd, x_top, both)
            z, x, n = jnp.exp(z - z_top), jnp.exp(x - x_top), jnp.exp(n - n_top)
            at = rows_of(h)
            ez_ref[at], ex_ref[at], en_ref[at] = z, x, n
            z_sum, x_sum, n_sum = (tile.sum(axis=0, keepdims=True) for tile in (z, x, n))
            z_sum = z_sum + jnp.where(odd, 0.0, x_sum)
            x_sum = jnp.maximum(x_sum, 1.0)
            for kept, top in ((z_tops, z_top), (x_tops, x_top), (n_tops, n_top)):
                kept.append(top)
            z_rows.append(z_top + jnp.log(z_sum))
            parts = (before[h : h + 1], n_top + jnp.log(n_sum) + near, x_top + jnp.log(x_sum) + local)
            highest = functools.reduce(jnp.maximum, parts)
            total = highest + jnp.log(functools.reduce(jnp.add, [jnp.exp(part - highest) for part in parts]))
            own_rows.append(total)
            d_share, n_share, x_share = (jnp.exp(part - total) for part in parts)
            xb = x.astype(jnp.bfloat16)
            joined = jnp.concatenate([z.astype(jnp.bfloat16), jnp.where(odd, jnp.zeros_like(xb), xb)], axis=0)
            weights.append(
                (joined, xb, n.astype(jnp.bfloat16), 1.0 / z_sum, d_share, n_share / n_sum, x_share / x_sum)
            )
        for h, (joined, xb, nb, z_scale, d_share, n_share, x_share) in zip(group, weights):
            at = rows_of(h)
            v2, vx = jnp.where(half, down_ref[SECOND, at], up_ref[SECOND, at]), vx_ref[:, at]
            out_z = mm(jnp.concatenate([v2, vx], axis=0), joined, TN) * z_scale
            own = out_ref[at] * d_share + mm(v2, nb, TN) * n_share + mm(vx, xb, TN) * x_share
            out_z, own = out_z.astype(jnp.bfloat16), own.astype(jnp.bfloat16)
            up_out_ref[at] = jnp.where(half, own, out_z)
            down_out_ref[at] = jnp.where(half, out_z, own)
    tail = slice(heads * HD, heads * HD + TAIL)
    z_tail, own_tail = split_rows(stack_rows(z_rows)), split_rows(stack_rows(own_rows))
    up_out_ref[tail] = jnp.where(half, own_tail, z_tail)
    down_out_ref[tail] = jnp.where(half, z_tail, own_tail)
    mz_ref[...] = stack_rows(z_tops)
    mx_ref[...] = stack_rows(x_tops)
    mn_ref[...] = stack_rows(n_tops)


def transpose_kernel(heads, up_ref, down_ref, out_ref):
    half = Place().half
    for h in range(heads):
        at = rows_of(h)
        out_ref[at] = jnp.where(half, up_ref[SECOND, at], down_ref[SECOND, at]).T


def merge_kernel(
    heads,
    bias_ref,
    up_ref,
    down_ref,
    up_in_ref,
    down_in_ref,
    ut_ref,
    uzt_ref,
    a_ref,
    az_ref,
    lse_ref,
    lsez_ref,
    sums_ref,
):
    half = Place().half
    tail = slice(heads * HD, heads * HD + TAIL)

    def select(rising, falling, at):
        first, second = rising[at], falling[at]
        return jnp.where(half, second, first), jnp.where(half, first, second)

    z_part, own_part = select(up_ref, down_ref, tail)
    help_part, ahead_part = select(up_in_ref, down_in_ref, tail)
    rows, shares = [], []
    for first, second in (
        (joined_rows(own_part), joined_rows(help_part) + bias_ref[HELPED : HELPED + 1]),
        (joined_rows(ahead_part), joined_rows(z_part)),
    ):
        highest = jnp.maximum(first, second)
        total = highest + jnp.log(jnp.exp(first - highest) + jnp.exp(second - highest))
        rows.append(total)
        shares.append((jnp.exp(first - total), jnp.exp(second - total)))
    lse_ref[...], lsez_ref[...] = rows
    sums = [jnp.zeros((8, BLOCK), jnp.float32)] * 4
    for h in range(heads):
        at, row = rows_of(h), slice(h, h + 1)
        z_out, own_out = select(up_ref, down_ref, at)
        help_out, ahead_out = select(up_in_ref, down_in_ref, at)
        for n, (first, second, u_ref, target) in enumerate(
            ((own_out, help_out, ut_ref, a_ref), (ahead_out, z_out, uzt_ref, az_ref))
        ):
            out = (
                first.astype(jnp.float32) * shares[n][0][row] + second.astype(jnp.float32) * shares[n][1][row]
            ).astype(jnp.bfloat16)
            target[at] = out
            wide = out.astype(jnp.float32)
            sums[2 * n] += (wide * wide).reshape(HD // 8, 8, BLOCK).sum(axis=0)
            sums[2 * n + 1] += (wide * u_ref[at].astype(jnp.float32)).reshape(HD // 8, 8, BLOCK).sum(axis=0)
    sums_ref[...] = stack_rows([part.sum(axis=0, keepdims=True) for part in sums])


def norm_rows(sums, first):
    inverse = lax.rsqrt(sums[first : first + 1] / WIDTH + EPSILON)
    return inverse, inverse**3 * sums[first + 1 : first + 2] / WIDTH


def upstream_part(norm, u, a):
    inverse, factor = norm
    wide = a.astype(jnp.float32)
    grad = (inverse * u.astype(jnp.float32) - wide * factor).astype(jnp.bfloat16)
    return grad, jnp.sum(grad.astype(jnp.float32) * wide, axis=0, keepdims=True)


def back_kernel(
    heads,
    bias_ref,
    sums_ref,
    a_ref,
    az_ref,
    lse_ref,
    lsez_ref,
    ut_ref,
    uzt_ref,
    up_ref,
    down_ref,
    kx_ref,
    vx_ref,
    ez_ref,
    ex_ref,
    en_ref,
    mz_ref,
    mx_ref,
    mn_ref,
    up_out_ref,
    down_out_ref,
    dvx_ref,
    dsz_ref,
    dsx_ref,
    dsn_ref,
    grad_ref,
    delta_ref,
):
    place = Place()
    odd, half = place.odd, place.half
    sums = sums_ref[...]
    own_norm, z_norm = norm_rows(sums, 0), norm_rows(sums, 2)
    lse, z_lse = lse_ref[...], lsez_ref[...]
    scales = (
        jnp.exp(mn_ref[...] - lse + bias_ref[NEAR : NEAR + 1]),
        jnp.exp(mz_ref[...] - z_lse + bias_ref[FAR : FAR + 1]),
        jnp.exp(mx_ref[...] - jnp.where(odd, lse, z_lse) + bias_ref[SIDE : SIDE + 1]),
    )
    deltas = []
    step = 2
    for start in range(0, heads, step):
        group = range(start, start + step)
        parts, products, scores = [], [], []
        for h in group:
            at = rows_of(h)
            grad, delta = upstream_part(own_norm, ut_ref[at], a_ref[at])
            gz, deltaz = upstream_part(z_norm, uzt_ref[at], az_ref[at])
            grad_ref[at] = grad
            deltas.append(delta)
            gx, deltax = jnp.where(odd, grad, gz), jnp.where(odd, delta, deltaz)
            parts.append(((grad, gz, gx), (delta, deltaz, deltax)))
        for h, ((grad, gz, gx), _) in zip(group, parts):
            at = rows_of(h)
            v2 = jnp.where(half, down_ref[SECOND, at], up_ref[SECOND, at])
            both = mm(v2, jnp.concatenate([grad, gz], axis=1), NN)
            products.append((both[:, :BLOCK], both[:, BLOCK:], mm(vx_ref[:, at], gx, NN)))
        for h, (_, delta), product in zip(group, parts, products):
            at = rows_of(h)
            tiles = []
            for n, (e_ref, ds_ref) in enumerate(((en_ref, dsn_ref), (ez_ref, dsz_ref), (ex_ref, dsx_ref))):
                weights = e_ref[at] * scales[n][h : h + 1]
                dscore = (weights * (product[n] - delta[n]) * SCALE).astype(jnp.bfloat16)
                ds_ref[at] = dscore
                tiles.append((weights.astype(jnp.bfloat16), dscore))
            scores.append(tiles)
        for h, ((grad, gz, gx), _), ((pn, _), (pz, dz), (px, dx)) in zip(group, parts, scores):
            at = rows_of(h)
            k2 = jnp.where(half, down_ref[FIRST, at], up_ref[FIRST, at])
            dv2 = mm(jnp.concatenate([pn, pz], axis=1), jnp.concatenate([grad, gz], axis=1), NT)
            dvx_ref[:, at] = mm(px, gx, NT).astype(jnp.bfloat16)
            joined = jnp.concatenate([dz, jnp.where(odd, jnp.zeros_like(dx), dx)], axis=0)
            dqz = mm(joined, jnp.concatenate([k2, kx_ref[:, at]], axis=0), TN).astype(jnp.bfloat16)
            dv2 = dv2.astype(jnp.bfloat16)
            up_out_ref[:, at] = jnp.where(half, dv2, dqz)
            down_out_ref[:, at] = jnp.where(half, dqz, dv2)
    delta_ref[...] = stack_rows(deltas)


def helper_keys_kernel(heads, q_ref, up_ref, down_ref, dsz_ref, dsx_ref, dsn_ref, dk_ref, dkx_ref):
    place = Place()
    for h in range(heads):
        at = rows_of(h)
        q, qz = q_ref[:, at], jnp.where(place.half, up_ref[FIRST, at], down_ref[FIRST, at])
        dk2 = mm(
            jnp.concatenate([dsn_ref[at], dsz_ref[at]], axis=1), jnp.concatenate([q, qz], axis=0), NN
        )
        dk_ref[:, at] = dk2.astype(jnp.bfloat16)
        dkx_ref[:, at] = mm(dsx_ref[at], jnp.where(place.odd, q, qz), NN).astype(jnp.bfloat16)


def diagonal_back_kernel(
    heads,
    sums_ref,
    q_ref,
    k_ref,
    v_ref,
    a_ref,
    lse_ref,
    grad_ref,
    delta_ref,
    ds_ref,
    dsx_ref,
    kx_ref,
    up_ref,
    down_ref,
    normed_ref,
    dq_ref,
    dk_ref,
    dv_ref,
):
    place = Place()
    half, odd = place.half, place.odd
    inverse, _ = norm_rows(sums_ref[...], 0)
    lse = lse_ref[...]
    causal = causal_mask()
    for h in range(heads):
        at, row = rows_of(h), slice(h, h + 1)
        normed_ref[:, at] = (a_ref[at].astype(jnp.float32) * inverse).astype(jnp.bfloat16).T
        q, k, v, grad = q_ref[:, at], k_ref[:, at], v_ref[:, at], grad_ref[at]
        weights = jnp.exp(jnp.where(causal, score_tile(k, q), NEG_BIG) - lse[row])
        dscore = (weights * (mm(v, grad, NN) - delta_ref[row]) * SCALE).astype(jnp.bfloat16)
        dk_ref[:, at] = mm(dscore, q, NN)
        dv_ref[:, at] = mm(weights.astype(jnp.bfloat16), grad, NT)
        k2 = jnp.where(half, down_ref[FIRST, at], up_ref[FIRST, at])
        dsx = jnp.where(odd, dsx_ref[at], jnp.zeros_like(dsx_ref[at]))
        dq_ref[:, at] = mm(dscore, k, TN) + mm(
            jnp.concatenate([ds_ref[at], dsx], axis=0), jnp.concatenate([k2, kx_ref[:, at]], axis=0), TN
        )


def final_first_kernel(heads, up_ref, down_ref, side_ref, dq_own_ref, dv_own_ref, dq_ref, dv_ref, token_ref):
    place = Place()
    half = place.half
    ahead = (place.me + 2 < lax.axis_size("ctx")).astype(jnp.float32)
    behind = (place.me >= 2).astype(jnp.float32)
    for h in range(heads):
        at = rows_of(h)
        up, down = up_ref[:, at], down_ref[:, at]
        dqz = jnp.where(half, down, up).astype(jnp.float32) * behind
        dv = jnp.where(half, up, down).astype(jnp.float32) * ahead
        dq_ref[:, at] = (dq_own_ref[:, at] + dqz).astype(jnp.bfloat16)
        dv_ref[:, at] = (dv_own_ref[:, at] + side_ref[:, at].astype(jnp.float32) + dv).astype(jnp.bfloat16)
    token_ref[...] = jnp.zeros_like(token_ref)


def final_keys_kernel(heads, back_ref, side_ref, dk_own_ref, dk_ref):
    ahead = (Place().me + 2 < lax.axis_size("ctx")).astype(jnp.float32)
    for h in range(heads):
        at = rows_of(h)
        dk = back_ref[:, at].astype(jnp.float32) * ahead
        dk_ref[:, at] = (dk_own_ref[:, at] + side_ref[:, at].astype(jnp.float32) + dk).astype(jnp.bfloat16)


def call(kernel, heads, flags, arrays, outs, flops, space=pltpu.VMEM, scratch=(), after=()):
    moved = sum(math.prod(a.shape) * a.dtype.itemsize for a in (*arrays, *outs))
    return pl.pallas_call(
        lambda *refs: kernel(heads, *refs[len(after) :]),
        out_shape=outs,
        in_specs=[pl.BlockSpec(memory_space=pl.ANY)] * len(after)
        + [pl.BlockSpec(memory_space=pltpu.SMEM)] * len(flags)
        + [pl.BlockSpec(memory_space=space)] * len(arrays),
        out_specs=[pl.BlockSpec(memory_space=pltpu.VMEM)] * len(outs),
        scratch_shapes=scratch,
        compiler_params=pltpu.CompilerParams(vmem_limit_bytes=24 * 2**20),
        cost_estimate=pl.CostEstimate(flops=flops, bytes_accessed=moved, transcendentals=0),
    )(*after, *flags, *arrays)


def cycles(blocks, members):
    route = []
    for block in range(blocks):
        for member in range(members):
            rising = member < members // 2
            other = member + members // 2 if rising else member - members // 2
            target = block + 2 if rising else block - 2
            inside = 0 <= target < blocks
            route.append(
                (block * members + member, target * members + member if inside else block * members + other)
            )
    return route


def meeting_shards(queries, keys, values, pattern, upstream):
    tokens, width = queries.shape
    heads = width // HD
    blocks, members = lax.axis_size("ctx"), lax.axis_size("head")
    unit = heads * 2 * BLOCK**3
    rising = cycles(blocks, members)
    falling = [(target, source) for source, target in rising]

    def cycle(up_array, down_array):
        return lax.ppermute(up_array, ("ctx", "head"), rising), lax.ppermute(
            down_array, ("ctx", "head"), falling
        )

    def swap(array):
        return lax.ppermute(array, "ctx", [(i, i ^ 1) for i in range(blocks)])

    def ring(array, distance):
        return lax.ppermute(array, "ctx", [(i, (i + distance) % blocks) for i in range(blocks)])

    def struct(*shape, dtype=jnp.bfloat16):
        return jax.ShapeDtypeStruct(shape, dtype)

    wide = struct(tokens, width, dtype=jnp.float32)
    wide_t = struct(width, tokens, dtype=jnp.float32)
    flat, flat_t = struct(tokens, width), struct(width, tokens)
    message = struct(width + TAIL, tokens)
    rows = struct(8, tokens, dtype=jnp.float32)

    payload = call(
        payload_kernel,
        heads,
        (),
        [pltpu.with_memory_space_constraint(a, pltpu.HBM) for a in (queries, keys, values, upstream)],
        [pltpu.VMEM((2 * tokens, width), jnp.bfloat16)] * 2,
        0,
        space=pltpu.HBM,
        scratch=(pltpu.SemaphoreType.DMA((4,)),),
    )
    received = cycle(*payload)
    keys_x, values_x = swap(keys), swap(values)
    diagonal, diagonal_lse, upstream_t, bias = call(
        diagonal_kernel,
        heads,
        (pattern,),
        (queries, keys, values, upstream),
        (wide_t, rows, flat_t, rows),
        3 * unit,
        after=(payload[0],),
    )
    up_out, down_out, *kept = call(
        forward_kernel,
        heads,
        (),
        (bias, *received, queries, keys_x, values_x, diagonal, diagonal_lse),
        (message, message, wide_t, wide_t, wide_t, rows, rows, rows),
        6 * unit,
    )
    up_in, down_in = cycle(up_out, down_out)
    (upstream_zt,) = call(transpose_kernel, heads, (), received, (flat_t,), 0, after=(kept[-1],))
    attention, attention_z, lse, lse_z, sums = call(
        merge_kernel,
        heads,
        (),
        (bias, up_out, down_out, up_in, down_in, upstream_t, upstream_zt),
        (flat_t, flat_t, rows, rows, rows),
        unit // 64,
    )
    others = [
        lax.ppermute(sums, "head", [(i, i ^ step) for i in range(members)]) for step in range(1, members)
    ]
    sums = functools.reduce(jnp.add, others, sums)
    up_out, down_out, side_dv, far_ds, side_ds, near_ds, grad_t, delta = call(
        back_kernel,
        heads,
        (),
        (bias, sums, attention, attention_z, lse, lse_z, upstream_t, upstream_zt, *received, keys_x, values_x)
        + tuple(kept),
        (flat, flat, flat, flat_t, flat_t, flat_t, flat_t, rows),
        8 * unit,
    )
    returned = cycle(up_out, down_out)
    out_dk, side_dk = call(
        helper_keys_kernel,
        heads,
        (),
        (queries, *received, far_ds, side_ds, near_ds),
        (flat, flat),
        3 * unit,
    )
    back_dk = ring(out_dk, -2)
    side_dv, side_dk = swap(side_dv), swap(side_dk)
    normed, dq_own, dk_own, dv_own = call(
        diagonal_back_kernel,
        heads,
        (),
        (sums, queries, keys, values, attention, lse, grad_t, delta, near_ds, side_ds, keys_x, *received),
        (flat, wide, wide, wide),
        7 * unit,
    )
    grad_queries, grad_values, token = call(
        final_first_kernel, heads, (), (*returned, side_dv, dq_own, dv_own), (flat, flat, rows), 0
    )
    (grad_keys,) = call(final_keys_kernel, heads, (), (back_dk, side_dk, dk_own), (flat,), 0, after=(token,))
    return (normed, grad_queries, grad_keys, grad_values)


def shards(queries, keys, values, pattern, upstream):
    fits = lax.axis_size("ctx") == 8 and lax.axis_size("head") == 4 and queries.shape == (BLOCK, 8 * HD)
    if fits:
        return meeting_shards(queries, keys, values, pattern, upstream)
    return generic_shards(queries, keys, values, pattern, upstream)


def solution(mesh):
    return jax.shard_map(
        shards,
        mesh=mesh,
        in_specs=(P("ctx", "head"), P("ctx", "head"), P("ctx", "head"), P(), P("ctx", "head")),
        out_specs=(P("ctx", "head"), P("ctx", "head"), P("ctx", "head"), P("ctx", "head")),
        check_vma=False,
    )
```

```python
import functools
import math

import jax
import jax.numpy as jnp
from jax import lax
from jax.experimental import pallas as pl
from jax.experimental.pallas import tpu as pltpu
from jax.sharding import PartitionSpec as P

HD = 128
BLOCK = 128
LEVELS = 7
WIDTH = 4096


NEG_BIG = -1e30
EPSILON = 1e-06


def shifted(block, axis, distance):
    devices = range(lax.axis_size(axis))
    route = [(i - distance, i) for i in devices if i - distance in devices]
    return lax.ppermute(block, axis, route)


def for_sending(x):
    return jax.tree.map(lambda a: a.astype(jnp.bfloat16) if a.dtype == jnp.float32 else a, x)


def route_table(blocks, levels):
    routing = []
    for query_block in range(blocks):
        for level_index in range(levels + 1):
            if level_index == levels:
                routing.append((0, query_block))
            else:
                distance = 2**level_index
                routing.append(
                    (-((query_block - distance) // blocks), (query_block - distance) % blocks)
                )
    return routing


def pair_grads(
    query_tiles, grad_tiles, lse_tiles, delta_tiles, key_tiles, value_tiles, keep_mask, score_scale
):
    scores = (
        jnp.einsum("pqhd,pkhd->phqk", query_tiles, key_tiles, preferred_element_type=jnp.float32)
        * score_scale
    )
    scores = jnp.where(keep_mask[:, None], scores, NEG_BIG)
    weights = jnp.exp(scores - lse_tiles[..., None])
    prob_tiles = weights.astype(jnp.bfloat16)
    grad_probs = jnp.einsum(
        "pqhd,pkhd->phqk", grad_tiles, value_tiles, preferred_element_type=jnp.float32
    )
    dscore = (weights * (grad_probs - delta_tiles[..., None]) * score_scale).astype(jnp.bfloat16)
    return (dscore, prob_tiles)


def key_grads(dscore, prob_tiles, query_tiles, grad_tiles):
    key_part = jnp.einsum(
        "phqk,pqhd->pkhd", dscore, query_tiles, preferred_element_type=jnp.float32
    )
    value_part = jnp.einsum(
        "phqk,pqhd->pkhd", prob_tiles, grad_tiles, preferred_element_type=jnp.float32
    )
    return jnp.stack((key_part, value_part))


def collect(partials, targets, blocks):
    pieces = []
    for key_index in range(blocks):
        summed = jnp.zeros((2,) + partials.shape[2:], jnp.float32)
        for row_index, target in enumerate(targets):
            if target == key_index:
                summed = summed + partials[:, row_index]
        pieces.append(summed)
    return jnp.stack(pieces, axis=1)


def generic_shards(queries, keys, values, pattern, upstream):
    tokens_here = queries.shape[0]
    heads_here = queries.shape[1] // HD
    blocks = tokens_here // BLOCK
    slot_count = LEVELS + 1
    pair_count = blocks * slot_count
    score_scale = HD ** (-0.5)
    ctx_count = lax.axis_size("ctx")
    device_index = lax.axis_index("ctx")
    routing = route_table(blocks, LEVELS)
    offsets = sorted(
        set((route_entry[0] for route_entry in routing if 0 < route_entry[0] < ctx_count))
    )
    tile_shape = (blocks, BLOCK, heads_here, HD)
    query_blocks = queries.reshape(tile_shape)
    own_pairs = jnp.stack((keys, values)).reshape((2,) + tile_shape)
    sources = {0: own_pairs}
    for offset in offsets:
        fetched = shifted(jnp.stack((keys, values)), "ctx", offset)
        sources[offset] = fetched.reshape((2,) + tile_shape)
    empty_tile = jnp.zeros((2, BLOCK, heads_here, HD), jnp.bfloat16)
    gathered = []
    for source, key_index in routing:
        if source in sources:
            gathered.append(sources[source][:, key_index])
        else:
            gathered.append(empty_tile)
    pair_kv = jnp.stack(gathered, axis=1)
    key_tiles = pair_kv[0]
    value_tiles = pair_kv[1]
    key_stack = key_tiles.reshape((blocks, slot_count) + tile_shape[1:])
    value_stack = value_tiles.reshape((blocks, slot_count) + tile_shape[1:])
    own_rows = lax.dynamic_slice_in_dim(pattern, device_index * blocks, blocks, 0)
    positions = jnp.arange(BLOCK)
    causal = positions[None, :] <= positions[:, None]
    self_slot = jnp.arange(slot_count) == LEVELS
    tile_keep = (own_rows >= 0)[:, :, None, None] & (
        jnp.logical_not(self_slot)[None, :, None, None] | causal[None, None]
    )
    scores = (
        jnp.einsum("bqhd,bskhd->bhqsk", query_blocks, key_stack, preferred_element_type=jnp.float32)
        * score_scale
    )
    scores = jnp.where(jnp.transpose(tile_keep, (0, 2, 1, 3))[:, None], scores, NEG_BIG)
    highest = jnp.max(scores, axis=(3, 4))
    log_total = highest + jnp.log(jnp.sum(jnp.exp(scores - highest[..., None, None]), axis=(3, 4)))
    prob_stack = jnp.exp(scores - log_total[..., None, None]).astype(jnp.bfloat16)
    attention = jnp.einsum(
        "bhqsk,bskhd->bqhd", prob_stack, value_stack, preferred_element_type=jnp.float32
    ).astype(jnp.bfloat16)
    attn_wide = attention.reshape(tokens_here, heads_here * HD).astype(jnp.float32)
    square_sum = lax.psum(jnp.sum(attn_wide * attn_wide, axis=1), "head")
    inverse = lax.rsqrt(square_sum / WIDTH + EPSILON)
    normed = (attn_wide * inverse[:, None]).astype(jnp.bfloat16)
    upstream_wide = upstream.astype(jnp.float32)
    cross_term = lax.psum(jnp.sum(upstream_wide * attn_wide, axis=1), "head")
    grad_attn = (
        inverse[:, None] * upstream_wide - attn_wide * (inverse**3 * cross_term / WIDTH)[:, None]
    ).astype(jnp.bfloat16)
    row_delta = jnp.sum(
        (grad_attn.astype(jnp.float32) * attn_wide).reshape(tokens_here, heads_here, HD), axis=2
    )
    row_delta = jnp.transpose(row_delta.reshape(blocks, BLOCK, heads_here), (0, 2, 1))

    def spread(array):
        return jnp.broadcast_to(array[:, None], (blocks, slot_count) + array.shape[1:]).reshape(
            (pair_count,) + array.shape[1:]
        )

    grad_blocks = grad_attn.reshape(tile_shape)
    query_pairs = spread(query_blocks)
    grad_pairs = spread(grad_blocks)
    keep_pairs = tile_keep.reshape(pair_count, BLOCK, BLOCK)
    dscore, prob_pairs = pair_grads(
        query_pairs,
        grad_pairs,
        spread(log_total),
        spread(row_delta),
        key_tiles,
        value_tiles,
        keep_pairs,
        score_scale,
    )
    grad_query = jnp.einsum(
        "phqk,pkhd->pqhd", dscore, key_tiles, preferred_element_type=jnp.float32
    )
    grad_query = jnp.sum(grad_query.reshape((blocks, slot_count) + tile_shape[1:]), axis=1)
    grad_queries = grad_query.astype(jnp.bfloat16).reshape(tokens_here, heads_here * HD)
    local_rows = [row_index for row_index in range(pair_count) if routing[row_index][0] == 0]
    chosen = jnp.array(local_rows, jnp.int32)
    local_terms = key_grads(
        dscore[chosen], prob_pairs[chosen], query_pairs[chosen], grad_pairs[chosen]
    )
    key_sum = collect(local_terms, [routing[row_index][1] for row_index in local_rows], blocks)
    for offset in offsets:
        remote_rows = [
            row_index for row_index in range(pair_count) if routing[row_index][0] == offset
        ]
        chosen = jnp.array(remote_rows, jnp.int32)
        remote_terms = key_grads(
            dscore[chosen], prob_pairs[chosen], query_pairs[chosen], grad_pairs[chosen]
        )
        outgoing = collect(
            remote_terms, [routing[row_index][1] for row_index in remote_rows], blocks
        )
        key_sum = key_sum + shifted(for_sending(outgoing), "ctx", -offset).astype(outgoing.dtype)
    grad_keys = key_sum[0].astype(jnp.bfloat16).reshape(tokens_here, heads_here * HD)
    grad_values = key_sum[1].astype(jnp.bfloat16).reshape(tokens_here, heads_here * HD)
    return (normed, grad_queries, grad_keys, grad_values)


NT = (((1,), (1,)), ((), ()))
NN = (((1,), (0,)), ((), ()))
TN = (((0,), (0,)), ((), ()))
SCALE = HD ** (-0.5)
TAIL = 32


NEAR, FAR, SIDE, HELPED, LOCAL = range(5)


class Place:
    def __init__(self):
        self.me = lax.axis_index("ctx")
        self.odd = lax.rem(self.me, 2) == 1
        self.half = lax.axis_index("head") >= lax.axis_size("head") // 2


def bias_rows(pattern_ref):
    place = Place()
    me, odd, even = place.me, place.odd, jnp.logical_not(place.odd)
    blocks = pattern_ref.shape[0]
    ahead = jnp.minimum(me + 2, blocks - 1)
    has_ahead = me + 2 < blocks
    ahead_side = jnp.logical_and(has_ahead, pattern_ref[ahead, 0] >= 0)
    own_side = pattern_ref[me, 0] >= 0
    local = jnp.logical_and(odd, own_side)
    held = {
        NEAR: pattern_ref[me, 1] >= 0,
        FAR: jnp.logical_and(has_ahead, pattern_ref[ahead, 2] >= 0),
        SIDE: jnp.logical_or(local, jnp.logical_and(even, ahead_side)),
        HELPED: jnp.logical_or(pattern_ref[me, 2] >= 0, jnp.logical_and(even, own_side)),
        LOCAL: local,
    }
    row = lax.broadcasted_iota(jnp.int32, (8, BLOCK), 0)
    rows = jnp.zeros((8, BLOCK), jnp.float32)
    for index, flag in held.items():
        rows = jnp.where(row == index, jnp.where(flag, 0.0, NEG_BIG), rows)
    return rows


def mm(a, b, dims):
    return lax.dot_general(a, b, dims, preferred_element_type=jnp.float32)


def rows_of(h):
    return slice(h * HD, (h + 1) * HD)


def causal_mask():
    keys = lax.broadcasted_iota(jnp.int32, (BLOCK, BLOCK), 0)
    return keys <= lax.broadcasted_iota(jnp.int32, (BLOCK, BLOCK), 1)


def split_rows(rows):
    first = rows.astype(jnp.bfloat16).astype(jnp.float32)
    second = (rows - first).astype(jnp.bfloat16).astype(jnp.float32)
    third = rows - first - second
    return jnp.concatenate([first, second, third, jnp.zeros_like(rows)], axis=0).astype(jnp.bfloat16)


def joined_rows(tile):
    wide = tile.astype(jnp.float32)
    return wide[0:8] + wide[8:16] + wide[16:24]


def stack_rows(rows):
    return jnp.concatenate(rows + [jnp.zeros((1, BLOCK), jnp.float32)] * (8 - len(rows)), axis=0)


def score_tile(keys, queries):
    return mm(keys, queries, NT) * SCALE


def softmax_parts(pairs):
    tops = [scores.max(axis=0, keepdims=True) for scores, _ in pairs]
    weights = [jnp.exp(scores - top) for (scores, _), top in zip(pairs, tops)]
    totals = [w.sum(axis=0, keepdims=True) for w in weights]
    outs = [
        mm(value, w.astype(jnp.bfloat16), TN) * (1.0 / total)
        for (_, value), w, total in zip(pairs, weights, totals)
    ]
    return [(out, top, top + jnp.log(total), w) for out, top, total, w in zip(outs, tops, totals, weights)]


FIRST, SECOND = slice(0, BLOCK), slice(BLOCK, 2 * BLOCK)


def payload_kernel(heads, q_ref, k_ref, v_ref, u_ref, up_ref, down_ref, sems):
    half = Place().half
    top, bottom = pl.ds(0, BLOCK), pl.ds(BLOCK, BLOCK)

    def move(sources):
        targets = (up_ref.at[top], up_ref.at[bottom], down_ref.at[top], down_ref.at[bottom])
        copies = [
            pltpu.make_async_copy(source, target, sems.at[n])
            for n, (source, target) in enumerate(zip(sources, targets))
        ]
        for copy in copies:
            copy.start()
        for copy in copies:
            copy.wait()

    @pl.when(jnp.logical_not(half))
    def _():
        move((k_ref, v_ref, q_ref, u_ref))

    @pl.when(half)
    def _():
        move((q_ref, u_ref, k_ref, v_ref))


def diagonal_kernel(heads, pattern_ref, q_ref, k_ref, v_ref, u_ref, out_ref, lse_ref, ut_ref, bias_ref):
    bias_ref[...] = bias_rows(pattern_ref)
    causal = causal_mask()
    rows = []
    for h in range(heads):
        at = rows_of(h)
        scores = jnp.where(causal, score_tile(k_ref[:, at], q_ref[:, at]), NEG_BIG)
        ((out, _, lse, _),) = softmax_parts([(scores, v_ref[:, at])])
        out_ref[at] = out
        rows.append(lse)
        ut_ref[at] = u_ref[:, at].T
    lse_ref[...] = stack_rows(rows)


def merged(parts):
    highest = functools.reduce(jnp.maximum, [lse for _, lse in parts])
    total = highest + jnp.log(functools.reduce(jnp.add, [jnp.exp(lse - highest) for _, lse in parts]))
    return functools.reduce(jnp.add, [out * jnp.exp(lse - total) for out, lse in parts]), total


def forward_kernel(
    heads,
    bias_ref,
    up_ref,
    down_ref,
    q_ref,
    kx_ref,
    vx_ref,
    out_ref,
    lse_ref,
    up_out_ref,
    down_out_ref,
    ez_ref,
    ex_ref,
    en_ref,
    mz_ref,
    mx_ref,
    mn_ref,
):
    place = Place()
    odd, half = place.odd, place.half
    near, far, side, local = (bias_ref[n : n + 1] for n in (NEAR, FAR, SIDE, LOCAL))
    before = lse_ref[...]
    step = heads
    z_rows, own_rows, z_tops, x_tops, n_tops = [], [], [], [], []
    for start in range(0, heads, step):
        group = range(start, start + step)
        scores, weights = [], []
        for h in group:
            at = rows_of(h)
            up_a, down_a = up_ref[FIRST, at], down_ref[FIRST, at]
            k2, qz = jnp.where(half, down_a, up_a), jnp.where(half, up_a, down_a)
            q = q_ref[:, at]
            both = score_tile(k2, jnp.concatenate([qz, q], axis=0))
            x = score_tile(kx_ref[:, at], jnp.where(odd, q, qz))
            scores.append((both[:, :BLOCK] + far, x + side, both[:, BLOCK:] + near))
        for h, (z, x, n) in zip(group, scores):
            z_top, x_top, n_top = (tile.max(axis=0, keepdims=True) for tile in (z, x, n))
            both = jnp.maximum(z_top, x_top)
            z_top, x_top = jnp.where(odd, z_top, both), jnp.where(odd, x_top, both)
            z, x, n = jnp.exp(z - z_top), jnp.exp(x - x_top), jnp.exp(n - n_top)
            at = rows_of(h)
            ez_ref[at], ex_ref[at], en_ref[at] = z, x, n
            z_sum, x_sum, n_sum = (tile.sum(axis=0, keepdims=True) for tile in (z, x, n))
            z_sum = z_sum + jnp.where(odd, 0.0, x_sum)
            x_sum = jnp.maximum(x_sum, 1.0)
            for tops, top in ((z_tops, z_top), (x_tops, x_top), (n_tops, n_top)):
                tops.append(top)
            z_rows.append(z_top + jnp.log(z_sum))
            parts = (before[h : h + 1], n_top + jnp.log(n_sum) + near, x_top + jnp.log(x_sum) + local)
            highest = functools.reduce(jnp.maximum, parts)
            total = highest + jnp.log(functools.reduce(jnp.add, [jnp.exp(part - highest) for part in parts]))
            own_rows.append(total)
            d_share, n_share, x_share = (jnp.exp(part - total) for part in parts)
            z_scale = 1.0 / z_sum
            sent = [z * z_scale, x * jnp.where(odd, 0.0, z_scale)]
            kept = [n * (n_share / n_sum), x * (x_share / x_sum)]
            joined = [jnp.concatenate(tiles, axis=0).astype(jnp.bfloat16) for tiles in (sent, kept)]
            weights.append((jnp.concatenate(joined, axis=1), d_share))
        for h, (joined, d_share) in zip(group, weights):
            at = rows_of(h)
            v2 = jnp.where(half, down_ref[SECOND, at], up_ref[SECOND, at])
            out = mm(jnp.concatenate([v2, vx_ref[:, at]], axis=0), joined, TN)
            out_z = out[:, :BLOCK].astype(jnp.bfloat16)
            own = (out_ref[at] * d_share + out[:, BLOCK:]).astype(jnp.bfloat16)
            up_out_ref[at] = jnp.where(half, own, out_z)
            down_out_ref[at] = jnp.where(half, out_z, own)
    tail = slice(heads * HD, heads * HD + TAIL)
    z_tail, own_tail = split_rows(stack_rows(z_rows)), split_rows(stack_rows(own_rows))
    up_out_ref[tail] = jnp.where(half, own_tail, z_tail)
    down_out_ref[tail] = jnp.where(half, z_tail, own_tail)
    mz_ref[...] = stack_rows(z_tops)
    mx_ref[...] = stack_rows(x_tops)
    mn_ref[...] = stack_rows(n_tops)


def transpose_kernel(heads, up_ref, down_ref, out_ref):
    half = Place().half
    for h in range(heads):
        at = rows_of(h)
        out_ref[at] = jnp.where(half, up_ref[SECOND, at], down_ref[SECOND, at]).T


def merge_kernel(
    heads,
    bias_ref,
    up_ref,
    down_ref,
    up_in_ref,
    down_in_ref,
    ut_ref,
    uzt_ref,
    a_ref,
    az_ref,
    lse_ref,
    lsez_ref,
    sums_ref,
):
    half = Place().half
    tail = slice(heads * HD, heads * HD + TAIL)

    def select(rising, falling, at):
        first, second = rising[at], falling[at]
        return jnp.where(half, second, first), jnp.where(half, first, second)

    z_part, own_part = select(up_ref, down_ref, tail)
    help_part, ahead_part = select(up_in_ref, down_in_ref, tail)
    rows, shares = [], []
    for first, second in (
        (joined_rows(own_part), joined_rows(help_part) + bias_ref[HELPED : HELPED + 1]),
        (joined_rows(ahead_part), joined_rows(z_part)),
    ):
        highest = jnp.maximum(first, second)
        total = highest + jnp.log(jnp.exp(first - highest) + jnp.exp(second - highest))
        rows.append(total)
        shares.append((jnp.exp(first - total), jnp.exp(second - total)))
    lse_ref[...], lsez_ref[...] = rows
    sums = [jnp.zeros((8, BLOCK), jnp.float32)] * 4
    for h in range(heads):
        at, row = rows_of(h), slice(h, h + 1)
        z_out, own_out = select(up_ref, down_ref, at)
        help_out, ahead_out = select(up_in_ref, down_in_ref, at)
        for n, (first, second, u_ref, target) in enumerate(
            ((own_out, help_out, ut_ref, a_ref), (ahead_out, z_out, uzt_ref, az_ref))
        ):
            out = (
                first.astype(jnp.float32) * shares[n][0][row] + second.astype(jnp.float32) * shares[n][1][row]
            ).astype(jnp.bfloat16)
            target[at] = out
            wide = out.astype(jnp.float32)
            sums[2 * n] += (wide * wide).reshape(HD // 8, 8, BLOCK).sum(axis=0)
            sums[2 * n + 1] += (wide * u_ref[at].astype(jnp.float32)).reshape(HD // 8, 8, BLOCK).sum(axis=0)
    sums_ref[...] = stack_rows([part.sum(axis=0, keepdims=True) for part in sums])


def norm_rows(sums, first):
    inverse = lax.rsqrt(sums[first : first + 1] / WIDTH + EPSILON)
    return inverse, inverse**3 * sums[first + 1 : first + 2] / WIDTH


def upstream_part(norm, u, a):
    inverse, factor = norm
    wide = a.astype(jnp.float32)
    grad = (inverse * u.astype(jnp.float32) - wide * factor).astype(jnp.bfloat16)
    return grad, jnp.sum(grad.astype(jnp.float32) * wide, axis=0, keepdims=True)


def back_kernel(
    heads,
    bias_ref,
    sums_ref,
    a_ref,
    az_ref,
    lse_ref,
    lsez_ref,
    ut_ref,
    uzt_ref,
    up_ref,
    down_ref,
    kx_ref,
    vx_ref,
    ez_ref,
    ex_ref,
    en_ref,
    mz_ref,
    mx_ref,
    mn_ref,
    up_out_ref,
    down_out_ref,
    dvx_ref,
    dsz_ref,
    dsx_ref,
    dsn_ref,
    grad_ref,
    delta_ref,
):
    place = Place()
    odd, half = place.odd, place.half
    sums = sums_ref[...]
    own_norm, z_norm = norm_rows(sums, 0), norm_rows(sums, 2)
    lse, z_lse = lse_ref[...], lsez_ref[...]
    scales = (
        jnp.exp(mn_ref[...] - lse + bias_ref[NEAR : NEAR + 1]),
        jnp.exp(mz_ref[...] - z_lse + bias_ref[FAR : FAR + 1]),
        jnp.exp(mx_ref[...] - jnp.where(odd, lse, z_lse) + bias_ref[SIDE : SIDE + 1]),
    )
    deltas = []
    step = heads
    for start in range(0, heads, step):
        group = range(start, start + step)
        parts, products, scores = [], [], []
        for h in group:
            at = rows_of(h)
            grad, delta = upstream_part(own_norm, ut_ref[at], a_ref[at])
            gz, deltaz = upstream_part(z_norm, uzt_ref[at], az_ref[at])
            grad_ref[at] = grad
            deltas.append(delta)
            gx, deltax = jnp.where(odd, grad, gz), jnp.where(odd, delta, deltaz)
            parts.append(((grad, gz, gx), (delta, deltaz, deltax)))
        for h, ((grad, gz, gx), _) in zip(group, parts):
            at = rows_of(h)
            v2 = jnp.where(half, down_ref[SECOND, at], up_ref[SECOND, at])
            both = mm(v2, jnp.concatenate([grad, gz], axis=1), NN)
            products.append((both[:, :BLOCK], both[:, BLOCK:], mm(vx_ref[:, at], gx, NN)))
        for h, (_, delta), product in zip(group, parts, products):
            at = rows_of(h)
            tiles = []
            for n, (e_ref, ds_ref) in enumerate(((en_ref, dsn_ref), (ez_ref, dsz_ref), (ex_ref, dsx_ref))):
                weights = e_ref[at] * scales[n][h : h + 1]
                dscore = (weights * (product[n] - delta[n]) * SCALE).astype(jnp.bfloat16)
                ds_ref[at] = dscore
                tiles.append((weights.astype(jnp.bfloat16), dscore))
            scores.append(tiles)
        for h, ((grad, gz, gx), _), ((pn, _), (pz, dz), (px, dx)) in zip(group, parts, scores):
            at = rows_of(h)
            k2 = jnp.where(half, down_ref[FIRST, at], up_ref[FIRST, at])
            dv2 = mm(jnp.concatenate([pn, pz], axis=1), jnp.concatenate([grad, gz], axis=1), NT)
            dvx_ref[:, at] = mm(px, gx, NT).astype(jnp.bfloat16)
            joined = jnp.concatenate([dz, jnp.where(odd, jnp.zeros_like(dx), dx)], axis=0)
            dqz = mm(joined, jnp.concatenate([k2, kx_ref[:, at]], axis=0), TN).astype(jnp.bfloat16)
            dv2 = dv2.astype(jnp.bfloat16)
            up_out_ref[:, at] = jnp.where(half, dv2, dqz)
            down_out_ref[:, at] = jnp.where(half, dqz, dv2)
    delta_ref[...] = stack_rows(deltas)


def helper_keys_kernel(heads, q_ref, up_ref, down_ref, dsz_ref, dsx_ref, dsn_ref, dk_ref, dkx_ref):
    place = Place()
    for h in range(heads):
        at = rows_of(h)
        q, qz = q_ref[:, at], jnp.where(place.half, up_ref[FIRST, at], down_ref[FIRST, at])
        dk2 = mm(
            jnp.concatenate([dsn_ref[at], dsz_ref[at]], axis=1), jnp.concatenate([q, qz], axis=0), NN
        )
        dk_ref[:, at] = dk2.astype(jnp.bfloat16)
        dkx_ref[:, at] = mm(dsx_ref[at], jnp.where(place.odd, q, qz), NN).astype(jnp.bfloat16)


def diagonal_back_kernel(
    heads,
    sums_ref,
    q_ref,
    k_ref,
    v_ref,
    a_ref,
    lse_ref,
    grad_ref,
    delta_ref,
    ds_ref,
    dsx_ref,
    kx_ref,
    up_ref,
    down_ref,
    normed_ref,
    dq_ref,
    dk_ref,
    dv_ref,
):
    place = Place()
    half, odd = place.half, place.odd
    inverse, _ = norm_rows(sums_ref[...], 0)
    lse = lse_ref[...]
    causal = causal_mask()
    for h in range(heads):
        at, row = rows_of(h), slice(h, h + 1)
        normed_ref[:, at] = (a_ref[at].astype(jnp.float32) * inverse).astype(jnp.bfloat16).T
        q, k, v, grad = q_ref[:, at], k_ref[:, at], v_ref[:, at], grad_ref[at]
        weights = jnp.exp(jnp.where(causal, score_tile(k, q), NEG_BIG) - lse[row])
        dscore = (weights * (mm(v, grad, NN) - delta_ref[row]) * SCALE).astype(jnp.bfloat16)
        dk_ref[:, at] = mm(dscore, q, NN)
        dv_ref[:, at] = mm(weights.astype(jnp.bfloat16), grad, NT)
        k2 = jnp.where(half, down_ref[FIRST, at], up_ref[FIRST, at])
        dsx = jnp.where(odd, dsx_ref[at], jnp.zeros_like(dsx_ref[at]))
        dq_ref[:, at] = mm(dscore, k, TN) + mm(
            jnp.concatenate([ds_ref[at], dsx], axis=0), jnp.concatenate([k2, kx_ref[:, at]], axis=0), TN
        )


def final_first_kernel(heads, up_ref, down_ref, side_ref, dq_own_ref, dv_own_ref, dq_ref, dv_ref, token_ref):
    place = Place()
    half = place.half
    ahead = (place.me + 2 < lax.axis_size("ctx")).astype(jnp.float32)
    behind = (place.me >= 2).astype(jnp.float32)
    for h in range(heads):
        at = rows_of(h)
        up, down = up_ref[:, at], down_ref[:, at]
        dqz = jnp.where(half, down, up).astype(jnp.float32) * behind
        dv = jnp.where(half, up, down).astype(jnp.float32) * ahead
        dq_ref[:, at] = (dq_own_ref[:, at] + dqz).astype(jnp.bfloat16)
        dv_ref[:, at] = (dv_own_ref[:, at] + side_ref[:, at].astype(jnp.float32) + dv).astype(jnp.bfloat16)
    token_ref[...] = jnp.zeros_like(token_ref)


def final_keys_kernel(heads, back_ref, side_ref, dk_own_ref, dk_ref):
    ahead = (Place().me + 2 < lax.axis_size("ctx")).astype(jnp.float32)
    for h in range(heads):
        at = rows_of(h)
        dk = back_ref[:, at].astype(jnp.float32) * ahead
        dk_ref[:, at] = (dk_own_ref[:, at] + side_ref[:, at].astype(jnp.float32) + dk).astype(jnp.bfloat16)


def call(kernel, heads, flags, arrays, outs, flops, space=pltpu.VMEM, scratch=(), after=()):
    moved = sum(math.prod(a.shape) * a.dtype.itemsize for a in (*arrays, *outs))
    return pl.pallas_call(
        lambda *refs: kernel(heads, *refs[len(after) :]),
        out_shape=outs,
        in_specs=[pl.BlockSpec(memory_space=pl.ANY)] * len(after)
        + [pl.BlockSpec(memory_space=pltpu.SMEM)] * len(flags)
        + [pl.BlockSpec(memory_space=space)] * len(arrays),
        out_specs=[pl.BlockSpec(memory_space=pltpu.VMEM)] * len(outs),
        scratch_shapes=scratch,
        compiler_params=pltpu.CompilerParams(vmem_limit_bytes=24 * 2**20),
        cost_estimate=pl.CostEstimate(flops=flops, bytes_accessed=moved, transcendentals=0),
    )(*after, *flags, *arrays)


def cycles(blocks, members):
    route = []
    for block in range(blocks):
        for member in range(members):
            rising = member < members // 2
            other = member + members // 2 if rising else member - members // 2
            target = block + 2 if rising else block - 2
            inside = 0 <= target < blocks
            route.append(
                (block * members + member, target * members + member if inside else block * members + other)
            )
    return route


def meeting_shards(queries, keys, values, pattern, upstream):
    tokens, width = queries.shape
    heads = width // HD
    blocks, members = lax.axis_size("ctx"), lax.axis_size("head")
    unit = heads * 2 * BLOCK**3
    rising = cycles(blocks, members)
    falling = [(target, source) for source, target in rising]

    def cycle(up_array, down_array):
        return lax.ppermute(up_array, ("ctx", "head"), rising), lax.ppermute(
            down_array, ("ctx", "head"), falling
        )

    def swap(array):
        return lax.ppermute(array, "ctx", [(i, i ^ 1) for i in range(blocks)])

    def ring(array, distance):
        return lax.ppermute(array, "ctx", [(i, (i + distance) % blocks) for i in range(blocks)])

    def struct(*shape, dtype=jnp.bfloat16):
        return jax.ShapeDtypeStruct(shape, dtype)

    wide = struct(tokens, width, dtype=jnp.float32)
    wide_t = struct(width, tokens, dtype=jnp.float32)
    flat, flat_t = struct(tokens, width), struct(width, tokens)
    message = struct(width + TAIL, tokens)
    rows = struct(8, tokens, dtype=jnp.float32)

    payload = call(
        payload_kernel,
        heads,
        (),
        [pltpu.with_memory_space_constraint(a, pltpu.HBM) for a in (queries, keys, values, upstream)],
        [pltpu.VMEM((2 * tokens, width), jnp.bfloat16)] * 2,
        0,
        space=pltpu.HBM,
        scratch=(pltpu.SemaphoreType.DMA((4,)),),
    )
    received = cycle(*payload)
    keys_x, values_x = swap(keys), swap(values)
    diagonal, diagonal_lse, upstream_t, bias = call(
        diagonal_kernel,
        heads,
        (pattern,),
        (queries, keys, values, upstream),
        (wide_t, rows, flat_t, rows),
        3 * unit,
        after=(payload[0],),
    )
    up_out, down_out, *kept = call(
        forward_kernel,
        heads,
        (),
        (bias, *received, queries, keys_x, values_x, diagonal, diagonal_lse),
        (message, message, wide_t, wide_t, wide_t, rows, rows, rows),
        6 * unit,
    )
    up_in, down_in = cycle(up_out, down_out)
    (upstream_zt,) = call(transpose_kernel, heads, (), received, (flat_t,), 0, after=(kept[-1],))
    attention, attention_z, lse, lse_z, sums = call(
        merge_kernel,
        heads,
        (),
        (bias, up_out, down_out, up_in, down_in, upstream_t, upstream_zt),
        (flat_t, flat_t, rows, rows, rows),
        unit // 64,
    )
    others = [
        lax.ppermute(sums, "head", [(i, i ^ step) for i in range(members)]) for step in range(1, members)
    ]
    sums = functools.reduce(jnp.add, others, sums)
    up_out, down_out, side_dv, far_ds, side_ds, near_ds, grad_t, delta = call(
        back_kernel,
        heads,
        (),
        (bias, sums, attention, attention_z, lse, lse_z, upstream_t, upstream_zt, *received, keys_x, values_x)
        + tuple(kept),
        (flat, flat, flat, flat_t, flat_t, flat_t, flat_t, rows),
        8 * unit,
    )
    returned = cycle(up_out, down_out)
    out_dk, side_dk = call(
        helper_keys_kernel,
        heads,
        (),
        (queries, *received, far_ds, side_ds, near_ds),
        (flat, flat),
        3 * unit,
    )
    back_dk = ring(out_dk, -2)
    side_dv, side_dk = swap(side_dv), swap(side_dk)
    normed, dq_own, dk_own, dv_own = call(
        diagonal_back_kernel,
        heads,
        (),
        (sums, queries, keys, values, attention, lse, grad_t, delta, near_ds, side_ds, keys_x, *received),
        (flat, wide, wide, wide),
        7 * unit,
    )
    grad_queries, grad_values, token = call(
        final_first_kernel, heads, (), (*returned, side_dv, dq_own, dv_own), (flat, flat, rows), 0
    )
    (grad_keys,) = call(final_keys_kernel, heads, (), (back_dk, side_dk, dk_own), (flat,), 0, after=(token,))
    return (normed, grad_queries, grad_keys, grad_values)


def shards(queries, keys, values, pattern, upstream):
    fits = lax.axis_size("ctx") == 8 and lax.axis_size("head") == 4 and queries.shape == (BLOCK, 8 * HD)
    if fits:
        return meeting_shards(queries, keys, values, pattern, upstream)
    return generic_shards(queries, keys, values, pattern, upstream)


def solution(mesh):
    return jax.shard_map(
        shards,
        mesh=mesh,
        in_specs=(P("ctx", "head"), P("ctx", "head"), P("ctx", "head"), P(), P("ctx", "head")),
        out_specs=(P("ctx", "head"), P("ctx", "head"), P("ctx", "head"), P("ctx", "head")),
        check_vma=False,
    )
```

```python
import functools
import math

import jax
import jax.numpy as jnp
from jax import lax
from jax.experimental import pallas as pl
from jax.experimental.pallas import tpu as pltpu
from jax.sharding import PartitionSpec as P

HD = 128
BLOCK = 128
LEVELS = 7
WIDTH = 4096


NEG_BIG = -1e30
EPSILON = 1e-06


def shifted(block, axis, distance):
    devices = range(lax.axis_size(axis))
    route = [(i - distance, i) for i in devices if i - distance in devices]
    return lax.ppermute(block, axis, route)


def for_sending(x):
    return jax.tree.map(lambda a: a.astype(jnp.bfloat16) if a.dtype == jnp.float32 else a, x)


def route_table(blocks, levels):
    routing = []
    for query_block in range(blocks):
        for level_index in range(levels + 1):
            if level_index == levels:
                routing.append((0, query_block))
            else:
                distance = 2**level_index
                routing.append(
                    (-((query_block - distance) // blocks), (query_block - distance) % blocks)
                )
    return routing


def pair_grads(
    query_tiles, grad_tiles, lse_tiles, delta_tiles, key_tiles, value_tiles, keep_mask, score_scale
):
    scores = (
        jnp.einsum("pqhd,pkhd->phqk", query_tiles, key_tiles, preferred_element_type=jnp.float32)
        * score_scale
    )
    scores = jnp.where(keep_mask[:, None], scores, NEG_BIG)
    weights = jnp.exp(scores - lse_tiles[..., None])
    prob_tiles = weights.astype(jnp.bfloat16)
    grad_probs = jnp.einsum(
        "pqhd,pkhd->phqk", grad_tiles, value_tiles, preferred_element_type=jnp.float32
    )
    dscore = (weights * (grad_probs - delta_tiles[..., None]) * score_scale).astype(jnp.bfloat16)
    return (dscore, prob_tiles)


def key_grads(dscore, prob_tiles, query_tiles, grad_tiles):
    key_part = jnp.einsum(
        "phqk,pqhd->pkhd", dscore, query_tiles, preferred_element_type=jnp.float32
    )
    value_part = jnp.einsum(
        "phqk,pqhd->pkhd", prob_tiles, grad_tiles, preferred_element_type=jnp.float32
    )
    return jnp.stack((key_part, value_part))


def collect(partials, targets, blocks):
    pieces = []
    for key_index in range(blocks):
        summed = jnp.zeros((2,) + partials.shape[2:], jnp.float32)
        for row_index, target in enumerate(targets):
            if target == key_index:
                summed = summed + partials[:, row_index]
        pieces.append(summed)
    return jnp.stack(pieces, axis=1)


def generic_shards(queries, keys, values, pattern, upstream):
    tokens_here = queries.shape[0]
    heads_here = queries.shape[1] // HD
    blocks = tokens_here // BLOCK
    slot_count = LEVELS + 1
    pair_count = blocks * slot_count
    score_scale = HD ** (-0.5)
    ctx_count = lax.axis_size("ctx")
    device_index = lax.axis_index("ctx")
    routing = route_table(blocks, LEVELS)
    offsets = sorted(
        set((route_entry[0] for route_entry in routing if 0 < route_entry[0] < ctx_count))
    )
    tile_shape = (blocks, BLOCK, heads_here, HD)
    query_blocks = queries.reshape(tile_shape)
    own_pairs = jnp.stack((keys, values)).reshape((2,) + tile_shape)
    sources = {0: own_pairs}
    for offset in offsets:
        fetched = shifted(jnp.stack((keys, values)), "ctx", offset)
        sources[offset] = fetched.reshape((2,) + tile_shape)
    empty_tile = jnp.zeros((2, BLOCK, heads_here, HD), jnp.bfloat16)
    gathered = []
    for source, key_index in routing:
        if source in sources:
            gathered.append(sources[source][:, key_index])
        else:
            gathered.append(empty_tile)
    pair_kv = jnp.stack(gathered, axis=1)
    key_tiles = pair_kv[0]
    value_tiles = pair_kv[1]
    key_stack = key_tiles.reshape((blocks, slot_count) + tile_shape[1:])
    value_stack = value_tiles.reshape((blocks, slot_count) + tile_shape[1:])
    own_rows = lax.dynamic_slice_in_dim(pattern, device_index * blocks, blocks, 0)
    positions = jnp.arange(BLOCK)
    causal = positions[None, :] <= positions[:, None]
    self_slot = jnp.arange(slot_count) == LEVELS
    tile_keep = (own_rows >= 0)[:, :, None, None] & (
        jnp.logical_not(self_slot)[None, :, None, None] | causal[None, None]
    )
    scores = (
        jnp.einsum("bqhd,bskhd->bhqsk", query_blocks, key_stack, preferred_element_type=jnp.float32)
        * score_scale
    )
    scores = jnp.where(jnp.transpose(tile_keep, (0, 2, 1, 3))[:, None], scores, NEG_BIG)
    highest = jnp.max(scores, axis=(3, 4))
    log_total = highest + jnp.log(jnp.sum(jnp.exp(scores - highest[..., None, None]), axis=(3, 4)))
    prob_stack = jnp.exp(scores - log_total[..., None, None]).astype(jnp.bfloat16)
    attention = jnp.einsum(
        "bhqsk,bskhd->bqhd", prob_stack, value_stack, preferred_element_type=jnp.float32
    ).astype(jnp.bfloat16)
    attn_wide = attention.reshape(tokens_here, heads_here * HD).astype(jnp.float32)
    square_sum = lax.psum(jnp.sum(attn_wide * attn_wide, axis=1), "head")
    inverse = lax.rsqrt(square_sum / WIDTH + EPSILON)
    normed = (attn_wide * inverse[:, None]).astype(jnp.bfloat16)
    upstream_wide = upstream.astype(jnp.float32)
    cross_term = lax.psum(jnp.sum(upstream_wide * attn_wide, axis=1), "head")
    grad_attn = (
        inverse[:, None] * upstream_wide - attn_wide * (inverse**3 * cross_term / WIDTH)[:, None]
    ).astype(jnp.bfloat16)
    row_delta = jnp.sum(
        (grad_attn.astype(jnp.float32) * attn_wide).reshape(tokens_here, heads_here, HD), axis=2
    )
    row_delta = jnp.transpose(row_delta.reshape(blocks, BLOCK, heads_here), (0, 2, 1))

    def spread(array):
        return jnp.broadcast_to(array[:, None], (blocks, slot_count) + array.shape[1:]).reshape(
            (pair_count,) + array.shape[1:]
        )

    grad_blocks = grad_attn.reshape(tile_shape)
    query_pairs = spread(query_blocks)
    grad_pairs = spread(grad_blocks)
    keep_pairs = tile_keep.reshape(pair_count, BLOCK, BLOCK)
    dscore, prob_pairs = pair_grads(
        query_pairs,
        grad_pairs,
        spread(log_total),
        spread(row_delta),
        key_tiles,
        value_tiles,
        keep_pairs,
        score_scale,
    )
    grad_query = jnp.einsum(
        "phqk,pkhd->pqhd", dscore, key_tiles, preferred_element_type=jnp.float32
    )
    grad_query = jnp.sum(grad_query.reshape((blocks, slot_count) + tile_shape[1:]), axis=1)
    grad_queries = grad_query.astype(jnp.bfloat16).reshape(tokens_here, heads_here * HD)
    local_rows = [row_index for row_index in range(pair_count) if routing[row_index][0] == 0]
    chosen = jnp.array(local_rows, jnp.int32)
    local_terms = key_grads(
        dscore[chosen], prob_pairs[chosen], query_pairs[chosen], grad_pairs[chosen]
    )
    key_sum = collect(local_terms, [routing[row_index][1] for row_index in local_rows], blocks)
    for offset in offsets:
        remote_rows = [
            row_index for row_index in range(pair_count) if routing[row_index][0] == offset
        ]
        chosen = jnp.array(remote_rows, jnp.int32)
        remote_terms = key_grads(
            dscore[chosen], prob_pairs[chosen], query_pairs[chosen], grad_pairs[chosen]
        )
        outgoing = collect(
            remote_terms, [routing[row_index][1] for row_index in remote_rows], blocks
        )
        key_sum = key_sum + shifted(for_sending(outgoing), "ctx", -offset).astype(outgoing.dtype)
    grad_keys = key_sum[0].astype(jnp.bfloat16).reshape(tokens_here, heads_here * HD)
    grad_values = key_sum[1].astype(jnp.bfloat16).reshape(tokens_here, heads_here * HD)
    return (normed, grad_queries, grad_keys, grad_values)


NT = (((1,), (1,)), ((), ()))
NN = (((1,), (0,)), ((), ()))
TN = (((0,), (0,)), ((), ()))
SCALE = HD ** (-0.5)
TAIL = 32


NEAR, FAR, SIDE, HELPED, LOCAL, KEY_NEAR, KEY_FAR, KEY_SIDE = range(8)


class Place:
    def __init__(self):
        self.me = lax.axis_index("ctx")
        self.odd = lax.rem(self.me, 2) == 1
        self.half = lax.axis_index("head") >= lax.axis_size("head") // 2


def bias_rows(pattern_ref):
    place = Place()
    me, odd, even = place.me, place.odd, jnp.logical_not(place.odd)
    blocks = pattern_ref.shape[0]
    ahead = jnp.minimum(me + 2, blocks - 1)
    has_ahead = me + 2 < blocks
    ahead_side = jnp.logical_and(has_ahead, pattern_ref[ahead, 0] >= 0)
    own_side = pattern_ref[me, 0] >= 0
    local = jnp.logical_and(odd, own_side)

    def ahead_holds(distance, level):
        entry = pattern_ref[jnp.minimum(me + distance, blocks - 1), level]
        return jnp.logical_and(me + distance < blocks, entry >= 0)

    held = {
        NEAR: pattern_ref[me, 1] >= 0,
        FAR: jnp.logical_and(has_ahead, pattern_ref[ahead, 2] >= 0),
        SIDE: jnp.logical_or(local, jnp.logical_and(even, ahead_side)),
        HELPED: jnp.logical_or(pattern_ref[me, 2] >= 0, jnp.logical_and(even, own_side)),
        LOCAL: local,
        KEY_NEAR: ahead_holds(2, 1),
        KEY_FAR: ahead_holds(4, 2),
        KEY_SIDE: ahead_holds(1, 0),
    }
    row = lax.broadcasted_iota(jnp.int32, (8, BLOCK), 0)
    rows = jnp.zeros((8, BLOCK), jnp.float32)
    for index, flag in held.items():
        rows = jnp.where(row == index, jnp.where(flag, 0.0, NEG_BIG), rows)
    return rows


def mm(a, b, dims):
    return lax.dot_general(a, b, dims, preferred_element_type=jnp.float32)


def rows_of(h):
    return slice(h * HD, (h + 1) * HD)


def causal_mask():
    keys = lax.broadcasted_iota(jnp.int32, (BLOCK, BLOCK), 0)
    return keys <= lax.broadcasted_iota(jnp.int32, (BLOCK, BLOCK), 1)


def split_rows(rows):
    first = rows.astype(jnp.bfloat16).astype(jnp.float32)
    second = (rows - first).astype(jnp.bfloat16).astype(jnp.float32)
    third = rows - first - second
    return jnp.concatenate([first, second, third, jnp.zeros_like(rows)], axis=0).astype(jnp.bfloat16)


def joined_rows(tile):
    wide = tile.astype(jnp.float32)
    return wide[0:8] + wide[8:16] + wide[16:24]


def stack_rows(rows):
    return jnp.concatenate(rows + [jnp.zeros((1, BLOCK), jnp.float32)] * (8 - len(rows)), axis=0)


def score_tile(keys, queries):
    return mm(keys, queries, NT) * SCALE


def softmax_parts(pairs):
    tops = [scores.max(axis=0, keepdims=True) for scores, _ in pairs]
    weights = [jnp.exp(scores - top) for (scores, _), top in zip(pairs, tops)]
    totals = [w.sum(axis=0, keepdims=True) for w in weights]
    outs = [
        mm(value, w.astype(jnp.bfloat16), TN) * (1.0 / total)
        for (_, value), w, total in zip(pairs, weights, totals)
    ]
    return [(out, top, top + jnp.log(total), w) for out, top, total, w in zip(outs, tops, totals, weights)]


FIRST, SECOND = slice(0, BLOCK), slice(BLOCK, 2 * BLOCK)


def payload_kernel(heads, q_ref, k_ref, v_ref, u_ref, up_ref, down_ref, sems):
    half = Place().half
    top, bottom = pl.ds(0, BLOCK), pl.ds(BLOCK, BLOCK)

    def move(sources):
        targets = (up_ref.at[top], up_ref.at[bottom], down_ref.at[top], down_ref.at[bottom])
        copies = [
            pltpu.make_async_copy(source, target, sems.at[n])
            for n, (source, target) in enumerate(zip(sources, targets))
        ]
        for copy in copies:
            copy.start()
        for copy in copies:
            copy.wait()

    @pl.when(jnp.logical_not(half))
    def _():
        move((k_ref, v_ref, q_ref, u_ref))

    @pl.when(half)
    def _():
        move((q_ref, u_ref, k_ref, v_ref))


def diagonal_kernel(heads, pattern_ref, q_ref, k_ref, v_ref, u_ref, out_ref, lse_ref, ut_ref, bias_ref):
    bias_ref[...] = bias_rows(pattern_ref)
    causal = causal_mask()
    rows = []
    for h in range(heads):
        at = rows_of(h)
        scores = jnp.where(causal, score_tile(k_ref[:, at], q_ref[:, at]), NEG_BIG)
        ((out, _, lse, _),) = softmax_parts([(scores, v_ref[:, at])])
        out_ref[at] = out
        rows.append(lse)
        ut_ref[at] = u_ref[:, at].T
    lse_ref[...] = stack_rows(rows)


def merged(parts):
    highest = functools.reduce(jnp.maximum, [lse for _, lse in parts])
    total = highest + jnp.log(functools.reduce(jnp.add, [jnp.exp(lse - highest) for _, lse in parts]))
    return functools.reduce(jnp.add, [out * jnp.exp(lse - total) for out, lse in parts]), total


def forward_kernel(
    heads,
    bias_ref,
    up_ref,
    down_ref,
    q_ref,
    kx_ref,
    vx_ref,
    out_ref,
    lse_ref,
    up_out_ref,
    down_out_ref,
    ez_ref,
    ex_ref,
    en_ref,
    mz_ref,
    mx_ref,
    mn_ref,
):
    place = Place()
    odd, half = place.odd, place.half
    near, far, side, local = (bias_ref[n : n + 1] for n in (NEAR, FAR, SIDE, LOCAL))
    before = lse_ref[...]
    step = heads
    z_rows, own_rows, z_tops, x_tops, n_tops = [], [], [], [], []
    for start in range(0, heads, step):
        group = range(start, start + step)
        scores, weights = [], []
        for h in group:
            at = rows_of(h)
            up_a, down_a = up_ref[FIRST, at], down_ref[FIRST, at]
            k2, qz = jnp.where(half, down_a, up_a), jnp.where(half, up_a, down_a)
            q = q_ref[:, at]
            both = score_tile(k2, jnp.concatenate([qz, q], axis=0))
            x = score_tile(kx_ref[:, at], jnp.where(odd, q, qz))
            scores.append((both[:, :BLOCK] + far, x + side, both[:, BLOCK:] + near))
        for h, (z, x, n) in zip(group, scores):
            z_top, x_top, n_top = (tile.max(axis=0, keepdims=True) for tile in (z, x, n))
            both = jnp.maximum(z_top, x_top)
            z_top, x_top = jnp.where(odd, z_top, both), jnp.where(odd, x_top, both)
            z, x, n = jnp.exp(z - z_top), jnp.exp(x - x_top), jnp.exp(n - n_top)
            at = rows_of(h)
            ez_ref[at], ex_ref[at], en_ref[at] = z, x, n
            z_sum, x_sum, n_sum = (tile.sum(axis=0, keepdims=True) for tile in (z, x, n))
            z_sum = z_sum + jnp.where(odd, 0.0, x_sum)
            x_sum = jnp.maximum(x_sum, 1.0)
            for tops, top in ((z_tops, z_top), (x_tops, x_top), (n_tops, n_top)):
                tops.append(top)
            z_rows.append(z_top + jnp.log(z_sum))
            parts = (before[h : h + 1], n_top + jnp.log(n_sum) + near, x_top + jnp.log(x_sum) + local)
            highest = functools.reduce(jnp.maximum, parts)
            total = highest + jnp.log(functools.reduce(jnp.add, [jnp.exp(part - highest) for part in parts]))
            own_rows.append(total)
            d_share, n_share, x_share = (jnp.exp(part - total) for part in parts)
            z_scale = 1.0 / z_sum
            sent = [z * z_scale, x * jnp.where(odd, 0.0, z_scale)]
            kept = [n * (n_share / n_sum), x * (x_share / x_sum)]
            joined = [jnp.concatenate(tiles, axis=0).astype(jnp.bfloat16) for tiles in (sent, kept)]
            weights.append((jnp.concatenate(joined, axis=1), d_share))
        for h, (joined, d_share) in zip(group, weights):
            at = rows_of(h)
            v2 = jnp.where(half, down_ref[SECOND, at], up_ref[SECOND, at])
            out = mm(jnp.concatenate([v2, vx_ref[:, at]], axis=0), joined, TN)
            out_z = out[:, :BLOCK].astype(jnp.bfloat16)
            own = (out_ref[at] * d_share + out[:, BLOCK:]).astype(jnp.bfloat16)
            up_out_ref[at] = jnp.where(half, own, out_z)
            down_out_ref[at] = jnp.where(half, out_z, own)
    tail = slice(heads * HD, heads * HD + TAIL)
    z_tail, own_tail = split_rows(stack_rows(z_rows)), split_rows(stack_rows(own_rows))
    up_out_ref[tail] = jnp.where(half, own_tail, z_tail)
    down_out_ref[tail] = jnp.where(half, z_tail, own_tail)
    mz_ref[...] = stack_rows(z_tops)
    mx_ref[...] = stack_rows(x_tops)
    mn_ref[...] = stack_rows(n_tops)


def transpose_kernel(heads, up_ref, down_ref, out_ref):
    half = Place().half
    for h in range(heads):
        at = rows_of(h)
        out_ref[at] = jnp.where(half, up_ref[SECOND, at], down_ref[SECOND, at]).T


def merge_kernel(
    heads,
    bias_ref,
    up_ref,
    down_ref,
    up_in_ref,
    down_in_ref,
    ut_ref,
    uzt_ref,
    a_ref,
    az_ref,
    lse_ref,
    lsez_ref,
    sums_ref,
):
    half = Place().half
    tail = slice(heads * HD, heads * HD + TAIL)

    def select(rising, falling, at):
        first, second = rising[at], falling[at]
        return jnp.where(half, second, first), jnp.where(half, first, second)

    z_part, own_part = select(up_ref, down_ref, tail)
    help_part, ahead_part = select(up_in_ref, down_in_ref, tail)
    rows, shares = [], []
    for first, second in (
        (joined_rows(own_part), joined_rows(help_part) + bias_ref[HELPED : HELPED + 1]),
        (joined_rows(ahead_part), joined_rows(z_part)),
    ):
        highest = jnp.maximum(first, second)
        total = highest + jnp.log(jnp.exp(first - highest) + jnp.exp(second - highest))
        rows.append(total)
        shares.append((jnp.exp(first - total), jnp.exp(second - total)))
    lse_ref[...], lsez_ref[...] = (jnp.maximum(total, -1e9) for total in rows)
    sums = [jnp.zeros((8, BLOCK), jnp.float32)] * 4
    for h in range(heads):
        at, row = rows_of(h), slice(h, h + 1)
        z_out, own_out = select(up_ref, down_ref, at)
        help_out, ahead_out = select(up_in_ref, down_in_ref, at)
        for n, (first, second, u_ref, target) in enumerate(
            ((own_out, help_out, ut_ref, a_ref), (ahead_out, z_out, uzt_ref, az_ref))
        ):
            out = (
                first.astype(jnp.float32) * shares[n][0][row] + second.astype(jnp.float32) * shares[n][1][row]
            ).astype(jnp.bfloat16)
            target[at] = out
            wide = out.astype(jnp.float32)
            sums[2 * n] += (wide * wide).reshape(HD // 8, 8, BLOCK).sum(axis=0)
            sums[2 * n + 1] += (wide * u_ref[at].astype(jnp.float32)).reshape(HD // 8, 8, BLOCK).sum(axis=0)
    sums_ref[...] = stack_rows([part.sum(axis=0, keepdims=True) for part in sums])


def norm_rows(sums, first):
    inverse = lax.rsqrt(sums[first : first + 1] / WIDTH + EPSILON)
    return inverse, inverse**3 * sums[first + 1 : first + 2] / WIDTH


def upstream_part(norm, u, a):
    inverse, factor = norm
    wide = a.astype(jnp.float32)
    grad = (inverse * u.astype(jnp.float32) - wide * factor).astype(jnp.bfloat16)
    return grad, jnp.sum(grad.astype(jnp.float32) * wide, axis=0, keepdims=True)


def side_queries_kernel(heads, q_ref, up_ref, down_ref, out_ref):
    place = Place()
    for h in range(heads):
        at = rows_of(h)
        qz = jnp.where(place.half, up_ref[FIRST, at], down_ref[FIRST, at])
        out_ref[:, at] = jnp.where(place.odd, q_ref[:, at], qz)


def relay_kernel(heads, up_ref, down_ref, out_ref):
    half = Place().half
    for h in range(heads):
        at = rows_of(h)
        out_ref[FIRST, at] = jnp.where(half, up_ref[FIRST, at], down_ref[FIRST, at])
    out_ref[BLOCK:] = jnp.zeros_like(out_ref[BLOCK:])


def back_kernel(
    heads,
    bias_ref,
    sums_ref,
    a_ref,
    az_ref,
    lse_ref,
    lsez_ref,
    ut_ref,
    uzt_ref,
    up_ref,
    down_ref,
    kx_ref,
    vx_ref,
    ez_ref,
    ex_ref,
    mz_ref,
    mx_ref,
    up_out_ref,
    down_out_ref,
    side_out_ref,
    dsx_ref,
    grad_ref,
    gz_ref,
    delta_ref,
    deltaz_ref,
):
    place = Place()
    odd, half = place.odd, place.half
    sums = sums_ref[...]
    own_norm, z_norm = norm_rows(sums, 0), norm_rows(sums, 2)
    lse, z_lse = lse_ref[...], lsez_ref[...]
    scales = (
        jnp.exp(mz_ref[...] - z_lse + bias_ref[FAR : FAR + 1]),
        jnp.exp(mx_ref[...] - jnp.where(odd, lse, z_lse) + bias_ref[SIDE : SIDE + 1]),
    )
    group = range(heads)
    deltas, z_deltas = [], []
    parts, products, scores = [], [], []
    for h in group:
        at = rows_of(h)
        grad, delta = upstream_part(own_norm, ut_ref[at], a_ref[at])
        gz, deltaz = upstream_part(z_norm, uzt_ref[at], az_ref[at])
        grad_ref[at], gz_ref[at] = grad, gz
        deltas.append(delta)
        z_deltas.append(deltaz)
        gx, deltax = jnp.where(odd, grad, gz), jnp.where(odd, delta, deltaz)
        side_out_ref[at] = gx
        parts.append(((gz, gx), (deltaz, deltax)))
    for h, ((gz, gx), _) in zip(group, parts):
        at = rows_of(h)
        v2 = jnp.where(half, down_ref[SECOND, at], up_ref[SECOND, at])
        products.append((mm(v2, gz, NN), mm(vx_ref[:, at], gx, NN)))
    for h, (_, delta), product in zip(group, parts, products):
        tiles = []
        for n, e_ref in enumerate((ez_ref, ex_ref)):
            weights = e_ref[rows_of(h)] * scales[n][h : h + 1]
            tiles.append((weights * (product[n] - delta[n]) * SCALE).astype(jnp.bfloat16))
        dsx_ref[rows_of(h)] = tiles[1]
        scores.append(tiles)
    for h, ((gz, _), _), (dz, dx) in zip(group, parts, scores):
        at = rows_of(h)
        k2 = jnp.where(half, down_ref[FIRST, at], up_ref[FIRST, at])
        joined = jnp.concatenate([dz, jnp.where(odd, jnp.zeros_like(dx), dx)], axis=0)
        dqz = mm(jnp.concatenate([k2, kx_ref[:, at]], axis=0), joined, TN).astype(jnp.bfloat16)
        up_out_ref[at] = jnp.where(half, gz, dqz)
        down_out_ref[at] = jnp.where(half, dqz, gz)
    delta, deltaz = stack_rows(deltas), stack_rows(z_deltas)
    delta_ref[...], deltaz_ref[...] = delta, deltaz
    tail = slice(heads * HD, heads * HD + 2 * TAIL)
    z_tail = jnp.concatenate([split_rows(z_lse), split_rows(deltaz)], axis=0)
    own_tail = jnp.concatenate([split_rows(lse), split_rows(delta)], axis=0)
    up_out_ref[tail] = jnp.where(half, z_tail, jnp.zeros_like(z_tail))
    down_out_ref[tail] = jnp.where(half, jnp.zeros_like(z_tail), z_tail)
    side_out_ref[tail] = jnp.where(odd, own_tail, z_tail)


def local_back_kernel(
    heads,
    bias_ref,
    sums_ref,
    q_ref,
    k_ref,
    v_ref,
    a_ref,
    lse_ref,
    lsez_ref,
    grad_ref,
    gz_ref,
    delta_ref,
    deltaz_ref,
    en_ref,
    mn_ref,
    dsx_ref,
    kx_ref,
    up_ref,
    down_ref,
    normed_ref,
    dq_ref,
    dk_ref,
    dv_ref,
):
    place = Place()
    odd, half = place.odd, place.half
    inverse, _ = norm_rows(sums_ref[...], 0)
    lse, z_lse = lse_ref[...], lsez_ref[...] - bias_ref[KEY_NEAR : KEY_NEAR + 1]
    near_scale = jnp.exp(mn_ref[...] - lse + bias_ref[NEAR : NEAR + 1])
    causal = causal_mask()
    for h in range(heads):
        at, row = rows_of(h), slice(h, h + 1)
        normed_ref[:, at] = (a_ref[at].astype(jnp.float32) * inverse).astype(jnp.bfloat16).T
        up_a, down_a = up_ref[FIRST, at], down_ref[FIRST, at]
        k2, qz = jnp.where(half, down_a, up_a), jnp.where(half, up_a, down_a)
        v2 = jnp.where(half, down_ref[SECOND, at], up_ref[SECOND, at])
        q, k, v, grad, gz = q_ref[:, at], k_ref[:, at], v_ref[:, at], grad_ref[at], gz_ref[at]
        queries, grads = jnp.concatenate([q, qz], axis=0), jnp.concatenate([grad, gz], axis=1)
        both = score_tile(k, queries)
        products = mm(v, grads, NN)
        own = jnp.exp(jnp.where(causal, both[:, :BLOCK], NEG_BIG) - lse[row])
        ahead = jnp.exp(both[:, BLOCK:] - z_lse[row])
        near = en_ref[at] * near_scale[row]
        own_ds = (own * (products[:, :BLOCK] - delta_ref[row]) * SCALE).astype(jnp.bfloat16)
        ahead_ds = (ahead * (products[:, BLOCK:] - deltaz_ref[row]) * SCALE).astype(jnp.bfloat16)
        near_ds = (near * (mm(v2, grad, NN) - delta_ref[row]) * SCALE).astype(jnp.bfloat16)
        dk_ref[:, at] = mm(jnp.concatenate([own_ds, ahead_ds], axis=1), queries, NN)
        probs = jnp.concatenate([own, ahead], axis=1).astype(jnp.bfloat16)
        dv_ref[:, at] = mm(probs, grads, NT)
        dsx = jnp.where(odd, dsx_ref[at], jnp.zeros_like(dsx_ref[at]))
        dq_ref[:, at] = mm(own_ds, k, TN) + mm(
            jnp.concatenate([near_ds, dsx], axis=0), jnp.concatenate([k2, kx_ref[:, at]], axis=0), TN
        )


def key_scores_kernel(heads, bias_ref, k_ref, far_ref, side_ref, out_ref):
    for h in range(heads):
        at = rows_of(h)
        both = score_tile(k_ref[:, at], jnp.concatenate([far_ref[FIRST, at], side_ref[:, at]], axis=0))
        out_ref[0, at] = both[:, :BLOCK] + bias_ref[KEY_FAR : KEY_FAR + 1]
        out_ref[1, at] = both[:, BLOCK:] + bias_ref[KEY_SIDE : KEY_SIDE + 1]


def final_kernel(
    heads,
    scores_ref,
    far_ref,
    sideq_ref,
    up_ref,
    down_ref,
    side_ref,
    v_ref,
    dq_own_ref,
    dk_own_ref,
    dv_own_ref,
    dq_ref,
    dk_ref,
    dv_ref,
):
    place = Place()
    half = place.half
    behind = (place.me >= 2).astype(jnp.float32)
    first = slice(heads * HD, heads * HD + TAIL)
    second = slice(heads * HD + TAIL, heads * HD + 2 * TAIL)
    lse, delta = (
        (joined_rows(jnp.where(half, up_ref[part], down_ref[part])), joined_rows(side_ref[part]))
        for part in (first, second)
    )
    group = range(heads)
    grads, products, tiles = [], [], []
    for h in group:
        at = rows_of(h)
        up, down = up_ref[at], down_ref[at]
        dqz = jnp.where(half, down, up).T.astype(jnp.float32) * behind
        dq_ref[:, at] = (dq_own_ref[:, at] + dqz).astype(jnp.bfloat16)
        grads.append(jnp.concatenate([jnp.where(half, up, down), side_ref[at]], axis=1))
    for h, grad in zip(group, grads):
        products.append(mm(v_ref[:, rows_of(h)], grad, NN))
    for h, product in zip(group, products):
        row = slice(h, h + 1)
        probs = [jnp.exp(scores_ref[n, rows_of(h)] - lse[n][row]) for n in range(2)]
        scores = [
            probs[n] * (product[:, n * BLOCK : (n + 1) * BLOCK] - delta[n][row]) * SCALE for n in range(2)
        ]
        tiles.append([jnp.concatenate(pair, axis=1).astype(jnp.bfloat16) for pair in (probs, scores)])
    for h, grad, (probs, scores) in zip(group, grads, tiles):
        at = rows_of(h)
        queries = jnp.concatenate([far_ref[FIRST, at], sideq_ref[:, at]], axis=0)
        dk_ref[:, at] = (dk_own_ref[:, at] + mm(scores, queries, NN)).astype(jnp.bfloat16)
        dv_ref[:, at] = (dv_own_ref[:, at] + mm(probs, grad, NT)).astype(jnp.bfloat16)


def call(kernel, heads, flags, arrays, outs, flops, space=pltpu.VMEM, scratch=(), after=()):
    moved = sum(math.prod(a.shape) * a.dtype.itemsize for a in (*arrays, *outs)) if flops else 0
    return pl.pallas_call(
        lambda *refs: kernel(heads, *refs[len(after) :]),
        out_shape=outs,
        in_specs=[pl.BlockSpec(memory_space=pl.ANY)] * len(after)
        + [pl.BlockSpec(memory_space=pltpu.SMEM)] * len(flags)
        + [pl.BlockSpec(memory_space=space)] * len(arrays),
        out_specs=[pl.BlockSpec(memory_space=pltpu.VMEM)] * len(outs),
        scratch_shapes=scratch,
        compiler_params=pltpu.CompilerParams(vmem_limit_bytes=24 * 2**20),
        cost_estimate=pl.CostEstimate(flops=flops, bytes_accessed=moved, transcendentals=0),
    )(*after, *flags, *arrays)


def cycles(blocks, members):
    route = []
    for block in range(blocks):
        for member in range(members):
            rising = member < members // 2
            other = member + members // 2 if rising else member - members // 2
            target = block + 2 if rising else block - 2
            inside = 0 <= target < blocks
            route.append(
                (block * members + member, target * members + member if inside else block * members + other)
            )
    return route


def meeting_shards(queries, keys, values, pattern, upstream):
    tokens, width = queries.shape
    heads = width // HD
    blocks, members = lax.axis_size("ctx"), lax.axis_size("head")
    unit = heads * 2 * BLOCK**3
    rising = cycles(blocks, members)
    falling = [(target, source) for source, target in rising]

    def cycle(up_array, down_array):
        return lax.ppermute(up_array, ("ctx", "head"), rising), lax.ppermute(
            down_array, ("ctx", "head"), falling
        )

    def swap(array):
        return lax.ppermute(array, "ctx", [(i, i ^ 1) for i in range(blocks)])

    def ring(array, distance):
        return lax.ppermute(array, "ctx", [(i, (i + distance) % blocks) for i in range(blocks)])

    def struct(*shape, dtype=jnp.bfloat16):
        return jax.ShapeDtypeStruct(shape, dtype)

    wide = struct(tokens, width, dtype=jnp.float32)
    wide_t = struct(width, tokens, dtype=jnp.float32)
    flat, flat_t = struct(tokens, width), struct(width, tokens)
    message = struct(width + TAIL, tokens)
    rows = struct(8, tokens, dtype=jnp.float32)

    payload = call(
        payload_kernel,
        heads,
        (),
        [pltpu.with_memory_space_constraint(a, pltpu.HBM) for a in (queries, keys, values, upstream)],
        [pltpu.VMEM((2 * tokens, width), jnp.bfloat16)] * 2,
        0,
        space=pltpu.HBM,
        scratch=(pltpu.SemaphoreType.DMA((4,)),),
    )
    received = cycle(*payload)
    keys_x, values_x = swap(keys), swap(values)
    diagonal, diagonal_lse, upstream_t, bias = call(
        diagonal_kernel,
        heads,
        (pattern,),
        (queries, keys, values, upstream),
        (wide_t, rows, flat_t, rows),
        3 * unit,
        after=(payload[0],),
    )
    up_out, down_out, *kept = call(
        forward_kernel,
        heads,
        (),
        (bias, *received, queries, keys_x, values_x, diagonal, diagonal_lse),
        (message, message, wide_t, wide_t, wide_t, rows, rows, rows),
        6 * unit,
    )
    ez, ex, en, mz, mx, mn = kept
    up_in, down_in = cycle(up_out, down_out)
    (side_queries,) = call(
        side_queries_kernel, heads, (), (queries, *received), (flat,), 0, after=(mn,)
    )
    side_queries = swap(side_queries)
    (upstream_zt,) = call(transpose_kernel, heads, (), received, (flat_t,), 0, after=(mn,))
    attention, attention_z, lse, lse_z, sums = call(
        merge_kernel,
        heads,
        (),
        (bias, up_out, down_out, up_in, down_in, upstream_t, upstream_zt),
        (flat_t, flat_t, rows, rows, rows),
        unit // 64,
    )
    others = [
        lax.ppermute(sums, "head", [(i, i ^ step) for i in range(members)]) for step in range(1, members)
    ]
    (far_queries,) = call(relay_kernel, heads, (), received, (struct(tokens + 16, width),), 0, after=(lse,))
    far_queries = ring(far_queries, -2)
    sums = functools.reduce(jnp.add, others, sums)
    longer = struct(width + 2 * TAIL, tokens)
    up_out, down_out, side_out, side_ds, grad_t, grad_zt, delta, delta_z = call(
        back_kernel,
        heads,
        (),
        (bias, sums, attention, attention_z, lse, lse_z, upstream_t, upstream_zt, *received, keys_x, values_x)
        + (ez, ex, mz, mx),
        (longer, longer, longer, flat_t, flat_t, flat_t, rows, rows),
        0,
        after=(side_queries,),
    )
    returned = cycle(up_out, down_out)
    side_grads = swap(side_out)
    normed, dq_own, dk_own, dv_own = call(
        local_back_kernel,
        heads,
        (),
        (bias, sums, queries, keys, values, attention, lse, lse_z, grad_t, grad_zt, delta, delta_z, en, mn)
        + (side_ds, keys_x, *received),
        (flat, wide, wide, wide),
        0,
    )
    (key_scores,) = call(
        key_scores_kernel,
        heads,
        (),
        (bias, keys, far_queries, side_queries),
        (struct(2, width, tokens, dtype=jnp.float32),),
        0,
    )
    grad_queries, grad_keys, grad_values = call(
        final_kernel,
        heads,
        (),
        (key_scores, far_queries, side_queries, *returned, side_grads, values, dq_own, dk_own, dv_own),
        (flat, flat, flat),
        6 * unit,
    )
    return (normed, grad_queries, grad_keys, grad_values)


def shards(queries, keys, values, pattern, upstream):
    fits = lax.axis_size("ctx") == 8 and lax.axis_size("head") == 4 and queries.shape == (BLOCK, 8 * HD)
    if fits:
        return meeting_shards(queries, keys, values, pattern, upstream)
    return generic_shards(queries, keys, values, pattern, upstream)


def solution(mesh):
    return jax.shard_map(
        shards,
        mesh=mesh,
        in_specs=(P("ctx", "head"), P("ctx", "head"), P("ctx", "head"), P(), P("ctx", "head")),
        out_specs=(P("ctx", "head"), P("ctx", "head"), P("ctx", "head"), P("ctx", "head")),
        check_vma=False,
    )
```

```python
import functools
import math

import jax
import jax.numpy as jnp
from jax import lax
from jax.experimental import pallas as pl
from jax.experimental.pallas import tpu as pltpu
from jax.sharding import PartitionSpec as P

HD = 128
BLOCK = 128
LEVELS = 7
WIDTH = 4096


NEG_BIG = -1e30
EPSILON = 1e-06


def shifted(block, axis, distance):
    devices = range(lax.axis_size(axis))
    route = [(i - distance, i) for i in devices if i - distance in devices]
    return lax.ppermute(block, axis, route)


def for_sending(x):
    return jax.tree.map(lambda a: a.astype(jnp.bfloat16) if a.dtype == jnp.float32 else a, x)


def route_table(blocks, levels):
    routing = []
    for query_block in range(blocks):
        for level_index in range(levels + 1):
            if level_index == levels:
                routing.append((0, query_block))
            else:
                distance = 2**level_index
                routing.append(
                    (-((query_block - distance) // blocks), (query_block - distance) % blocks)
                )
    return routing


def pair_grads(
    query_tiles, grad_tiles, lse_tiles, delta_tiles, key_tiles, value_tiles, keep_mask, score_scale
):
    scores = (
        jnp.einsum("pqhd,pkhd->phqk", query_tiles, key_tiles, preferred_element_type=jnp.float32)
        * score_scale
    )
    scores = jnp.where(keep_mask[:, None], scores, NEG_BIG)
    weights = jnp.exp(scores - lse_tiles[..., None])
    prob_tiles = weights.astype(jnp.bfloat16)
    grad_probs = jnp.einsum(
        "pqhd,pkhd->phqk", grad_tiles, value_tiles, preferred_element_type=jnp.float32
    )
    dscore = (weights * (grad_probs - delta_tiles[..., None]) * score_scale).astype(jnp.bfloat16)
    return (dscore, prob_tiles)


def key_grads(dscore, prob_tiles, query_tiles, grad_tiles):
    key_part = jnp.einsum(
        "phqk,pqhd->pkhd", dscore, query_tiles, preferred_element_type=jnp.float32
    )
    value_part = jnp.einsum(
        "phqk,pqhd->pkhd", prob_tiles, grad_tiles, preferred_element_type=jnp.float32
    )
    return jnp.stack((key_part, value_part))


def collect(partials, targets, blocks):
    pieces = []
    for key_index in range(blocks):
        summed = jnp.zeros((2,) + partials.shape[2:], jnp.float32)
        for row_index, target in enumerate(targets):
            if target == key_index:
                summed = summed + partials[:, row_index]
        pieces.append(summed)
    return jnp.stack(pieces, axis=1)


def generic_shards(queries, keys, values, pattern, upstream):
    tokens_here = queries.shape[0]
    heads_here = queries.shape[1] // HD
    blocks = tokens_here // BLOCK
    slot_count = LEVELS + 1
    pair_count = blocks * slot_count
    score_scale = HD ** (-0.5)
    ctx_count = lax.axis_size("ctx")
    device_index = lax.axis_index("ctx")
    routing = route_table(blocks, LEVELS)
    offsets = sorted(
        set((route_entry[0] for route_entry in routing if 0 < route_entry[0] < ctx_count))
    )
    tile_shape = (blocks, BLOCK, heads_here, HD)
    query_blocks = queries.reshape(tile_shape)
    own_pairs = jnp.stack((keys, values)).reshape((2,) + tile_shape)
    sources = {0: own_pairs}
    for offset in offsets:
        fetched = shifted(jnp.stack((keys, values)), "ctx", offset)
        sources[offset] = fetched.reshape((2,) + tile_shape)
    empty_tile = jnp.zeros((2, BLOCK, heads_here, HD), jnp.bfloat16)
    gathered = []
    for source, key_index in routing:
        if source in sources:
            gathered.append(sources[source][:, key_index])
        else:
            gathered.append(empty_tile)
    pair_kv = jnp.stack(gathered, axis=1)
    key_tiles = pair_kv[0]
    value_tiles = pair_kv[1]
    key_stack = key_tiles.reshape((blocks, slot_count) + tile_shape[1:])
    value_stack = value_tiles.reshape((blocks, slot_count) + tile_shape[1:])
    own_rows = lax.dynamic_slice_in_dim(pattern, device_index * blocks, blocks, 0)
    positions = jnp.arange(BLOCK)
    causal = positions[None, :] <= positions[:, None]
    self_slot = jnp.arange(slot_count) == LEVELS
    tile_keep = (own_rows >= 0)[:, :, None, None] & (
        jnp.logical_not(self_slot)[None, :, None, None] | causal[None, None]
    )
    scores = (
        jnp.einsum("bqhd,bskhd->bhqsk", query_blocks, key_stack, preferred_element_type=jnp.float32)
        * score_scale
    )
    scores = jnp.where(jnp.transpose(tile_keep, (0, 2, 1, 3))[:, None], scores, NEG_BIG)
    highest = jnp.max(scores, axis=(3, 4))
    log_total = highest + jnp.log(jnp.sum(jnp.exp(scores - highest[..., None, None]), axis=(3, 4)))
    prob_stack = jnp.exp(scores - log_total[..., None, None]).astype(jnp.bfloat16)
    attention = jnp.einsum(
        "bhqsk,bskhd->bqhd", prob_stack, value_stack, preferred_element_type=jnp.float32
    ).astype(jnp.bfloat16)
    attn_wide = attention.reshape(tokens_here, heads_here * HD).astype(jnp.float32)
    square_sum = lax.psum(jnp.sum(attn_wide * attn_wide, axis=1), "head")
    inverse = lax.rsqrt(square_sum / WIDTH + EPSILON)
    normed = (attn_wide * inverse[:, None]).astype(jnp.bfloat16)
    upstream_wide = upstream.astype(jnp.float32)
    cross_term = lax.psum(jnp.sum(upstream_wide * attn_wide, axis=1), "head")
    grad_attn = (
        inverse[:, None] * upstream_wide - attn_wide * (inverse**3 * cross_term / WIDTH)[:, None]
    ).astype(jnp.bfloat16)
    row_delta = jnp.sum(
        (grad_attn.astype(jnp.float32) * attn_wide).reshape(tokens_here, heads_here, HD), axis=2
    )
    row_delta = jnp.transpose(row_delta.reshape(blocks, BLOCK, heads_here), (0, 2, 1))

    def spread(array):
        return jnp.broadcast_to(array[:, None], (blocks, slot_count) + array.shape[1:]).reshape(
            (pair_count,) + array.shape[1:]
        )

    grad_blocks = grad_attn.reshape(tile_shape)
    query_pairs = spread(query_blocks)
    grad_pairs = spread(grad_blocks)
    keep_pairs = tile_keep.reshape(pair_count, BLOCK, BLOCK)
    dscore, prob_pairs = pair_grads(
        query_pairs,
        grad_pairs,
        spread(log_total),
        spread(row_delta),
        key_tiles,
        value_tiles,
        keep_pairs,
        score_scale,
    )
    grad_query = jnp.einsum(
        "phqk,pkhd->pqhd", dscore, key_tiles, preferred_element_type=jnp.float32
    )
    grad_query = jnp.sum(grad_query.reshape((blocks, slot_count) + tile_shape[1:]), axis=1)
    grad_queries = grad_query.astype(jnp.bfloat16).reshape(tokens_here, heads_here * HD)
    local_rows = [row_index for row_index in range(pair_count) if routing[row_index][0] == 0]
    chosen = jnp.array(local_rows, jnp.int32)
    local_terms = key_grads(
        dscore[chosen], prob_pairs[chosen], query_pairs[chosen], grad_pairs[chosen]
    )
    key_sum = collect(local_terms, [routing[row_index][1] for row_index in local_rows], blocks)
    for offset in offsets:
        remote_rows = [
            row_index for row_index in range(pair_count) if routing[row_index][0] == offset
        ]
        chosen = jnp.array(remote_rows, jnp.int32)
        remote_terms = key_grads(
            dscore[chosen], prob_pairs[chosen], query_pairs[chosen], grad_pairs[chosen]
        )
        outgoing = collect(
            remote_terms, [routing[row_index][1] for row_index in remote_rows], blocks
        )
        key_sum = key_sum + shifted(for_sending(outgoing), "ctx", -offset).astype(outgoing.dtype)
    grad_keys = key_sum[0].astype(jnp.bfloat16).reshape(tokens_here, heads_here * HD)
    grad_values = key_sum[1].astype(jnp.bfloat16).reshape(tokens_here, heads_here * HD)
    return (normed, grad_queries, grad_keys, grad_values)


NT = (((1,), (1,)), ((), ()))
NN = (((1,), (0,)), ((), ()))
TN = (((0,), (0,)), ((), ()))
SCALE = HD ** (-0.5)
TAIL = 32


NEAR, FAR, SIDE, HELPED, LOCAL, KEY_NEAR, KEY_FAR, KEY_SIDE = range(8)


class Place:
    def __init__(self):
        self.me = lax.axis_index("ctx")
        self.odd = lax.rem(self.me, 2) == 1
        self.half = lax.axis_index("head") >= lax.axis_size("head") // 2


def bias_rows(pattern_ref):
    place = Place()
    me, odd, even = place.me, place.odd, jnp.logical_not(place.odd)
    blocks = pattern_ref.shape[0]
    ahead = jnp.minimum(me + 2, blocks - 1)
    has_ahead = me + 2 < blocks
    ahead_side = jnp.logical_and(has_ahead, pattern_ref[ahead, 0] >= 0)
    own_side = pattern_ref[me, 0] >= 0
    local = jnp.logical_and(odd, own_side)

    def ahead_holds(distance, level):
        entry = pattern_ref[jnp.minimum(me + distance, blocks - 1), level]
        return jnp.logical_and(me + distance < blocks, entry >= 0)

    held = {
        NEAR: pattern_ref[me, 1] >= 0,
        FAR: jnp.logical_and(has_ahead, pattern_ref[ahead, 2] >= 0),
        SIDE: jnp.logical_or(local, jnp.logical_and(even, ahead_side)),
        HELPED: jnp.logical_or(pattern_ref[me, 2] >= 0, jnp.logical_and(even, own_side)),
        LOCAL: local,
        KEY_NEAR: ahead_holds(2, 1),
        KEY_FAR: ahead_holds(4, 2),
        KEY_SIDE: ahead_holds(1, 0),
    }
    row = lax.broadcasted_iota(jnp.int32, (8, BLOCK), 0)
    rows = jnp.zeros((8, BLOCK), jnp.float32)
    for index, flag in held.items():
        rows = jnp.where(row == index, jnp.where(flag, 0.0, NEG_BIG), rows)
    return rows


def mm(a, b, dims):
    return lax.dot_general(a, b, dims, preferred_element_type=jnp.float32)


def rows_of(h):
    return slice(h * HD, (h + 1) * HD)


def causal_mask():
    keys = lax.broadcasted_iota(jnp.int32, (BLOCK, BLOCK), 0)
    return keys <= lax.broadcasted_iota(jnp.int32, (BLOCK, BLOCK), 1)


def split_rows(rows):
    first = rows.astype(jnp.bfloat16).astype(jnp.float32)
    second = (rows - first).astype(jnp.bfloat16).astype(jnp.float32)
    third = rows - first - second
    return jnp.concatenate([first, second, third, jnp.zeros_like(rows)], axis=0).astype(jnp.bfloat16)


def joined_rows(tile):
    wide = tile.astype(jnp.float32)
    return wide[0:8] + wide[8:16] + wide[16:24]


def stack_rows(rows):
    return jnp.concatenate(rows + [jnp.zeros((1, BLOCK), jnp.float32)] * (8 - len(rows)), axis=0)


def score_tile(keys, queries):
    return mm(keys, queries, NT) * SCALE


def softmax_parts(pairs):
    tops = [scores.max(axis=0, keepdims=True) for scores, _ in pairs]
    weights = [jnp.exp(scores - top) for (scores, _), top in zip(pairs, tops)]
    totals = [w.sum(axis=0, keepdims=True) for w in weights]
    outs = [
        mm(value, w.astype(jnp.bfloat16), TN) * (1.0 / total)
        for (_, value), w, total in zip(pairs, weights, totals)
    ]
    return [(out, top, top + jnp.log(total), w) for out, top, total, w in zip(outs, tops, totals, weights)]


FIRST, SECOND = slice(0, BLOCK), slice(BLOCK, 2 * BLOCK)


def payload_kernel(heads, q_ref, k_ref, v_ref, u_ref, up_ref, down_ref, sems):
    half = Place().half
    top, bottom = pl.ds(0, BLOCK), pl.ds(BLOCK, BLOCK)

    def move(sources):
        targets = (up_ref.at[top], up_ref.at[bottom], down_ref.at[top], down_ref.at[bottom])
        copies = [
            pltpu.make_async_copy(source, target, sems.at[n])
            for n, (source, target) in enumerate(zip(sources, targets))
        ]
        for copy in copies:
            copy.start()
        for copy in copies:
            copy.wait()

    @pl.when(jnp.logical_not(half))
    def _():
        move((k_ref, v_ref, q_ref, u_ref))

    @pl.when(half)
    def _():
        move((q_ref, u_ref, k_ref, v_ref))


def diagonal_kernel(heads, pattern_ref, q_ref, k_ref, v_ref, u_ref, out_ref, lse_ref, ut_ref, bias_ref):
    bias_ref[...] = bias_rows(pattern_ref)
    causal = causal_mask()
    rows = []
    for h in range(heads):
        at = rows_of(h)
        scores = jnp.where(causal, score_tile(k_ref[:, at], q_ref[:, at]), NEG_BIG)
        ((out, _, lse, _),) = softmax_parts([(scores, v_ref[:, at])])
        out_ref[at] = out
        rows.append(lse)
        ut_ref[at] = u_ref[:, at].T
    lse_ref[...] = stack_rows(rows)


def merged(parts):
    highest = functools.reduce(jnp.maximum, [lse for _, lse in parts])
    total = highest + jnp.log(functools.reduce(jnp.add, [jnp.exp(lse - highest) for _, lse in parts]))
    return functools.reduce(jnp.add, [out * jnp.exp(lse - total) for out, lse in parts]), total


def forward_kernel(
    heads,
    bias_ref,
    up_ref,
    down_ref,
    q_ref,
    kx_ref,
    vx_ref,
    out_ref,
    lse_ref,
    up_out_ref,
    down_out_ref,
    ez_ref,
    ex_ref,
    en_ref,
    mz_ref,
    mx_ref,
    mn_ref,
):
    place = Place()
    odd, half = place.odd, place.half
    near, far, side, local = (bias_ref[n : n + 1] for n in (NEAR, FAR, SIDE, LOCAL))
    before = lse_ref[...]
    step = heads
    z_rows, own_rows, z_tops, x_tops, n_tops = [], [], [], [], []
    for start in range(0, heads, step):
        group = range(start, start + step)
        scores, weights = [], []
        for h in group:
            at = rows_of(h)
            up_a, down_a = up_ref[FIRST, at], down_ref[FIRST, at]
            k2, qz = jnp.where(half, down_a, up_a), jnp.where(half, up_a, down_a)
            q = q_ref[:, at]
            both = score_tile(k2, jnp.concatenate([qz, q], axis=0))
            x = score_tile(kx_ref[:, at], jnp.where(odd, q, qz))
            scores.append((both[:, :BLOCK] + far, x + side, both[:, BLOCK:] + near))
        for h, (z, x, n) in zip(group, scores):
            z_top, x_top, n_top = (tile.max(axis=0, keepdims=True) for tile in (z, x, n))
            both = jnp.maximum(z_top, x_top)
            z_top, x_top = jnp.where(odd, z_top, both), jnp.where(odd, x_top, both)
            z, x, n = jnp.exp(z - z_top), jnp.exp(x - x_top), jnp.exp(n - n_top)
            at = rows_of(h)
            ez_ref[at], ex_ref[at], en_ref[at] = z, x, n
            z_sum, x_sum, n_sum = (tile.sum(axis=0, keepdims=True) for tile in (z, x, n))
            z_sum = z_sum + jnp.where(odd, 0.0, x_sum)
            x_sum = jnp.maximum(x_sum, 1.0)
            for tops, top in ((z_tops, z_top), (x_tops, x_top), (n_tops, n_top)):
                tops.append(top)
            z_rows.append(z_top + jnp.log(z_sum))
            parts = (before[h : h + 1], n_top + jnp.log(n_sum) + near, x_top + jnp.log(x_sum) + local)
            highest = functools.reduce(jnp.maximum, parts)
            total = highest + jnp.log(functools.reduce(jnp.add, [jnp.exp(part - highest) for part in parts]))
            own_rows.append(total)
            d_share, n_share, x_share = (jnp.exp(part - total) for part in parts)
            z_scale = 1.0 / z_sum
            sent = [z * z_scale, x * jnp.where(odd, 0.0, z_scale)]
            kept = [n * (n_share / n_sum), x * (x_share / x_sum)]
            joined = [jnp.concatenate(tiles, axis=0).astype(jnp.bfloat16) for tiles in (sent, kept)]
            weights.append((jnp.concatenate(joined, axis=1), d_share))
        for h, (joined, d_share) in zip(group, weights):
            at = rows_of(h)
            v2 = jnp.where(half, down_ref[SECOND, at], up_ref[SECOND, at])
            out = mm(jnp.concatenate([v2, vx_ref[:, at]], axis=0), joined, TN)
            out_z = out[:, :BLOCK].astype(jnp.bfloat16)
            own = (out_ref[at] * d_share + out[:, BLOCK:]).astype(jnp.bfloat16)
            up_out_ref[at] = jnp.where(half, own, out_z)
            down_out_ref[at] = jnp.where(half, out_z, own)
    tail = slice(heads * HD, heads * HD + TAIL)
    z_tail, own_tail = split_rows(stack_rows(z_rows)), split_rows(stack_rows(own_rows))
    up_out_ref[tail] = jnp.where(half, own_tail, z_tail)
    down_out_ref[tail] = jnp.where(half, z_tail, own_tail)
    mz_ref[...] = stack_rows(z_tops)
    mx_ref[...] = stack_rows(x_tops)
    mn_ref[...] = stack_rows(n_tops)


def transpose_kernel(heads, up_ref, down_ref, out_ref):
    half = Place().half
    for h in range(heads):
        at = rows_of(h)
        out_ref[at] = jnp.where(half, up_ref[SECOND, at], down_ref[SECOND, at]).T


def merge_kernel(
    heads,
    bias_ref,
    up_ref,
    down_ref,
    up_in_ref,
    down_in_ref,
    ut_ref,
    uzt_ref,
    a_ref,
    az_ref,
    lse_ref,
    lsez_ref,
    sums_ref,
):
    half = Place().half
    tail = slice(heads * HD, heads * HD + TAIL)

    def select(rising, falling, at):
        first, second = rising[at], falling[at]
        return jnp.where(half, second, first), jnp.where(half, first, second)

    z_part, own_part = select(up_ref, down_ref, tail)
    help_part, ahead_part = select(up_in_ref, down_in_ref, tail)
    rows, shares = [], []
    for first, second in (
        (joined_rows(own_part), joined_rows(help_part) + bias_ref[HELPED : HELPED + 1]),
        (joined_rows(ahead_part), joined_rows(z_part)),
    ):
        highest = jnp.maximum(first, second)
        total = highest + jnp.log(jnp.exp(first - highest) + jnp.exp(second - highest))
        rows.append(total)
        shares.append((jnp.exp(first - total), jnp.exp(second - total)))
    lse_ref[...], lsez_ref[...] = (jnp.maximum(total, -1e9) for total in rows)
    sums = [jnp.zeros((8, BLOCK), jnp.float32)] * 4
    for h in range(heads):
        at, row = rows_of(h), slice(h, h + 1)
        z_out, own_out = select(up_ref, down_ref, at)
        help_out, ahead_out = select(up_in_ref, down_in_ref, at)
        for n, (first, second, u_ref, target) in enumerate(
            ((own_out, help_out, ut_ref, a_ref), (ahead_out, z_out, uzt_ref, az_ref))
        ):
            out = (
                first.astype(jnp.float32) * shares[n][0][row] + second.astype(jnp.float32) * shares[n][1][row]
            ).astype(jnp.bfloat16)
            target[at] = out
            wide = out.astype(jnp.float32)
            sums[2 * n] += (wide * wide).reshape(HD // 8, 8, BLOCK).sum(axis=0)
            sums[2 * n + 1] += (wide * u_ref[at].astype(jnp.float32)).reshape(HD // 8, 8, BLOCK).sum(axis=0)
    sums_ref[...] = stack_rows([part.sum(axis=0, keepdims=True) for part in sums])


def norm_rows(sums, first):
    inverse = lax.rsqrt(sums[first : first + 1] / WIDTH + EPSILON)
    return inverse, inverse**3 * sums[first + 1 : first + 2] / WIDTH


def upstream_part(norm, u, a):
    inverse, factor = norm
    wide = a.astype(jnp.float32)
    grad = (inverse * u.astype(jnp.float32) - wide * factor).astype(jnp.bfloat16)
    return grad, jnp.sum(grad.astype(jnp.float32) * wide, axis=0, keepdims=True)


def side_queries_kernel(heads, q_ref, up_ref, down_ref, out_ref):
    place = Place()
    for h in range(heads):
        at = rows_of(h)
        qz = jnp.where(place.half, up_ref[FIRST, at], down_ref[FIRST, at])
        out_ref[:, at] = jnp.where(place.odd, q_ref[:, at], qz)


def relay_kernel(heads, up_ref, down_ref, out_ref):
    half = Place().half
    for h in range(heads):
        at = rows_of(h)
        out_ref[:, at] = jnp.where(half, up_ref[FIRST, at], down_ref[FIRST, at])


def back_kernel(
    heads,
    bias_ref,
    sums_ref,
    a_ref,
    az_ref,
    lse_ref,
    lsez_ref,
    ut_ref,
    uzt_ref,
    up_ref,
    down_ref,
    kx_ref,
    vx_ref,
    ez_ref,
    ex_ref,
    mz_ref,
    mx_ref,
    up_out_ref,
    down_out_ref,
    side_out_ref,
    dsx_ref,
    grad_ref,
    gz_ref,
    delta_ref,
    deltaz_ref,
):
    place = Place()
    odd, half = place.odd, place.half
    sums = sums_ref[...]
    own_norm, z_norm = norm_rows(sums, 0), norm_rows(sums, 2)
    lse, z_lse = lse_ref[...], lsez_ref[...]
    scales = (
        jnp.exp(mz_ref[...] - z_lse + bias_ref[FAR : FAR + 1]),
        jnp.exp(mx_ref[...] - jnp.where(odd, lse, z_lse) + bias_ref[SIDE : SIDE + 1]),
    )
    group = range(heads)
    deltas, z_deltas = [], []
    parts, products, scores = [], [], []
    for h in group:
        at = rows_of(h)
        grad, delta = upstream_part(own_norm, ut_ref[at], a_ref[at])
        gz, deltaz = upstream_part(z_norm, uzt_ref[at], az_ref[at])
        grad_ref[at], gz_ref[at] = grad, gz
        deltas.append(delta)
        z_deltas.append(deltaz)
        gx, deltax = jnp.where(odd, grad, gz), jnp.where(odd, delta, deltaz)
        side_out_ref[at] = gx
        parts.append(((gz, gx), (deltaz, deltax)))
    for h, ((gz, gx), _) in zip(group, parts):
        at = rows_of(h)
        v2 = jnp.where(half, down_ref[SECOND, at], up_ref[SECOND, at])
        products.append((mm(v2, gz, NN), mm(vx_ref[:, at], gx, NN)))
    for h, (_, delta), product in zip(group, parts, products):
        tiles = []
        for n, e_ref in enumerate((ez_ref, ex_ref)):
            weights = e_ref[rows_of(h)] * scales[n][h : h + 1]
            tiles.append((weights * (product[n] - delta[n]) * SCALE).astype(jnp.bfloat16))
        dsx_ref[rows_of(h)] = tiles[1]
        scores.append(tiles)
    for h, ((gz, _), _), (dz, dx) in zip(group, parts, scores):
        at = rows_of(h)
        k2 = jnp.where(half, down_ref[FIRST, at], up_ref[FIRST, at])
        joined = jnp.concatenate([dz, jnp.where(odd, jnp.zeros_like(dx), dx)], axis=0)
        dqz = mm(jnp.concatenate([k2, kx_ref[:, at]], axis=0), joined, TN).astype(jnp.bfloat16)
        up_out_ref[at] = jnp.where(half, gz, dqz)
        down_out_ref[at] = jnp.where(half, dqz, gz)
    delta, deltaz = stack_rows(deltas), stack_rows(z_deltas)
    delta_ref[...], deltaz_ref[...] = delta, deltaz
    tail = slice(heads * HD, heads * HD + 2 * TAIL)
    z_tail = jnp.concatenate([split_rows(z_lse), split_rows(deltaz)], axis=0)
    own_tail = jnp.concatenate([split_rows(lse), split_rows(delta)], axis=0)
    up_out_ref[tail] = jnp.where(half, z_tail, jnp.zeros_like(z_tail))
    down_out_ref[tail] = jnp.where(half, jnp.zeros_like(z_tail), z_tail)
    side_out_ref[tail] = jnp.where(odd, own_tail, z_tail)


def local_back_kernel(
    heads,
    bias_ref,
    sums_ref,
    q_ref,
    k_ref,
    v_ref,
    a_ref,
    lse_ref,
    lsez_ref,
    grad_ref,
    gz_ref,
    delta_ref,
    deltaz_ref,
    en_ref,
    mn_ref,
    dsx_ref,
    kx_ref,
    up_ref,
    down_ref,
    normed_ref,
    dq_ref,
    dk_ref,
    dv_ref,
):
    place = Place()
    odd, half = place.odd, place.half
    inverse, _ = norm_rows(sums_ref[...], 0)
    lse, z_lse = lse_ref[...], lsez_ref[...] - bias_ref[KEY_NEAR : KEY_NEAR + 1]
    near_scale = jnp.exp(mn_ref[...] - lse + bias_ref[NEAR : NEAR + 1])
    causal = causal_mask()
    for h in range(heads):
        at, row = rows_of(h), slice(h, h + 1)
        normed_ref[:, at] = (a_ref[at].astype(jnp.float32) * inverse).astype(jnp.bfloat16).T
        up_a, down_a = up_ref[FIRST, at], down_ref[FIRST, at]
        k2, qz = jnp.where(half, down_a, up_a), jnp.where(half, up_a, down_a)
        v2 = jnp.where(half, down_ref[SECOND, at], up_ref[SECOND, at])
        q, k, v, grad, gz = q_ref[:, at], k_ref[:, at], v_ref[:, at], grad_ref[at], gz_ref[at]
        queries, grads = jnp.concatenate([q, qz], axis=0), jnp.concatenate([grad, gz], axis=1)
        both = score_tile(k, queries)
        products = mm(v, grads, NN)
        own = jnp.exp(jnp.where(causal, both[:, :BLOCK], NEG_BIG) - lse[row])
        ahead = jnp.exp(both[:, BLOCK:] - z_lse[row])
        near = en_ref[at] * near_scale[row]
        own_ds = (own * (products[:, :BLOCK] - delta_ref[row]) * SCALE).astype(jnp.bfloat16)
        ahead_ds = (ahead * (products[:, BLOCK:] - deltaz_ref[row]) * SCALE).astype(jnp.bfloat16)
        near_ds = (near * (mm(v2, grad, NN) - delta_ref[row]) * SCALE).astype(jnp.bfloat16)
        dk_ref[:, at] = mm(jnp.concatenate([own_ds, ahead_ds], axis=1), queries, NN)
        probs = jnp.concatenate([own, ahead], axis=1).astype(jnp.bfloat16)
        dv_ref[:, at] = mm(probs, grads, NT)
        dsx = jnp.where(odd, dsx_ref[at], jnp.zeros_like(dsx_ref[at]))
        dq_ref[:, at] = mm(own_ds, k, TN) + mm(
            jnp.concatenate([near_ds, dsx], axis=0), jnp.concatenate([k2, kx_ref[:, at]], axis=0), TN
        )


def key_scores_kernel(heads, bias_ref, k_ref, far_ref, side_ref, out_ref):
    for h in range(heads):
        at = rows_of(h)
        both = score_tile(k_ref[:, at], jnp.concatenate([far_ref[:, at], side_ref[:, at]], axis=0))
        out_ref[0, at] = both[:, :BLOCK] + bias_ref[KEY_FAR : KEY_FAR + 1]
        out_ref[1, at] = both[:, BLOCK:] + bias_ref[KEY_SIDE : KEY_SIDE + 1]


def final_kernel(
    heads,
    scores_ref,
    far_ref,
    sideq_ref,
    up_ref,
    down_ref,
    side_ref,
    v_ref,
    dq_own_ref,
    dk_own_ref,
    dv_own_ref,
    dq_ref,
    dk_ref,
    dv_ref,
):
    place = Place()
    half = place.half
    behind = (place.me >= 2).astype(jnp.float32)
    first = slice(heads * HD, heads * HD + TAIL)
    second = slice(heads * HD + TAIL, heads * HD + 2 * TAIL)
    lse, delta = (
        (joined_rows(jnp.where(half, up_ref[part], down_ref[part])), joined_rows(side_ref[part]))
        for part in (first, second)
    )
    group = range(heads)
    grads, products, tiles = [], [], []
    for h in group:
        at = rows_of(h)
        up, down = up_ref[at], down_ref[at]
        dqz = jnp.where(half, down, up).T.astype(jnp.float32) * behind
        dq_ref[:, at] = (dq_own_ref[:, at] + dqz).astype(jnp.bfloat16)
        grads.append(jnp.concatenate([jnp.where(half, up, down), side_ref[at]], axis=1))
    for h, grad in zip(group, grads):
        products.append(mm(v_ref[:, rows_of(h)], grad, NN))
    for h, product in zip(group, products):
        row = slice(h, h + 1)
        probs = [jnp.exp(scores_ref[n, rows_of(h)] - lse[n][row]) for n in range(2)]
        scores = [
            probs[n] * (product[:, n * BLOCK : (n + 1) * BLOCK] - delta[n][row]) * SCALE for n in range(2)
        ]
        tiles.append([jnp.concatenate(pair, axis=1).astype(jnp.bfloat16) for pair in (probs, scores)])
    for h, grad, (probs, scores) in zip(group, grads, tiles):
        at = rows_of(h)
        queries = jnp.concatenate([far_ref[:, at], sideq_ref[:, at]], axis=0)
        dk_ref[:, at] = (dk_own_ref[:, at] + mm(scores, queries, NN)).astype(jnp.bfloat16)
        dv_ref[:, at] = (dv_own_ref[:, at] + mm(probs, grad, NT)).astype(jnp.bfloat16)


def call(kernel, heads, flags, arrays, outs, flops, space=pltpu.VMEM, scratch=(), after=()):
    moved = sum(math.prod(a.shape) * a.dtype.itemsize for a in (*arrays, *outs)) if flops else 0
    return pl.pallas_call(
        lambda *refs: kernel(heads, *refs[len(after) :]),
        out_shape=outs,
        in_specs=[pl.BlockSpec(memory_space=pl.ANY)] * len(after)
        + [pl.BlockSpec(memory_space=pltpu.SMEM)] * len(flags)
        + [pl.BlockSpec(memory_space=space)] * len(arrays),
        out_specs=[pl.BlockSpec(memory_space=pltpu.VMEM)] * len(outs),
        scratch_shapes=scratch,
        compiler_params=pltpu.CompilerParams(vmem_limit_bytes=24 * 2**20),
        cost_estimate=pl.CostEstimate(flops=flops, bytes_accessed=moved, transcendentals=0),
    )(*after, *flags, *arrays)


def cycles(blocks, members):
    route = []
    for block in range(blocks):
        for member in range(members):
            rising = member < members // 2
            other = member + members // 2 if rising else member - members // 2
            target = block + 2 if rising else block - 2
            inside = 0 <= target < blocks
            route.append(
                (block * members + member, target * members + member if inside else block * members + other)
            )
    return route


def meeting_shards(queries, keys, values, pattern, upstream):
    tokens, width = queries.shape
    heads = width // HD
    blocks, members = lax.axis_size("ctx"), lax.axis_size("head")
    unit = heads * 2 * BLOCK**3
    rising = cycles(blocks, members)
    falling = [(target, source) for source, target in rising]

    def cycle(up_array, down_array):
        return lax.ppermute(up_array, ("ctx", "head"), rising), lax.ppermute(
            down_array, ("ctx", "head"), falling
        )

    def swap(array):
        return lax.ppermute(array, "ctx", [(i, i ^ 1) for i in range(blocks)])

    def ring(array, distance):
        return lax.ppermute(array, "ctx", [(i, (i + distance) % blocks) for i in range(blocks)])

    def struct(*shape, dtype=jnp.bfloat16):
        return jax.ShapeDtypeStruct(shape, dtype)

    wide = struct(tokens, width, dtype=jnp.float32)
    wide_t = struct(width, tokens, dtype=jnp.float32)
    flat, flat_t = struct(tokens, width), struct(width, tokens)
    message = struct(width + TAIL, tokens)
    rows = struct(8, tokens, dtype=jnp.float32)

    payload = call(
        payload_kernel,
        heads,
        (),
        [pltpu.with_memory_space_constraint(a, pltpu.HBM) for a in (queries, keys, values, upstream)],
        [pltpu.VMEM((2 * tokens, width), jnp.bfloat16)] * 2,
        0,
        space=pltpu.HBM,
        scratch=(pltpu.SemaphoreType.DMA((4,)),),
    )
    received = cycle(*payload)
    keys_x, values_x = swap(keys), swap(values)
    diagonal, diagonal_lse, upstream_t, bias = call(
        diagonal_kernel,
        heads,
        (pattern,),
        (queries, keys, values, upstream),
        (wide_t, rows, flat_t, rows),
        3 * unit,
        after=(payload[0],),
    )
    up_out, down_out, *kept = call(
        forward_kernel,
        heads,
        (),
        (bias, *received, queries, keys_x, values_x, diagonal, diagonal_lse),
        (message, message, wide_t, wide_t, wide_t, rows, rows, rows),
        6 * unit,
    )
    ez, ex, en, mz, mx, mn = kept
    up_in, down_in = cycle(up_out, down_out)
    (side_queries,) = call(
        side_queries_kernel, heads, (), (queries, *received), (flat,), 0, after=(mn,)
    )
    side_queries = swap(side_queries)
    (far_queries,) = call(relay_kernel, heads, (), received, (flat,), 0, after=(mn,))
    far_queries = lax.ppermute(far_queries, "ctx", [(i, i - 2) for i in range(2, blocks - 2)])
    (upstream_zt,) = call(transpose_kernel, heads, (), received, (flat_t,), 0, after=(mn,))
    attention, attention_z, lse, lse_z, sums = call(
        merge_kernel,
        heads,
        (),
        (bias, up_out, down_out, up_in, down_in, upstream_t, upstream_zt),
        (flat_t, flat_t, rows, rows, rows),
        unit // 64,
    )
    others = [
        lax.ppermute(sums, "head", [(i, i ^ step) for i in range(members)]) for step in range(1, members)
    ]
    sums = functools.reduce(jnp.add, others, sums)
    longer = struct(width + 2 * TAIL, tokens)
    up_out, down_out, side_out, side_ds, grad_t, grad_zt, delta, delta_z = call(
        back_kernel,
        heads,
        (),
        (bias, sums, attention, attention_z, lse, lse_z, upstream_t, upstream_zt, *received, keys_x, values_x)
        + (ez, ex, mz, mx),
        (longer, longer, longer, flat_t, flat_t, flat_t, rows, rows),
        0,
        after=(side_queries, far_queries),
    )
    returned = cycle(up_out, down_out)
    side_grads = swap(side_out)
    normed, dq_own, dk_own, dv_own = call(
        local_back_kernel,
        heads,
        (),
        (bias, sums, queries, keys, values, attention, lse, lse_z, grad_t, grad_zt, delta, delta_z, en, mn)
        + (side_ds, keys_x, *received),
        (flat, wide, wide, wide),
        0,
    )
    (key_scores,) = call(
        key_scores_kernel,
        heads,
        (),
        (bias, keys, far_queries, side_queries),
        (struct(2, width, tokens, dtype=jnp.float32),),
        0,
    )
    grad_queries, grad_keys, grad_values = call(
        final_kernel,
        heads,
        (),
        (key_scores, far_queries, side_queries, *returned, side_grads, values, dq_own, dk_own, dv_own),
        (flat, flat, flat),
        6 * unit,
    )
    return (normed, grad_queries, grad_keys, grad_values)


def shards(queries, keys, values, pattern, upstream):
    fits = lax.axis_size("ctx") == 8 and lax.axis_size("head") == 4 and queries.shape == (BLOCK, 8 * HD)
    if fits:
        return meeting_shards(queries, keys, values, pattern, upstream)
    return generic_shards(queries, keys, values, pattern, upstream)


def solution(mesh):
    return jax.shard_map(
        shards,
        mesh=mesh,
        in_specs=(P("ctx", "head"), P("ctx", "head"), P("ctx", "head"), P(), P("ctx", "head")),
        out_specs=(P("ctx", "head"), P("ctx", "head"), P("ctx", "head"), P("ctx", "head")),
        check_vma=False,
    )
```

```python
import functools
import math

import jax
import jax.numpy as jnp
from jax import lax
from jax.experimental import pallas as pl
from jax.experimental.pallas import tpu as pltpu
from jax.sharding import PartitionSpec as P

HD = 128
BLOCK = 128
LEVELS = 7
WIDTH = 4096


NEG_BIG = -1e30
EPSILON = 1e-06


def shifted(block, axis, distance):
    devices = range(lax.axis_size(axis))
    route = [(i - distance, i) for i in devices if i - distance in devices]
    return lax.ppermute(block, axis, route)


def for_sending(x):
    return jax.tree.map(lambda a: a.astype(jnp.bfloat16) if a.dtype == jnp.float32 else a, x)


def route_table(blocks, levels):
    routing = []
    for query_block in range(blocks):
        for level_index in range(levels + 1):
            if level_index == levels:
                routing.append((0, query_block))
            else:
                distance = 2**level_index
                routing.append(
                    (-((query_block - distance) // blocks), (query_block - distance) % blocks)
                )
    return routing


def pair_grads(
    query_tiles, grad_tiles, lse_tiles, delta_tiles, key_tiles, value_tiles, keep_mask, score_scale
):
    scores = (
        jnp.einsum("pqhd,pkhd->phqk", query_tiles, key_tiles, preferred_element_type=jnp.float32)
        * score_scale
    )
    scores = jnp.where(keep_mask[:, None], scores, NEG_BIG)
    weights = jnp.exp(scores - lse_tiles[..., None])
    prob_tiles = weights.astype(jnp.bfloat16)
    grad_probs = jnp.einsum(
        "pqhd,pkhd->phqk", grad_tiles, value_tiles, preferred_element_type=jnp.float32
    )
    dscore = (weights * (grad_probs - delta_tiles[..., None]) * score_scale).astype(jnp.bfloat16)
    return (dscore, prob_tiles)


def key_grads(dscore, prob_tiles, query_tiles, grad_tiles):
    key_part = jnp.einsum(
        "phqk,pqhd->pkhd", dscore, query_tiles, preferred_element_type=jnp.float32
    )
    value_part = jnp.einsum(
        "phqk,pqhd->pkhd", prob_tiles, grad_tiles, preferred_element_type=jnp.float32
    )
    return jnp.stack((key_part, value_part))


def collect(partials, targets, blocks):
    pieces = []
    for key_index in range(blocks):
        summed = jnp.zeros((2,) + partials.shape[2:], jnp.float32)
        for row_index, target in enumerate(targets):
            if target == key_index:
                summed = summed + partials[:, row_index]
        pieces.append(summed)
    return jnp.stack(pieces, axis=1)


def generic_shards(queries, keys, values, pattern, upstream):
    tokens_here = queries.shape[0]
    heads_here = queries.shape[1] // HD
    blocks = tokens_here // BLOCK
    slot_count = LEVELS + 1
    pair_count = blocks * slot_count
    score_scale = HD ** (-0.5)
    ctx_count = lax.axis_size("ctx")
    device_index = lax.axis_index("ctx")
    routing = route_table(blocks, LEVELS)
    offsets = sorted(
        set((route_entry[0] for route_entry in routing if 0 < route_entry[0] < ctx_count))
    )
    tile_shape = (blocks, BLOCK, heads_here, HD)
    query_blocks = queries.reshape(tile_shape)
    own_pairs = jnp.stack((keys, values)).reshape((2,) + tile_shape)
    sources = {0: own_pairs}
    for offset in offsets:
        fetched = shifted(jnp.stack((keys, values)), "ctx", offset)
        sources[offset] = fetched.reshape((2,) + tile_shape)
    empty_tile = jnp.zeros((2, BLOCK, heads_here, HD), jnp.bfloat16)
    gathered = []
    for source, key_index in routing:
        if source in sources:
            gathered.append(sources[source][:, key_index])
        else:
            gathered.append(empty_tile)
    pair_kv = jnp.stack(gathered, axis=1)
    key_tiles = pair_kv[0]
    value_tiles = pair_kv[1]
    key_stack = key_tiles.reshape((blocks, slot_count) + tile_shape[1:])
    value_stack = value_tiles.reshape((blocks, slot_count) + tile_shape[1:])
    own_rows = lax.dynamic_slice_in_dim(pattern, device_index * blocks, blocks, 0)
    positions = jnp.arange(BLOCK)
    causal = positions[None, :] <= positions[:, None]
    self_slot = jnp.arange(slot_count) == LEVELS
    tile_keep = (own_rows >= 0)[:, :, None, None] & (
        jnp.logical_not(self_slot)[None, :, None, None] | causal[None, None]
    )
    scores = (
        jnp.einsum("bqhd,bskhd->bhqsk", query_blocks, key_stack, preferred_element_type=jnp.float32)
        * score_scale
    )
    scores = jnp.where(jnp.transpose(tile_keep, (0, 2, 1, 3))[:, None], scores, NEG_BIG)
    highest = jnp.max(scores, axis=(3, 4))
    log_total = highest + jnp.log(jnp.sum(jnp.exp(scores - highest[..., None, None]), axis=(3, 4)))
    prob_stack = jnp.exp(scores - log_total[..., None, None]).astype(jnp.bfloat16)
    attention = jnp.einsum(
        "bhqsk,bskhd->bqhd", prob_stack, value_stack, preferred_element_type=jnp.float32
    ).astype(jnp.bfloat16)
    attn_wide = attention.reshape(tokens_here, heads_here * HD).astype(jnp.float32)
    square_sum = lax.psum(jnp.sum(attn_wide * attn_wide, axis=1), "head")
    inverse = lax.rsqrt(square_sum / WIDTH + EPSILON)
    normed = (attn_wide * inverse[:, None]).astype(jnp.bfloat16)
    upstream_wide = upstream.astype(jnp.float32)
    cross_term = lax.psum(jnp.sum(upstream_wide * attn_wide, axis=1), "head")
    grad_attn = (
        inverse[:, None] * upstream_wide - attn_wide * (inverse**3 * cross_term / WIDTH)[:, None]
    ).astype(jnp.bfloat16)
    row_delta = jnp.sum(
        (grad_attn.astype(jnp.float32) * attn_wide).reshape(tokens_here, heads_here, HD), axis=2
    )
    row_delta = jnp.transpose(row_delta.reshape(blocks, BLOCK, heads_here), (0, 2, 1))

    def spread(array):
        return jnp.broadcast_to(array[:, None], (blocks, slot_count) + array.shape[1:]).reshape(
            (pair_count,) + array.shape[1:]
        )

    grad_blocks = grad_attn.reshape(tile_shape)
    query_pairs = spread(query_blocks)
    grad_pairs = spread(grad_blocks)
    keep_pairs = tile_keep.reshape(pair_count, BLOCK, BLOCK)
    dscore, prob_pairs = pair_grads(
        query_pairs,
        grad_pairs,
        spread(log_total),
        spread(row_delta),
        key_tiles,
        value_tiles,
        keep_pairs,
        score_scale,
    )
    grad_query = jnp.einsum(
        "phqk,pkhd->pqhd", dscore, key_tiles, preferred_element_type=jnp.float32
    )
    grad_query = jnp.sum(grad_query.reshape((blocks, slot_count) + tile_shape[1:]), axis=1)
    grad_queries = grad_query.astype(jnp.bfloat16).reshape(tokens_here, heads_here * HD)
    local_rows = [row_index for row_index in range(pair_count) if routing[row_index][0] == 0]
    chosen = jnp.array(local_rows, jnp.int32)
    local_terms = key_grads(
        dscore[chosen], prob_pairs[chosen], query_pairs[chosen], grad_pairs[chosen]
    )
    key_sum = collect(local_terms, [routing[row_index][1] for row_index in local_rows], blocks)
    for offset in offsets:
        remote_rows = [
            row_index for row_index in range(pair_count) if routing[row_index][0] == offset
        ]
        chosen = jnp.array(remote_rows, jnp.int32)
        remote_terms = key_grads(
            dscore[chosen], prob_pairs[chosen], query_pairs[chosen], grad_pairs[chosen]
        )
        outgoing = collect(
            remote_terms, [routing[row_index][1] for row_index in remote_rows], blocks
        )
        key_sum = key_sum + shifted(for_sending(outgoing), "ctx", -offset).astype(outgoing.dtype)
    grad_keys = key_sum[0].astype(jnp.bfloat16).reshape(tokens_here, heads_here * HD)
    grad_values = key_sum[1].astype(jnp.bfloat16).reshape(tokens_here, heads_here * HD)
    return (normed, grad_queries, grad_keys, grad_values)


NT = (((1,), (1,)), ((), ()))
NN = (((1,), (0,)), ((), ()))
TN = (((0,), (0,)), ((), ()))
SCALE = HD ** (-0.5)
TAIL = 32


NEAR, FAR, SIDE, HELPED, LOCAL, KEY_NEAR, KEY_FAR, KEY_SIDE = range(8)


class Place:
    def __init__(self):
        self.me = lax.axis_index("ctx")
        self.odd = lax.rem(self.me, 2) == 1
        self.half = lax.axis_index("head") >= lax.axis_size("head") // 2


def bias_rows(pattern_ref):
    place = Place()
    me, odd, even = place.me, place.odd, jnp.logical_not(place.odd)
    blocks = pattern_ref.shape[0]
    ahead = jnp.minimum(me + 2, blocks - 1)
    has_ahead = me + 2 < blocks
    ahead_side = jnp.logical_and(has_ahead, pattern_ref[ahead, 0] >= 0)
    own_side = pattern_ref[me, 0] >= 0
    local = jnp.logical_and(odd, own_side)

    def ahead_holds(distance, level):
        entry = pattern_ref[jnp.minimum(me + distance, blocks - 1), level]
        return jnp.logical_and(me + distance < blocks, entry >= 0)

    held = {
        NEAR: pattern_ref[me, 1] >= 0,
        FAR: jnp.logical_and(has_ahead, pattern_ref[ahead, 2] >= 0),
        SIDE: jnp.logical_or(local, jnp.logical_and(even, ahead_side)),
        HELPED: jnp.logical_or(pattern_ref[me, 2] >= 0, jnp.logical_and(even, own_side)),
        LOCAL: local,
        KEY_NEAR: ahead_holds(2, 1),
        KEY_FAR: ahead_holds(4, 2),
        KEY_SIDE: ahead_holds(1, 0),
    }
    row = lax.broadcasted_iota(jnp.int32, (8, BLOCK), 0)
    rows = jnp.zeros((8, BLOCK), jnp.float32)
    for index, flag in held.items():
        rows = jnp.where(row == index, jnp.where(flag, 0.0, NEG_BIG), rows)
    return rows


def mm(a, b, dims):
    return lax.dot_general(a, b, dims, preferred_element_type=jnp.float32)


def rows_of(h):
    return slice(h * HD, (h + 1) * HD)


def causal_mask():
    keys = lax.broadcasted_iota(jnp.int32, (BLOCK, BLOCK), 0)
    return keys <= lax.broadcasted_iota(jnp.int32, (BLOCK, BLOCK), 1)


def split_rows(rows):
    first = rows.astype(jnp.bfloat16).astype(jnp.float32)
    second = (rows - first).astype(jnp.bfloat16).astype(jnp.float32)
    third = rows - first - second
    return jnp.concatenate([first, second, third, jnp.zeros_like(rows)], axis=0).astype(jnp.bfloat16)


def joined_rows(tile):
    wide = tile.astype(jnp.float32)
    return wide[0:8] + wide[8:16] + wide[16:24]


def stack_rows(rows):
    return jnp.concatenate(rows + [jnp.zeros((1, BLOCK), jnp.float32)] * (8 - len(rows)), axis=0)


def score_tile(keys, queries):
    return mm(keys, queries, NT) * SCALE


def softmax_parts(pairs):
    tops = [scores.max(axis=0, keepdims=True) for scores, _ in pairs]
    weights = [jnp.exp(scores - top) for (scores, _), top in zip(pairs, tops)]
    totals = [w.sum(axis=0, keepdims=True) for w in weights]
    outs = [
        mm(value, w.astype(jnp.bfloat16), TN) * (1.0 / total)
        for (_, value), w, total in zip(pairs, weights, totals)
    ]
    return [(out, top, top + jnp.log(total), w) for out, top, total, w in zip(outs, tops, totals, weights)]


FIRST, SECOND = slice(0, BLOCK), slice(BLOCK, 2 * BLOCK)


def payload_kernel(heads, q_ref, k_ref, v_ref, u_ref, up_ref, down_ref, sems):
    half = Place().half
    top, bottom = pl.ds(0, BLOCK), pl.ds(BLOCK, BLOCK)

    def move(sources):
        targets = (up_ref.at[top], up_ref.at[bottom], down_ref.at[top], down_ref.at[bottom])
        copies = [
            pltpu.make_async_copy(source, target, sems.at[n])
            for n, (source, target) in enumerate(zip(sources, targets))
        ]
        for copy in copies:
            copy.start()
        for copy in copies:
            copy.wait()

    @pl.when(jnp.logical_not(half))
    def _():
        move((k_ref, v_ref, q_ref, u_ref))

    @pl.when(half)
    def _():
        move((q_ref, u_ref, k_ref, v_ref))


def diagonal_kernel(heads, pattern_ref, q_ref, k_ref, v_ref, u_ref, out_ref, lse_ref, ut_ref, bias_ref):
    bias_ref[...] = bias_rows(pattern_ref)
    causal = causal_mask()
    rows = []
    for h in range(heads):
        at = rows_of(h)
        scores = jnp.where(causal, score_tile(k_ref[:, at], q_ref[:, at]), NEG_BIG)
        ((out, _, lse, _),) = softmax_parts([(scores, v_ref[:, at])])
        out_ref[at] = out
        rows.append(lse)
        ut_ref[at] = u_ref[:, at].T
    lse_ref[...] = stack_rows(rows)


def merged(parts):
    highest = functools.reduce(jnp.maximum, [lse for _, lse in parts])
    total = highest + jnp.log(functools.reduce(jnp.add, [jnp.exp(lse - highest) for _, lse in parts]))
    return functools.reduce(jnp.add, [out * jnp.exp(lse - total) for out, lse in parts]), total


def forward_kernel(
    heads,
    bias_ref,
    up_ref,
    down_ref,
    q_ref,
    kx_ref,
    vx_ref,
    out_ref,
    lse_ref,
    up_out_ref,
    down_out_ref,
    ez_ref,
    ex_ref,
    en_ref,
    mz_ref,
    mx_ref,
    mn_ref,
):
    place = Place()
    odd, half = place.odd, place.half
    near, far, side, local = (bias_ref[n : n + 1] for n in (NEAR, FAR, SIDE, LOCAL))
    before = lse_ref[...]
    step = heads
    z_rows, own_rows, z_tops, x_tops, n_tops = [], [], [], [], []
    for start in range(0, heads, step):
        group = range(start, start + step)
        scores, weights = [], []
        for h in group:
            at = rows_of(h)
            up_a, down_a = up_ref[FIRST, at], down_ref[FIRST, at]
            k2, qz = jnp.where(half, down_a, up_a), jnp.where(half, up_a, down_a)
            q = q_ref[:, at]
            both = score_tile(k2, jnp.concatenate([qz, q], axis=0))
            x = score_tile(kx_ref[:, at], jnp.where(odd, q, qz))
            scores.append((both[:, :BLOCK] + far, x + side, both[:, BLOCK:] + near))
        for h, (z, x, n) in zip(group, scores):
            z_top, x_top, n_top = (tile.max(axis=0, keepdims=True) for tile in (z, x, n))
            both = jnp.maximum(z_top, x_top)
            z_top, x_top = jnp.where(odd, z_top, both), jnp.where(odd, x_top, both)
            z, x, n = jnp.exp(z - z_top), jnp.exp(x - x_top), jnp.exp(n - n_top)
            at = rows_of(h)
            ez_ref[at], ex_ref[at], en_ref[at] = z, x, n
            z_sum, x_sum, n_sum = (tile.sum(axis=0, keepdims=True) for tile in (z, x, n))
            z_sum = z_sum + jnp.where(odd, 0.0, x_sum)
            x_sum = jnp.maximum(x_sum, 1.0)
            for tops, top in ((z_tops, z_top), (x_tops, x_top), (n_tops, n_top)):
                tops.append(top)
            z_rows.append(z_top + jnp.log(z_sum))
            parts = (before[h : h + 1], n_top + jnp.log(n_sum) + near, x_top + jnp.log(x_sum) + local)
            highest = functools.reduce(jnp.maximum, parts)
            total = highest + jnp.log(functools.reduce(jnp.add, [jnp.exp(part - highest) for part in parts]))
            own_rows.append(total)
            d_share, n_share, x_share = (jnp.exp(part - total) for part in parts)
            z_scale = 1.0 / z_sum
            sent = [z * z_scale, x * jnp.where(odd, 0.0, z_scale)]
            kept = [n * (n_share / n_sum), x * (x_share / x_sum)]
            joined = [jnp.concatenate(tiles, axis=0).astype(jnp.bfloat16) for tiles in (sent, kept)]
            weights.append((jnp.concatenate(joined, axis=1), d_share))
        for h, (joined, d_share) in zip(group, weights):
            at = rows_of(h)
            v2 = jnp.where(half, down_ref[SECOND, at], up_ref[SECOND, at])
            out = mm(jnp.concatenate([v2, vx_ref[:, at]], axis=0), joined, TN)
            out_z = out[:, :BLOCK].astype(jnp.bfloat16)
            own = (out_ref[at] * d_share + out[:, BLOCK:]).astype(jnp.bfloat16)
            up_out_ref[at] = jnp.where(half, own, out_z)
            down_out_ref[at] = jnp.where(half, out_z, own)
    tail = slice(heads * HD, heads * HD + TAIL)
    z_tail, own_tail = split_rows(stack_rows(z_rows)), split_rows(stack_rows(own_rows))
    up_out_ref[tail] = jnp.where(half, own_tail, z_tail)
    down_out_ref[tail] = jnp.where(half, z_tail, own_tail)
    mz_ref[...] = stack_rows(z_tops)
    mx_ref[...] = stack_rows(x_tops)
    mn_ref[...] = stack_rows(n_tops)


def transpose_kernel(heads, up_ref, down_ref, out_ref):
    half = Place().half
    for h in range(heads):
        at = rows_of(h)
        out_ref[at] = jnp.where(half, up_ref[SECOND, at], down_ref[SECOND, at]).T


def merge_kernel(
    heads,
    bias_ref,
    up_ref,
    down_ref,
    up_in_ref,
    down_in_ref,
    ut_ref,
    uzt_ref,
    a_ref,
    az_ref,
    lse_ref,
    lsez_ref,
    sums_ref,
):
    half = Place().half
    tail = slice(heads * HD, heads * HD + TAIL)

    def select(rising, falling, at):
        first, second = rising[at], falling[at]
        return jnp.where(half, second, first), jnp.where(half, first, second)

    z_part, own_part = select(up_ref, down_ref, tail)
    help_part, ahead_part = select(up_in_ref, down_in_ref, tail)
    rows, shares = [], []
    for first, second in (
        (joined_rows(own_part), joined_rows(help_part) + bias_ref[HELPED : HELPED + 1]),
        (joined_rows(ahead_part), joined_rows(z_part)),
    ):
        highest = jnp.maximum(first, second)
        total = highest + jnp.log(jnp.exp(first - highest) + jnp.exp(second - highest))
        rows.append(total)
        shares.append((jnp.exp(first - total), jnp.exp(second - total)))
    lse_ref[...], lsez_ref[...] = (jnp.maximum(total, -1e9) for total in rows)
    sums = [jnp.zeros((8, BLOCK), jnp.float32)] * 4
    for h in range(heads):
        at, row = rows_of(h), slice(h, h + 1)
        z_out, own_out = select(up_ref, down_ref, at)
        help_out, ahead_out = select(up_in_ref, down_in_ref, at)
        for n, (first, second, u_ref, target) in enumerate(
            ((own_out, help_out, ut_ref, a_ref), (ahead_out, z_out, uzt_ref, az_ref))
        ):
            out = (
                first.astype(jnp.float32) * shares[n][0][row] + second.astype(jnp.float32) * shares[n][1][row]
            ).astype(jnp.bfloat16)
            target[at] = out
            wide = out.astype(jnp.float32)
            sums[2 * n] += (wide * wide).reshape(HD // 8, 8, BLOCK).sum(axis=0)
            sums[2 * n + 1] += (wide * u_ref[at].astype(jnp.float32)).reshape(HD // 8, 8, BLOCK).sum(axis=0)
    sums_ref[...] = stack_rows([part.sum(axis=0, keepdims=True) for part in sums])


def norm_rows(sums, first):
    inverse = lax.rsqrt(sums[first : first + 1] / WIDTH + EPSILON)
    return inverse, inverse**3 * sums[first + 1 : first + 2] / WIDTH


def upstream_part(norm, u, a):
    inverse, factor = norm
    wide = a.astype(jnp.float32)
    grad = (inverse * u.astype(jnp.float32) - wide * factor).astype(jnp.bfloat16)
    return grad, jnp.sum(grad.astype(jnp.float32) * wide, axis=0, keepdims=True)


def side_queries_kernel(heads, q_ref, up_ref, down_ref, out_ref):
    place = Place()
    for h in range(heads):
        at = rows_of(h)
        qz = jnp.where(place.half, up_ref[FIRST, at], down_ref[FIRST, at])
        out_ref[:, at] = jnp.where(place.odd, q_ref[:, at], qz)


def relay_kernel(heads, up_ref, down_ref, out_ref):
    half = Place().half
    for h in range(heads):
        at = rows_of(h)
        out_ref[:, at] = jnp.where(half, up_ref[FIRST, at], down_ref[FIRST, at])


def back_kernel(
    heads,
    bias_ref,
    sums_ref,
    a_ref,
    az_ref,
    lse_ref,
    lsez_ref,
    ut_ref,
    uzt_ref,
    up_ref,
    down_ref,
    kx_ref,
    vx_ref,
    ez_ref,
    ex_ref,
    mz_ref,
    mx_ref,
    up_out_ref,
    down_out_ref,
    side_out_ref,
    dsx_ref,
    grad_ref,
    gz_ref,
    delta_ref,
    deltaz_ref,
):
    place = Place()
    odd, half = place.odd, place.half
    sums = sums_ref[...]
    own_norm, z_norm = norm_rows(sums, 0), norm_rows(sums, 2)
    lse, z_lse = lse_ref[...], lsez_ref[...]
    scales = (
        jnp.exp(mz_ref[...] - z_lse + bias_ref[FAR : FAR + 1]),
        jnp.exp(mx_ref[...] - jnp.where(odd, lse, z_lse) + bias_ref[SIDE : SIDE + 1]),
    )
    group = range(heads)
    deltas, z_deltas = [], []
    parts, products, scores = [], [], []
    for h in group:
        at = rows_of(h)
        grad, delta = upstream_part(own_norm, ut_ref[at], a_ref[at])
        gz, deltaz = upstream_part(z_norm, uzt_ref[at], az_ref[at])
        grad_ref[at], gz_ref[at] = grad, gz
        deltas.append(delta)
        z_deltas.append(deltaz)
        gx, deltax = jnp.where(odd, grad, gz), jnp.where(odd, delta, deltaz)
        side_out_ref[at] = gx
        parts.append(((gz, gx), (deltaz, deltax)))
    for h, ((gz, gx), _) in zip(group, parts):
        at = rows_of(h)
        v2 = jnp.where(half, down_ref[SECOND, at], up_ref[SECOND, at])
        products.append((mm(v2, gz, NN), mm(vx_ref[:, at], gx, NN)))
    for h, (_, delta), product in zip(group, parts, products):
        tiles = []
        for n, e_ref in enumerate((ez_ref, ex_ref)):
            weights = e_ref[rows_of(h)] * scales[n][h : h + 1]
            tiles.append((weights * (product[n] - delta[n]) * SCALE).astype(jnp.bfloat16))
        dsx_ref[rows_of(h)] = tiles[1]
        scores.append(tiles)
    for h, ((gz, _), _), (dz, dx) in zip(group, parts, scores):
        at = rows_of(h)
        k2 = jnp.where(half, down_ref[FIRST, at], up_ref[FIRST, at])
        joined = jnp.concatenate([dz, jnp.where(odd, jnp.zeros_like(dx), dx)], axis=0)
        dqz = mm(jnp.concatenate([k2, kx_ref[:, at]], axis=0), joined, TN).astype(jnp.bfloat16)
        up_out_ref[at] = jnp.where(half, gz, dqz)
        down_out_ref[at] = jnp.where(half, dqz, gz)
    delta, deltaz = stack_rows(deltas), stack_rows(z_deltas)
    delta_ref[...], deltaz_ref[...] = delta, deltaz
    tail = slice(heads * HD, heads * HD + 2 * TAIL)
    z_tail = jnp.concatenate([split_rows(z_lse), split_rows(deltaz)], axis=0)
    own_tail = jnp.concatenate([split_rows(lse), split_rows(delta)], axis=0)
    up_out_ref[tail] = jnp.where(half, z_tail, jnp.zeros_like(z_tail))
    down_out_ref[tail] = jnp.where(half, jnp.zeros_like(z_tail), z_tail)
    side_out_ref[tail] = jnp.where(odd, own_tail, z_tail)


def local_back_kernel(
    heads,
    bias_ref,
    sums_ref,
    q_ref,
    k_ref,
    v_ref,
    a_ref,
    lse_ref,
    lsez_ref,
    grad_ref,
    gz_ref,
    delta_ref,
    deltaz_ref,
    en_ref,
    mn_ref,
    dsx_ref,
    kx_ref,
    up_ref,
    down_ref,
    normed_ref,
    dq_ref,
    dk_ref,
    dv_ref,
):
    place = Place()
    odd, half = place.odd, place.half
    inverse, _ = norm_rows(sums_ref[...], 0)
    lse, z_lse = lse_ref[...], lsez_ref[...] - bias_ref[KEY_NEAR : KEY_NEAR + 1]
    near_scale = jnp.exp(mn_ref[...] - lse + bias_ref[NEAR : NEAR + 1])
    causal = causal_mask()
    for h in range(heads):
        at, row = rows_of(h), slice(h, h + 1)
        normed_ref[:, at] = (a_ref[at].astype(jnp.float32) * inverse).astype(jnp.bfloat16).T
        up_a, down_a = up_ref[FIRST, at], down_ref[FIRST, at]
        k2, qz = jnp.where(half, down_a, up_a), jnp.where(half, up_a, down_a)
        v2 = jnp.where(half, down_ref[SECOND, at], up_ref[SECOND, at])
        q, k, v, grad, gz = q_ref[:, at], k_ref[:, at], v_ref[:, at], grad_ref[at], gz_ref[at]
        queries, grads = jnp.concatenate([q, qz], axis=0), jnp.concatenate([grad, gz], axis=1)
        both = score_tile(k, queries)
        products = mm(v, grads, NN)
        own = jnp.exp(jnp.where(causal, both[:, :BLOCK], NEG_BIG) - lse[row])
        ahead = jnp.exp(both[:, BLOCK:] - z_lse[row])
        near = en_ref[at] * near_scale[row]
        own_ds = (own * (products[:, :BLOCK] - delta_ref[row]) * SCALE).astype(jnp.bfloat16)
        ahead_ds = (ahead * (products[:, BLOCK:] - deltaz_ref[row]) * SCALE).astype(jnp.bfloat16)
        near_ds = (near * (mm(v2, grad, NN) - delta_ref[row]) * SCALE).astype(jnp.bfloat16)
        dk_ref[:, at] = mm(jnp.concatenate([own_ds, ahead_ds], axis=1), queries, NN)
        probs = jnp.concatenate([own, ahead], axis=1).astype(jnp.bfloat16)
        dv_ref[:, at] = mm(probs, grads, NT)
        dsx = jnp.where(odd, dsx_ref[at], jnp.zeros_like(dsx_ref[at]))
        dq_ref[:, at] = mm(own_ds, k, TN) + mm(
            jnp.concatenate([near_ds, dsx], axis=0), jnp.concatenate([k2, kx_ref[:, at]], axis=0), TN
        )


def key_scores_kernel(heads, bias_ref, k_ref, far_ref, side_ref, out_ref):
    for h in range(heads):
        at = rows_of(h)
        both = score_tile(k_ref[:, at], jnp.concatenate([far_ref[:, at], side_ref[:, at]], axis=0))
        out_ref[0, at] = both[:, :BLOCK] + bias_ref[KEY_FAR : KEY_FAR + 1]
        out_ref[1, at] = both[:, BLOCK:] + bias_ref[KEY_SIDE : KEY_SIDE + 1]


def final_kernel(
    heads,
    scores_ref,
    far_ref,
    sideq_ref,
    up_ref,
    down_ref,
    side_ref,
    v_ref,
    dq_own_ref,
    dk_own_ref,
    dv_own_ref,
    dq_ref,
    dk_ref,
    dv_ref,
):
    place = Place()
    half = place.half
    behind = (place.me >= 2).astype(jnp.float32)
    first = slice(heads * HD, heads * HD + TAIL)
    second = slice(heads * HD + TAIL, heads * HD + 2 * TAIL)
    lse, delta = (
        (joined_rows(jnp.where(half, up_ref[part], down_ref[part])), joined_rows(side_ref[part]))
        for part in (first, second)
    )
    group = range(heads)
    grads, products, tiles = [], [], []
    for h in group:
        at = rows_of(h)
        up, down = up_ref[at], down_ref[at]
        dqz = jnp.where(half, down, up).T.astype(jnp.float32) * behind
        dq_ref[:, at] = (dq_own_ref[:, at] + dqz).astype(jnp.bfloat16)
        grads.append(jnp.concatenate([jnp.where(half, up, down), side_ref[at]], axis=1))
    for h, grad in zip(group, grads):
        products.append(mm(v_ref[:, rows_of(h)], grad, NN))
    for h, product in zip(group, products):
        row = slice(h, h + 1)
        probs = [jnp.exp(scores_ref[n, rows_of(h)] - lse[n][row]) for n in range(2)]
        scores = [
            probs[n] * (product[:, n * BLOCK : (n + 1) * BLOCK] - delta[n][row]) * SCALE for n in range(2)
        ]
        tiles.append([jnp.concatenate(pair, axis=1).astype(jnp.bfloat16) for pair in (probs, scores)])
    for h, grad, (probs, scores) in zip(group, grads, tiles):
        at = rows_of(h)
        queries = jnp.concatenate([far_ref[:, at], sideq_ref[:, at]], axis=0)
        dk_ref[:, at] = (dk_own_ref[:, at] + mm(scores, queries, NN)).astype(jnp.bfloat16)
        dv_ref[:, at] = (dv_own_ref[:, at] + mm(probs, grad, NT)).astype(jnp.bfloat16)


def call(kernel, heads, flags, arrays, outs, flops, space=pltpu.VMEM, scratch=(), after=()):
    moved = sum(math.prod(a.shape) * a.dtype.itemsize for a in (*arrays, *outs)) if flops else 0
    return pl.pallas_call(
        lambda *refs: kernel(heads, *refs[len(after) :]),
        out_shape=outs,
        in_specs=[pl.BlockSpec(memory_space=pl.ANY)] * len(after)
        + [pl.BlockSpec(memory_space=pltpu.SMEM)] * len(flags)
        + [pl.BlockSpec(memory_space=space)] * len(arrays),
        out_specs=[pl.BlockSpec(memory_space=pltpu.VMEM)] * len(outs),
        scratch_shapes=scratch,
        compiler_params=pltpu.CompilerParams(vmem_limit_bytes=24 * 2**20),
        cost_estimate=pl.CostEstimate(flops=flops, bytes_accessed=moved, transcendentals=0),
    )(*after, *flags, *arrays)


def cycles(blocks, members):
    route = []
    for block in range(blocks):
        for member in range(members):
            rising = member < members // 2
            other = member + members // 2 if rising else member - members // 2
            target = block + 2 if rising else block - 2
            inside = 0 <= target < blocks
            route.append(
                (block * members + member, target * members + member if inside else block * members + other)
            )
    return route


def meeting_shards(queries, keys, values, pattern, upstream):
    tokens, width = queries.shape
    heads = width // HD
    blocks, members = lax.axis_size("ctx"), lax.axis_size("head")
    unit = heads * 2 * BLOCK**3
    rising = cycles(blocks, members)
    falling = [(target, source) for source, target in rising]

    def cycle(up_array, down_array):
        return lax.ppermute(up_array, ("ctx", "head"), rising), lax.ppermute(
            down_array, ("ctx", "head"), falling
        )

    def swap(array):
        return lax.ppermute(array, "ctx", [(i, i ^ 1) for i in range(blocks)])

    def ring(array, distance):
        return lax.ppermute(array, "ctx", [(i, (i + distance) % blocks) for i in range(blocks)])

    def struct(*shape, dtype=jnp.bfloat16):
        return jax.ShapeDtypeStruct(shape, dtype)

    wide = struct(tokens, width, dtype=jnp.float32)
    wide_t = struct(width, tokens, dtype=jnp.float32)
    flat, flat_t = struct(tokens, width), struct(width, tokens)
    message = struct(width + TAIL, tokens)
    rows = struct(8, tokens, dtype=jnp.float32)

    payload = call(
        payload_kernel,
        heads,
        (),
        [pltpu.with_memory_space_constraint(a, pltpu.HBM) for a in (queries, keys, values, upstream)],
        [pltpu.VMEM((2 * tokens, width), jnp.bfloat16)] * 2,
        0,
        space=pltpu.HBM,
        scratch=(pltpu.SemaphoreType.DMA((4,)),),
    )
    received = cycle(*payload)
    keys_x, values_x = swap(keys), swap(values)
    diagonal, diagonal_lse, upstream_t, bias = call(
        diagonal_kernel,
        heads,
        (pattern,),
        (queries, keys, values, upstream),
        (wide_t, rows, flat_t, rows),
        3 * unit,
        after=(payload[0],),
    )
    up_out, down_out, *kept = call(
        forward_kernel,
        heads,
        (),
        (bias, *received, queries, keys_x, values_x, diagonal, diagonal_lse),
        (message, message, wide_t, wide_t, wide_t, rows, rows, rows),
        6 * unit,
    )
    ez, ex, en, mz, mx, mn = kept
    up_in, down_in = cycle(up_out, down_out)
    (side_queries,) = call(
        side_queries_kernel, heads, (), (queries, *received), (flat,), 0, after=(mn,)
    )
    side_queries = swap(side_queries)
    (far_queries,) = call(relay_kernel, heads, (), received, (flat,), 0, after=(down_in,))
    far_queries = lax.ppermute(far_queries, "ctx", [(i, i - 2) for i in range(2, blocks - 2)])
    (upstream_zt,) = call(transpose_kernel, heads, (), received, (flat_t,), 0, after=(mn,))
    attention, attention_z, lse, lse_z, sums = call(
        merge_kernel,
        heads,
        (),
        (bias, up_out, down_out, up_in, down_in, upstream_t, upstream_zt),
        (flat_t, flat_t, rows, rows, rows),
        unit // 64,
    )
    others = [
        lax.ppermute(sums, "head", [(i, i ^ step) for i in range(members)]) for step in range(1, members)
    ]
    sums = functools.reduce(jnp.add, others, sums)
    longer = struct(width + 2 * TAIL, tokens)
    up_out, down_out, side_out, side_ds, grad_t, grad_zt, delta, delta_z = call(
        back_kernel,
        heads,
        (),
        (bias, sums, attention, attention_z, lse, lse_z, upstream_t, upstream_zt, *received, keys_x, values_x)
        + (ez, ex, mz, mx),
        (longer, longer, longer, flat_t, flat_t, flat_t, rows, rows),
        0,
        after=(side_queries,),
    )
    returned = cycle(up_out, down_out)
    side_grads = swap(lax.optimization_barrier((side_out, far_queries))[0])
    normed, dq_own, dk_own, dv_own = call(
        local_back_kernel,
        heads,
        (),
        (bias, sums, queries, keys, values, attention, lse, lse_z, grad_t, grad_zt, delta, delta_z, en, mn)
        + (side_ds, keys_x, *received),
        (flat, wide, wide, wide),
        0,
    )
    (key_scores,) = call(
        key_scores_kernel,
        heads,
        (),
        (bias, keys, far_queries, side_queries),
        (struct(2, width, tokens, dtype=jnp.float32),),
        0,
    )
    grad_queries, grad_keys, grad_values = call(
        final_kernel,
        heads,
        (),
        (key_scores, far_queries, side_queries, *returned, side_grads, values, dq_own, dk_own, dv_own),
        (flat, flat, flat),
        6 * unit,
    )
    return (normed, grad_queries, grad_keys, grad_values)


def shards(queries, keys, values, pattern, upstream):
    fits = lax.axis_size("ctx") == 8 and lax.axis_size("head") == 4 and queries.shape == (BLOCK, 8 * HD)
    if fits:
        return meeting_shards(queries, keys, values, pattern, upstream)
    return generic_shards(queries, keys, values, pattern, upstream)


def solution(mesh):
    return jax.shard_map(
        shards,
        mesh=mesh,
        in_specs=(P("ctx", "head"), P("ctx", "head"), P("ctx", "head"), P(), P("ctx", "head")),
        out_specs=(P("ctx", "head"), P("ctx", "head"), P("ctx", "head"), P("ctx", "head")),
        check_vma=False,
    )
```

```python
import functools
import math

import jax
import jax.numpy as jnp
from jax import lax
from jax.experimental import pallas as pl
from jax.experimental.pallas import tpu as pltpu
from jax.sharding import PartitionSpec as P

HD = 128
BLOCK = 128
LEVELS = 7
WIDTH = 4096


NEG_BIG = -1e30
EPSILON = 1e-06


def shifted(block, axis, distance):
    devices = range(lax.axis_size(axis))
    route = [(i - distance, i) for i in devices if i - distance in devices]
    return lax.ppermute(block, axis, route)


def for_sending(x):
    return jax.tree.map(lambda a: a.astype(jnp.bfloat16) if a.dtype == jnp.float32 else a, x)


def route_table(blocks, levels):
    routing = []
    for query_block in range(blocks):
        for level_index in range(levels + 1):
            if level_index == levels:
                routing.append((0, query_block))
            else:
                distance = 2**level_index
                routing.append(
                    (-((query_block - distance) // blocks), (query_block - distance) % blocks)
                )
    return routing


def pair_grads(
    query_tiles, grad_tiles, lse_tiles, delta_tiles, key_tiles, value_tiles, keep_mask, score_scale
):
    scores = (
        jnp.einsum("pqhd,pkhd->phqk", query_tiles, key_tiles, preferred_element_type=jnp.float32)
        * score_scale
    )
    scores = jnp.where(keep_mask[:, None], scores, NEG_BIG)
    weights = jnp.exp(scores - lse_tiles[..., None])
    prob_tiles = weights.astype(jnp.bfloat16)
    grad_probs = jnp.einsum(
        "pqhd,pkhd->phqk", grad_tiles, value_tiles, preferred_element_type=jnp.float32
    )
    dscore = (weights * (grad_probs - delta_tiles[..., None]) * score_scale).astype(jnp.bfloat16)
    return (dscore, prob_tiles)


def key_grads(dscore, prob_tiles, query_tiles, grad_tiles):
    key_part = jnp.einsum(
        "phqk,pqhd->pkhd", dscore, query_tiles, preferred_element_type=jnp.float32
    )
    value_part = jnp.einsum(
        "phqk,pqhd->pkhd", prob_tiles, grad_tiles, preferred_element_type=jnp.float32
    )
    return jnp.stack((key_part, value_part))


def collect(partials, targets, blocks):
    pieces = []
    for key_index in range(blocks):
        summed = jnp.zeros((2,) + partials.shape[2:], jnp.float32)
        for row_index, target in enumerate(targets):
            if target == key_index:
                summed = summed + partials[:, row_index]
        pieces.append(summed)
    return jnp.stack(pieces, axis=1)


def generic_shards(queries, keys, values, pattern, upstream):
    tokens_here = queries.shape[0]
    heads_here = queries.shape[1] // HD
    blocks = tokens_here // BLOCK
    slot_count = LEVELS + 1
    pair_count = blocks * slot_count
    score_scale = HD ** (-0.5)
    ctx_count = lax.axis_size("ctx")
    device_index = lax.axis_index("ctx")
    routing = route_table(blocks, LEVELS)
    offsets = sorted(
        set((route_entry[0] for route_entry in routing if 0 < route_entry[0] < ctx_count))
    )
    tile_shape = (blocks, BLOCK, heads_here, HD)
    query_blocks = queries.reshape(tile_shape)
    own_pairs = jnp.stack((keys, values)).reshape((2,) + tile_shape)
    sources = {0: own_pairs}
    for offset in offsets:
        fetched = shifted(jnp.stack((keys, values)), "ctx", offset)
        sources[offset] = fetched.reshape((2,) + tile_shape)
    empty_tile = jnp.zeros((2, BLOCK, heads_here, HD), jnp.bfloat16)
    gathered = []
    for source, key_index in routing:
        if source in sources:
            gathered.append(sources[source][:, key_index])
        else:
            gathered.append(empty_tile)
    pair_kv = jnp.stack(gathered, axis=1)
    key_tiles = pair_kv[0]
    value_tiles = pair_kv[1]
    key_stack = key_tiles.reshape((blocks, slot_count) + tile_shape[1:])
    value_stack = value_tiles.reshape((blocks, slot_count) + tile_shape[1:])
    own_rows = lax.dynamic_slice_in_dim(pattern, device_index * blocks, blocks, 0)
    positions = jnp.arange(BLOCK)
    causal = positions[None, :] <= positions[:, None]
    self_slot = jnp.arange(slot_count) == LEVELS
    tile_keep = (own_rows >= 0)[:, :, None, None] & (
        jnp.logical_not(self_slot)[None, :, None, None] | causal[None, None]
    )
    scores = (
        jnp.einsum("bqhd,bskhd->bhqsk", query_blocks, key_stack, preferred_element_type=jnp.float32)
        * score_scale
    )
    scores = jnp.where(jnp.transpose(tile_keep, (0, 2, 1, 3))[:, None], scores, NEG_BIG)
    highest = jnp.max(scores, axis=(3, 4))
    log_total = highest + jnp.log(jnp.sum(jnp.exp(scores - highest[..., None, None]), axis=(3, 4)))
    prob_stack = jnp.exp(scores - log_total[..., None, None]).astype(jnp.bfloat16)
    attention = jnp.einsum(
        "bhqsk,bskhd->bqhd", prob_stack, value_stack, preferred_element_type=jnp.float32
    ).astype(jnp.bfloat16)
    attn_wide = attention.reshape(tokens_here, heads_here * HD).astype(jnp.float32)
    square_sum = lax.psum(jnp.sum(attn_wide * attn_wide, axis=1), "head")
    inverse = lax.rsqrt(square_sum / WIDTH + EPSILON)
    normed = (attn_wide * inverse[:, None]).astype(jnp.bfloat16)
    upstream_wide = upstream.astype(jnp.float32)
    cross_term = lax.psum(jnp.sum(upstream_wide * attn_wide, axis=1), "head")
    grad_attn = (
        inverse[:, None] * upstream_wide - attn_wide * (inverse**3 * cross_term / WIDTH)[:, None]
    ).astype(jnp.bfloat16)
    row_delta = jnp.sum(
        (grad_attn.astype(jnp.float32) * attn_wide).reshape(tokens_here, heads_here, HD), axis=2
    )
    row_delta = jnp.transpose(row_delta.reshape(blocks, BLOCK, heads_here), (0, 2, 1))

    def spread(array):
        return jnp.broadcast_to(array[:, None], (blocks, slot_count) + array.shape[1:]).reshape(
            (pair_count,) + array.shape[1:]
        )

    grad_blocks = grad_attn.reshape(tile_shape)
    query_pairs = spread(query_blocks)
    grad_pairs = spread(grad_blocks)
    keep_pairs = tile_keep.reshape(pair_count, BLOCK, BLOCK)
    dscore, prob_pairs = pair_grads(
        query_pairs,
        grad_pairs,
        spread(log_total),
        spread(row_delta),
        key_tiles,
        value_tiles,
        keep_pairs,
        score_scale,
    )
    grad_query = jnp.einsum(
        "phqk,pkhd->pqhd", dscore, key_tiles, preferred_element_type=jnp.float32
    )
    grad_query = jnp.sum(grad_query.reshape((blocks, slot_count) + tile_shape[1:]), axis=1)
    grad_queries = grad_query.astype(jnp.bfloat16).reshape(tokens_here, heads_here * HD)
    local_rows = [row_index for row_index in range(pair_count) if routing[row_index][0] == 0]
    chosen = jnp.array(local_rows, jnp.int32)
    local_terms = key_grads(
        dscore[chosen], prob_pairs[chosen], query_pairs[chosen], grad_pairs[chosen]
    )
    key_sum = collect(local_terms, [routing[row_index][1] for row_index in local_rows], blocks)
    for offset in offsets:
        remote_rows = [
            row_index for row_index in range(pair_count) if routing[row_index][0] == offset
        ]
        chosen = jnp.array(remote_rows, jnp.int32)
        remote_terms = key_grads(
            dscore[chosen], prob_pairs[chosen], query_pairs[chosen], grad_pairs[chosen]
        )
        outgoing = collect(
            remote_terms, [routing[row_index][1] for row_index in remote_rows], blocks
        )
        key_sum = key_sum + shifted(for_sending(outgoing), "ctx", -offset).astype(outgoing.dtype)
    grad_keys = key_sum[0].astype(jnp.bfloat16).reshape(tokens_here, heads_here * HD)
    grad_values = key_sum[1].astype(jnp.bfloat16).reshape(tokens_here, heads_here * HD)
    return (normed, grad_queries, grad_keys, grad_values)


NT = (((1,), (1,)), ((), ()))
NN = (((1,), (0,)), ((), ()))
TN = (((0,), (0,)), ((), ()))
SCALE = HD ** (-0.5)
TAIL = 32


NEAR, FAR, SIDE, HELPED, LOCAL, KEY_NEAR, KEY_FAR, KEY_SIDE = range(8)


class Place:
    def __init__(self):
        self.me = lax.axis_index("ctx")
        self.odd = lax.rem(self.me, 2) == 1
        self.half = lax.axis_index("head") >= lax.axis_size("head") // 2


def bias_rows(pattern_ref):
    place = Place()
    me, odd, even = place.me, place.odd, jnp.logical_not(place.odd)
    blocks = pattern_ref.shape[0]
    ahead = jnp.minimum(me + 2, blocks - 1)
    has_ahead = me + 2 < blocks
    ahead_side = jnp.logical_and(has_ahead, pattern_ref[ahead, 0] >= 0)
    own_side = pattern_ref[me, 0] >= 0
    local = jnp.logical_and(odd, own_side)

    def ahead_holds(distance, level):
        entry = pattern_ref[jnp.minimum(me + distance, blocks - 1), level]
        return jnp.logical_and(me + distance < blocks, entry >= 0)

    held = {
        NEAR: pattern_ref[me, 1] >= 0,
        FAR: jnp.logical_and(has_ahead, pattern_ref[ahead, 2] >= 0),
        SIDE: jnp.logical_or(local, jnp.logical_and(even, ahead_side)),
        HELPED: jnp.logical_or(pattern_ref[me, 2] >= 0, jnp.logical_and(even, own_side)),
        LOCAL: local,
        KEY_NEAR: ahead_holds(2, 1),
        KEY_FAR: ahead_holds(4, 2),
        KEY_SIDE: ahead_holds(1, 0),
    }
    row = lax.broadcasted_iota(jnp.int32, (8, BLOCK), 0)
    rows = jnp.zeros((8, BLOCK), jnp.float32)
    for index, flag in held.items():
        rows = jnp.where(row == index, jnp.where(flag, 0.0, NEG_BIG), rows)
    return rows


def mm(a, b, dims):
    return lax.dot_general(a, b, dims, preferred_element_type=jnp.float32)


def rows_of(h):
    return slice(h * HD, (h + 1) * HD)


def causal_mask():
    keys = lax.broadcasted_iota(jnp.int32, (BLOCK, BLOCK), 0)
    return keys <= lax.broadcasted_iota(jnp.int32, (BLOCK, BLOCK), 1)


def split_rows(rows):
    first = rows.astype(jnp.bfloat16).astype(jnp.float32)
    second = (rows - first).astype(jnp.bfloat16).astype(jnp.float32)
    third = rows - first - second
    return jnp.concatenate([first, second, third, jnp.zeros_like(rows)], axis=0).astype(jnp.bfloat16)


def joined_rows(tile):
    wide = tile.astype(jnp.float32)
    return wide[0:8] + wide[8:16] + wide[16:24]


def stack_rows(rows):
    return jnp.concatenate(rows + [jnp.zeros((1, BLOCK), jnp.float32)] * (8 - len(rows)), axis=0)


def score_tile(keys, queries):
    return mm(keys, queries, NT) * SCALE


def softmax_parts(pairs):
    tops = [scores.max(axis=0, keepdims=True) for scores, _ in pairs]
    weights = [jnp.exp(scores - top) for (scores, _), top in zip(pairs, tops)]
    totals = [w.sum(axis=0, keepdims=True) for w in weights]
    outs = [
        mm(value, w.astype(jnp.bfloat16), TN) * (1.0 / total)
        for (_, value), w, total in zip(pairs, weights, totals)
    ]
    return [(out, top, top + jnp.log(total), w) for out, top, total, w in zip(outs, tops, totals, weights)]


FIRST, SECOND = slice(0, BLOCK), slice(BLOCK, 2 * BLOCK)


def payload_kernel(heads, q_ref, k_ref, v_ref, u_ref, up_ref, down_ref, sems):
    half = Place().half
    top, bottom = pl.ds(0, BLOCK), pl.ds(BLOCK, BLOCK)

    def move(sources):
        targets = (up_ref.at[top], up_ref.at[bottom], down_ref.at[top], down_ref.at[bottom])
        copies = [
            pltpu.make_async_copy(source, target, sems.at[n])
            for n, (source, target) in enumerate(zip(sources, targets))
        ]
        for copy in copies:
            copy.start()
        for copy in copies:
            copy.wait()

    @pl.when(jnp.logical_not(half))
    def _():
        move((k_ref, v_ref, q_ref, u_ref))

    @pl.when(half)
    def _():
        move((q_ref, u_ref, k_ref, v_ref))


def diagonal_kernel(heads, pattern_ref, q_ref, k_ref, v_ref, u_ref, out_ref, lse_ref, ut_ref, bias_ref):
    bias_ref[...] = bias_rows(pattern_ref)
    causal = causal_mask()
    rows = []
    for h in range(heads):
        at = rows_of(h)
        scores = jnp.where(causal, score_tile(k_ref[:, at], q_ref[:, at]), NEG_BIG)
        ((out, _, lse, _),) = softmax_parts([(scores, v_ref[:, at])])
        out_ref[at] = out
        rows.append(lse)
        ut_ref[at] = u_ref[:, at].T
    lse_ref[...] = stack_rows(rows)


def merged(parts):
    highest = functools.reduce(jnp.maximum, [lse for _, lse in parts])
    total = highest + jnp.log(functools.reduce(jnp.add, [jnp.exp(lse - highest) for _, lse in parts]))
    return functools.reduce(jnp.add, [out * jnp.exp(lse - total) for out, lse in parts]), total


def forward_kernel(
    heads,
    bias_ref,
    up_ref,
    down_ref,
    q_ref,
    kx_ref,
    vx_ref,
    out_ref,
    lse_ref,
    up_out_ref,
    down_out_ref,
    ez_ref,
    ex_ref,
    en_ref,
    mz_ref,
    mx_ref,
    mn_ref,
):
    place = Place()
    odd, half = place.odd, place.half
    near, far, side, local = (bias_ref[n : n + 1] for n in (NEAR, FAR, SIDE, LOCAL))
    before = lse_ref[...]
    step = heads
    z_rows, own_rows, z_tops, x_tops, n_tops = [], [], [], [], []
    for start in range(0, heads, step):
        group = range(start, start + step)
        scores, weights = [], []
        for h in group:
            at = rows_of(h)
            up_a, down_a = up_ref[FIRST, at], down_ref[FIRST, at]
            k2, qz = jnp.where(half, down_a, up_a), jnp.where(half, up_a, down_a)
            q = q_ref[:, at]
            both = score_tile(k2, jnp.concatenate([qz, q], axis=0))
            x = score_tile(kx_ref[:, at], jnp.where(odd, q, qz))
            scores.append((both[:, :BLOCK] + far, x + side, both[:, BLOCK:] + near))
        for h, (z, x, n) in zip(group, scores):
            z_top, x_top, n_top = (tile.max(axis=0, keepdims=True) for tile in (z, x, n))
            both = jnp.maximum(z_top, x_top)
            z_top, x_top = jnp.where(odd, z_top, both), jnp.where(odd, x_top, both)
            z, x, n = jnp.exp(z - z_top), jnp.exp(x - x_top), jnp.exp(n - n_top)
            at = rows_of(h)
            ez_ref[at], ex_ref[at], en_ref[at] = z, x, n
            z_sum, x_sum, n_sum = (tile.sum(axis=0, keepdims=True) for tile in (z, x, n))
            z_sum = z_sum + jnp.where(odd, 0.0, x_sum)
            x_sum = jnp.maximum(x_sum, 1.0)
            for tops, top in ((z_tops, z_top), (x_tops, x_top), (n_tops, n_top)):
                tops.append(top)
            z_rows.append(z_top + jnp.log(z_sum))
            parts = (before[h : h + 1], n_top + jnp.log(n_sum) + near, x_top + jnp.log(x_sum) + local)
            highest = functools.reduce(jnp.maximum, parts)
            total = highest + jnp.log(functools.reduce(jnp.add, [jnp.exp(part - highest) for part in parts]))
            own_rows.append(total)
            d_share, n_share, x_share = (jnp.exp(part - total) for part in parts)
            z_scale = 1.0 / z_sum
            sent = [z * z_scale, x * jnp.where(odd, 0.0, z_scale)]
            kept = [n * (n_share / n_sum), x * (x_share / x_sum)]
            joined = [jnp.concatenate(tiles, axis=0).astype(jnp.bfloat16) for tiles in (sent, kept)]
            weights.append((jnp.concatenate(joined, axis=1), d_share))
        for h, (joined, d_share) in zip(group, weights):
            at = rows_of(h)
            v2 = jnp.where(half, down_ref[SECOND, at], up_ref[SECOND, at])
            out = mm(jnp.concatenate([v2, vx_ref[:, at]], axis=0), joined, TN)
            out_z = out[:, :BLOCK].astype(jnp.bfloat16)
            own = (out_ref[at] * d_share + out[:, BLOCK:]).astype(jnp.bfloat16)
            up_out_ref[at] = jnp.where(half, own, out_z)
            down_out_ref[at] = jnp.where(half, out_z, own)
    tail = slice(heads * HD, heads * HD + TAIL)
    z_tail, own_tail = split_rows(stack_rows(z_rows)), split_rows(stack_rows(own_rows))
    up_out_ref[tail] = jnp.where(half, own_tail, z_tail)
    down_out_ref[tail] = jnp.where(half, z_tail, own_tail)
    mz_ref[...] = stack_rows(z_tops)
    mx_ref[...] = stack_rows(x_tops)
    mn_ref[...] = stack_rows(n_tops)


def transpose_kernel(heads, up_ref, down_ref, out_ref):
    half = Place().half
    for h in range(heads):
        at = rows_of(h)
        out_ref[at] = jnp.where(half, up_ref[SECOND, at], down_ref[SECOND, at]).T


def merge_kernel(
    heads,
    bias_ref,
    up_ref,
    down_ref,
    down_in_ref,
    up_in_ref,
    ut_ref,
    uzt_ref,
    a_ref,
    az_ref,
    lse_ref,
    lsez_ref,
    sums_ref,
):
    half = Place().half
    tail = slice(heads * HD, heads * HD + TAIL)

    def select(rising, falling, at):
        first, second = rising[at], falling[at]
        return jnp.where(half, second, first), jnp.where(half, first, second)

    z_part, own_part = select(up_ref, down_ref, tail)
    help_part, ahead_part = select(up_in_ref, down_in_ref, tail)
    rows, shares = [], []
    for first, second in (
        (joined_rows(own_part), joined_rows(help_part) + bias_ref[HELPED : HELPED + 1]),
        (joined_rows(ahead_part), joined_rows(z_part)),
    ):
        highest = jnp.maximum(first, second)
        total = highest + jnp.log(jnp.exp(first - highest) + jnp.exp(second - highest))
        rows.append(total)
        shares.append((jnp.exp(first - total), jnp.exp(second - total)))
    lse_ref[...], lsez_ref[...] = (jnp.maximum(total, -1e9) for total in rows)
    sums = [jnp.zeros((8, BLOCK), jnp.float32)] * 4
    for h in range(heads):
        at, row = rows_of(h), slice(h, h + 1)
        z_out, own_out = select(up_ref, down_ref, at)
        help_out, ahead_out = select(up_in_ref, down_in_ref, at)
        for n, (first, second, u_ref, target) in enumerate(
            ((own_out, help_out, ut_ref, a_ref), (ahead_out, z_out, uzt_ref, az_ref))
        ):
            out = (
                first.astype(jnp.float32) * shares[n][0][row] + second.astype(jnp.float32) * shares[n][1][row]
            ).astype(jnp.bfloat16)
            target[at] = out
            wide = out.astype(jnp.float32)
            sums[2 * n] += (wide * wide).reshape(HD // 8, 8, BLOCK).sum(axis=0)
            sums[2 * n + 1] += (wide * u_ref[at].astype(jnp.float32)).reshape(HD // 8, 8, BLOCK).sum(axis=0)
    sums_ref[...] = stack_rows([part.sum(axis=0, keepdims=True) for part in sums])


def norm_rows(sums, first):
    inverse = lax.rsqrt(sums[first : first + 1] / WIDTH + EPSILON)
    return inverse, inverse**3 * sums[first + 1 : first + 2] / WIDTH


def upstream_part(norm, u, a):
    inverse, factor = norm
    wide = a.astype(jnp.float32)
    grad = (inverse * u.astype(jnp.float32) - wide * factor).astype(jnp.bfloat16)
    return grad, jnp.sum(grad.astype(jnp.float32) * wide, axis=0, keepdims=True)


def side_queries_kernel(heads, q_ref, up_ref, down_ref, out_ref):
    place = Place()
    for h in range(heads):
        at = rows_of(h)
        qz = jnp.where(place.half, up_ref[FIRST, at], down_ref[FIRST, at])
        out_ref[:, at] = jnp.where(place.odd, q_ref[:, at], qz)


def relay_kernel(heads, up_ref, down_ref, out_ref):
    half = Place().half
    for h in range(heads):
        at = rows_of(h)
        out_ref[:, at] = jnp.where(half, up_ref[FIRST, at], down_ref[FIRST, at])


def back_kernel(
    heads,
    bias_ref,
    sums_ref,
    a_ref,
    az_ref,
    lse_ref,
    lsez_ref,
    ut_ref,
    uzt_ref,
    up_ref,
    down_ref,
    kx_ref,
    vx_ref,
    ez_ref,
    ex_ref,
    mz_ref,
    mx_ref,
    up_out_ref,
    down_out_ref,
    side_out_ref,
    dsx_ref,
    grad_ref,
    gz_ref,
    delta_ref,
    deltaz_ref,
):
    place = Place()
    odd, half = place.odd, place.half
    sums = sums_ref[...]
    own_norm, z_norm = norm_rows(sums, 0), norm_rows(sums, 2)
    lse, z_lse = lse_ref[...], lsez_ref[...]
    scales = (
        jnp.exp(mz_ref[...] - z_lse + bias_ref[FAR : FAR + 1]),
        jnp.exp(mx_ref[...] - jnp.where(odd, lse, z_lse) + bias_ref[SIDE : SIDE + 1]),
    )
    group = range(heads)
    deltas, z_deltas = [], []
    parts, products, scores = [], [], []
    for h in group:
        at = rows_of(h)
        grad, delta = upstream_part(own_norm, ut_ref[at], a_ref[at])
        gz, deltaz = upstream_part(z_norm, uzt_ref[at], az_ref[at])
        grad_ref[at], gz_ref[at] = grad, gz
        deltas.append(delta)
        z_deltas.append(deltaz)
        gx, deltax = jnp.where(odd, grad, gz), jnp.where(odd, delta, deltaz)
        side_out_ref[at] = gx
        parts.append(((gz, gx), (deltaz, deltax)))
    for h, ((gz, gx), _) in zip(group, parts):
        at = rows_of(h)
        v2 = jnp.where(half, down_ref[SECOND, at], up_ref[SECOND, at])
        products.append((mm(v2, gz, NN), mm(vx_ref[:, at], gx, NN)))
    for h, (_, delta), product in zip(group, parts, products):
        tiles = []
        for n, e_ref in enumerate((ez_ref, ex_ref)):
            weights = e_ref[rows_of(h)] * scales[n][h : h + 1]
            tiles.append((weights * (product[n] - delta[n]) * SCALE).astype(jnp.bfloat16))
        dsx_ref[rows_of(h)] = tiles[1]
        scores.append(tiles)
    for h, ((gz, _), _), (dz, dx) in zip(group, parts, scores):
        at = rows_of(h)
        k2 = jnp.where(half, down_ref[FIRST, at], up_ref[FIRST, at])
        joined = jnp.concatenate([dz, jnp.where(odd, jnp.zeros_like(dx), dx)], axis=0)
        dqz = mm(jnp.concatenate([k2, kx_ref[:, at]], axis=0), joined, TN).astype(jnp.bfloat16)
        up_out_ref[at] = jnp.where(half, gz, dqz)
        down_out_ref[at] = jnp.where(half, dqz, gz)
    delta, deltaz = stack_rows(deltas), stack_rows(z_deltas)
    delta_ref[...], deltaz_ref[...] = delta, deltaz
    tail = slice(heads * HD, heads * HD + 2 * TAIL)
    z_tail = jnp.concatenate([split_rows(z_lse), split_rows(deltaz)], axis=0)
    own_tail = jnp.concatenate([split_rows(lse), split_rows(delta)], axis=0)
    up_out_ref[tail] = jnp.where(half, z_tail, jnp.zeros_like(z_tail))
    down_out_ref[tail] = jnp.where(half, jnp.zeros_like(z_tail), z_tail)
    side_out_ref[tail] = jnp.where(odd, own_tail, z_tail)


def local_back_kernel(
    heads,
    bias_ref,
    sums_ref,
    q_ref,
    k_ref,
    v_ref,
    a_ref,
    lse_ref,
    lsez_ref,
    grad_ref,
    gz_ref,
    delta_ref,
    deltaz_ref,
    en_ref,
    mn_ref,
    dsx_ref,
    kx_ref,
    up_ref,
    down_ref,
    normed_ref,
    dq_ref,
    dk_ref,
    dv_ref,
):
    place = Place()
    odd, half = place.odd, place.half
    inverse, _ = norm_rows(sums_ref[...], 0)
    lse, z_lse = lse_ref[...], lsez_ref[...] - bias_ref[KEY_NEAR : KEY_NEAR + 1]
    near_scale = jnp.exp(mn_ref[...] - lse + bias_ref[NEAR : NEAR + 1])
    causal = causal_mask()
    for h in range(heads):
        at, row = rows_of(h), slice(h, h + 1)
        normed_ref[:, at] = (a_ref[at].astype(jnp.float32) * inverse).astype(jnp.bfloat16).T
        up_a, down_a = up_ref[FIRST, at], down_ref[FIRST, at]
        k2, qz = jnp.where(half, down_a, up_a), jnp.where(half, up_a, down_a)
        v2 = jnp.where(half, down_ref[SECOND, at], up_ref[SECOND, at])
        q, k, v, grad, gz = q_ref[:, at], k_ref[:, at], v_ref[:, at], grad_ref[at], gz_ref[at]
        queries, grads = jnp.concatenate([q, qz], axis=0), jnp.concatenate([grad, gz], axis=1)
        both = score_tile(k, queries)
        products = mm(v, grads, NN)
        own = jnp.exp(jnp.where(causal, both[:, :BLOCK], NEG_BIG) - lse[row])
        ahead = jnp.exp(both[:, BLOCK:] - z_lse[row])
        near = en_ref[at] * near_scale[row]
        own_ds = (own * (products[:, :BLOCK] - delta_ref[row]) * SCALE).astype(jnp.bfloat16)
        ahead_ds = (ahead * (products[:, BLOCK:] - deltaz_ref[row]) * SCALE).astype(jnp.bfloat16)
        near_ds = (near * (mm(v2, grad, NN) - delta_ref[row]) * SCALE).astype(jnp.bfloat16)
        dk_ref[:, at] = mm(jnp.concatenate([own_ds, ahead_ds], axis=1), queries, NN)
        probs = jnp.concatenate([own, ahead], axis=1).astype(jnp.bfloat16)
        dv_ref[:, at] = mm(probs, grads, NT)
        dsx = jnp.where(odd, dsx_ref[at], jnp.zeros_like(dsx_ref[at]))
        dq_ref[:, at] = mm(own_ds, k, TN) + mm(
            jnp.concatenate([near_ds, dsx], axis=0), jnp.concatenate([k2, kx_ref[:, at]], axis=0), TN
        )


def key_scores_kernel(heads, bias_ref, k_ref, far_ref, side_ref, out_ref):
    for h in range(heads):
        at = rows_of(h)
        both = score_tile(k_ref[:, at], jnp.concatenate([far_ref[:, at], side_ref[:, at]], axis=0))
        out_ref[0, at] = both[:, :BLOCK] + bias_ref[KEY_FAR : KEY_FAR + 1]
        out_ref[1, at] = both[:, BLOCK:] + bias_ref[KEY_SIDE : KEY_SIDE + 1]


def final_kernel(
    heads,
    scores_ref,
    far_ref,
    sideq_ref,
    up_ref,
    down_ref,
    side_ref,
    v_ref,
    dq_own_ref,
    dk_own_ref,
    dv_own_ref,
    dq_ref,
    dk_ref,
    dv_ref,
):
    place = Place()
    half = place.half
    behind = (place.me >= 2).astype(jnp.float32)
    first = slice(heads * HD, heads * HD + TAIL)
    second = slice(heads * HD + TAIL, heads * HD + 2 * TAIL)
    lse, delta = (
        (joined_rows(jnp.where(half, up_ref[part], down_ref[part])), joined_rows(side_ref[part]))
        for part in (first, second)
    )
    group = range(heads)
    grads, products, tiles = [], [], []
    for h in group:
        at = rows_of(h)
        up, down = up_ref[at], down_ref[at]
        dqz = jnp.where(half, down, up).T.astype(jnp.float32) * behind
        dq_ref[:, at] = (dq_own_ref[:, at] + dqz).astype(jnp.bfloat16)
        grads.append(jnp.concatenate([jnp.where(half, up, down), side_ref[at]], axis=1))
    for h, grad in zip(group, grads):
        products.append(mm(v_ref[:, rows_of(h)], grad, NN))
    for h, product in zip(group, products):
        row = slice(h, h + 1)
        probs = [jnp.exp(scores_ref[n, rows_of(h)] - lse[n][row]) for n in range(2)]
        scores = [
            probs[n] * (product[:, n * BLOCK : (n + 1) * BLOCK] - delta[n][row]) * SCALE for n in range(2)
        ]
        tiles.append([jnp.concatenate(pair, axis=1).astype(jnp.bfloat16) for pair in (probs, scores)])
    for h, grad, (probs, scores) in zip(group, grads, tiles):
        at = rows_of(h)
        queries = jnp.concatenate([far_ref[:, at], sideq_ref[:, at]], axis=0)
        dk_ref[:, at] = (dk_own_ref[:, at] + mm(scores, queries, NN)).astype(jnp.bfloat16)
        dv_ref[:, at] = (dv_own_ref[:, at] + mm(probs, grad, NT)).astype(jnp.bfloat16)


def call(kernel, heads, flags, arrays, outs, flops, space=pltpu.VMEM, scratch=(), after=()):
    moved = sum(math.prod(a.shape) * a.dtype.itemsize for a in (*arrays, *outs)) if flops else 0
    return pl.pallas_call(
        lambda *refs: kernel(heads, *refs[len(after) :]),
        out_shape=outs,
        in_specs=[pl.BlockSpec(memory_space=pl.ANY)] * len(after)
        + [pl.BlockSpec(memory_space=pltpu.SMEM)] * len(flags)
        + [pl.BlockSpec(memory_space=space)] * len(arrays),
        out_specs=[pl.BlockSpec(memory_space=pltpu.VMEM)] * len(outs),
        scratch_shapes=scratch,
        compiler_params=pltpu.CompilerParams(vmem_limit_bytes=24 * 2**20),
        cost_estimate=pl.CostEstimate(flops=flops, bytes_accessed=moved, transcendentals=0),
    )(*after, *flags, *arrays)


def cycles(blocks, members):
    route = []
    for block in range(blocks):
        for member in range(members):
            rising = member < members // 2
            other = member + members // 2 if rising else member - members // 2
            target = block + 2 if rising else block - 2
            inside = 0 <= target < blocks
            route.append(
                (block * members + member, target * members + member if inside else block * members + other)
            )
    return route


def meeting_shards(queries, keys, values, pattern, upstream):
    tokens, width = queries.shape
    heads = width // HD
    blocks, members = lax.axis_size("ctx"), lax.axis_size("head")
    unit = heads * 2 * BLOCK**3
    rising = cycles(blocks, members)
    falling = [(target, source) for source, target in rising]

    def cycle(up_array, down_array):
        return lax.ppermute(up_array, ("ctx", "head"), rising), lax.ppermute(
            down_array, ("ctx", "head"), falling
        )

    def swap(array):
        return lax.ppermute(array, "ctx", [(i, i ^ 1) for i in range(blocks)])

    def ring(array, distance):
        return lax.ppermute(array, "ctx", [(i, (i + distance) % blocks) for i in range(blocks)])

    def struct(*shape, dtype=jnp.bfloat16):
        return jax.ShapeDtypeStruct(shape, dtype)

    wide = struct(tokens, width, dtype=jnp.float32)
    wide_t = struct(width, tokens, dtype=jnp.float32)
    flat, flat_t = struct(tokens, width), struct(width, tokens)
    message = struct(width + TAIL, tokens)
    rows = struct(8, tokens, dtype=jnp.float32)

    payload = call(
        payload_kernel,
        heads,
        (),
        [pltpu.with_memory_space_constraint(a, pltpu.HBM) for a in (queries, keys, values, upstream)],
        [pltpu.VMEM((2 * tokens, width), jnp.bfloat16)] * 2,
        0,
        space=pltpu.HBM,
        scratch=(pltpu.SemaphoreType.DMA((4,)),),
    )
    received = cycle(*payload)
    keys_x, values_x = swap(keys), swap(values)
    diagonal, diagonal_lse, upstream_t, bias = call(
        diagonal_kernel,
        heads,
        (pattern,),
        (queries, keys, values, upstream),
        (wide_t, rows, flat_t, rows),
        3 * unit,
        after=(payload[0],),
    )
    up_out, down_out, *kept = call(
        forward_kernel,
        heads,
        (),
        (bias, *received, queries, keys_x, values_x, diagonal, diagonal_lse),
        (message, message, wide_t, wide_t, wide_t, rows, rows, rows),
        6 * unit,
    )
    ez, ex, en, mz, mx, mn = kept
    up_in, down_in = cycle(up_out, down_out)
    (side_queries,) = call(
        side_queries_kernel, heads, (), (queries, *received), (flat,), 0, after=(mn,)
    )
    side_queries = swap(side_queries)
    (far_queries,) = call(relay_kernel, heads, (), received, (flat,), 0, after=(mn,))
    far_queries = lax.ppermute(far_queries, "ctx", [(i, i - 2) for i in range(2, blocks - 2)])
    (upstream_zt,) = call(transpose_kernel, heads, (), received, (flat_t,), 0, after=(mn,))
    attention, attention_z, lse, lse_z, sums = call(
        merge_kernel,
        heads,
        (),
        (bias, up_out, down_out, down_in, up_in, upstream_t, upstream_zt),
        (flat_t, flat_t, rows, rows, rows),
        unit // 64,
    )
    others = [
        lax.ppermute(sums, "head", [(i, i ^ step) for i in range(members)]) for step in (2, 1, 3)
    ]
    sums = functools.reduce(jnp.add, others, sums)
    longer = struct(width + 2 * TAIL, tokens)
    up_out, down_out, side_out, side_ds, grad_t, grad_zt, delta, delta_z = call(
        back_kernel,
        heads,
        (),
        (bias, sums, attention, attention_z, lse, lse_z, upstream_t, upstream_zt, *received, keys_x, values_x)
        + (ez, ex, mz, mx),
        (longer, longer, longer, flat_t, flat_t, flat_t, rows, rows),
        0,
        after=(side_queries, far_queries),
    )
    returned = cycle(up_out, down_out)
    side_grads = swap(side_out)
    normed, dq_own, dk_own, dv_own = call(
        local_back_kernel,
        heads,
        (),
        (bias, sums, queries, keys, values, attention, lse, lse_z, grad_t, grad_zt, delta, delta_z, en, mn)
        + (side_ds, keys_x, *received),
        (flat, wide, wide, wide),
        0,
    )
    (key_scores,) = call(
        key_scores_kernel,
        heads,
        (),
        (bias, keys, far_queries, side_queries),
        (struct(2, width, tokens, dtype=jnp.float32),),
        0,
    )
    grad_queries, grad_keys, grad_values = call(
        final_kernel,
        heads,
        (),
        (key_scores, far_queries, side_queries, *returned, side_grads, values, dq_own, dk_own, dv_own),
        (flat, flat, flat),
        6 * unit,
    )
    return (normed, grad_queries, grad_keys, grad_values)


def shards(queries, keys, values, pattern, upstream):
    fits = lax.axis_size("ctx") == 8 and lax.axis_size("head") == 4 and queries.shape == (BLOCK, 8 * HD)
    if fits:
        return meeting_shards(queries, keys, values, pattern, upstream)
    return generic_shards(queries, keys, values, pattern, upstream)


def solution(mesh):
    return jax.shard_map(
        shards,
        mesh=mesh,
        in_specs=(P("ctx", "head"), P("ctx", "head"), P("ctx", "head"), P(), P("ctx", "head")),
        out_specs=(P("ctx", "head"), P("ctx", "head"), P("ctx", "head"), P("ctx", "head")),
        check_vma=False,
    )
```

```python
import functools
import math

import jax
import jax.numpy as jnp
from jax import lax
from jax.experimental import pallas as pl
from jax.experimental.pallas import tpu as pltpu
from jax.sharding import PartitionSpec as P

HD = 128
BLOCK = 128
LEVELS = 7
WIDTH = 4096


NEG_BIG = -1e30
EPSILON = 1e-06


def shifted(block, axis, distance):
    devices = range(lax.axis_size(axis))
    route = [(i - distance, i) for i in devices if i - distance in devices]
    return lax.ppermute(block, axis, route)


def for_sending(x):
    return jax.tree.map(lambda a: a.astype(jnp.bfloat16) if a.dtype == jnp.float32 else a, x)


def route_table(blocks, levels):
    routing = []
    for query_block in range(blocks):
        for level_index in range(levels + 1):
            if level_index == levels:
                routing.append((0, query_block))
            else:
                distance = 2**level_index
                routing.append(
                    (-((query_block - distance) // blocks), (query_block - distance) % blocks)
                )
    return routing


def pair_grads(
    query_tiles, grad_tiles, lse_tiles, delta_tiles, key_tiles, value_tiles, keep_mask, score_scale
):
    scores = (
        jnp.einsum("pqhd,pkhd->phqk", query_tiles, key_tiles, preferred_element_type=jnp.float32)
        * score_scale
    )
    scores = jnp.where(keep_mask[:, None], scores, NEG_BIG)
    weights = jnp.exp(scores - lse_tiles[..., None])
    prob_tiles = weights.astype(jnp.bfloat16)
    grad_probs = jnp.einsum(
        "pqhd,pkhd->phqk", grad_tiles, value_tiles, preferred_element_type=jnp.float32
    )
    dscore = (weights * (grad_probs - delta_tiles[..., None]) * score_scale).astype(jnp.bfloat16)
    return (dscore, prob_tiles)


def key_grads(dscore, prob_tiles, query_tiles, grad_tiles):
    key_part = jnp.einsum(
        "phqk,pqhd->pkhd", dscore, query_tiles, preferred_element_type=jnp.float32
    )
    value_part = jnp.einsum(
        "phqk,pqhd->pkhd", prob_tiles, grad_tiles, preferred_element_type=jnp.float32
    )
    return jnp.stack((key_part, value_part))


def collect(partials, targets, blocks):
    pieces = []
    for key_index in range(blocks):
        summed = jnp.zeros((2,) + partials.shape[2:], jnp.float32)
        for row_index, target in enumerate(targets):
            if target == key_index:
                summed = summed + partials[:, row_index]
        pieces.append(summed)
    return jnp.stack(pieces, axis=1)


def generic_shards(queries, keys, values, pattern, upstream):
    tokens_here = queries.shape[0]
    heads_here = queries.shape[1] // HD
    blocks = tokens_here // BLOCK
    slot_count = LEVELS + 1
    pair_count = blocks * slot_count
    score_scale = HD ** (-0.5)
    ctx_count = lax.axis_size("ctx")
    device_index = lax.axis_index("ctx")
    routing = route_table(blocks, LEVELS)
    offsets = sorted(
        set((route_entry[0] for route_entry in routing if 0 < route_entry[0] < ctx_count))
    )
    tile_shape = (blocks, BLOCK, heads_here, HD)
    query_blocks = queries.reshape(tile_shape)
    own_pairs = jnp.stack((keys, values)).reshape((2,) + tile_shape)
    sources = {0: own_pairs}
    for offset in offsets:
        fetched = shifted(jnp.stack((keys, values)), "ctx", offset)
        sources[offset] = fetched.reshape((2,) + tile_shape)
    empty_tile = jnp.zeros((2, BLOCK, heads_here, HD), jnp.bfloat16)
    gathered = []
    for source, key_index in routing:
        if source in sources:
            gathered.append(sources[source][:, key_index])
        else:
            gathered.append(empty_tile)
    pair_kv = jnp.stack(gathered, axis=1)
    key_tiles = pair_kv[0]
    value_tiles = pair_kv[1]
    key_stack = key_tiles.reshape((blocks, slot_count) + tile_shape[1:])
    value_stack = value_tiles.reshape((blocks, slot_count) + tile_shape[1:])
    own_rows = lax.dynamic_slice_in_dim(pattern, device_index * blocks, blocks, 0)
    positions = jnp.arange(BLOCK)
    causal = positions[None, :] <= positions[:, None]
    self_slot = jnp.arange(slot_count) == LEVELS
    tile_keep = (own_rows >= 0)[:, :, None, None] & (
        jnp.logical_not(self_slot)[None, :, None, None] | causal[None, None]
    )
    scores = (
        jnp.einsum("bqhd,bskhd->bhqsk", query_blocks, key_stack, preferred_element_type=jnp.float32)
        * score_scale
    )
    scores = jnp.where(jnp.transpose(tile_keep, (0, 2, 1, 3))[:, None], scores, NEG_BIG)
    highest = jnp.max(scores, axis=(3, 4))
    log_total = highest + jnp.log(jnp.sum(jnp.exp(scores - highest[..., None, None]), axis=(3, 4)))
    prob_stack = jnp.exp(scores - log_total[..., None, None]).astype(jnp.bfloat16)
    attention = jnp.einsum(
        "bhqsk,bskhd->bqhd", prob_stack, value_stack, preferred_element_type=jnp.float32
    ).astype(jnp.bfloat16)
    attn_wide = attention.reshape(tokens_here, heads_here * HD).astype(jnp.float32)
    square_sum = lax.psum(jnp.sum(attn_wide * attn_wide, axis=1), "head")
    inverse = lax.rsqrt(square_sum / WIDTH + EPSILON)
    normed = (attn_wide * inverse[:, None]).astype(jnp.bfloat16)
    upstream_wide = upstream.astype(jnp.float32)
    cross_term = lax.psum(jnp.sum(upstream_wide * attn_wide, axis=1), "head")
    grad_attn = (
        inverse[:, None] * upstream_wide - attn_wide * (inverse**3 * cross_term / WIDTH)[:, None]
    ).astype(jnp.bfloat16)
    row_delta = jnp.sum(
        (grad_attn.astype(jnp.float32) * attn_wide).reshape(tokens_here, heads_here, HD), axis=2
    )
    row_delta = jnp.transpose(row_delta.reshape(blocks, BLOCK, heads_here), (0, 2, 1))

    def spread(array):
        return jnp.broadcast_to(array[:, None], (blocks, slot_count) + array.shape[1:]).reshape(
            (pair_count,) + array.shape[1:]
        )

    grad_blocks = grad_attn.reshape(tile_shape)
    query_pairs = spread(query_blocks)
    grad_pairs = spread(grad_blocks)
    keep_pairs = tile_keep.reshape(pair_count, BLOCK, BLOCK)
    dscore, prob_pairs = pair_grads(
        query_pairs,
        grad_pairs,
        spread(log_total),
        spread(row_delta),
        key_tiles,
        value_tiles,
        keep_pairs,
        score_scale,
    )
    grad_query = jnp.einsum(
        "phqk,pkhd->pqhd", dscore, key_tiles, preferred_element_type=jnp.float32
    )
    grad_query = jnp.sum(grad_query.reshape((blocks, slot_count) + tile_shape[1:]), axis=1)
    grad_queries = grad_query.astype(jnp.bfloat16).reshape(tokens_here, heads_here * HD)
    local_rows = [row_index for row_index in range(pair_count) if routing[row_index][0] == 0]
    chosen = jnp.array(local_rows, jnp.int32)
    local_terms = key_grads(
        dscore[chosen], prob_pairs[chosen], query_pairs[chosen], grad_pairs[chosen]
    )
    key_sum = collect(local_terms, [routing[row_index][1] for row_index in local_rows], blocks)
    for offset in offsets:
        remote_rows = [
            row_index for row_index in range(pair_count) if routing[row_index][0] == offset
        ]
        chosen = jnp.array(remote_rows, jnp.int32)
        remote_terms = key_grads(
            dscore[chosen], prob_pairs[chosen], query_pairs[chosen], grad_pairs[chosen]
        )
        outgoing = collect(
            remote_terms, [routing[row_index][1] for row_index in remote_rows], blocks
        )
        key_sum = key_sum + shifted(for_sending(outgoing), "ctx", -offset).astype(outgoing.dtype)
    grad_keys = key_sum[0].astype(jnp.bfloat16).reshape(tokens_here, heads_here * HD)
    grad_values = key_sum[1].astype(jnp.bfloat16).reshape(tokens_here, heads_here * HD)
    return (normed, grad_queries, grad_keys, grad_values)


NT = (((1,), (1,)), ((), ()))
NN = (((1,), (0,)), ((), ()))
TN = (((0,), (0,)), ((), ()))
SCALE = HD ** (-0.5)
TAIL = 32


NEAR, FAR, SIDE, HELPED, LOCAL, KEY_NEAR, KEY_FAR, KEY_SIDE = range(8)


class Place:
    def __init__(self):
        self.me = lax.axis_index("ctx")
        self.odd = lax.rem(self.me, 2) == 1
        self.half = lax.axis_index("head") >= lax.axis_size("head") // 2


def bias_rows(pattern_ref):
    place = Place()
    me, odd, even = place.me, place.odd, jnp.logical_not(place.odd)
    blocks = pattern_ref.shape[0]
    ahead = jnp.minimum(me + 2, blocks - 1)
    has_ahead = me + 2 < blocks
    ahead_side = jnp.logical_and(has_ahead, pattern_ref[ahead, 0] >= 0)
    own_side = pattern_ref[me, 0] >= 0
    local = jnp.logical_and(odd, own_side)

    def ahead_holds(distance, level):
        entry = pattern_ref[jnp.minimum(me + distance, blocks - 1), level]
        return jnp.logical_and(me + distance < blocks, entry >= 0)

    held = {
        NEAR: pattern_ref[me, 1] >= 0,
        FAR: jnp.logical_and(has_ahead, pattern_ref[ahead, 2] >= 0),
        SIDE: jnp.logical_or(local, jnp.logical_and(even, ahead_side)),
        HELPED: jnp.logical_or(pattern_ref[me, 2] >= 0, jnp.logical_and(even, own_side)),
        LOCAL: local,
        KEY_NEAR: ahead_holds(2, 1),
        KEY_FAR: ahead_holds(4, 2),
        KEY_SIDE: ahead_holds(1, 0),
    }
    row = lax.broadcasted_iota(jnp.int32, (8, BLOCK), 0)
    rows = jnp.zeros((8, BLOCK), jnp.float32)
    for index, flag in held.items():
        rows = jnp.where(row == index, jnp.where(flag, 0.0, NEG_BIG), rows)
    return rows


def mm(a, b, dims):
    return lax.dot_general(a, b, dims, preferred_element_type=jnp.float32)


def rows_of(h):
    return slice(h * HD, (h + 1) * HD)


def causal_mask():
    keys = lax.broadcasted_iota(jnp.int32, (BLOCK, BLOCK), 0)
    return keys <= lax.broadcasted_iota(jnp.int32, (BLOCK, BLOCK), 1)


def split_rows(rows):
    first = rows.astype(jnp.bfloat16).astype(jnp.float32)
    second = (rows - first).astype(jnp.bfloat16).astype(jnp.float32)
    third = rows - first - second
    return jnp.concatenate([first, second, third, jnp.zeros_like(rows)], axis=0).astype(jnp.bfloat16)


def joined_rows(tile):
    wide = tile.astype(jnp.float32)
    return wide[0:8] + wide[8:16] + wide[16:24]


def stack_rows(rows):
    return jnp.concatenate(rows + [jnp.zeros((1, BLOCK), jnp.float32)] * (8 - len(rows)), axis=0)


def score_tile(keys, queries):
    return mm(keys, queries, NT) * SCALE


def softmax_parts(pairs):
    tops = [scores.max(axis=0, keepdims=True) for scores, _ in pairs]
    weights = [jnp.exp(scores - top) for (scores, _), top in zip(pairs, tops)]
    totals = [w.sum(axis=0, keepdims=True) for w in weights]
    outs = [
        mm(value, w.astype(jnp.bfloat16), TN) * (1.0 / total)
        for (_, value), w, total in zip(pairs, weights, totals)
    ]
    return [(out, top, top + jnp.log(total), w) for out, top, total, w in zip(outs, tops, totals, weights)]


FIRST, SECOND = slice(0, BLOCK), slice(BLOCK, 2 * BLOCK)


def payload_kernel(heads, q_ref, k_ref, v_ref, u_ref, up_ref, down_ref, sems):
    half = Place().half
    top, bottom = pl.ds(0, BLOCK), pl.ds(BLOCK, BLOCK)

    def move(sources):
        targets = (up_ref.at[top], up_ref.at[bottom], down_ref.at[top], down_ref.at[bottom])
        copies = [
            pltpu.make_async_copy(source, target, sems.at[n])
            for n, (source, target) in enumerate(zip(sources, targets))
        ]
        for copy in copies:
            copy.start()
        for copy in copies:
            copy.wait()

    @pl.when(jnp.logical_not(half))
    def _():
        move((k_ref, v_ref, q_ref, u_ref))

    @pl.when(half)
    def _():
        move((q_ref, u_ref, k_ref, v_ref))


def diagonal_kernel(heads, pattern_ref, q_ref, k_ref, v_ref, u_ref, out_ref, lse_ref, ut_ref, bias_ref):
    bias_ref[...] = bias_rows(pattern_ref)
    causal = causal_mask()
    rows = []
    for h in range(heads):
        at = rows_of(h)
        scores = jnp.where(causal, score_tile(k_ref[:, at], q_ref[:, at]), NEG_BIG)
        ((out, _, lse, _),) = softmax_parts([(scores, v_ref[:, at])])
        out_ref[at] = out
        rows.append(lse)
        ut_ref[at] = u_ref[:, at].T
    lse_ref[...] = stack_rows(rows)


def merged(parts):
    highest = functools.reduce(jnp.maximum, [lse for _, lse in parts])
    total = highest + jnp.log(functools.reduce(jnp.add, [jnp.exp(lse - highest) for _, lse in parts]))
    return functools.reduce(jnp.add, [out * jnp.exp(lse - total) for out, lse in parts]), total


def forward_kernel(
    heads,
    bias_ref,
    up_ref,
    down_ref,
    q_ref,
    kx_ref,
    vx_ref,
    out_ref,
    lse_ref,
    up_out_ref,
    down_out_ref,
    ez_ref,
    ex_ref,
    en_ref,
    mz_ref,
    mx_ref,
    mn_ref,
):
    place = Place()
    odd, half = place.odd, place.half
    near, far, side, local = (bias_ref[n : n + 1] for n in (NEAR, FAR, SIDE, LOCAL))
    before = lse_ref[...]
    step = heads
    z_rows, own_rows, z_tops, x_tops, n_tops = [], [], [], [], []
    for start in range(0, heads, step):
        group = range(start, start + step)
        scores, weights = [], []
        for h in group:
            at = rows_of(h)
            up_a, down_a = up_ref[FIRST, at], down_ref[FIRST, at]
            k2, qz = jnp.where(half, down_a, up_a), jnp.where(half, up_a, down_a)
            q = q_ref[:, at]
            both = score_tile(k2, jnp.concatenate([qz, q], axis=0))
            x = score_tile(kx_ref[:, at], jnp.where(odd, q, qz))
            scores.append((both[:, :BLOCK] + far, x + side, both[:, BLOCK:] + near))
        for h, (z, x, n) in zip(group, scores):
            z_top, x_top, n_top = (tile.max(axis=0, keepdims=True) for tile in (z, x, n))
            both = jnp.maximum(z_top, x_top)
            z_top, x_top = jnp.where(odd, z_top, both), jnp.where(odd, x_top, both)
            z, x, n = jnp.exp(z - z_top), jnp.exp(x - x_top), jnp.exp(n - n_top)
            at = rows_of(h)
            ez_ref[at], ex_ref[at], en_ref[at] = z, x, n
            z_sum, x_sum, n_sum = (tile.sum(axis=0, keepdims=True) for tile in (z, x, n))
            z_sum = z_sum + jnp.where(odd, 0.0, x_sum)
            x_sum = jnp.maximum(x_sum, 1.0)
            for tops, top in ((z_tops, z_top), (x_tops, x_top), (n_tops, n_top)):
                tops.append(top)
            z_rows.append(z_top + jnp.log(z_sum))
            parts = (before[h : h + 1], n_top + jnp.log(n_sum) + near, x_top + jnp.log(x_sum) + local)
            highest = functools.reduce(jnp.maximum, parts)
            total = highest + jnp.log(functools.reduce(jnp.add, [jnp.exp(part - highest) for part in parts]))
            own_rows.append(total)
            d_share, n_share, x_share = (jnp.exp(part - total) for part in parts)
            z_scale = 1.0 / z_sum
            sent = [z * z_scale, x * jnp.where(odd, 0.0, z_scale)]
            kept = [n * (n_share / n_sum), x * (x_share / x_sum)]
            joined = [jnp.concatenate(tiles, axis=0).astype(jnp.bfloat16) for tiles in (sent, kept)]
            weights.append((jnp.concatenate(joined, axis=1), d_share))
        for h, (joined, d_share) in zip(group, weights):
            at = rows_of(h)
            v2 = jnp.where(half, down_ref[SECOND, at], up_ref[SECOND, at])
            out = mm(jnp.concatenate([v2, vx_ref[:, at]], axis=0), joined, TN)
            out_z = out[:, :BLOCK].astype(jnp.bfloat16)
            own = (out_ref[at] * d_share + out[:, BLOCK:]).astype(jnp.bfloat16)
            up_out_ref[at] = jnp.where(half, own, out_z)
            down_out_ref[at] = jnp.where(half, out_z, own)
    tail = slice(heads * HD, heads * HD + TAIL)
    z_tail, own_tail = split_rows(stack_rows(z_rows)), split_rows(stack_rows(own_rows))
    up_out_ref[tail] = jnp.where(half, own_tail, z_tail)
    down_out_ref[tail] = jnp.where(half, z_tail, own_tail)
    mz_ref[...] = stack_rows(z_tops)
    mx_ref[...] = stack_rows(x_tops)
    mn_ref[...] = stack_rows(n_tops)


def transpose_kernel(heads, up_ref, down_ref, out_ref):
    half = Place().half
    for h in range(heads):
        at = rows_of(h)
        out_ref[at] = jnp.where(half, up_ref[SECOND, at], down_ref[SECOND, at]).T


def merge_kernel(
    heads,
    bias_ref,
    up_ref,
    down_ref,
    up_in_ref,
    down_in_ref,
    ut_ref,
    uzt_ref,
    a_ref,
    az_ref,
    lse_ref,
    lsez_ref,
    sums_ref,
):
    half = Place().half
    tail = slice(heads * HD, heads * HD + TAIL)

    def select(rising, falling, at):
        first, second = rising[at], falling[at]
        return jnp.where(half, second, first), jnp.where(half, first, second)

    z_part, own_part = select(up_ref, down_ref, tail)
    help_part, ahead_part = select(up_in_ref, down_in_ref, tail)
    rows, shares = [], []
    for first, second in (
        (joined_rows(own_part), joined_rows(help_part) + bias_ref[HELPED : HELPED + 1]),
        (joined_rows(ahead_part), joined_rows(z_part)),
    ):
        highest = jnp.maximum(first, second)
        total = highest + jnp.log(jnp.exp(first - highest) + jnp.exp(second - highest))
        rows.append(total)
        shares.append((jnp.exp(first - total), jnp.exp(second - total)))
    lse_ref[...], lsez_ref[...] = (jnp.maximum(total, -1e9) for total in rows)
    sums = [jnp.zeros((8, BLOCK), jnp.float32)] * 4
    for h in range(heads):
        at, row = rows_of(h), slice(h, h + 1)
        z_out, own_out = select(up_ref, down_ref, at)
        help_out, ahead_out = select(up_in_ref, down_in_ref, at)
        for n, (first, second, u_ref, target) in enumerate(
            ((own_out, help_out, ut_ref, a_ref), (ahead_out, z_out, uzt_ref, az_ref))
        ):
            out = (
                first.astype(jnp.float32) * shares[n][0][row] + second.astype(jnp.float32) * shares[n][1][row]
            ).astype(jnp.bfloat16)
            target[at] = out
            wide = out.astype(jnp.float32)
            sums[2 * n] += (wide * wide).reshape(HD // 8, 8, BLOCK).sum(axis=0)
            sums[2 * n + 1] += (wide * u_ref[at].astype(jnp.float32)).reshape(HD // 8, 8, BLOCK).sum(axis=0)
    sums_ref[...] = stack_rows([part.sum(axis=0, keepdims=True) for part in sums])


def norm_rows(sums, first):
    inverse = lax.rsqrt(sums[first : first + 1] / WIDTH + EPSILON)
    return inverse, inverse**3 * sums[first + 1 : first + 2] / WIDTH


def upstream_part(norm, u, a):
    inverse, factor = norm
    wide = a.astype(jnp.float32)
    grad = (inverse * u.astype(jnp.float32) - wide * factor).astype(jnp.bfloat16)
    return grad, jnp.sum(grad.astype(jnp.float32) * wide, axis=0, keepdims=True)


def side_queries_kernel(heads, q_ref, up_ref, down_ref, out_ref):
    place = Place()
    for h in range(heads):
        at = rows_of(h)
        qz = jnp.where(place.half, up_ref[FIRST, at], down_ref[FIRST, at])
        out_ref[:, at] = jnp.where(place.odd, q_ref[:, at], qz)


def relay_kernel(heads, up_ref, down_ref, out_ref):
    half = Place().half
    for h in range(heads):
        at = rows_of(h)
        out_ref[:, at] = jnp.where(half, up_ref[FIRST, at], down_ref[FIRST, at])


def back_kernel(
    heads,
    bias_ref,
    sums_ref,
    a_ref,
    az_ref,
    lse_ref,
    lsez_ref,
    ut_ref,
    uzt_ref,
    up_ref,
    down_ref,
    kx_ref,
    vx_ref,
    ez_ref,
    ex_ref,
    mz_ref,
    mx_ref,
    up_out_ref,
    down_out_ref,
    side_out_ref,
    dsx_ref,
    grad_ref,
    gz_ref,
    delta_ref,
    deltaz_ref,
):
    place = Place()
    odd, half = place.odd, place.half
    sums = sums_ref[...]
    own_norm, z_norm = norm_rows(sums, 0), norm_rows(sums, 2)
    lse, z_lse = lse_ref[...], lsez_ref[...]
    scales = (
        jnp.exp(mz_ref[...] - z_lse + bias_ref[FAR : FAR + 1]),
        jnp.exp(mx_ref[...] - jnp.where(odd, lse, z_lse) + bias_ref[SIDE : SIDE + 1]),
    )
    group = range(heads)
    deltas, z_deltas = [], []
    parts, products, scores = [], [], []
    for h in group:
        at = rows_of(h)
        grad, delta = upstream_part(own_norm, ut_ref[at], a_ref[at])
        gz, deltaz = upstream_part(z_norm, uzt_ref[at], az_ref[at])
        grad_ref[at], gz_ref[at] = grad, gz
        deltas.append(delta)
        z_deltas.append(deltaz)
        gx, deltax = jnp.where(odd, grad, gz), jnp.where(odd, delta, deltaz)
        side_out_ref[at] = gx
        parts.append(((gz, gx), (deltaz, deltax)))
    for h, ((gz, gx), _) in zip(group, parts):
        at = rows_of(h)
        v2 = jnp.where(half, down_ref[SECOND, at], up_ref[SECOND, at])
        products.append((mm(v2, gz, NN), mm(vx_ref[:, at], gx, NN)))
    for h, (_, delta), product in zip(group, parts, products):
        tiles = []
        for n, e_ref in enumerate((ez_ref, ex_ref)):
            weights = e_ref[rows_of(h)] * scales[n][h : h + 1]
            tiles.append((weights * (product[n] - delta[n]) * SCALE).astype(jnp.bfloat16))
        dsx_ref[rows_of(h)] = tiles[1]
        scores.append(tiles)
    for h, ((gz, _), _), (dz, dx) in zip(group, parts, scores):
        at = rows_of(h)
        k2 = jnp.where(half, down_ref[FIRST, at], up_ref[FIRST, at])
        joined = jnp.concatenate([dz, jnp.where(odd, jnp.zeros_like(dx), dx)], axis=0)
        dqz = mm(jnp.concatenate([k2, kx_ref[:, at]], axis=0), joined, TN).astype(jnp.bfloat16)
        up_out_ref[at] = jnp.where(half, gz, dqz)
        down_out_ref[at] = jnp.where(half, dqz, gz)
    delta, deltaz = stack_rows(deltas), stack_rows(z_deltas)
    delta_ref[...], deltaz_ref[...] = delta, deltaz
    tail = slice(heads * HD, heads * HD + 2 * TAIL)
    z_tail = jnp.concatenate([split_rows(z_lse), split_rows(deltaz)], axis=0)
    own_tail = jnp.concatenate([split_rows(lse), split_rows(delta)], axis=0)
    up_out_ref[tail] = jnp.where(half, z_tail, jnp.zeros_like(z_tail))
    down_out_ref[tail] = jnp.where(half, jnp.zeros_like(z_tail), z_tail)
    side_out_ref[tail] = jnp.where(odd, own_tail, z_tail)


def local_back_kernel(
    heads,
    bias_ref,
    sums_ref,
    q_ref,
    k_ref,
    v_ref,
    a_ref,
    lse_ref,
    lsez_ref,
    grad_ref,
    gz_ref,
    delta_ref,
    deltaz_ref,
    en_ref,
    mn_ref,
    dsx_ref,
    kx_ref,
    up_ref,
    down_ref,
    normed_ref,
    dq_ref,
    dk_ref,
    dv_ref,
):
    place = Place()
    odd, half = place.odd, place.half
    inverse, _ = norm_rows(sums_ref[...], 0)
    lse, z_lse = lse_ref[...], lsez_ref[...] - bias_ref[KEY_NEAR : KEY_NEAR + 1]
    near_scale = jnp.exp(mn_ref[...] - lse + bias_ref[NEAR : NEAR + 1])
    causal = causal_mask()
    for h in range(heads):
        at, row = rows_of(h), slice(h, h + 1)
        normed_ref[:, at] = (a_ref[at].astype(jnp.float32) * inverse).astype(jnp.bfloat16).T
        up_a, down_a = up_ref[FIRST, at], down_ref[FIRST, at]
        k2, qz = jnp.where(half, down_a, up_a), jnp.where(half, up_a, down_a)
        v2 = jnp.where(half, down_ref[SECOND, at], up_ref[SECOND, at])
        q, k, v, grad, gz = q_ref[:, at], k_ref[:, at], v_ref[:, at], grad_ref[at], gz_ref[at]
        queries, grads = jnp.concatenate([q, qz], axis=0), jnp.concatenate([grad, gz], axis=1)
        both = score_tile(k, queries)
        products = mm(v, grads, NN)
        own = jnp.exp(jnp.where(causal, both[:, :BLOCK], NEG_BIG) - lse[row])
        ahead = jnp.exp(both[:, BLOCK:] - z_lse[row])
        near = en_ref[at] * near_scale[row]
        own_ds = (own * (products[:, :BLOCK] - delta_ref[row]) * SCALE).astype(jnp.bfloat16)
        ahead_ds = (ahead * (products[:, BLOCK:] - deltaz_ref[row]) * SCALE).astype(jnp.bfloat16)
        near_ds = (near * (mm(v2, grad, NN) - delta_ref[row]) * SCALE).astype(jnp.bfloat16)
        dk_ref[:, at] = mm(jnp.concatenate([own_ds, ahead_ds], axis=1), queries, NN)
        probs = jnp.concatenate([own, ahead], axis=1).astype(jnp.bfloat16)
        dv_ref[:, at] = mm(probs, grads, NT)
        dsx = jnp.where(odd, dsx_ref[at], jnp.zeros_like(dsx_ref[at]))
        dq_ref[:, at] = mm(own_ds, k, TN) + mm(
            jnp.concatenate([near_ds, dsx], axis=0), jnp.concatenate([k2, kx_ref[:, at]], axis=0), TN
        )


def key_scores_kernel(heads, bias_ref, k_ref, far_ref, side_ref, out_ref):
    for h in range(heads):
        at = rows_of(h)
        both = score_tile(k_ref[:, at], jnp.concatenate([far_ref[:, at], side_ref[:, at]], axis=0))
        out_ref[0, at] = both[:, :BLOCK] + bias_ref[KEY_FAR : KEY_FAR + 1]
        out_ref[1, at] = both[:, BLOCK:] + bias_ref[KEY_SIDE : KEY_SIDE + 1]


def final_kernel(
    heads,
    scores_ref,
    far_ref,
    sideq_ref,
    up_ref,
    down_ref,
    side_ref,
    v_ref,
    dq_own_ref,
    dk_own_ref,
    dv_own_ref,
    dq_out,
    dk_out,
    dv_out,
    dq_ref,
    dk_ref,
    dv_ref,
    sems,
):
    place = Place()
    half = place.half
    behind = (place.me >= 2).astype(jnp.float32)
    first = slice(heads * HD, heads * HD + TAIL)
    second = slice(heads * HD + TAIL, heads * HD + 2 * TAIL)
    lse, delta = (
        (joined_rows(jnp.where(half, up_ref[part], down_ref[part])), joined_rows(side_ref[part]))
        for part in (first, second)
    )
    group = range(heads)
    grads, products, tiles, copies = [], [], [], []

    def leave(stage, out, columns):
        copies.append(pltpu.make_async_copy(stage.at[:, columns], out.at[:, columns], sems.at[len(copies)]))
        copies[-1].start()

    for h in group:
        at = rows_of(h)
        up, down = up_ref[at], down_ref[at]
        dqz = jnp.where(half, down, up).T.astype(jnp.float32) * behind
        dq_ref[:, at] = (dq_own_ref[:, at] + dqz).astype(jnp.bfloat16)
        grads.append(jnp.concatenate([jnp.where(half, up, down), side_ref[at]], axis=1))
    leave(dq_ref, dq_out, slice(0, heads * HD))
    for h, grad in zip(group, grads):
        products.append(mm(v_ref[:, rows_of(h)], grad, NN))
    for h, product in zip(group, products):
        row = slice(h, h + 1)
        probs = [jnp.exp(scores_ref[n, rows_of(h)] - lse[n][row]) for n in range(2)]
        scores = [
            probs[n] * (product[:, n * BLOCK : (n + 1) * BLOCK] - delta[n][row]) * SCALE for n in range(2)
        ]
        tiles.append([jnp.concatenate(pair, axis=1).astype(jnp.bfloat16) for pair in (probs, scores)])
    for h, grad, (probs, scores) in zip(group, grads, tiles):
        at = rows_of(h)
        queries = jnp.concatenate([far_ref[:, at], sideq_ref[:, at]], axis=0)
        dk_ref[:, at] = (dk_own_ref[:, at] + mm(scores, queries, NN)).astype(jnp.bfloat16)
        dv_ref[:, at] = (dv_own_ref[:, at] + mm(probs, grad, NT)).astype(jnp.bfloat16)
        if h % (heads // 2) == heads // 2 - 1:
            columns = slice((h + 1 - heads // 2) * HD, (h + 1) * HD)
            leave(dk_ref, dk_out, columns)
            leave(dv_ref, dv_out, columns)
    for copy in copies:
        copy.wait()


def call(kernel, heads, flags, arrays, outs, flops, space=pltpu.VMEM, scratch=(), after=(), out_space=pltpu.VMEM):
    moved = sum(math.prod(a.shape) * a.dtype.itemsize for a in (*arrays, *outs)) if flops else 0
    return pl.pallas_call(
        lambda *refs: kernel(heads, *refs[len(after) :]),
        out_shape=outs,
        in_specs=[pl.BlockSpec(memory_space=pl.ANY)] * len(after)
        + [pl.BlockSpec(memory_space=pltpu.SMEM)] * len(flags)
        + [pl.BlockSpec(memory_space=space)] * len(arrays),
        out_specs=[pl.BlockSpec(memory_space=out_space)] * len(outs),
        scratch_shapes=scratch,
        compiler_params=pltpu.CompilerParams(vmem_limit_bytes=24 * 2**20),
        cost_estimate=pl.CostEstimate(flops=flops, bytes_accessed=moved, transcendentals=0),
    )(*after, *flags, *arrays)


def cycles(blocks, members):
    route = []
    for block in range(blocks):
        for member in range(members):
            rising = member < members // 2
            other = member + members // 2 if rising else member - members // 2
            target = block + 2 if rising else block - 2
            inside = 0 <= target < blocks
            route.append(
                (block * members + member, target * members + member if inside else block * members + other)
            )
    return route


def meeting_shards(queries, keys, values, pattern, upstream):
    tokens, width = queries.shape
    heads = width // HD
    blocks, members = lax.axis_size("ctx"), lax.axis_size("head")
    unit = heads * 2 * BLOCK**3
    rising = cycles(blocks, members)
    falling = [(target, source) for source, target in rising]

    def cycle(up_array, down_array):
        return lax.ppermute(up_array, ("ctx", "head"), rising), lax.ppermute(
            down_array, ("ctx", "head"), falling
        )

    def swap(array):
        return lax.ppermute(array, "ctx", [(i, i ^ 1) for i in range(blocks)])

    def ring(array, distance):
        return lax.ppermute(array, "ctx", [(i, (i + distance) % blocks) for i in range(blocks)])

    def struct(*shape, dtype=jnp.bfloat16):
        return jax.ShapeDtypeStruct(shape, dtype)

    wide = struct(tokens, width, dtype=jnp.float32)
    wide_t = struct(width, tokens, dtype=jnp.float32)
    flat, flat_t = struct(tokens, width), struct(width, tokens)
    message = struct(width + TAIL, tokens)
    rows = struct(8, tokens, dtype=jnp.float32)

    payload = call(
        payload_kernel,
        heads,
        (),
        [pltpu.with_memory_space_constraint(a, pltpu.HBM) for a in (queries, keys, values, upstream)],
        [pltpu.VMEM((2 * tokens, width), jnp.bfloat16)] * 2,
        0,
        space=pltpu.HBM,
        scratch=(pltpu.SemaphoreType.DMA((4,)),),
    )
    received = cycle(*payload)
    keys_x, values_x = swap(keys), swap(values)
    diagonal, diagonal_lse, upstream_t, bias = call(
        diagonal_kernel,
        heads,
        (pattern,),
        (queries, keys, values, upstream),
        (wide_t, rows, flat_t, rows),
        3 * unit,
        after=(payload[0],),
    )
    up_out, down_out, *kept = call(
        forward_kernel,
        heads,
        (),
        (bias, *received, queries, keys_x, values_x, diagonal, diagonal_lse),
        (message, message, wide_t, wide_t, wide_t, rows, rows, rows),
        6 * unit,
    )
    ez, ex, en, mz, mx, mn = kept
    up_in, down_in = cycle(up_out, down_out)
    (side_queries,) = call(
        side_queries_kernel, heads, (), (queries, *received), (flat,), 0, after=(mn,)
    )
    side_queries = swap(side_queries)
    (far_queries,) = call(relay_kernel, heads, (), received, (flat,), 0, after=(down_in,))
    far_queries = lax.ppermute(far_queries, "ctx", [(i, i - 2) for i in range(2, blocks - 2)])
    (upstream_zt,) = call(transpose_kernel, heads, (), received, (flat_t,), 0, after=(mn,))
    attention, attention_z, lse, lse_z, sums = call(
        merge_kernel,
        heads,
        (),
        (bias, up_out, down_out, up_in, down_in, upstream_t, upstream_zt),
        (flat_t, flat_t, rows, rows, rows),
        unit // 64,
    )
    others = [
        lax.ppermute(sums, "head", [(i, i ^ step) for i in range(members)]) for step in range(1, members)
    ]
    sums = functools.reduce(jnp.add, others, sums)
    longer = struct(width + 2 * TAIL, tokens)
    up_out, down_out, side_out, side_ds, grad_t, grad_zt, delta, delta_z = call(
        back_kernel,
        heads,
        (),
        (bias, sums, attention, attention_z, lse, lse_z, upstream_t, upstream_zt, *received, keys_x, values_x)
        + (ez, ex, mz, mx),
        (longer, longer, longer, flat_t, flat_t, flat_t, rows, rows),
        0,
        after=(side_queries,),
    )
    returned = cycle(up_out, down_out)
    side_grads = swap(lax.optimization_barrier((side_out, far_queries))[0])
    normed, dq_own, dk_own, dv_own = call(
        local_back_kernel,
        heads,
        (),
        (bias, sums, queries, keys, values, attention, lse, lse_z, grad_t, grad_zt, delta, delta_z, en, mn)
        + (side_ds, keys_x, *received),
        (flat, wide, wide, wide),
        0,
    )
    (key_scores,) = call(
        key_scores_kernel,
        heads,
        (),
        (bias, keys, far_queries, side_queries),
        (struct(2, width, tokens, dtype=jnp.float32),),
        0,
    )
    grad_queries, grad_keys, grad_values = call(
        final_kernel,
        heads,
        (),
        (key_scores, far_queries, side_queries, *returned, side_grads, values, dq_own, dk_own, dv_own),
        (flat, flat, flat),
        6 * unit,
        scratch=(pltpu.VMEM((tokens, width), jnp.bfloat16),) * 3 + (pltpu.SemaphoreType.DMA((5,)),),
        out_space=pltpu.HBM,
    )
    return (normed, grad_queries, grad_keys, grad_values)


def shards(queries, keys, values, pattern, upstream):
    fits = lax.axis_size("ctx") == 8 and lax.axis_size("head") == 4 and queries.shape == (BLOCK, 8 * HD)
    if fits:
        return meeting_shards(queries, keys, values, pattern, upstream)
    return generic_shards(queries, keys, values, pattern, upstream)


def solution(mesh):
    return jax.shard_map(
        shards,
        mesh=mesh,
        in_specs=(P("ctx", "head"), P("ctx", "head"), P("ctx", "head"), P(), P("ctx", "head")),
        out_specs=(P("ctx", "head"), P("ctx", "head"), P("ctx", "head"), P("ctx", "head")),
        check_vma=False,
    )
```
